32 devices in a mesh: dp: 16 (over z, x, core), rank: 2 (over y).
Axes of the slice: x: 2, y: 2, z: 4, core: 2. Of those that a mesh axis runs over, the one named last changes fastest.
Arguments:
- block_input: bfloat16 [8192, 2048], P(('dp', 'rank')), may hold values from -6 to 6
- seq_lens: int32 [32, 3], P(('dp', 'rank')), may hold values from 1 to 170, 256 in all within a row
- attn_gain: float32 [2048], P(('dp', 'rank')), may hold values from 0.1 to 1.9
- latent_down: float32 [1024, 2048], P('rank', 'dp'), may hold values from -0.30935922 to 0.30935922
- latent_gain: float32 [1024], P('rank'), may hold values from 0.1 to 1.9
- latent_up: float32 [1024, 4096], P('rank', 'dp'), may hold values from -0.1875 to 0.1875
- shared_kv: float32 [2048, 256], P(('dp', 'rank')), may hold values from -0.125 to 0.125
- out_proj: float32 [4096, 2048], P(('dp', 'rank')), may hold values from -0.25 to 0.25
- mlp_gain: float32 [2048], P(('dp', 'rank')), may hold values from 0.1 to 1.9
- gate_weight: float32 [2048, 5632], P(('dp', 'rank')), may hold values from -0.125 to 0.125
- up_weight: float32 [2048, 5632], P(('dp', 'rank')), may hold values from -0.125 to 0.125
- down_weight: float32 [5632, 2048], P(('dp', 'rank')), may hold values from -0.078125 to 0.078125
- out_cotangent: bfloat16 [8192, 2048], P(('dp', 'rank')), may hold values from -6 to 6
Outputs:
- block_output: bfloat16 [8192, 2048], P(('dp', 'rank'))
- input_grad: bfloat16 [8192, 2048], P(('dp', 'rank'))
- attn_gain_grad: float32 [2048], P(('dp', 'rank'))
- latent_down_grad: float32 [1024, 2048], P('rank', 'dp')
- latent_gain_grad: float32 [1024], P('rank')
- latent_up_grad: float32 [1024, 4096], P('rank', 'dp')
- shared_kv_grad: float32 [2048, 256], P(('dp', 'rank'))
- out_proj_grad: float32 [4096, 2048], P(('dp', 'rank'))
- mlp_gain_grad: float32 [2048], P(('dp', 'rank'))
- gate_grad: float32 [2048, 5632], P(('dp', 'rank'))
- up_grad: float32 [2048, 5632], P(('dp', 'rank'))
- down_grad: float32 [5632, 2048], P(('dp', 'rank'))
The draws below stay inside these ranges and needn't reach their ends.
Inputs may be any that keep to these rules, and one draw needn't show every extreme that they name: `seq_lens`: row b lists the lengths of the 3 sequences of block b in order; they sum to 256 and the longest of each row is exactly 170.
All inputs are finite; a program needn't handle non-finite values.
Results may differ from the reference program's by a relative error of at most 0.015.
The reference program's roundings to bfloat16 on the way count: a program that leaves them out, or rounds other values in their place, can miss the bound.
Values may be sent and summed in bfloat16 or wider, within the bound.
A program may use at most 384 MiB of HBM per device.

```python
import math
import jax
import jax.numpy as jnp
import numpy as np
from jax import lax

D = 2048
LATENT = 1024
HEADS = 16
HEAD_DIM = 256
FF = 5632
TOK_DEV = 256
SEQS = 3
SEQ_MOST = 170
TOKENS = 8192
DEVICES = 32


def draw_latent_down(key, part):
    key_one = jax.random.fold_in(key, 11)
    key_two = jax.random.fold_in(key, 12)
    row_index = jnp.arange(LATENT, dtype=jnp.float32)
    rising = 0.5 + 1.5 * row_index / LATENT
    jitter = jnp.exp(jax.random.uniform(key_two, (LATENT, 1), minval=-0.3, maxval=0.3))
    base_draw = jnp.clip(jax.random.normal(key_one, (LATENT, D)), -5.0, 5.0)
    return (base_draw * (rising[:, None] * jitter) * D ** (-0.5)).astype(jnp.float32)


def spiked(drawn, stream_key, source, target, blocks, factor):
    owner, partner = [(jnp.arange(drawn.shape[dim]) // (drawn.shape[dim] // blocks)).reshape([-1 if axis == dim else 1 for axis in range(drawn.ndim)]) for dim in (source, target)]
    chosen = jax.random.permutation(stream_key, blocks)[partner]
    strong = (owner == chosen) | (owner == (partner + blocks // 2) % blocks)
    return jnp.where(strong, factor * drawn, drawn)


def steps_of(rng, shape, shards, least, high):
    loudness, own = 1.0, jax.random.fold_in(rng, 6)
    for axis_at, parts in shards:
        steps = jnp.exp(jax.random.uniform(jax.random.fold_in(own, axis_at), (parts,), jnp.float32, least / len(shards), high / len(shards)))
        loudness = loudness * jnp.repeat(steps, shape[axis_at] // parts).reshape([-1 if axis == axis_at else 1 for axis in range(len(shape))])
    return loudness


def profile(count, total, most, slope):
    weights = [(1 << 20) // math.isqrt(standing ** slope) + 1 for standing in range(2, count + 1)]
    surplus, holding = total - most - (count - 1), [1] * (count - 1)
    while surplus > 0:
        free = [i for i in range(count - 1) if holding[i] < most]
        whole, left = sum([weights[i] for i in free]), surplus
        for i in free:
            extra = min(most - holding[i], max(1, left * weights[i] // whole), surplus)
            holding[i] = holding[i] + extra
            surplus = surplus - extra
    return np.array([most] + holding)


def uneven(rng, amount, total, bound, lean):
    if amount == 2:
        one = jax.random.randint(rng, (), max(1, total - bound), min(bound, total - 1) + 1)
        return jnp.stack([one, total - one])
    sizes = jnp.asarray(profile(amount, total, bound, lean), jnp.int32)
    pairs = (amount - 1) // 2
    source_of, receiver = sizes[1:1 + 2 * pairs:2], sizes[2:2 + 2 * pairs:2]
    room = jnp.minimum(source_of - 1, bound - receiver)
    shifted = jax.random.randint(jax.random.fold_in(rng, 1), (pairs,), 0, 1 << 20) % (room + 1)
    sizes = sizes.at[1:1 + 2 * pairs:2].set(source_of - shifted).at[2:2 + 2 * pairs:2].set(receiver + shifted)
    return sizes[jax.random.permutation(jax.random.fold_in(rng, 2), amount)]


def normal_values(own_key, shape, deviation, limit, cuts=(), held_as=jnp.bfloat16):
    values = jax.random.normal(own_key, shape, jnp.float32) * deviation
    if len(cuts) > 0:
        values = steps_of(own_key, shape, cuts, -0.22, 0.18) * values
    return jnp.clip(values, min=-limit, max=limit).astype(held_as)


def heavy_noise(own_key, extent, scale, bound, cuts, heavy, kind=jnp.bfloat16):
    array = scale * jax.random.normal(own_key, extent, jnp.float32)
    if cuts:
        array = array * steps_of(own_key, extent, cuts, -0.22, 0.18)
    return jnp.clip(spiked(array, jax.random.fold_in(own_key, 3), *heavy), -bound, bound).astype(kind)


def setup_inputs(seed: int = 0) -> dict:
    seeds = jax.random.split(jax.random.key(seed), 14)
    return {
        "block_input": heavy_noise(seeds[0], (TOKENS, D), 1.0, 6.0, ((0, 32),), (0, 1, 32, 2.75)),
        "seq_lens": jax.vmap(lambda own: uneven(own, SEQS, TOK_DEV, SEQ_MOST, 1))(jax.random.split(seeds[1], DEVICES)).reshape((DEVICES, SEQS)).astype(jnp.int32),
        "attn_gain": jnp.clip(1.0 + 0.18 * jax.random.normal(seeds[2], (D,), jnp.float32), 0.1, 1.9),
        "latent_down": draw_latent_down(jax.random.fold_in(seeds[13], 71), 0),
        "latent_gain": jnp.clip(1.0 + 0.18 * jax.random.normal(seeds[4], (LATENT,), jnp.float32), 0.1, 1.9),
        "latent_up": normal_values(seeds[5], (LATENT, HEADS * HEAD_DIM), LATENT ** -0.5, 0.1875, ((0, 2), (1, 16)), jnp.float32),
        "shared_kv": normal_values(seeds[6], (D, HEAD_DIM), D ** -0.5, 0.125, ((0, 32),), jnp.float32),
        "out_proj": normal_values(seeds[7], (HEADS * HEAD_DIM, D), (HEADS * HEAD_DIM // 8) ** -0.5, 0.25, ((0, 32),), jnp.float32),
        "mlp_gain": jnp.clip(1.0 + 0.18 * jax.random.normal(seeds[8], (D,), jnp.float32), 0.1, 1.9),
        "gate_weight": normal_values(seeds[9], (D, FF), D ** -0.5, 0.125, ((0, 32),), jnp.float32),
        "up_weight": normal_values(seeds[10], (D, FF), D ** -0.5, 0.125, ((0, 32),), jnp.float32),
        "down_weight": normal_values(seeds[11], (FF, D), FF ** -0.5, 0.078125, ((0, 32),), jnp.float32),
        "out_cotangent": normal_values(seeds[12], (TOKENS, D), 1.0, 6.0, ((0, 32),)),
    }


EPS = 1e-06
NEGATIVE = -1e+30

@jax.custom_vjp
def low(v):
    return lax.optimization_barrier(v.astype(jnp.bfloat16)).astype(jnp.float32)

@jax.custom_vjp
def low_back(v):
    return v

def low_keep(v):
    return (low(v), None)

def low_pass(kept, grad):
    return (grad,)

def back_keep(v):
    return (v, None)

def back_low(kept, grad):
    return (low(grad),)
low.defvjp(low_keep, low_pass)
low_back.defvjp(back_keep, back_low)

def layout(lengths, count):
    ends = jnp.cumsum(lengths)
    starts = ends - lengths
    places = jnp.arange(count, dtype=jnp.int32)
    segment = lax.optimization_barrier(jnp.sum((places[:, None] >= ends[None, :]).astype(jnp.int32), axis=1))
    member = segment[:, None] == jnp.arange(lengths.shape[0], dtype=jnp.int32)[None, :]
    offset = lax.optimization_barrier(jnp.sum(jnp.where(member, starts[None, :], 0), axis=1)).astype(jnp.int32)
    position = (places - offset).astype(jnp.float32)
    allowed = (segment[:, None] == segment[None, :]) & (places[None, :] <= places[:, None])
    return (position, allowed)

def rope_tables(position, width):
    half = width // 2
    steps = jnp.arange(half, dtype=jnp.float32)
    freqs = jnp.exp(steps * (-math.log(10000.0) / half))
    angles = position[:, None] * freqs[None, :]
    return (jnp.cos(angles), jnp.sin(angles))

def rotate(values, cosine, sine):
    half = values.shape[-1] // 2
    first = values[..., :half]
    second = values[..., half:]
    return jnp.concatenate([first * cosine - second * sine, second * cosine + first * sine], axis=-1)

def attend(pieces):
    q_rot, k_rot, values, lengths = pieces
    count = k_rot.shape[0]
    position, allowed = layout(lengths, count)
    raw = jnp.einsum('thd,sd->hts', q_rot, k_rot, precision=lax.Precision.HIGHEST) * HEAD_DIM ** (-0.5)
    scores = jnp.where(allowed[None], low_back(raw), NEGATIVE)
    peak = lax.optimization_barrier(jnp.max(scores, axis=-1, keepdims=True))
    expo = jnp.exp(scores - peak)
    probs = expo / lax.optimization_barrier(jnp.sum(expo, axis=-1, keepdims=True))
    return jnp.einsum('hts,sd->thd', low(probs), values, precision=lax.Precision.HIGHEST)

def forward(inputs, attn_gain, latent_down, latent_gain, latent_up, shared_kv, out_proj, mlp_gain, gate_weight, up_weight, down_weight, seq_lens):
    exact = lax.Precision.HIGHEST
    tokens = inputs.shape[0]
    blocks = seq_lens.shape[0]
    count = tokens // blocks
    rms_one = lax.rsqrt(lax.optimization_barrier(jnp.mean(inputs * inputs, axis=-1, keepdims=True)) + EPS)
    normed = low(inputs * rms_one * low(attn_gain))
    latent = low_back(jnp.dot(normed, low(latent_down).T, precision=exact))
    rms_lat = lax.rsqrt(lax.optimization_barrier(jnp.mean(latent * latent, axis=-1, keepdims=True)) + EPS)
    latent_n = low(latent * rms_lat * latent_gain)
    queries = low_back(jnp.dot(latent_n, low(latent_up), precision=exact))
    shared = low_back(jnp.dot(normed, low(shared_kv), precision=exact))
    position = jax.vmap(lambda lengths: layout(lengths, count)[0])(seq_lens).reshape(tokens)
    cosine, sine = rope_tables(position, HEAD_DIM)
    q_rot = low(rotate(queries.reshape(tokens, HEADS, HEAD_DIM), cosine[:, None], sine[:, None]))
    k_rot = low(rotate(shared, cosine, sine))
    values = low(shared)
    attended = lax.map(jax.checkpoint(attend), (q_rot.reshape(blocks, count, HEADS, HEAD_DIM), k_rot.reshape(blocks, count, HEAD_DIM), values.reshape(blocks, count, HEAD_DIM), seq_lens))
    attended = low(low_back(attended.reshape(tokens, HEADS * HEAD_DIM)))
    branch = low_back(jnp.dot(attended, low(out_proj), precision=exact))
    middle = inputs + branch
    rms_two = lax.rsqrt(lax.optimization_barrier(jnp.mean(middle * middle, axis=-1, keepdims=True)) + EPS)
    normed_two = low(middle * rms_two * low(mlp_gain))
    gate = low_back(jnp.dot(normed_two, low(gate_weight), precision=exact))
    upval = low_back(jnp.dot(normed_two, low(up_weight), precision=exact))
    hidden = low(jax.nn.silu(gate) * upval)
    return middle + jnp.dot(hidden, low(down_weight), precision=exact)

def reference(block_input, seq_lens, attn_gain, latent_down, latent_gain, latent_up, shared_kv, out_proj, mlp_gain, gate_weight, up_weight, down_weight, out_cotangent):
    params = (block_input.astype(jnp.float32), attn_gain, latent_down, latent_gain, latent_up, shared_kv, out_proj, mlp_gain, gate_weight, up_weight, down_weight)

    def wrapped(*values):
        return forward(*values, seq_lens)
    result, pullback = jax.vjp(wrapped, *params)
    grads = pullback(out_cotangent.astype(jnp.float32))
    return (result.astype(jnp.bfloat16), grads[0].astype(jnp.bfloat16), grads[1], grads[2], grads[3], grads[4], grads[5], grads[6], grads[7], grads[8], grads[9], grads[10])
```

```python
import functools
import math

import jax
import jax.numpy as jnp
from jax import lax
from jax.sharding import Mesh
from jax.sharding import PartitionSpec as P

HEADS = 16
HEAD_DIM = 256
EPS = 1e-06
NEGATIVE = -1e30
F32 = jnp.float32
BF16 = jnp.bfloat16


def contract(left, right, left_dim, right_dim):
    return lax.dot_general(
        left, right, (((left_dim,), (right_dim,)), ((), ())), preferred_element_type=F32
    )


def after(value, *first):
    return lax.optimization_barrier((value, *first))[0]


def layout(lengths, count):
    spots = jnp.arange(lengths.shape[-1], dtype=jnp.int32)
    ends = jnp.sum(jnp.where(spots[None, :] <= spots[:, None], lengths[..., None, :], 0), axis=-1)
    places = jnp.arange(count, dtype=jnp.int32)
    passed = places[:, None] >= ends[..., None, :]
    segment = jnp.sum(passed.astype(jnp.int32), axis=-1)
    offset = jnp.sum(jnp.where(passed, lengths[..., None, :], 0), axis=-1)
    position = (places - offset).astype(F32)
    same = segment[..., :, None] == segment[..., None, :]
    return position, same & (places[None, :] <= places[:, None])


def rope_tables(position, width):
    half = width // 2
    steps = jnp.arange(half, dtype=F32)
    freqs = jnp.exp(steps * (-math.log(10000.0) / half))
    angles = position[..., None] * freqs
    return jnp.cos(angles), jnp.sin(angles)


def rotate(values, cosine, sine):
    half = values.shape[-1] // 2
    first, second = values[..., :half], values[..., half:]
    return jnp.concatenate(
        [first * cosine - second * sine, second * cosine + first * sine], axis=-1
    )


def unrotate(grads, cosine, sine):
    return rotate(grads, cosine, -sine)


def line_gather(block, count):
    place = lax.axis_index("f")
    full = lax.dynamic_update_index_in_dim(
        jnp.zeros((count, *block.shape), block.dtype), block, place, 0
    )
    ups, downs = [block], [block]
    for step in range(1, count):
        ups.append(
            lax.ppermute(ups[-1], "f", [(i, i + 1) for i in range(step - 1, count - 1)])
        )
        downs.append(
            lax.ppermute(downs[-1], "f", [(i, i - 1) for i in range(1, count - step + 1)])
        )
    for step in range(1, count):
        got = jnp.where(place >= step, ups[step], downs[count - step])
        full = lax.dynamic_update_index_in_dim(full, got, lax.rem(place - step + count, count), 0)
    return full


def line_scatter(parts, count):
    place = lax.axis_index("f")

    def part(at):
        return lax.dynamic_index_in_dim(parts, lax.rem(at + 2 * count, count), 0, keepdims=False)

    up = down = None
    for step in range(1, count):
        mine_up, mine_down = part(place - step), part(place + step)
        if up is not None:
            mine_up, mine_down = mine_up + up.astype(F32), mine_down + down.astype(F32)
        up = lax.ppermute(mine_up.astype(BF16), "f", [(i, i + 1) for i in range(min(step, count - 1))])
        down = lax.ppermute(
            mine_down.astype(BF16), "f", [(i, i - 1) for i in range(count - step, count)]
        )
    return part(place) + up.astype(F32) + down.astype(F32)


SWAP = [(0, 1), (1, 0)]
DIAGONAL = [(0, 3), (3, 0), (1, 2), (2, 1)]


def plane_gather(block):
    half = block.shape[0] // 2
    by_x, by_y = lax.ppermute(block, "x", SWAP), lax.ppermute(block, "y", SWAP)
    by_both = jnp.concatenate(
        [lax.ppermute(by_x[:half], "y", SWAP), lax.ppermute(by_y[half:], "x", SWAP)], axis=0
    )
    chips = [block, by_y, by_x, by_both]
    others = [lax.ppermute(a, "c", SWAP) for a in chips]
    order = [chips[0], chips[1], others[0], others[1], chips[2], chips[3], others[2], others[3]]
    return jnp.stack(order)


def plane_scatter(parts):
    low = parts.astype(BF16)
    sums = []
    for chip, (near, far) in enumerate(((0, 2), (1, 3), (4, 6), (5, 7))):
        sums.append(parts[near].astype(F32) + lax.ppermute(low[far], "c", SWAP).astype(F32))
    by_y = lax.ppermute(sums[1].astype(BF16), "y", SWAP)
    by_x = lax.ppermute(sums[2].astype(BF16), "x", SWAP)
    by_both = lax.ppermute(sums[3].astype(BF16), ("x", "y"), DIAGONAL)
    return sums[0] + by_x.astype(F32) + by_y.astype(F32) + by_both.astype(F32)


def place_in_plane():
    return 4 * lax.axis_index("x") + 2 * lax.axis_index("c") + lax.axis_index("y")


def relabel(blocks):
    place = place_in_plane()
    full = jnp.zeros_like(blocks)
    for i in range(8):
        full = lax.dynamic_update_index_in_dim(full, blocks[i], place ^ i, 0)
    return full


def by_owner(array, axis, count, f_first):
    lead, size, tail = array.shape[:axis], array.shape[axis], array.shape[axis + 1 :]
    part = size // (8 * count)
    n = len(lead)
    rest = [*range(n), n + 4, *range(n + 5, n + 5 + len(tail))]
    if f_first:
        array = array.reshape(*lead, count, 2, 2, 2, part, *tail)
        array = array.transpose(n, n + 1, n + 2, n + 3, *rest)
    else:
        array = array.reshape(*lead, 2, 2, count, 2, part, *tail)
        array = array.transpose(n + 2, n, n + 1, n + 3, *rest)
    return array.reshape(count, 8, *lead, part, *tail)


def from_owner(array, axis, f_first):
    count, _, *body = array.shape
    lead, part, tail = body[:axis], body[axis], body[axis + 1 :]
    n = axis
    array = array.reshape(count, 2, 2, 2, *body)
    inner = (0, 1, 2, 3) if f_first else (1, 2, 0, 3)
    array = array.transpose(
        *range(4, 4 + n), *inner, 4 + n, *range(5 + n, 5 + n + len(tail))
    )
    return array.reshape(*lead, 8 * count * part, *tail)


def scores_of(q_rot, k_rot, allowed):
    raw = jnp.einsum("bthd,bsd->bhts", q_rot, k_rot, preferred_element_type=F32)
    return jnp.where(allowed[:, None], raw * HEAD_DIM**-0.5, NEGATIVE)


def per_device(
    count,
    f_first,
    block_input,
    seq_lens,
    attn_gain,
    latent_down,
    latent_gain,
    latent_up,
    shared_kv,
    out_proj,
    mlp_gain,
    gate_weight,
    up_weight,
    down_weight,
    out_cotangent,
):
    tokens, width = block_input.shape
    rank = 2 * latent_down.shape[0]
    half_rank = latent_down.shape[0]
    units = down_weight.shape[0]
    mine = units * count
    padded = -(-mine // 256) * 256
    y = lax.axis_index("y")
    place = lax.axis_index("f")
    x_c = 2 * lax.axis_index("x") + lax.axis_index("c")

    def rows_of(array):
        flat = array.reshape(-1)
        lines = -(-flat.shape[0] // 128)
        return jnp.pad(flat, (0, lines * 128 - flat.shape[0])).reshape(lines, 128)

    gain_high = latent_gain.astype(BF16)
    gain_low = (latent_gain - gain_high.astype(F32)).astype(BF16)
    pieces = [
        latent_down.astype(BF16).reshape(-1, 128),
        shared_kv.astype(BF16).reshape(-1, 2, 128).transpose(1, 0, 2).reshape(-1, 128),
        rows_of(gain_high),
        rows_of(gain_low),
        rows_of(attn_gain.astype(BF16)),
        rows_of(mlp_gain.astype(BF16)),
        rows_of(seq_lens.astype(BF16)),
    ]
    marks = [0]
    for piece in pieces:
        marks.append(marks[-1] + piece.shape[0])
    total = -(-marks[-1] // 32) * 32
    first = jnp.pad(jnp.concatenate(pieces), ((0, total - marks[-1]), (0, 0)))
    first = line_gather(first, count)
    first = plane_gather(first.reshape(count * total, 128)).reshape(8, count, total, 128)
    lengths = lax.dynamic_index_in_dim(first[:, :, marks[6], :3], place, 1, keepdims=False)
    lengths = lengths.astype(jnp.int32)
    first = relabel(first)
    owned = first.transpose(1, 0, 2, 3)

    def piece_of(i):
        return owned[:, :, marks[i] : marks[i + 1]]

    columns = width // (4 * count)
    down_full = piece_of(0).reshape(count, 2, 2, 2, half_rank, columns)
    down_full = down_full.transpose((3, 4, 0, 1, 2, 5) if f_first else (3, 4, 1, 2, 0, 5))
    down_full = down_full.reshape(rank, width)
    kv_rows = shared_kv.shape[0]
    kv_full = piece_of(1).reshape(count, 8, 2, kv_rows, 128).transpose(0, 1, 3, 2, 4)
    kv_full = from_owner(kv_full.reshape(count, 8, kv_rows, HEAD_DIM), 0, f_first)
    gain_lat = (piece_of(2)[0, :2].astype(F32) + piece_of(3)[0, :2].astype(F32)).reshape(rank)
    gain_rows = attn_gain.shape[0]

    def gain_of(i):
        return from_owner(piece_of(i).reshape(count, 8, -1)[:, :, :gain_rows], 0, f_first)

    gain_one, gain_two = gain_of(4).astype(F32), gain_of(5).astype(F32)

    up_line = line_gather(after(latent_up.astype(BF16), first), count)
    out_line = line_gather(after(out_proj.astype(BF16), first), count)
    up_heads = up_line.transpose(1, 0, 2).reshape(half_rank, 4, HEAD_DIM)
    per_head = count // 4
    out_heads = out_line.reshape(4, per_head, -1, width)

    def own_heads(array, axis):
        return lax.dynamic_slice_in_dim(array, 2 * y, 2, axis)

    def other_heads(array, axis):
        return lax.dynamic_slice_in_dim(array, 2 - 2 * y, 2, axis)

    def join(own, other, axis):
        low = jnp.where(y == 0, own, other)
        high = jnp.where(y == 0, other, own)
        return jnp.stack([low, high], axis)

    up_full = join(own_heads(up_heads, 1), lax.ppermute(other_heads(up_heads, 1), "y", SWAP), 0)
    up_full = up_full.reshape(rank, 2 * HEAD_DIM)
    out_full = join(own_heads(out_heads, 0), lax.ppermute(other_heads(out_heads, 0), "y", SWAP), 2)
    out_full = out_full.reshape(2 * HEAD_DIM, width)

    def unit_blocks(weight):
        blocks = by_owner(weight.astype(BF16), 1, count, f_first)
        blocks = blocks.transpose(1, 2, 0, 3).reshape(8, -1, mine)
        return jnp.pad(blocks, ((0, 0), (0, 0), (0, padded - mine)))

    both = jnp.concatenate([unit_blocks(gate_weight), unit_blocks(up_weight)], axis=2)
    both = lax.all_to_all(both, ("x", "c", "y"), 0, 0, tiled=True)
    both = line_gather(after(both, up_line, out_line), count)
    both = from_owner(both, 0, f_first)
    ff_down = line_gather(after(down_weight.astype(BF16), up_line, out_line), count)
    ff_down = jnp.pad(ff_down.reshape(mine, width), ((0, padded - mine), (0, 0)))

    inputs = block_input.astype(F32)
    rms_one = lax.rsqrt(jnp.mean(inputs * inputs, axis=-1, keepdims=True) + EPS)
    normed = (inputs * rms_one * gain_one).astype(BF16)
    latent = contract(normed, down_full, 1, 1)
    rms_lat = lax.rsqrt(jnp.mean(latent * latent, axis=-1, keepdims=True) + EPS)
    latent_n = (latent * rms_lat * gain_lat).astype(BF16)
    shared = jnp.dot(normed, kv_full, preferred_element_type=F32)
    position, allowed = layout(lengths, tokens)
    cosine, sine = rope_tables(position, HEAD_DIM)
    k_own = rotate(shared, cosine[0], sine[0]).astype(BF16)

    parcel = plane_gather(jnp.concatenate([latent_n, k_own, shared.astype(BF16)], axis=1))
    lat_all = parcel[:, :, :rank].reshape(8 * tokens, rank)
    k_rot = parcel[:, :, rank : rank + HEAD_DIM]
    values = parcel[:, :, rank + HEAD_DIM :]
    g_all = plane_gather(after(out_cotangent, parcel)).reshape(8 * tokens, width)
    queries = jnp.dot(lat_all, up_full, preferred_element_type=F32)
    wide_cos, wide_sin = cosine[:, :, None], sine[:, :, None]
    q_rot = rotate(queries.reshape(8, tokens, 2, HEAD_DIM), wide_cos, wide_sin).astype(BF16)
    scores = scores_of(q_rot, k_rot, allowed)
    peak = jnp.max(scores, axis=-1, keepdims=True)
    log_total = peak + jnp.log(jnp.sum(jnp.exp(scores - peak), axis=-1, keepdims=True))
    probs = jnp.exp(scores - log_total)
    attended = jnp.einsum("bhts,bsd->bthd", probs.astype(BF16), values, preferred_element_type=F32)
    attended = attended.reshape(8 * tokens, 2 * HEAD_DIM).astype(BF16)
    branch = jnp.dot(attended, out_full, preferred_element_type=F32)
    branch = plane_scatter(branch.reshape(8, tokens, width))

    middle = inputs + branch
    rms_two = lax.rsqrt(jnp.mean(middle * middle, axis=-1, keepdims=True) + EPS)
    normed_two = (middle * rms_two * gain_two).astype(BF16)
    two_all = plane_gather(normed_two).reshape(8 * tokens, width)
    gate_up = jnp.dot(two_all, both, preferred_element_type=F32)
    gate, upval = gate_up[:, :padded], gate_up[:, padded:]
    sigma = jax.nn.sigmoid(gate)
    hidden = (gate * sigma * upval).astype(BF16)

    d_hidden = contract(g_all, ff_down, 1, 1)
    d_gate = (d_hidden * upval * sigma * (1.0 + gate * (1.0 - sigma))).astype(BF16)
    d_up = (d_hidden * gate * sigma).astype(BF16)
    d_both = jnp.concatenate([d_gate, d_up], axis=1)
    d_two = plane_scatter(contract(d_both, both, 1, 1).reshape(8, tokens, width))

    result = jnp.dot(hidden, ff_down, preferred_element_type=F32)
    result = plane_scatter(after(result.reshape(8, tokens, width), d_two))
    block_output = (middle + result).astype(BF16)

    both_grad = contract(two_all, d_both, 0, 0)
    both_grad = line_scatter(by_owner(both_grad, 0, count, f_first), count)
    both_grad = lax.all_to_all(both_grad.astype(BF16), ("x", "c", "y"), 0, 0, tiled=True)

    def whole_rows(blocks):
        blocks = blocks[:, :, :mine].astype(F32).reshape(8, -1, count, units)
        return from_owner(blocks.transpose(2, 0, 1, 3), 1, f_first)

    gate_grad, up_grad = whole_rows(both_grad[..., :padded]), whole_rows(both_grad[..., padded:])
    down_grad = contract(hidden, g_all, 0, 0)[:mine].reshape(count, units, width)
    down_grad = line_scatter(down_grad, count)

    upstream = out_cotangent.astype(F32)
    gain_two_part = jnp.sum(d_two * middle * rms_two, axis=0)
    scaled_two = d_two * gain_two
    d_middle = (
        upstream
        + rms_two * scaled_two
        - middle * (rms_two**3) * jnp.mean(scaled_two * middle, axis=-1, keepdims=True)
    )

    d_branch = plane_gather(d_middle.astype(BF16)).reshape(8 * tokens, width)
    d_attended = contract(d_branch, out_full, 1, 1).astype(BF16)
    d_attended = d_attended.reshape(8, tokens, 2, HEAD_DIM)
    d_probs = jnp.einsum("bthd,bsd->bhts", d_attended, values, preferred_element_type=F32)
    inner = jnp.sum(probs * d_probs, axis=-1, keepdims=True)
    d_scores = (probs * (d_probs - inner)).astype(BF16)
    scale = HEAD_DIM**-0.5
    d_qrot = jnp.einsum("bhts,bsd->bthd", d_scores, k_rot, preferred_element_type=F32) * scale
    d_queries = unrotate(d_qrot, wide_cos, wide_sin).astype(BF16)
    d_queries = d_queries.reshape(8 * tokens, 2 * HEAD_DIM)
    d_krot = jnp.einsum("bhts,bthd->bsd", d_scores, q_rot, preferred_element_type=F32) * scale
    value_part = jnp.einsum(
        "bhts,bthd->bsd", probs.astype(BF16), d_attended, preferred_element_type=F32
    )
    shared_part = unrotate(d_krot, cosine, sine) + value_part
    lat_part = contract(d_queries, up_full, 1, 1).reshape(8, tokens, rank)
    back = plane_scatter(jnp.concatenate([lat_part, shared_part], axis=2))
    d_lat_n, d_shared = back[:, :rank], back[:, rank:].astype(BF16)

    up_grad_heads = contract(lat_all, d_queries, 0, 0).reshape(2, half_rank, 2, HEAD_DIM)
    out_grad_heads = contract(attended, d_branch, 0, 0).reshape(2, per_head, 2, -1, width)

    def swap_halves(array, axis):
        own = lax.dynamic_index_in_dim(array, y, axis, keepdims=False)
        other = lax.dynamic_index_in_dim(array, 1 - y, axis, keepdims=False).astype(BF16)
        return own, lax.ppermute(other, "y", SWAP).astype(F32)

    up_line_grad = join(*swap_halves(up_grad_heads, 0), 1).reshape(half_rank, count, -1)
    latent_up_grad = line_scatter(up_line_grad.transpose(1, 0, 2), count)
    out_line_grad = join(*swap_halves(out_grad_heads, 2), 0)
    out_proj_grad = line_scatter(out_line_grad.reshape(count, -1, width), count)

    gain_lat_part = jnp.sum(d_lat_n * latent * rms_lat, axis=0)
    scaled_lat = d_lat_n * gain_lat
    inner_lat = jnp.sum(scaled_lat * latent, axis=-1, keepdims=True)
    d_latent = (rms_lat * scaled_lat - latent * (rms_lat**3) * inner_lat / rank).astype(BF16)
    d_normed = contract(d_shared, kv_full, 1, 1) + jnp.dot(
        d_latent, down_full, preferred_element_type=F32
    )
    gain_one_part = jnp.sum(d_normed * inputs * rms_one, axis=0)
    scaled_one = d_normed * gain_one
    input_grad = (
        d_middle
        + rms_one * scaled_one
        - inputs * (rms_one**3) * jnp.mean(scaled_one * inputs, axis=-1, keepdims=True)
    ).astype(BF16)

    down_part = contract(d_latent, normed, 0, 0)
    if f_first:
        down_part = down_part.reshape(2, half_rank, count, 2, 2, columns).transpose(2, 3, 4, 0, 1, 5)
    else:
        down_part = down_part.reshape(2, half_rank, 2, 2, count, columns).transpose(4, 2, 3, 0, 1, 5)
    down_part = down_part.reshape(count, 8, -1, 128)
    kv_part = by_owner(contract(normed, d_shared, 0, 0), 0, count, f_first)
    kv_part = kv_part.reshape(count, 8, kv_rows, 2, 128).transpose(0, 1, 3, 2, 4)
    kv_part = kv_part.reshape(count, 8, -1, 128)

    def gain_rows_of(part):
        part = by_owner(part, 0, count, f_first)
        return jnp.pad(part, ((0, 0), (0, 0), (0, 128 - gain_rows)))[:, :, None]

    lat_rows = jnp.broadcast_to(
        gain_lat_part.reshape(1, 1, 2, -1, 128), (count, 4, 2, half_rank // 128, 128)
    )
    lat_rows = lat_rows.reshape(count, 8, -1, 128)
    pieces = [down_part, kv_part, lat_rows, gain_rows_of(gain_one_part), gain_rows_of(gain_two_part)]
    marks = [0]
    for piece in pieces:
        marks.append(marks[-1] + piece.shape[2])
    last_rows = -(-marks[-1] // 32) * 32
    last = jnp.pad(jnp.concatenate(pieces, axis=2), ((0, 0), (0, 0), (0, last_rows - marks[-1]), (0, 0)))
    last = relabel(last.transpose(1, 0, 2, 3).astype(BF16))
    last = line_scatter(plane_scatter(last), count)
    latent_down_grad = last[marks[0] : marks[1]].reshape(half_rank, columns)
    shared_kv_grad = last[marks[1] : marks[2]].reshape(2, kv_rows, 128).transpose(1, 0, 2)
    shared_kv_grad = shared_kv_grad.reshape(kv_rows, HEAD_DIM)
    latent_gain_grad = last[marks[2] : marks[3]].reshape(half_rank)
    attn_gain_grad = last[marks[3], :gain_rows]
    mlp_gain_grad = last[marks[4], :gain_rows]
    return (
        block_output,
        input_grad,
        attn_gain_grad,
        latent_down_grad,
        latent_gain_grad,
        latent_up_grad,
        shared_kv_grad,
        out_proj_grad,
        mlp_gain_grad,
        gate_grad,
        up_grad,
        down_grad,
    )


def solution(mesh):
    devices = mesh.devices
    split = devices.shape[0]
    count = split // 4
    f_first = split == HEADS
    if f_first:
        names, sizes = ("f", "x", "c", "y"), (count, 2, 2, 2)
    else:
        names, sizes = ("x", "c", "f", "y"), (2, 2, count, 2)
    fine = Mesh(devices.reshape(sizes), names)
    dp = names[:3]
    return jax.shard_map(
        functools.partial(per_device, count, f_first),
        mesh=fine,
        in_specs=(
            P(names, None),
            P(names, None),
            P(names),
            P("y", dp),
            P("y"),
            P("y", dp),
            P(names, None),
            P(names, None),
            P(names),
            P(names, None),
            P(names, None),
            P(names, None),
            P(names, None),
        ),
        out_specs=(
            P(names, None),
            P(names, None),
            P(names),
            P("y", dp),
            P("y"),
            P("y", dp),
            P(names, None),
            P(names, None),
            P(names),
            P(names, None),
            P(names, None),
            P(names, None),
        ),
        check_vma=False,
    )
```

```python
import functools
import math

import jax
import jax.numpy as jnp
from jax import lax
from jax.experimental import pallas as pl
from jax.experimental.pallas import tpu as pltpu
from jax.sharding import Mesh
from jax.sharding import PartitionSpec as P

HEADS = 16
HEAD_DIM = 256
EPS = 1e-06
NEGATIVE = -1e30
F32 = jnp.float32
BF16 = jnp.bfloat16


def contract(left, right, left_dim, right_dim):
    return lax.dot_general(
        left, right, (((left_dim,), (right_dim,)), ((), ())), preferred_element_type=F32
    )


def after(value, *first):
    return lax.optimization_barrier((value, *first))[0]


def layout(lengths, count):
    spots = jnp.arange(lengths.shape[-1], dtype=jnp.int32)
    ends = jnp.sum(jnp.where(spots[None, :] <= spots[:, None], lengths[..., None, :], 0), axis=-1)
    places = jnp.arange(count, dtype=jnp.int32)
    passed = places[:, None] >= ends[..., None, :]
    segment = jnp.sum(passed.astype(jnp.int32), axis=-1)
    offset = jnp.sum(jnp.where(passed, lengths[..., None, :], 0), axis=-1)
    position = (places - offset).astype(F32)
    same = segment[..., :, None] == segment[..., None, :]
    return position, same & (places[None, :] <= places[:, None])


def rope_tables(position, width):
    half = width // 2
    steps = jnp.arange(half, dtype=F32)
    freqs = jnp.exp(steps * (-math.log(10000.0) / half))
    angles = position[..., None] * freqs
    return jnp.cos(angles), jnp.sin(angles)


def rotate(values, cosine, sine):
    half = values.shape[-1] // 2
    first, second = values[..., :half], values[..., half:]
    return jnp.concatenate(
        [first * cosine - second * sine, second * cosine + first * sine], axis=-1
    )


def unrotate(grads, cosine, sine):
    return rotate(grads, cosine, -sine)


SWAP = [(0, 1), (1, 0)]
DIAGONAL = [(0, 3), (3, 0), (1, 2), (2, 1)]


def plane_scatter(parts):
    low = parts.astype(BF16)
    sums = []
    for near, far in ((0, 2), (1, 3), (4, 6), (5, 7)):
        sums.append(parts[near].astype(F32) + lax.ppermute(low[far], "c", SWAP).astype(F32))
    by_y = lax.ppermute(sums[1].astype(BF16), "y", SWAP)
    by_x = lax.ppermute(sums[2].astype(BF16), "x", SWAP)
    by_both = lax.ppermute(sums[3].astype(BF16), ("x", "y"), DIAGONAL)
    return sums[0] + by_x.astype(F32) + by_y.astype(F32) + by_both.astype(F32)


X_BIT, C_BIT, Y_BIT = 4, 2, 1
VMEM_MOST = 56 * 2**20


def other(bits):
    flips = {"x": bits // 4, "c": bits // 2 % 2, "y": bits % 2}
    return {name: 1 - lax.axis_index(name) for name, flip in flips.items() if flip}


def greet(partners):
    barrier = pltpu.get_barrier_semaphore()
    for partner in partners:
        pl.semaphore_signal(barrier, inc=1, device_id=partner)
    pl.semaphore_wait(barrier, len(partners))


def send(source, target, send_sem, recv_sem, device):
    return pltpu.make_async_remote_copy(
        src_ref=source, dst_ref=target, send_sem=send_sem, recv_sem=recv_sem, device_id=device
    )


def gathering(chunks, in_ref, out_ref, send_sem, recv_sem):
    rows = in_ref.shape[0] // chunks
    both = X_BIT | Y_BIT

    def to(slot, k, bits, source):
        part = pl.ds(k * rows, rows)
        return send(
            source.at[part], out_ref.at[slot, part], send_sem.at[slot, k], recv_sem.at[slot, k], other(bits)
        )

    def own():
        for k in range(chunks):
            to(X_BIT, k, X_BIT, in_ref).start()
            to(Y_BIT, k, Y_BIT, in_ref).start()
        for k in range(chunks):
            to(C_BIT, k, C_BIT, in_ref).start()

    def relay(first, last):
        for k in range(first, last):
            to(X_BIT, k, X_BIT, in_ref).wait_recv()
            if k < chunks // 2:
                to(both, k, Y_BIT, out_ref.at[X_BIT]).start()
            to(X_BIT | C_BIT, k, C_BIT, out_ref.at[X_BIT]).start()
            to(Y_BIT, k, Y_BIT, in_ref).wait_recv()
            if k >= chunks // 2:
                to(both, k, X_BIT, out_ref.at[Y_BIT]).start()
            to(Y_BIT | C_BIT, k, C_BIT, out_ref.at[Y_BIT]).start()

    def far():
        for k in range(chunks):
            to(both, k, Y_BIT, in_ref).wait_recv()
            to(7, k, C_BIT, out_ref.at[both]).start()

    def end():
        for slot in range(1, 8):
            for k in range(chunks):
                copy = to(slot, k, slot, in_ref)
                if slot & C_BIT:
                    copy.wait_recv()
                copy.wait_send()

    return own, relay, far, end


def gather_kernel(chunks, in_ref, out_ref, own_sem, send_sem, recv_sem):
    greet([other(C_BIT), other(X_BIT), other(Y_BIT)])
    copy = pltpu.make_async_copy(in_ref, out_ref.at[0], own_sem)
    copy.start()
    own, relay, far, end = gathering(chunks, in_ref, out_ref, send_sem, recv_sem)
    own()
    relay(0, chunks)
    far()
    copy.wait()
    end()


def plane_gather(block, name, chunks=4):
    return pl.pallas_call(
        functools.partial(gather_kernel, chunks),
        out_shape=jax.ShapeDtypeStruct((8, *block.shape), block.dtype),
        in_specs=[pl.BlockSpec(memory_space=pl.ANY)],
        out_specs=pl.BlockSpec(memory_space=pl.ANY),
        scratch_shapes=[
            pltpu.SemaphoreType.DMA,
            pltpu.SemaphoreType.DMA((8, chunks)),
            pltpu.SemaphoreType.DMA((8, chunks)),
        ],
        compiler_params=pltpu.CompilerParams(collective_id=name, has_side_effects=True),
        cost_estimate=pl.CostEstimate(flops=0, bytes_accessed=160 * 2**20, transcendentals=0),
    )(block)


def matmul_scatter_kernel(flip, wide, *refs):
    left_ref, right_ref, *more_ref, out_ref, part_ref, near_ref, sum_ref, far_ref = refs[:-4]
    near_send, near_recv, chip_send, chip_recv = refs[-4:]
    tokens = out_ref.shape[0]
    step = 256
    greet([other(C_BIT), other(X_BIT), other(Y_BIT), other(X_BIT | Y_BIT)])

    def product(slot, target):
        @pl.loop(0, wide // step)
        def _(i):
            at = pl.ds(pl.multiple_of(i * step, step), step)
            rows = left_ref[slot * tokens : (slot + 1) * tokens, :]
            if flip:
                got = contract(rows, right_ref[at, :], 1, 1)
            else:
                got = contract(rows, right_ref[:, at], 1, 0)
            target[:, at] = got.astype(BF16)

        for ref in more_ref:
            target[:, wide:] = ref[slot * tokens : (slot + 1) * tokens, :].astype(BF16)

    chips = (X_BIT | Y_BIT, X_BIT, Y_BIT, 0)
    near, far = [], []
    for i, chip in enumerate(chips):
        product(chip | C_BIT, part_ref.at[i])
        copy = send(part_ref.at[i], near_ref.at[i], near_send.at[i], near_recv.at[i], other(C_BIT))
        copy.start()
        near.append(copy)
        product(chip, sum_ref.at[i])
        copy.wait_recv()

        @pl.loop(0, tokens // 32)
        def _(r):
            at = pl.ds(pl.multiple_of(r * 32, 32), 32)
            total = sum_ref[i, at, :].astype(F32) + near_ref[i, at, :].astype(F32)
            if chip:
                sum_ref[i, at, :] = total.astype(BF16)
            else:
                out_ref[at, :] = total

        if chip:
            copy = send(sum_ref.at[i], far_ref.at[i], chip_send.at[i], chip_recv.at[i], other(chip))
            copy.start()
            far.append(copy)
    for copy in far:
        copy.wait_recv()

    @pl.loop(0, tokens // 32)
    def _(r):
        at = pl.ds(pl.multiple_of(r * 32, 32), 32)
        total = out_ref[at, :]
        for i in range(3):
            total = total + far_ref[i, at, :].astype(F32)
        out_ref[at, :] = total

    for copy in (*near, *far):
        copy.wait_send()


def matmul_scatter(left, right, name, flip=False, *more):
    tokens, depth = left.shape[0] // 8, left.shape[1]
    wide = right.shape[0 if flip else 1]
    full = wide + sum(array.shape[1] for array in more)
    block = pltpu.VMEM((4, tokens, full), BF16)
    return pl.pallas_call(
        functools.partial(matmul_scatter_kernel, flip, wide),
        out_shape=jax.ShapeDtypeStruct((tokens, full), F32),
        in_specs=[pl.BlockSpec(memory_space=pltpu.VMEM)] * (2 + len(more)),
        out_specs=pl.BlockSpec(memory_space=pltpu.VMEM),
        scratch_shapes=[
            block,
            block,
            block,
            pltpu.VMEM((3, tokens, full), BF16),
            *[pltpu.SemaphoreType.DMA((4,))] * 2,
            *[pltpu.SemaphoreType.DMA((3,))] * 2,
        ],
        compiler_params=pltpu.CompilerParams(
            collective_id=name, has_side_effects=True, vmem_limit_bytes=VMEM_MOST
        ),
        cost_estimate=pl.CostEstimate(
            flops=16 * tokens * wide * depth, bytes_accessed=160 * 2**20, transcendentals=0
        ),
    )(left, right, *more)


def in_plane():
    return 4 * lax.axis_index("x") + 2 * lax.axis_index("c") + lax.axis_index("y")


def start_kernel(
    count, chunks, first_ref, up_ref, out_ref, wide_ref, rows_ref,
    first_all, up_line, out_line, up_far, out_far, wide_all, rows_all,
    local_sem, line_send, line_recv, plane_send, plane_recv, far_send, far_recv, wide_send, wide_recv,
    rows_send, rows_recv,
):
    f, y, me = lax.axis_index("f"), lax.axis_index("y"), in_plane()
    half = count // 2
    barrier = pltpu.get_barrier_semaphore()
    for bits in range(1, 8):
        pl.semaphore_signal(barrier, inc=1, device_id=other(bits))
    lower, upper = f > 0, f < count - 1

    @pl.when(lower)
    def _():
        pl.semaphore_signal(barrier, inc=1, device_id={"f": f - 1})

    @pl.when(upper)
    def _():
        pl.semaphore_signal(barrier, inc=1, device_id={"f": f + 1})

    pl.semaphore_wait(barrier, 7 + lower.astype(jnp.int32) + upper.astype(jnp.int32))

    locals_ = [
        pltpu.make_async_copy(source, target, local_sem.at[i])
        for i, (source, target) in enumerate(
            (
                (first_ref, first_all.at[me, f]),
                (up_ref, up_line.at[f]),
                (out_ref, out_line.at[f]),
                (wide_ref.at[me], wide_all.at[me]),
                (rows_ref, rows_all.at[0]),
            )
        )
    ]
    for copy in locals_:
        copy.start()

    own = (first_ref, up_ref, out_ref)
    lines = (first_all.at[me], up_line, out_line)
    fars = (None, up_far, out_far)

    def hop(i, j, up, source):
        return send(
            source, lines[i].at[j], line_send.at[i, 0 if up else 1, j], line_recv.at[i, j],
            {"f": f + 1 if up else f - 1},
        )

    def line_own(i):
        pl.when(upper)(lambda: hop(i, f, True, own[i]).start())
        pl.when(lower)(lambda: hop(i, f, False, own[i]).start())

    def line_step(i, step, then):
        @pl.when(f - step >= 0)
        def _():
            j = f - step
            hop(i, j, True, lines[i].at[j]).wait_recv()
            pl.when(upper)(lambda: hop(i, j, True, lines[i].at[j]).start())
            then(j, lines[i].at[j])

        @pl.when(f + step <= count - 1)
        def _():
            j = f + step
            hop(i, j, False, lines[i].at[j]).wait_recv()
            pl.when(lower)(lambda: hop(i, j, False, lines[i].at[j]).start())
            then(j, lines[i].at[j])

    def line_end(i):
        for j in range(count):
            pl.when(upper & (f >= j))(lambda: hop(i, j, True, own[i]).wait_send())
            pl.when(lower & (f <= j))(lambda: hop(i, j, False, own[i]).wait_send())

    def spread(slot, bits, j, source):
        return send(
            source, first_all.at[me ^ bits ^ slot, j], plane_send.at[slot, j], plane_recv.at[slot, j], other(bits)
        )

    def to_plane(j, source):
        spread(X_BIT, X_BIT, j, source).start()
        spread(Y_BIT, Y_BIT, j, source).start()
        spread(C_BIT, C_BIT, j, source).start()

    def relay(j):
        by_x, by_y = first_all.at[me ^ X_BIT, j], first_all.at[me ^ Y_BIT, j]
        spread(X_BIT, X_BIT, j, by_x).wait_recv()
        pl.when(j % 2 == 0)(lambda: spread(5, Y_BIT, j, by_x).start())
        spread(6, C_BIT, j, by_x).start()
        spread(Y_BIT, Y_BIT, j, by_y).wait_recv()
        pl.when(j % 2 == 1)(lambda: spread(5, X_BIT, j, by_y).start())
        spread(3, C_BIT, j, by_y).start()

    def relay_far(j):
        by_both = first_all.at[me ^ 5, j]
        spread(5, Y_BIT, j, by_both).wait_recv()
        spread(7, C_BIT, j, by_both).start()

    def in_order(do):
        do(f)
        for step in range(1, count):
            pl.when(f - step >= 0)(lambda: do(f - step))
            pl.when(f + step <= count - 1)(lambda: do(f + step))

    def across(i, slot, source):
        return send(source, fars[i].at[slot], far_send.at[i, slot], far_recv.at[i, slot], other(Y_BIT))

    def swap(i):
        return lambda j, source: pl.when(j // half != y)(lambda: across(i, j % half, source).start())

    def wide(bits):
        return send(wide_ref.at[me ^ bits], wide_all.at[me], wide_send.at[bits], wide_recv.at[bits], other(bits))

    rows_own, rows_relay, rows_far, rows_end = gathering(
        chunks, rows_ref, rows_all, rows_send, rows_recv
    )
    line_own(0)
    to_plane(f, first_ref)
    for step in range(1, count):
        line_step(0, step, to_plane)
        if step == min(2, count - 1):
            line_own(1)
            line_own(2)
    in_order(relay)
    for i in (1, 2):
        swap(i)(f, own[i])
    for bits in (5, 7, 4, 6, 1, 3, 2):
        wide(bits).start()
    rows_own()
    for step in range(1, count):
        line_step(1, step, swap(1))
        line_step(2, step, swap(2))
        if step == 1:
            in_order(relay_far)
        if step == count - 2:
            rows_relay(0, chunks // 2)
    rows_relay(chunks // 2, chunks)
    rows_far()
    for copy in locals_:
        copy.wait()
    rows_end()
    for i in range(3):
        line_end(i)
    for slot in range(1, 8):
        for j in range(count):
            copy = spread(slot, slot, j, first_ref)
            if slot & C_BIT:
                copy.wait_recv()
            copy.wait_send()
    for i in (1, 2):
        for slot in range(half):
            copy = across(i, slot, own[i])
            copy.wait_recv()
            copy.wait_send()
    for bits in range(1, 8):
        wide(bits).wait_recv()
        wide(bits).wait_send()


def start(first, up, out, wide, rows, count, name, chunks=4):
    half = count // 2
    any_space = pl.BlockSpec(memory_space=pl.ANY)
    dma = pltpu.SemaphoreType.DMA
    return pl.pallas_call(
        functools.partial(start_kernel, count, chunks),
        out_shape=[
            jax.ShapeDtypeStruct((8, count, *first.shape), BF16),
            jax.ShapeDtypeStruct((count, *up.shape), BF16),
            jax.ShapeDtypeStruct((count, *out.shape), BF16),
            jax.ShapeDtypeStruct((half, *up.shape), BF16),
            jax.ShapeDtypeStruct((half, *out.shape), BF16),
            jax.ShapeDtypeStruct(wide.shape, BF16),
            jax.ShapeDtypeStruct((8, *rows.shape), BF16),
        ],
        in_specs=[any_space] * 5,
        out_specs=[any_space] * 7,
        scratch_shapes=[
            dma((5,)),
            dma((3, 2, count)), dma((3, count)),
            dma((8, count)), dma((8, count)),
            dma((3, half)), dma((3, half)),
            dma((8,)), dma((8,)),
            dma((8, chunks)), dma((8, chunks)),
        ],
        compiler_params=pltpu.CompilerParams(collective_id=name, has_side_effects=True),
        cost_estimate=pl.CostEstimate(flops=0, bytes_accessed=240 * 2**20, transcendentals=0),
    )(first, up, out, wide, rows)


def end_kernel(
    count, last_ref, up_ref, out_ref, wide_ref,
    last_sum, up_sum, out_sum, wide_all,
    total_ref, near_ref, chip_ref, far_ref, *rest,
):
    grown = [rest[4 * i : 4 * i + 4] for i in range(3)]
    local_sem, near_send, near_recv, chip_send, chip_recv, line_send, line_recv, wide_send, wide_recv = rest[12:]
    f, me = lax.axis_index("f"), in_plane()
    barrier = pltpu.get_barrier_semaphore()
    for bits in range(1, 8):
        pl.semaphore_signal(barrier, inc=1, device_id=other(bits))
    lower, upper = f > 0, f < count - 1

    @pl.when(lower)
    def _():
        pl.semaphore_signal(barrier, inc=1, device_id={"f": f - 1})

    @pl.when(upper)
    def _():
        pl.semaphore_signal(barrier, inc=1, device_id={"f": f + 1})

    pl.semaphore_wait(barrier, 7 + lower.astype(jnp.int32) + upper.astype(jnp.int32))

    def rows(ref_rows, do):
        size = 16 if ref_rows % 32 else 32

        @pl.loop(0, ref_rows // size)
        def _(r):
            do(pl.ds(pl.multiple_of(r * size, size), size))

    parts = (total_ref, up_ref, out_ref)
    sums = (last_sum, up_sum, out_sum)

    def hop(i, d, up):
        outgoing, incoming = grown[i][0 if up else 2], grown[i][1 if up else 3]
        way = 0 if up else 1
        return send(
            outgoing.at[d], incoming.at[d], line_send.at[i, way, d], line_recv.at[i, way, d],
            {"f": f + 1 if up else f - 1},
        )

    def pass_on(i, d, up):
        outgoing, incoming = grown[i][0 if up else 2], grown[i][1 if up else 3]
        behind = lower if up else upper

        @pl.when((d > f) if up else (d < f))
        def _():
            @pl.when(behind)
            def _():
                hop(i, d, up).wait_recv()

                def add(at):
                    total = parts[i][d, at, :].astype(F32) + incoming[d, at, :].astype(F32)
                    outgoing[d, at, :] = total.astype(BF16)

                rows(parts[i].shape[1], add)

            @pl.when(jnp.logical_not(behind))
            def _():
                def keep(at):
                    outgoing[d, at, :] = parts[i][d, at, :].astype(BF16)

                rows(parts[i].shape[1], keep)

            hop(i, d, up).start()

    def line_step(i, step):
        pass_on(i, count - step, True)
        pass_on(i, step - 1, False)

    def line_end(i):
        def keep(at):
            sums[i][at, :] = parts[i][f, at, :].astype(F32)

        rows(parts[i].shape[1], keep)
        for up, there in ((True, lower), (False, upper)):
            incoming = grown[i][1 if up else 3]

            @pl.when(there)
            def _(up=up, incoming=incoming):
                hop(i, f, up).wait_recv()

                def add(at):
                    sums[i][at, :] = sums[i][at, :] + incoming[f, at, :].astype(F32)

                rows(parts[i].shape[1], add)

        for d in range(count):
            pl.when(f < d)(lambda: hop(i, d, True).wait_send())
            pl.when(f > d)(lambda: hop(i, d, False).wait_send())

    def wide(bits):
        return send(wide_ref.at[me ^ bits], wide_all.at[me], wide_send.at[bits], wide_recv.at[bits], other(bits))

    chips = (X_BIT | Y_BIT, X_BIT, Y_BIT, 0)

    def near(i):
        return send(
            last_ref.at[me ^ (chips[i] | C_BIT)], near_ref.at[i], near_send.at[i], near_recv.at[i], other(C_BIT)
        )

    def far(i):
        return send(chip_ref.at[i], far_ref.at[i], chip_send.at[i], chip_recv.at[i], other(chips[i]))

    local = pltpu.make_async_copy(wide_ref.at[me], wide_all.at[me], local_sem)
    local.start()
    for i in range(4):
        near(i).start()
    line_step(1, 1)
    line_step(2, 1)
    for i in range(4):
        near(i).wait_recv()
        for j in range(count):

            def add(at, i=i, j=j):
                total = last_ref[me ^ chips[i], j, at, :].astype(F32) + near_ref[i, j, at, :].astype(F32)
                if i < 3:
                    chip_ref[i, j, at, :] = total.astype(BF16)
                else:
                    total_ref[j, at, :] = total

            rows(total_ref.shape[1], add)
        if i < 3:
            far(i).start()
    for bits in (5, 7, 4, 6, 1, 3, 2):
        wide(bits).start()
    for step in range(2, count):
        line_step(1, step)
        line_step(2, step)
    for i in range(3):
        far(i).wait_recv()
    for j in range(count):

        def add(at, j=j):
            total = total_ref[j, at, :]
            for i in range(3):
                total = total + far_ref[i, j, at, :].astype(F32)
            total_ref[j, at, :] = total

        rows(total_ref.shape[1], add)
    for step in range(1, count):
        line_step(0, step)
    for i in (1, 2, 0):
        line_end(i)
    local.wait()
    for i in range(4):
        near(i).wait_send()
    for i in range(3):
        far(i).wait_send()
    for bits in range(1, 8):
        wide(bits).wait_recv()
        wide(bits).wait_send()


def end(last, up, out, wide, count, name):
    any_space, vmem = pl.BlockSpec(memory_space=pl.ANY), pl.BlockSpec(memory_space=pltpu.VMEM)
    dma = pltpu.SemaphoreType.DMA
    body = last.shape[1:]
    return pl.pallas_call(
        functools.partial(end_kernel, count),
        out_shape=[
            jax.ShapeDtypeStruct(body[1:], F32),
            jax.ShapeDtypeStruct(up.shape[1:], F32),
            jax.ShapeDtypeStruct(out.shape[1:], F32),
            jax.ShapeDtypeStruct(wide.shape, BF16),
        ],
        in_specs=[vmem, vmem, vmem, any_space],
        out_specs=[vmem, vmem, vmem, any_space],
        scratch_shapes=[
            pltpu.VMEM(body, F32),
            pltpu.VMEM((4, *body), BF16),
            pltpu.VMEM((3, *body), BF16),
            pltpu.VMEM((3, *body), BF16),
            *[pltpu.VMEM(body, BF16)] * 4,
            *[pltpu.VMEM(up.shape, BF16)] * 4,
            *[pltpu.VMEM(out.shape, BF16)] * 4,
            dma,
            dma((4,)), dma((4,)),
            dma((3,)), dma((3,)),
            dma((3, 2, count)), dma((3, 2, count)),
            dma((8,)), dma((8,)),
        ],
        compiler_params=pltpu.CompilerParams(
            collective_id=name, has_side_effects=True, vmem_limit_bytes=VMEM_MOST
        ),
        cost_estimate=pl.CostEstimate(flops=0, bytes_accessed=240 * 2**20, transcendentals=0),
    )(last, up, out, wide)


def by_owner(array, axis, count, f_first):
    lead, size, tail = array.shape[:axis], array.shape[axis], array.shape[axis + 1 :]
    part = size // (8 * count)
    n = len(lead)
    rest = [*range(n), n + 4, *range(n + 5, n + 5 + len(tail))]
    if f_first:
        array = array.reshape(*lead, count, 2, 2, 2, part, *tail)
        array = array.transpose(n, n + 1, n + 2, n + 3, *rest)
    else:
        array = array.reshape(*lead, 2, 2, count, 2, part, *tail)
        array = array.transpose(n + 2, n, n + 1, n + 3, *rest)
    return array.reshape(count, 8, *lead, part, *tail)


def from_owner(array, axis, f_first):
    count, _, *body = array.shape
    lead, part, tail = body[:axis], body[axis], body[axis + 1 :]
    n = axis
    array = array.reshape(count, 2, 2, 2, *body)
    inner = (0, 1, 2, 3) if f_first else (1, 2, 0, 3)
    array = array.transpose(
        *range(4, 4 + n), *inner, 4 + n, *range(5 + n, 5 + n + len(tail))
    )
    return array.reshape(*lead, 8 * count * part, *tail)


def scores_of(q_rot, k_rot, allowed):
    raw = jnp.einsum("bthd,bsd->bhts", q_rot, k_rot, preferred_element_type=F32)
    return jnp.where(allowed[:, None], raw * HEAD_DIM**-0.5, NEGATIVE)


def per_device(
    count,
    f_first,
    block_input,
    seq_lens,
    attn_gain,
    latent_down,
    latent_gain,
    latent_up,
    shared_kv,
    out_proj,
    mlp_gain,
    gate_weight,
    up_weight,
    down_weight,
    out_cotangent,
):
    tokens, width = block_input.shape
    rank = 2 * latent_down.shape[0]
    half_rank = latent_down.shape[0]
    units = down_weight.shape[0]
    mine = units * count
    padded = -(-mine // 256) * 256
    y = lax.axis_index("y")
    place = lax.axis_index("f")
    x_c = 2 * lax.axis_index("x") + lax.axis_index("c")

    def rows_of(array):
        flat = array.reshape(-1)
        lines = -(-flat.shape[0] // 128)
        return jnp.pad(flat, (0, lines * 128 - flat.shape[0])).reshape(lines, 128)

    gain_high = latent_gain.astype(BF16)
    gain_low = (latent_gain - gain_high.astype(F32)).astype(BF16)
    pieces = [
        latent_down.astype(BF16).reshape(-1, 128),
        shared_kv.astype(BF16).reshape(-1, 2, 128).transpose(1, 0, 2).reshape(-1, 128),
        rows_of(gain_high),
        rows_of(gain_low),
        rows_of(attn_gain.astype(BF16)),
        rows_of(mlp_gain.astype(BF16)),
        rows_of(seq_lens.astype(BF16)),
    ]
    marks = [0]
    for piece in pieces:
        marks.append(marks[-1] + piece.shape[0])
    total = -(-marks[-1] // 32) * 32
    first = jnp.pad(jnp.concatenate(pieces), ((0, total - marks[-1]), (0, 0)))

    def unit_blocks(weight):
        blocks = by_owner(weight.astype(BF16), 1, count, f_first)
        blocks = blocks.transpose(1, 2, 0, 3).reshape(8, -1, mine)
        return jnp.pad(blocks, ((0, 0), (0, 0), (0, padded - mine)))

    both = jnp.concatenate([unit_blocks(gate_weight), unit_blocks(up_weight)], axis=2)
    first, up_line, out_line, up_far, out_far, both, g_all = start(
        first, latent_up.astype(BF16), out_proj.astype(BF16), both, out_cotangent, count, 0
    )
    g_all = g_all.reshape(8 * tokens, width)
    both = lax.all_gather(both, "f", axis=0)
    both = from_owner(both, 0, f_first)
    ff_down = lax.all_gather(after(down_weight.astype(BF16), up_line, both), "f", axis=0)
    ff_down = jnp.pad(ff_down.reshape(mine, width), ((0, padded - mine), (0, 0)))

    lengths = lax.dynamic_index_in_dim(first[:, :, marks[6], :3], place, 1, keepdims=False)
    lengths = jnp.stack(
        [lax.dynamic_index_in_dim(lengths, in_plane() ^ i, 0, keepdims=False) for i in range(8)]
    ).astype(jnp.int32)
    owned = first.transpose(1, 0, 2, 3)

    def piece_of(i):
        return owned[:, :, marks[i] : marks[i + 1]]

    columns = width // (4 * count)
    down_full = piece_of(0).reshape(count, 2, 2, 2, half_rank, columns)
    down_full = down_full.transpose((3, 4, 0, 1, 2, 5) if f_first else (3, 4, 1, 2, 0, 5))
    down_full = down_full.reshape(rank, width)
    kv_rows = shared_kv.shape[0]
    kv_full = piece_of(1).reshape(count, 8, 2, kv_rows, 128).transpose(0, 1, 3, 2, 4)
    kv_full = from_owner(kv_full.reshape(count, 8, kv_rows, HEAD_DIM), 0, f_first)
    gain_lat = (piece_of(2)[0, :2].astype(F32) + piece_of(3)[0, :2].astype(F32)).reshape(rank)
    gain_rows = attn_gain.shape[0]

    def gain_of(i):
        return from_owner(piece_of(i).reshape(count, 8, -1)[:, :, :gain_rows], 0, f_first)

    gain_one, gain_two = gain_of(4).astype(F32), gain_of(5).astype(F32)

    half = count // 2
    per_head = count // 4

    def join(own, other_part, axis):
        low = jnp.where(y == 0, own, other_part)
        high = jnp.where(y == 0, other_part, own)
        return jnp.stack([low, high], axis)

    up_own = lax.dynamic_slice_in_dim(up_line, half * y, half, 0)
    out_own = lax.dynamic_slice_in_dim(out_line, half * y, half, 0)
    up_full = join(up_own, up_far, 0).transpose(0, 2, 1, 3).reshape(rank, 2 * HEAD_DIM)
    out_full = join(out_own, out_far, 1).reshape(2 * HEAD_DIM, width)

    inputs = block_input.astype(F32)
    rms_one = lax.rsqrt(jnp.mean(inputs * inputs, axis=-1, keepdims=True) + EPS)
    normed = (inputs * rms_one * gain_one).astype(BF16)
    latent = contract(normed, down_full, 1, 1)
    rms_lat = lax.rsqrt(jnp.mean(latent * latent, axis=-1, keepdims=True) + EPS)
    latent_n = (latent * rms_lat * gain_lat).astype(BF16)
    shared = jnp.dot(normed, kv_full, preferred_element_type=F32)
    position, allowed = layout(lengths, tokens)
    cosine, sine = rope_tables(position, HEAD_DIM)
    k_own = rotate(shared, cosine[0], sine[0]).astype(BF16)

    parcel = plane_gather(jnp.concatenate([latent_n, k_own, shared.astype(BF16)], axis=1), 1)
    lat_all = parcel[:, :, :rank].reshape(8 * tokens, rank)
    k_rot = parcel[:, :, rank : rank + HEAD_DIM]
    values = parcel[:, :, rank + HEAD_DIM :]
    queries = jnp.dot(lat_all, up_full, preferred_element_type=F32)
    wide_cos, wide_sin = cosine[:, :, None], sine[:, :, None]
    q_rot = rotate(queries.reshape(8, tokens, 2, HEAD_DIM), wide_cos, wide_sin).astype(BF16)
    scores = scores_of(q_rot, k_rot, allowed)
    peak = jnp.max(scores, axis=-1, keepdims=True)
    log_total = peak + jnp.log(jnp.sum(jnp.exp(scores - peak), axis=-1, keepdims=True))
    probs = jnp.exp(scores - log_total)
    attended = jnp.einsum("bhts,bsd->bthd", probs.astype(BF16), values, preferred_element_type=F32)
    attended = attended.reshape(8 * tokens, 2 * HEAD_DIM).astype(BF16)
    branch = matmul_scatter(attended, out_full, 2)

    middle = inputs + branch
    rms_two = lax.rsqrt(jnp.mean(middle * middle, axis=-1, keepdims=True) + EPS)
    normed_two = (middle * rms_two * gain_two).astype(BF16)
    two_all = plane_gather(normed_two, 3).reshape(8 * tokens, width)
    gate_up = jnp.dot(two_all, both, preferred_element_type=F32)
    gate, upval = gate_up[:, :padded], gate_up[:, padded:]
    sigma = jax.nn.sigmoid(gate)
    hidden = (gate * sigma * upval).astype(BF16)

    d_hidden = contract(g_all, ff_down, 1, 1)
    d_gate = (d_hidden * upval * sigma * (1.0 + gate * (1.0 - sigma))).astype(BF16)
    d_up = (d_hidden * gate * sigma).astype(BF16)
    d_both = jnp.concatenate([d_gate, d_up], axis=1)
    d_two = matmul_scatter(d_both, both, 4, True)

    result = jnp.dot(hidden, ff_down, preferred_element_type=F32)
    result = plane_scatter(after(result.reshape(8, tokens, width), d_two))
    block_output = (middle + result).astype(BF16)

    both_grad = contract(two_all, d_both, 0, 0)
    both_grad = by_owner(both_grad.astype(BF16), 0, count, f_first)
    both_grad = lax.psum_scatter(both_grad, "f", scatter_dimension=0)

    down_grad = contract(hidden, g_all, 0, 0)[:mine].reshape(count, units, width)
    down_grad = lax.psum_scatter(down_grad.astype(BF16), "f", scatter_dimension=0).astype(F32)

    upstream = out_cotangent.astype(F32)
    gain_two_part = jnp.sum(d_two * middle * rms_two, axis=0)
    scaled_two = d_two * gain_two
    d_middle = (
        upstream
        + rms_two * scaled_two
        - middle * (rms_two**3) * jnp.mean(scaled_two * middle, axis=-1, keepdims=True)
    )

    d_branch = plane_gather(d_middle.astype(BF16), 5).reshape(8 * tokens, width)
    d_attended = contract(d_branch, out_full, 1, 1).astype(BF16)
    d_attended = d_attended.reshape(8, tokens, 2, HEAD_DIM)
    d_probs = jnp.einsum("bthd,bsd->bhts", d_attended, values, preferred_element_type=F32)
    inner = jnp.sum(probs * d_probs, axis=-1, keepdims=True)
    d_scores = (probs * (d_probs - inner)).astype(BF16)
    scale = HEAD_DIM**-0.5
    d_qrot = jnp.einsum("bhts,bsd->bthd", d_scores, k_rot, preferred_element_type=F32) * scale
    d_queries = unrotate(d_qrot, wide_cos, wide_sin).astype(BF16)
    d_queries = d_queries.reshape(8 * tokens, 2 * HEAD_DIM)
    d_krot = jnp.einsum("bhts,bthd->bsd", d_scores, q_rot, preferred_element_type=F32) * scale
    value_part = jnp.einsum(
        "bhts,bthd->bsd", probs.astype(BF16), d_attended, preferred_element_type=F32
    )
    shared_part = unrotate(d_krot, cosine, sine) + value_part
    back = matmul_scatter(d_queries, up_full, 6, True, shared_part.reshape(8 * tokens, HEAD_DIM))
    d_lat_n, d_shared = back[:, :rank], back[:, rank:].astype(BF16)

    up_grad_heads = contract(lat_all, d_queries, 0, 0).reshape(2, half_rank, 2, HEAD_DIM)
    out_grad_heads = contract(attended, d_branch, 0, 0).reshape(2, per_head, 2, -1, width)

    def swap_halves(array, axis):
        own = lax.dynamic_index_in_dim(array, y, axis, keepdims=False)
        other = lax.dynamic_index_in_dim(array, 1 - y, axis, keepdims=False).astype(BF16)
        return own, lax.ppermute(other, "y", SWAP).astype(F32)

    up_line_grad = join(*swap_halves(up_grad_heads, 0), 1).reshape(half_rank, count, -1)
    up_line_grad = up_line_grad.transpose(1, 0, 2).astype(BF16)
    out_line_grad = join(*swap_halves(out_grad_heads, 2), 0)
    out_line_grad = out_line_grad.reshape(count, -1, width).astype(BF16)

    gain_lat_part = jnp.sum(d_lat_n * latent * rms_lat, axis=0)
    scaled_lat = d_lat_n * gain_lat
    inner_lat = jnp.sum(scaled_lat * latent, axis=-1, keepdims=True)
    d_latent = (rms_lat * scaled_lat - latent * (rms_lat**3) * inner_lat / rank).astype(BF16)
    d_normed = contract(d_shared, kv_full, 1, 1) + jnp.dot(
        d_latent, down_full, preferred_element_type=F32
    )
    gain_one_part = jnp.sum(d_normed * inputs * rms_one, axis=0)
    scaled_one = d_normed * gain_one
    input_grad = (
        d_middle
        + rms_one * scaled_one
        - inputs * (rms_one**3) * jnp.mean(scaled_one * inputs, axis=-1, keepdims=True)
    ).astype(BF16)

    down_part = contract(d_latent, normed, 0, 0)
    if f_first:
        down_part = down_part.reshape(2, half_rank, count, 2, 2, columns).transpose(2, 3, 4, 0, 1, 5)
    else:
        down_part = down_part.reshape(2, half_rank, 2, 2, count, columns).transpose(4, 2, 3, 0, 1, 5)
    down_part = down_part.reshape(count, 8, -1, 128)
    kv_part = by_owner(contract(normed, d_shared, 0, 0), 0, count, f_first)
    kv_part = kv_part.reshape(count, 8, kv_rows, 2, 128).transpose(0, 1, 3, 2, 4)
    kv_part = kv_part.reshape(count, 8, -1, 128)

    def gain_rows_of(part):
        part = by_owner(part, 0, count, f_first)
        return jnp.pad(part, ((0, 0), (0, 0), (0, 128 - gain_rows)))[:, :, None]

    lat_rows = jnp.broadcast_to(
        gain_lat_part.reshape(1, 1, 2, -1, 128), (count, 4, 2, half_rank // 128, 128)
    )
    lat_rows = lat_rows.reshape(count, 8, -1, 128)
    pieces = [down_part, kv_part, lat_rows, gain_rows_of(gain_one_part), gain_rows_of(gain_two_part)]
    marks = [0]
    for piece in pieces:
        marks.append(marks[-1] + piece.shape[2])
    last_rows = -(-marks[-1] // 32) * 32
    last = jnp.pad(jnp.concatenate(pieces, axis=2), ((0, 0), (0, 0), (0, last_rows - marks[-1]), (0, 0)))
    last = last.transpose(1, 0, 2, 3).astype(BF16)
    last, latent_up_grad, out_proj_grad, both_grad = end(
        last, up_line_grad, out_line_grad, both_grad.astype(BF16), count, 7
    )

    def whole_rows(blocks):
        blocks = blocks[:, :, :mine].astype(F32).reshape(8, -1, count, units)
        return from_owner(blocks.transpose(2, 0, 1, 3), 1, f_first)

    gate_grad, up_grad = whole_rows(both_grad[..., :padded]), whole_rows(both_grad[..., padded:])
    latent_down_grad = last[marks[0] : marks[1]].reshape(half_rank, columns)
    shared_kv_grad = last[marks[1] : marks[2]].reshape(2, kv_rows, 128).transpose(1, 0, 2)
    shared_kv_grad = shared_kv_grad.reshape(kv_rows, HEAD_DIM)
    latent_gain_grad = last[marks[2] : marks[3]].reshape(half_rank)
    attn_gain_grad = last[marks[3], :gain_rows]
    mlp_gain_grad = last[marks[4], :gain_rows]
    return (
        block_output,
        input_grad,
        attn_gain_grad,
        latent_down_grad,
        latent_gain_grad,
        latent_up_grad,
        shared_kv_grad,
        out_proj_grad,
        mlp_gain_grad,
        gate_grad,
        up_grad,
        down_grad,
    )


def solution(mesh):
    devices = mesh.devices
    split = devices.shape[0]
    count = split // 4
    f_first = split == HEADS
    if f_first:
        names, sizes = ("f", "x", "c", "y"), (count, 2, 2, 2)
    else:
        names, sizes = ("x", "c", "f", "y"), (2, 2, count, 2)
    fine = Mesh(devices.reshape(sizes), names)
    dp = names[:3]
    return jax.shard_map(
        functools.partial(per_device, count, f_first),
        mesh=fine,
        in_specs=(
            P(names, None),
            P(names, None),
            P(names),
            P("y", dp),
            P("y"),
            P("y", dp),
            P(names, None),
            P(names, None),
            P(names),
            P(names, None),
            P(names, None),
            P(names, None),
            P(names, None),
        ),
        out_specs=(
            P(names, None),
            P(names, None),
            P(names),
            P("y", dp),
            P("y"),
            P("y", dp),
            P(names, None),
            P(names, None),
            P(names),
            P(names, None),
            P(names, None),
            P(names, None),
        ),
        check_vma=False,
    )
```

```python
import functools
import math

import jax
import jax.numpy as jnp
from jax import lax
from jax.experimental import pallas as pl
from jax.experimental.pallas import tpu as pltpu
from jax.sharding import Mesh
from jax.sharding import PartitionSpec as P

HEADS = 16
HEAD_DIM = 256
EPS = 1e-06
NEGATIVE = -1e30
F32 = jnp.float32
BF16 = jnp.bfloat16


def contract(left, right, left_dim, right_dim):
    return lax.dot_general(
        left, right, (((left_dim,), (right_dim,)), ((), ())), preferred_element_type=F32
    )


def after(value, *first):
    return lax.optimization_barrier((value, *first))[0]


def layout(lengths, count):
    spots = jnp.arange(lengths.shape[-1], dtype=jnp.int32)
    ends = jnp.sum(jnp.where(spots[None, :] <= spots[:, None], lengths[..., None, :], 0), axis=-1)
    places = jnp.arange(count, dtype=jnp.int32)
    passed = places[:, None] >= ends[..., None, :]
    segment = jnp.sum(passed.astype(jnp.int32), axis=-1)
    offset = jnp.sum(jnp.where(passed, lengths[..., None, :], 0), axis=-1)
    position = (places - offset).astype(F32)
    same = segment[..., :, None] == segment[..., None, :]
    return position, same & (places[None, :] <= places[:, None])


def rope_tables(position, width):
    half = width // 2
    steps = jnp.arange(half, dtype=F32)
    freqs = jnp.exp(steps * (-math.log(10000.0) / half))
    angles = position[..., None] * freqs
    return jnp.cos(angles), jnp.sin(angles)


def rotate(values, cosine, sine):
    half = values.shape[-1] // 2
    first, second = values[..., :half], values[..., half:]
    return jnp.concatenate(
        [first * cosine - second * sine, second * cosine + first * sine], axis=-1
    )


def unrotate(grads, cosine, sine):
    return rotate(grads, cosine, -sine)


SWAP = [(0, 1), (1, 0)]
DIAGONAL = [(0, 3), (3, 0), (1, 2), (2, 1)]


def plane_scatter(parts):
    low = parts.astype(BF16)
    sums = []
    for near, far in ((0, 2), (1, 3), (4, 6), (5, 7)):
        sums.append(parts[near].astype(F32) + lax.ppermute(low[far], "c", SWAP).astype(F32))
    by_y = lax.ppermute(sums[1].astype(BF16), "y", SWAP)
    by_x = lax.ppermute(sums[2].astype(BF16), "x", SWAP)
    by_both = lax.ppermute(sums[3].astype(BF16), ("x", "y"), DIAGONAL)
    return sums[0], by_x, by_y, by_both


X_BIT, C_BIT, Y_BIT = 4, 2, 1
VMEM_MOST = 56 * 2**20


def other(bits):
    flips = {"x": bits // 4, "c": bits // 2 % 2, "y": bits % 2}
    return {name: 1 - lax.axis_index(name) for name, flip in flips.items() if flip}


def greet(partners):
    barrier = pltpu.get_barrier_semaphore()
    for partner in partners:
        pl.semaphore_signal(barrier, inc=1, device_id=partner)
    pl.semaphore_wait(barrier, len(partners))


def send(source, target, send_sem, recv_sem, device):
    return pltpu.make_async_remote_copy(
        src_ref=source, dst_ref=target, send_sem=send_sem, recv_sem=recv_sem, device_id=device
    )


def gathering(chunks, in_ref, out_ref, send_sem, recv_sem):
    rows = in_ref.shape[0] // chunks
    both = X_BIT | Y_BIT

    def to(slot, k, bits, source):
        part = pl.ds(k * rows, rows)
        return send(
            source.at[part], out_ref.at[slot, part], send_sem.at[slot, k], recv_sem.at[slot, k], other(bits)
        )

    def own():
        for k in range(chunks):
            to(X_BIT, k, X_BIT, in_ref).start()
            to(Y_BIT, k, Y_BIT, in_ref).start()
        for k in range(chunks):
            to(C_BIT, k, C_BIT, in_ref).start()

    def relay(first, last):
        for k in range(first, last):
            to(X_BIT, k, X_BIT, in_ref).wait_recv()
            if k < chunks // 2:
                to(both, k, Y_BIT, out_ref.at[X_BIT]).start()
            to(X_BIT | C_BIT, k, C_BIT, out_ref.at[X_BIT]).start()
            to(Y_BIT, k, Y_BIT, in_ref).wait_recv()
            if k >= chunks // 2:
                to(both, k, X_BIT, out_ref.at[Y_BIT]).start()
            to(Y_BIT | C_BIT, k, C_BIT, out_ref.at[Y_BIT]).start()

    def far():
        for k in range(chunks):
            to(both, k, Y_BIT, in_ref).wait_recv()
            to(7, k, C_BIT, out_ref.at[both]).start()

    def end():
        for slot in range(1, 8):
            for k in range(chunks):
                copy = to(slot, k, slot, in_ref)
                if slot & C_BIT:
                    copy.wait_recv()
                copy.wait_send()

    return own, relay, far, end


def gather_kernel(chunks, in_ref, out_ref, own_sem, send_sem, recv_sem):
    greet([other(C_BIT), other(X_BIT), other(Y_BIT)])
    copy = pltpu.make_async_copy(in_ref, out_ref.at[0], own_sem)
    copy.start()
    own, relay, far, end = gathering(chunks, in_ref, out_ref, send_sem, recv_sem)
    own()
    relay(0, chunks)
    far()
    copy.wait()
    end()


def plane_gather(block, name, chunks=4):
    return pl.pallas_call(
        functools.partial(gather_kernel, chunks),
        out_shape=jax.ShapeDtypeStruct((8, *block.shape), block.dtype),
        in_specs=[pl.BlockSpec(memory_space=pl.ANY)],
        out_specs=pl.BlockSpec(memory_space=pl.ANY),
        scratch_shapes=[
            pltpu.SemaphoreType.DMA,
            pltpu.SemaphoreType.DMA((8, chunks)),
            pltpu.SemaphoreType.DMA((8, chunks)),
        ],
        compiler_params=pltpu.CompilerParams(collective_id=name, has_side_effects=True),
        cost_estimate=pl.CostEstimate(flops=0, bytes_accessed=160 * 2**20, transcendentals=0),
    )(block)


def matmul_scatter_kernel(flip, wide, *refs):
    left_ref, right_ref, *more_ref, out_ref, part_ref, near_ref, sum_ref, far_ref = refs[:-4]
    near_send, near_recv, chip_send, chip_recv = refs[-4:]
    tokens = out_ref.shape[0]
    step = 256
    greet([other(C_BIT), other(X_BIT), other(Y_BIT), other(X_BIT | Y_BIT)])

    def product(slot, target):
        @pl.loop(0, wide // step)
        def _(i):
            at = pl.ds(pl.multiple_of(i * step, step), step)
            rows = left_ref[slot * tokens : (slot + 1) * tokens, :]
            if flip:
                got = contract(rows, right_ref[at, :], 1, 1)
            else:
                got = contract(rows, right_ref[:, at], 1, 0)
            target[:, at] = got.astype(BF16)

        for ref in more_ref:
            target[:, wide:] = ref[slot * tokens : (slot + 1) * tokens, :].astype(BF16)

    chips = (X_BIT | Y_BIT, X_BIT, Y_BIT, 0)
    near, far = [], []
    for i, chip in enumerate(chips):
        product(chip | C_BIT, part_ref.at[i])
        copy = send(part_ref.at[i], near_ref.at[i], near_send.at[i], near_recv.at[i], other(C_BIT))
        copy.start()
        near.append(copy)
        product(chip, sum_ref.at[i])
        copy.wait_recv()

        @pl.loop(0, tokens // 32)
        def _(r):
            at = pl.ds(pl.multiple_of(r * 32, 32), 32)
            total = sum_ref[i, at, :].astype(F32) + near_ref[i, at, :].astype(F32)
            if chip:
                sum_ref[i, at, :] = total.astype(BF16)
            else:
                out_ref[at, :] = total

        if chip:
            copy = send(sum_ref.at[i], far_ref.at[i], chip_send.at[i], chip_recv.at[i], other(chip))
            copy.start()
            far.append(copy)
    for copy in far:
        copy.wait_recv()

    @pl.loop(0, tokens // 32)
    def _(r):
        at = pl.ds(pl.multiple_of(r * 32, 32), 32)
        total = out_ref[at, :]
        for i in range(3):
            total = total + far_ref[i, at, :].astype(F32)
        out_ref[at, :] = total

    for copy in (*near, *far):
        copy.wait_send()


def matmul_scatter(left, right, name, flip=False, *more):
    tokens, depth = left.shape[0] // 8, left.shape[1]
    wide = right.shape[0 if flip else 1]
    full = wide + sum(array.shape[1] for array in more)
    block = pltpu.VMEM((4, tokens, full), BF16)
    return pl.pallas_call(
        functools.partial(matmul_scatter_kernel, flip, wide),
        out_shape=jax.ShapeDtypeStruct((tokens, full), F32),
        in_specs=[pl.BlockSpec(memory_space=pltpu.VMEM)] * (2 + len(more)),
        out_specs=pl.BlockSpec(memory_space=pltpu.VMEM),
        scratch_shapes=[
            block,
            block,
            block,
            pltpu.VMEM((3, tokens, full), BF16),
            *[pltpu.SemaphoreType.DMA((4,))] * 2,
            *[pltpu.SemaphoreType.DMA((3,))] * 2,
        ],
        compiler_params=pltpu.CompilerParams(
            collective_id=name, has_side_effects=True, vmem_limit_bytes=VMEM_MOST
        ),
        cost_estimate=pl.CostEstimate(
            flops=16 * tokens * wide * depth, bytes_accessed=160 * 2**20, transcendentals=0
        ),
    )(left, right, *more)


def in_plane():
    return 4 * lax.axis_index("x") + 2 * lax.axis_index("c") + lax.axis_index("y")


class Parcel:
    def __init__(self, count, f_first, rank_rows, columns, kv_rows):
        self.count, self.f_first = count, f_first
        self.rank_rows, self.columns, self.kv_rows = rank_rows, columns, kv_rows
        self.windows = columns % 128 == 0

    def down_shape(self):
        if self.windows:
            return (2 * self.rank_rows, 4 * self.count * self.columns)
        return (8, self.count, self.rank_rows, self.columns)

    def down_from(self, array):
        if self.windows:
            return array
        array = array.reshape(2, 2, 2, self.count, self.rank_rows, self.columns)
        array = array.transpose((2, 4, 3, 0, 1, 5) if self.f_first else (2, 4, 0, 1, 3, 5))
        return array.reshape(2 * self.rank_rows, -1)

    def down_to(self, array):
        if self.windows:
            return array
        inner = (self.count, 2, 2) if self.f_first else (2, 2, self.count)
        array = array.reshape(2, self.rank_rows, *inner, self.columns)
        array = array.transpose((3, 4, 0, 2, 1, 5) if self.f_first else (2, 3, 0, 4, 1, 5))
        return array.reshape(self.down_shape())

    def blocks(self, refs, place, j):
        down, kv, small = refs
        pair, y = place // 2, place % 2
        at = j * 4 + pair if self.f_first else pair * self.count + j
        if self.windows:
            down = down.at[
                pl.ds(pl.multiple_of(y * self.rank_rows, self.rank_rows), self.rank_rows),
                pl.ds(pl.multiple_of(at * self.columns, self.columns), self.columns),
            ]
        else:
            down = down.at[place, j]
        start_row = pl.multiple_of((2 * at + y) * self.kv_rows, self.kv_rows)
        return down, kv.at[pl.ds(start_row, self.kv_rows)], small.at[place, j]

    def unit_pieces(self):
        for shard in range(8 * self.count):
            if self.f_first:
                yield shard % 8, shard // 8, shard
            else:
                yield shard // (2 * self.count) * 2 + shard % 2, shard // 2 % self.count, shard


def greet_all(count):
    f = lax.axis_index("f")
    lower, upper = f > 0, f < count - 1
    barrier = pltpu.get_barrier_semaphore()
    for bits in range(1, 8):
        pl.semaphore_signal(barrier, inc=1, device_id=other(bits))
    pl.when(lower)(lambda: pl.semaphore_signal(barrier, inc=1, device_id={"f": f - 1}))
    pl.when(upper)(lambda: pl.semaphore_signal(barrier, inc=1, device_id={"f": f + 1}))
    pl.semaphore_wait(barrier, 7 + lower.astype(jnp.int32) + upper.astype(jnp.int32))
    return lower, upper


def begin(copies):
    for copy in copies:
        copy.start()


def arrive(copies):
    for copy in copies:
        copy.wait_recv()


def gone(copies):
    for copy in copies:
        copy.wait_send()


FAR_FIRST = (7, 5, 6, 4, 3, 1, 2)


def start_kernel(
    parcel, chunks, units, padded, down_ref, kv_ref, small_ref, gate_ref, up_ref, rows_ref,
    down_all, kv_all, small_all, wide_all, rows_all,
    down_low, kv_low, wide_ref,
    local_sem, line_send, line_recv, plane_send, plane_recv, wide_send, wide_recv, rows_send, rows_recv,
):
    count = parcel.count
    f, me = lax.axis_index("f"), in_plane()
    lower, upper = greet_all(count)
    own = (down_low, kv_low, small_ref)
    alls = (down_all, kv_all, small_all)
    down_low[...] = down_ref[...].astype(BF16)
    kv_low[...] = kv_ref[...].astype(BF16)

    def hop(j, up, sources):
        return [
            send(
                source, target, line_send.at[i, 0 if up else 1, j], line_recv.at[i, j],
                {"f": f + 1 if up else f - 1},
            )
            for i, (source, target) in enumerate(zip(sources, parcel.blocks(alls, me, j)))
        ]

    def spread(slot, bits, j, sources):
        targets = parcel.blocks(alls, me ^ bits ^ slot, j)
        return [
            send(source, target, plane_send.at[i, slot, j], plane_recv.at[i, slot, j], other(bits))
            for i, (source, target) in enumerate(zip(sources, targets))
        ]

    def to_plane(j, sources):
        for bits in (X_BIT, Y_BIT, C_BIT):
            begin(spread(bits, bits, j, sources))

    def line_step(step):
        @pl.when(f - step >= 0)
        def _():
            j = f - step
            blocks = parcel.blocks(alls, me, j)
            arrive(hop(j, True, blocks))
            pl.when(upper)(lambda: begin(hop(j, True, blocks)))
            to_plane(j, blocks)

        @pl.when(f + step <= count - 1)
        def _():
            j = f + step
            blocks = parcel.blocks(alls, me, j)
            arrive(hop(j, False, blocks))
            pl.when(lower)(lambda: begin(hop(j, False, blocks)))
            to_plane(j, blocks)

    def relay(j):
        by_x, by_y = parcel.blocks(alls, me ^ X_BIT, j), parcel.blocks(alls, me ^ Y_BIT, j)
        arrive(spread(X_BIT, X_BIT, j, by_x))
        pl.when(j % 2 == 0)(lambda: begin(spread(5, Y_BIT, j, by_x)))
        begin(spread(6, C_BIT, j, by_x))
        arrive(spread(Y_BIT, Y_BIT, j, by_y))
        pl.when(j % 2 == 1)(lambda: begin(spread(5, X_BIT, j, by_y)))
        begin(spread(3, C_BIT, j, by_y))

    def relay_far(j):
        by_both = parcel.blocks(alls, me ^ 5, j)
        arrive(spread(5, Y_BIT, j, by_both))
        begin(spread(7, C_BIT, j, by_both))

    def in_order(do):
        do(f)
        for step in range(1, count):
            pl.when(f - step >= 0)(lambda: do(f - step))
            pl.when(f + step <= count - 1)(lambda: do(f + step))

    def wide(bits):
        return send(wide_ref.at[me ^ bits], wide_all.at[me], wide_send.at[bits], wide_recv.at[bits], other(bits))

    pl.when(upper)(lambda: begin(hop(f, True, own)))
    pl.when(lower)(lambda: begin(hop(f, False, own)))
    to_plane(f, own)
    for place, j, shard in parcel.unit_pieces():
        for first, ref in ((0, gate_ref), (padded, up_ref)):
            piece = ref[:, shard * units : (shard + 1) * units].astype(BF16)
            wide_ref[place, :, first + j * units : first + (j + 1) * units] = piece
    for first in (count * units, padded + count * units):
        size = padded - count * units
        wide_ref[:, :, first : first + size] = jnp.zeros((8, wide_ref.shape[1], size), BF16)
    for bits in FAR_FIRST:
        wide(bits).start()
    locals_ = [
        pltpu.make_async_copy(source, target, local_sem.at[i])
        for i, (source, target) in enumerate(
            (
                *zip(own, parcel.blocks(alls, me, f)),
                (wide_ref.at[me], wide_all.at[me]),
                (rows_ref, rows_all.at[0]),
            )
        )
    ]
    begin(locals_)
    rows_own, rows_relay, rows_far, rows_end = gathering(chunks, rows_ref, rows_all, rows_send, rows_recv)
    for step in range(1, count):
        line_step(step)
    rows_own()
    in_order(relay)
    rows_relay(0, chunks // 2)
    in_order(relay_far)
    rows_relay(chunks // 2, chunks)
    rows_far()
    for copy in locals_:
        copy.wait()
    for j in range(count):
        pl.when(upper & (f >= j))(lambda: gone(hop(j, True, own)))
        pl.when(lower & (f <= j))(lambda: gone(hop(j, False, own)))
    for slot in range(1, 8):
        for j in range(count):
            for copy in spread(slot, slot, j, own):
                if slot & C_BIT:
                    copy.wait_recv()
                copy.wait_send()
    for bits in range(1, 8):
        wide(bits).wait_recv()
        wide(bits).wait_send()
    rows_end()


def start(parcel, down, kv, small, gate, up, rows, units, padded, name, chunks=4):
    count = parcel.count
    any_space, vmem = pl.BlockSpec(memory_space=pl.ANY), pl.BlockSpec(memory_space=pltpu.VMEM)
    dma = pltpu.SemaphoreType.DMA
    wide = (8, gate.shape[0], 2 * padded)
    return pl.pallas_call(
        functools.partial(start_kernel, parcel, chunks, units, padded),
        out_shape=[
            jax.ShapeDtypeStruct(parcel.down_shape(), BF16),
            jax.ShapeDtypeStruct((8 * count * kv.shape[0], kv.shape[1]), BF16),
            jax.ShapeDtypeStruct((8, count, *small.shape), BF16),
            jax.ShapeDtypeStruct(wide, BF16),
            jax.ShapeDtypeStruct((8, *rows.shape), BF16),
        ],
        in_specs=[vmem] * 5 + [any_space],
        out_specs=[any_space] * 5,
        scratch_shapes=[
            pltpu.VMEM(down.shape, BF16),
            pltpu.VMEM(kv.shape, BF16),
            pltpu.VMEM(wide, BF16),
            dma((5,)),
            dma((3, 2, count)), dma((3, count)),
            dma((3, 8, count)), dma((3, 8, count)),
            dma((8,)), dma((8,)),
            dma((8, chunks)), dma((8, chunks)),
        ],
        compiler_params=pltpu.CompilerParams(
            collective_id=name, has_side_effects=True, vmem_limit_bytes=VMEM_MOST
        ),
        cost_estimate=pl.CostEstimate(flops=0, bytes_accessed=240 * 2**20, transcendentals=0),
    )(down, kv, small, gate, up, rows)


def end_kernel(
    parcel, units, padded, down_ref, kv_ref, small_ref, wide_ref,
    down_sum, kv_sum, small_sum, gate_sum, up_sum, *rest,
):
    count = parcel.count
    held = [rest[8 * i : 8 * i + 8] for i in range(3)]
    wide_all, near_send, near_recv, chip_send, chip_recv, line_send, line_recv, wide_send, wide_recv = rest[24:]
    f, me = lax.axis_index("f"), in_plane()
    lower, upper = greet_all(count)
    parts = (down_ref, kv_ref, small_ref)
    sums = (down_sum, kv_sum, small_sum)
    chips = (X_BIT | Y_BIT, X_BIT, Y_BIT, 0)

    def rows(amount, do):
        size = 16 if amount % 64 else 64

        @pl.loop(0, amount // size)
        def _(r):
            do(pl.ds(pl.multiple_of(r * size, size), size))

    def near(n, j):
        sources = parcel.blocks(parts, me ^ (chips[n] | C_BIT), j)
        return [
            send(source, held[i][1].at[n, j], near_send.at[i, n, j], near_recv.at[i, n, j], other(C_BIT))
            for i, source in enumerate(sources)
        ]

    def far(n):
        return [
            send(held[i][2].at[n], held[i][3].at[n], chip_send.at[i, n], chip_recv.at[i, n], other(chips[n]))
            for i in range(3)
        ]

    def wide(bits):
        return send(wide_ref.at[me ^ bits], wide_all.at[me], wide_send.at[bits], wide_recv.at[bits], other(bits))

    def hop(d, up):
        way = 0 if up else 1
        return [
            send(
                held[i][4 + 2 * way].at[d], held[i][5 + 2 * way].at[d],
                line_send.at[i, way, d], line_recv.at[i, way, d],
                {"f": f + 1 if up else f - 1},
            )
            for i in range(3)
        ]

    def pass_on(d, up):
        way = 0 if up else 1
        behind = lower if up else upper

        @pl.when((d > f) if up else (d < f))
        def _():
            @pl.when(behind)
            def _():
                for copy in hop(d, up):
                    copy.wait_recv()
                for total, outgoing, incoming in ((h[0], h[4 + 2 * way], h[5 + 2 * way]) for h in held):

                    def add(at, total=total, outgoing=outgoing, incoming=incoming):
                        outgoing[d, at, :] = (total[d, at, :] + incoming[d, at, :].astype(F32)).astype(BF16)

                    rows(total.shape[1], add)

            @pl.when(jnp.logical_not(behind))
            def _():
                for total, outgoing in ((h[0], h[4 + 2 * way]) for h in held):

                    def keep(at, total=total, outgoing=outgoing):
                        outgoing[d, at, :] = total[d, at, :].astype(BF16)

                    rows(total.shape[1], keep)

            for copy in hop(d, up):
                copy.start()

    for n in range(4):
        for j in range(count):
            for copy in near(n, j):
                copy.start()
    for bits in FAR_FIRST:
        wide(bits).start()
    for n in range(4):
        for j in range(count):
            for copy in near(n, j):
                copy.wait_recv()
            for i, source in enumerate(parcel.blocks(parts, me ^ chips[n], j)):
                total, near_ref, chip_ref = held[i][:3]

                def add(at, source=source, total=total, near_ref=near_ref, chip_ref=chip_ref):
                    both = source[at, :].astype(F32) + near_ref[n, j, at, :].astype(F32)
                    if n < 3:
                        chip_ref[n, j, at, :] = both.astype(BF16)
                    else:
                        total[j, at, :] = both

                rows(total.shape[1], add)
        if n < 3:
            for copy in far(n):
                copy.start()

    wide_all[me] = wide_ref[me]
    for bits in range(1, 8):
        wide(bits).wait_recv()
    for place, j, shard in parcel.unit_pieces():
        for first, ref in ((0, gate_sum), (padded, up_sum)):
            piece = wide_all[place, :, first + j * units : first + (j + 1) * units]
            ref[:, shard * units : (shard + 1) * units] = piece.astype(F32)

    for n in range(3):
        for copy in far(n):
            copy.wait_recv()
    for i in range(3):
        total, far_ref = held[i][0], held[i][3]
        for j in range(count):

            def add(at, total=total, far_ref=far_ref, j=j):
                value = total[j, at, :]
                for n in range(3):
                    value = value + far_ref[n, j, at, :].astype(F32)
                total[j, at, :] = value

            rows(total.shape[1], add)
    for step in range(1, count):
        pass_on(count - step, True)
        pass_on(step - 1, False)
    for i in range(3):

        def keep(at, i=i):
            sums[i][at, :] = held[i][0][f, at, :]

        rows(sums[i].shape[0], keep)
    for up, there in ((True, lower), (False, upper)):

        @pl.when(there)
        def _(up=up):
            for copy in hop(f, up):
                copy.wait_recv()
            for i in range(3):
                incoming = held[i][5 if up else 7]

                def add(at, i=i, incoming=incoming):
                    sums[i][at, :] = sums[i][at, :] + incoming[f, at, :].astype(F32)

                rows(sums[i].shape[0], add)

    for d in range(count):
        pl.when(f < d)(lambda: gone(hop(d, True)))
        pl.when(f > d)(lambda: gone(hop(d, False)))
    for n in range(4):
        for j in range(count):
            for copy in near(n, j):
                copy.wait_send()
    for n in range(3):
        for copy in far(n):
            copy.wait_send()
    for bits in range(1, 8):
        wide(bits).wait_send()


def end(parcel, down, kv, small, wide, units, padded, name):
    vmem = pl.BlockSpec(memory_space=pltpu.VMEM)
    dma = pltpu.SemaphoreType.DMA
    count = parcel.count
    bodies = (
        (count, parcel.rank_rows, parcel.columns),
        (count, parcel.kv_rows, kv.shape[1]),
        (count, *small.shape[2:]),
    )
    scratch = []
    for body in bodies:
        low = pltpu.VMEM(body, BF16)
        three = pltpu.VMEM((3, *body), BF16)
        scratch += [pltpu.VMEM(body, F32), pltpu.VMEM((4, *body), BF16), three, three, low, low, low, low]
    every = 8 * count * units
    return pl.pallas_call(
        functools.partial(end_kernel, parcel, units, padded),
        out_shape=[
            *[jax.ShapeDtypeStruct(body[1:], F32) for body in bodies],
            *[jax.ShapeDtypeStruct((wide.shape[1], every), F32)] * 2,
        ],
        in_specs=[vmem] * 4,
        out_specs=[vmem] * 5,
        scratch_shapes=[
            *scratch,
            pltpu.VMEM(wide.shape, BF16),
            dma((3, 4, count)), dma((3, 4, count)),
            dma((3, 3)), dma((3, 3)),
            dma((3, 2, count)), dma((3, 2, count)),
            dma((8,)), dma((8,)),
        ],
        compiler_params=pltpu.CompilerParams(
            collective_id=name, has_side_effects=True, vmem_limit_bytes=VMEM_MOST
        ),
        cost_estimate=pl.CostEstimate(flops=0, bytes_accessed=240 * 2**20, transcendentals=0),
    )(down, kv, small, wide)


def by_owner(array, axis, count, f_first):
    lead, size, tail = array.shape[:axis], array.shape[axis], array.shape[axis + 1 :]
    part = size // (8 * count)
    n = len(lead)
    rest = [*range(n), n + 4, *range(n + 5, n + 5 + len(tail))]
    if f_first:
        array = array.reshape(*lead, count, 2, 2, 2, part, *tail)
        array = array.transpose(n, n + 1, n + 2, n + 3, *rest)
    else:
        array = array.reshape(*lead, 2, 2, count, 2, part, *tail)
        array = array.transpose(n + 2, n, n + 1, n + 3, *rest)
    return array.reshape(count, 8, *lead, part, *tail)


def from_owner(array, axis, f_first):
    count, _, *body = array.shape
    lead, part, tail = body[:axis], body[axis], body[axis + 1 :]
    n = axis
    array = array.reshape(count, 2, 2, 2, *body)
    inner = (0, 1, 2, 3) if f_first else (1, 2, 0, 3)
    array = array.transpose(
        *range(4, 4 + n), *inner, 4 + n, *range(5 + n, 5 + n + len(tail))
    )
    return array.reshape(*lead, 8 * count * part, *tail)


def scores_of(q_rot, k_rot, allowed):
    raw = jnp.einsum("bthd,bsd->bhts", q_rot, k_rot, preferred_element_type=F32)
    return jnp.where(allowed[:, None], raw * HEAD_DIM**-0.5, NEGATIVE)


def per_device(
    count,
    f_first,
    block_input,
    seq_lens,
    attn_gain,
    latent_down,
    latent_gain,
    latent_up,
    shared_kv,
    out_proj,
    mlp_gain,
    gate_weight,
    up_weight,
    down_weight,
    out_cotangent,
):
    tokens, width = block_input.shape
    rank = 2 * latent_down.shape[0]
    half_rank = latent_down.shape[0]
    units = down_weight.shape[0]
    mine = units * count
    padded = -(-mine // 256) * 256
    y = lax.axis_index("y")
    place = lax.axis_index("f")
    x_c = 2 * lax.axis_index("x") + lax.axis_index("c")

    def rows_of(array):
        flat = array.reshape(-1)
        lines = -(-flat.shape[0] // 128)
        return jnp.pad(flat, (0, lines * 128 - flat.shape[0])).reshape(lines, 128)

    gain_high = latent_gain.astype(BF16)
    gain_low = (latent_gain - gain_high.astype(F32)).astype(BF16)
    gain_rows = attn_gain.shape[0]
    lat_lines = half_rank // 128
    small = jnp.concatenate(
        [
            rows_of(gain_high),
            rows_of(gain_low),
            rows_of(attn_gain.astype(BF16)),
            rows_of(mlp_gain.astype(BF16)),
            rows_of(seq_lens.astype(BF16)),
        ]
    )
    at_gain = 2 * lat_lines
    small = jnp.pad(small, ((0, -small.shape[0] % 16), (0, 0)))
    parcel = Parcel(count, f_first, half_rank, latent_down.shape[1], shared_kv.shape[0])
    down_full, kv_full, small, both, g_all = start(
        parcel, latent_down, shared_kv, small, gate_weight, up_weight, out_cotangent, units, padded, 0
    )
    down_full = parcel.down_from(down_full)
    g_all = g_all.reshape(8 * tokens, width)

    half = count // 2
    per_head = count // 4
    up_line = lax.all_gather(latent_up.astype(BF16), "f", axis=0)
    out_line = lax.all_gather(after(out_proj.astype(BF16), up_line), "f", axis=0)

    def heads(line):
        own = lax.dynamic_slice_in_dim(line, half * y, half, 0)
        far = lax.dynamic_slice_in_dim(line, half - half * y, half, 0)
        return own, lax.ppermute(far, "y", SWAP)

    def join(own, other_part, axis):
        low = jnp.where(y == 0, own, other_part)
        high = jnp.where(y == 0, other_part, own)
        return jnp.stack([low, high], axis)

    up_full = join(*heads(up_line), 0).transpose(0, 2, 1, 3).reshape(rank, 2 * HEAD_DIM)
    out_full = join(*heads(out_line), 1).reshape(2 * HEAD_DIM, width)

    both = lax.all_gather(after(both, out_line), "f", axis=0)
    both = from_owner(both, 0, f_first)
    ff_down = lax.all_gather(after(down_weight.astype(BF16), both), "f", axis=0)
    ff_down = jnp.pad(ff_down.reshape(mine, width), ((0, padded - mine), (0, 0)))

    gain_lat = small[:2, 0, :lat_lines].astype(F32) + small[:2, 0, lat_lines:at_gain].astype(F32)
    gain_lat = gain_lat.reshape(rank)
    by_line = small.transpose(1, 0, 2, 3)
    gain_one = from_owner(by_line[:, :, at_gain, :gain_rows], 0, f_first).astype(F32)
    gain_two = from_owner(by_line[:, :, at_gain + 1, :gain_rows], 0, f_first).astype(F32)
    lengths = lax.dynamic_index_in_dim(small[:, :, at_gain + 2, :3], place, 1, keepdims=False)
    lengths = jnp.stack(
        [lax.dynamic_index_in_dim(lengths, in_plane() ^ i, 0, keepdims=False) for i in range(8)]
    ).astype(jnp.int32)

    inputs = block_input.astype(F32)
    rms_one = lax.rsqrt(jnp.mean(inputs * inputs, axis=-1, keepdims=True) + EPS)
    normed = (inputs * rms_one * gain_one).astype(BF16)
    latent = contract(normed, down_full, 1, 1)
    rms_lat = lax.rsqrt(jnp.mean(latent * latent, axis=-1, keepdims=True) + EPS)
    latent_n = (latent * rms_lat * gain_lat).astype(BF16)
    shared = jnp.dot(normed, kv_full, preferred_element_type=F32)
    position, allowed = layout(lengths, tokens)
    cosine, sine = rope_tables(position, HEAD_DIM)
    k_own = rotate(shared, cosine[0], sine[0]).astype(BF16)

    rows_all = plane_gather(jnp.concatenate([latent_n, k_own, shared.astype(BF16)], axis=1), 1)
    lat_all = rows_all[:, :, :rank].reshape(8 * tokens, rank)
    k_rot = rows_all[:, :, rank : rank + HEAD_DIM]
    values = rows_all[:, :, rank + HEAD_DIM :]
    queries = jnp.dot(lat_all, up_full, preferred_element_type=F32)
    wide_cos, wide_sin = cosine[:, :, None], sine[:, :, None]
    q_rot = rotate(queries.reshape(8, tokens, 2, HEAD_DIM), wide_cos, wide_sin).astype(BF16)
    scores = scores_of(q_rot, k_rot, allowed)
    peak = jnp.max(scores, axis=-1, keepdims=True)
    log_total = peak + jnp.log(jnp.sum(jnp.exp(scores - peak), axis=-1, keepdims=True))
    probs = jnp.exp(scores - log_total)
    attended = jnp.einsum("bhts,bsd->bthd", probs.astype(BF16), values, preferred_element_type=F32)
    attended = attended.reshape(8 * tokens, 2 * HEAD_DIM).astype(BF16)
    branch = matmul_scatter(attended, out_full, 2)

    middle = inputs + branch
    rms_two = lax.rsqrt(jnp.mean(middle * middle, axis=-1, keepdims=True) + EPS)
    normed_two = (middle * rms_two * gain_two).astype(BF16)
    two_all = plane_gather(normed_two, 3).reshape(8 * tokens, width)
    gate_up = jnp.dot(two_all, both, preferred_element_type=F32)
    gate, upval = gate_up[:, :padded], gate_up[:, padded:]
    sigma = jax.nn.sigmoid(gate)
    hidden = (gate * sigma * upval).astype(BF16)

    d_hidden = contract(g_all, ff_down, 1, 1)
    d_gate = (d_hidden * upval * sigma * (1.0 + gate * (1.0 - sigma))).astype(BF16)
    d_up = (d_hidden * gate * sigma).astype(BF16)
    d_both = jnp.concatenate([d_gate, d_up], axis=1)
    d_two = matmul_scatter(d_both, both, 4, True)

    result = jnp.dot(hidden, ff_down, preferred_element_type=F32)
    result = plane_scatter(after(result.reshape(8, tokens, width), d_two))

    both_grad = contract(two_all, d_both, 0, 0)
    both_grad = by_owner(both_grad.astype(BF16), 0, count, f_first)
    both_grad = lax.psum_scatter(both_grad, "f", scatter_dimension=0)

    down_grad = contract(hidden, g_all, 0, 0)[:mine].reshape(count, units, width)
    down_grad = lax.psum_scatter(down_grad.astype(BF16), "f", scatter_dimension=0).astype(F32)

    upstream = out_cotangent.astype(F32)
    gain_two_part = jnp.sum(d_two * middle * rms_two, axis=0)
    scaled_two = d_two * gain_two
    d_middle = (
        upstream
        + rms_two * scaled_two
        - middle * (rms_two**3) * jnp.mean(scaled_two * middle, axis=-1, keepdims=True)
    )

    d_branch = plane_gather(d_middle.astype(BF16), 5).reshape(8 * tokens, width)
    d_attended = contract(d_branch, out_full, 1, 1).astype(BF16)
    d_attended = d_attended.reshape(8, tokens, 2, HEAD_DIM)
    d_probs = jnp.einsum("bthd,bsd->bhts", d_attended, values, preferred_element_type=F32)
    inner = jnp.sum(probs * d_probs, axis=-1, keepdims=True)
    d_scores = (probs * (d_probs - inner)).astype(BF16)
    scale = HEAD_DIM**-0.5
    d_qrot = jnp.einsum("bhts,bsd->bthd", d_scores, k_rot, preferred_element_type=F32) * scale
    d_queries = unrotate(d_qrot, wide_cos, wide_sin).astype(BF16)
    d_queries = d_queries.reshape(8 * tokens, 2 * HEAD_DIM)
    d_krot = jnp.einsum("bhts,bthd->bsd", d_scores, q_rot, preferred_element_type=F32) * scale
    value_part = jnp.einsum(
        "bhts,bthd->bsd", probs.astype(BF16), d_attended, preferred_element_type=F32
    )
    shared_part = unrotate(d_krot, cosine, sine) + value_part
    back = matmul_scatter(d_queries, up_full, 6, True, shared_part.reshape(8 * tokens, HEAD_DIM))
    d_lat_n, d_shared = back[:, :rank], back[:, rank:].astype(BF16)

    own, *arrived = after(result, back)
    block_output = (middle + own + sum(part.astype(F32) for part in arrived)).astype(BF16)

    up_grad_heads = contract(lat_all, d_queries, 0, 0).reshape(2, half_rank, 2, HEAD_DIM)
    out_grad_heads = contract(attended, d_branch, 0, 0).reshape(2, per_head, 2, -1, width)

    def swap_halves(array, axis):
        own = lax.dynamic_index_in_dim(array, y, axis, keepdims=False)
        other = lax.dynamic_index_in_dim(array, 1 - y, axis, keepdims=False).astype(BF16)
        return own, lax.ppermute(other, "y", SWAP).astype(F32)

    up_line_grad = join(*swap_halves(up_grad_heads, 0), 1).reshape(half_rank, count, -1)
    up_line_grad = up_line_grad.transpose(1, 0, 2).astype(BF16)
    latent_up_grad = lax.psum_scatter(up_line_grad, "f", scatter_dimension=0).astype(F32)
    out_line_grad = join(*swap_halves(out_grad_heads, 2), 0)
    out_line_grad = out_line_grad.reshape(count, -1, width).astype(BF16)
    out_proj_grad = lax.psum_scatter(out_line_grad, "f", scatter_dimension=0).astype(F32)

    gain_lat_part = jnp.sum(d_lat_n * latent * rms_lat, axis=0)
    scaled_lat = d_lat_n * gain_lat
    inner_lat = jnp.sum(scaled_lat * latent, axis=-1, keepdims=True)
    d_latent = (rms_lat * scaled_lat - latent * (rms_lat**3) * inner_lat / rank).astype(BF16)
    d_normed = contract(d_shared, kv_full, 1, 1) + jnp.dot(
        d_latent, down_full, preferred_element_type=F32
    )
    gain_one_part = jnp.sum(d_normed * inputs * rms_one, axis=0)
    scaled_one = d_normed * gain_one
    input_grad = (
        d_middle
        + rms_one * scaled_one
        - inputs * (rms_one**3) * jnp.mean(scaled_one * inputs, axis=-1, keepdims=True)
    ).astype(BF16)

    down_part = parcel.down_to(contract(d_latent, normed, 0, 0).astype(BF16))
    kv_part = contract(normed, d_shared, 0, 0).astype(BF16)

    def gain_rows_of(part):
        part = by_owner(part.astype(BF16), 0, count, f_first).transpose(1, 0, 2)
        return jnp.pad(part, ((0, 0), (0, 0), (0, 128 - gain_rows)))[:, :, None]

    lat_rows = jnp.broadcast_to(
        gain_lat_part.astype(BF16).reshape(1, 2, 1, lat_lines, 128), (4, 2, count, lat_lines, 128)
    )
    small_part = jnp.concatenate(
        [
            lat_rows.reshape(8, count, lat_lines, 128),
            gain_rows_of(gain_one_part),
            gain_rows_of(gain_two_part),
        ],
        axis=2,
    )
    small_part = jnp.pad(small_part, ((0, 0), (0, 0), (0, -small_part.shape[2] % 16), (0, 0)))
    latent_down_grad, shared_kv_grad, small_sum, gate_grad, up_grad = end(
        parcel, down_part, kv_part, small_part, both_grad, units, padded, 7
    )
    latent_gain_grad = small_sum[:lat_lines].reshape(half_rank)
    attn_gain_grad = small_sum[lat_lines, :gain_rows]
    mlp_gain_grad = small_sum[lat_lines + 1, :gain_rows]
    return (
        block_output,
        input_grad,
        attn_gain_grad,
        latent_down_grad,
        latent_gain_grad,
        latent_up_grad,
        shared_kv_grad,
        out_proj_grad,
        mlp_gain_grad,
        gate_grad,
        up_grad,
        down_grad,
    )


def solution(mesh):
    devices = mesh.devices
    split = devices.shape[0]
    count = split // 4
    f_first = split == HEADS
    if f_first:
        names, sizes = ("f", "x", "c", "y"), (count, 2, 2, 2)
    else:
        names, sizes = ("x", "c", "f", "y"), (2, 2, count, 2)
    fine = Mesh(devices.reshape(sizes), names)
    dp = names[:3]
    return jax.shard_map(
        functools.partial(per_device, count, f_first),
        mesh=fine,
        in_specs=(
            P(names, None),
            P(names, None),
            P(names),
            P("y", dp),
            P("y"),
            P("y", dp),
            P(names, None),
            P(names, None),
            P(names),
            P(names, None),
            P(names, None),
            P(names, None),
            P(names, None),
        ),
        out_specs=(
            P(names, None),
            P(names, None),
            P(names),
            P("y", dp),
            P("y"),
            P("y", dp),
            P(names, None),
            P(names, None),
            P(names),
            P(names, None),
            P(names, None),
            P(names, None),
        ),
        check_vma=False,
    )
```

```python
import functools
import math

import jax
import jax.numpy as jnp
from jax import lax
from jax.experimental import pallas as pl
from jax.experimental.pallas import tpu as pltpu
from jax.sharding import Mesh
from jax.sharding import PartitionSpec as P

HEADS = 16
HEAD_DIM = 256
EPS = 1e-06
NEGATIVE = -1e30
F32 = jnp.float32
BF16 = jnp.bfloat16


def contract(left, right, left_dim, right_dim):
    return lax.dot_general(
        left, right, (((left_dim,), (right_dim,)), ((), ())), preferred_element_type=F32
    )


def after(value, *first):
    return lax.optimization_barrier((value, *first))[0]


def layout(lengths, count):
    spots = jnp.arange(lengths.shape[-1], dtype=jnp.int32)
    ends = jnp.sum(jnp.where(spots[None, :] <= spots[:, None], lengths[..., None, :], 0), axis=-1)
    places = jnp.arange(count, dtype=jnp.int32)
    passed = places[:, None] >= ends[..., None, :]
    offset = jnp.sum(jnp.where(passed, lengths[..., None, :], 0), axis=-1)
    return (places - offset).astype(F32), offset


def rope_tables(position, width):
    half = width // 2
    steps = jnp.arange(half, dtype=F32)
    freqs = jnp.exp(steps * (-math.log(10000.0) / half))
    angles = position[..., None] * freqs
    return jnp.cos(angles), jnp.sin(angles)


def rotate(values, cosine, sine):
    half = values.shape[-1] // 2
    first, second = values[..., :half], values[..., half:]
    return jnp.concatenate(
        [first * cosine - second * sine, second * cosine + first * sine], axis=-1
    )


SWAP = [(0, 1), (1, 0)]
DIAGONAL = [(0, 3), (3, 0), (1, 2), (2, 1)]


X_BIT, Y_BIT, C_BIT = 4, 2, 1
BOTH = X_BIT | Y_BIT
VMEM_MOST = 60 * 2**20


def other(bits):
    flips = {"x": bits // 4, "y": bits // 2 % 2, "c": bits % 2}
    return {name: 1 - lax.axis_index(name) for name, flip in flips.items() if flip}


def greet(partners):
    barrier = pltpu.get_barrier_semaphore()
    for partner in partners:
        pl.semaphore_signal(barrier, inc=1, device_id=partner)
    pl.semaphore_wait(barrier, len(partners))


def send(source, target, send_sem, recv_sem, device):
    return pltpu.make_async_remote_copy(
        src_ref=source, dst_ref=target, send_sem=send_sem, recv_sem=recv_sem, device_id=device
    )


def begin(copies):
    for copy in copies:
        copy.start()


def arrive(copies):
    for copy in copies:
        copy.wait_recv()


def gone(copies):
    for copy in copies:
        copy.wait_send()


def gathering(chunks, in_ref, out_ref, send_sem, recv_sem):
    tokens = in_ref.shape[0]
    rows = tokens // chunks

    def to(slot, k, bits, source=None):
        target = out_ref.at[pl.ds(slot * tokens + k * rows, rows)]
        if source is None:
            source = in_ref.at[pl.ds(k * rows, rows)]
        else:
            source = out_ref.at[pl.ds(source * tokens + k * rows, rows)]
        return send(source, target, send_sem.at[slot, k], recv_sem.at[slot, k], other(bits))

    def own():
        for k in range(chunks):
            to(X_BIT, k, X_BIT).start()
            to(Y_BIT, k, Y_BIT).start()
        for k in range(chunks):
            to(C_BIT, k, C_BIT).start()

    def relay(first, last):
        for k in range(first, last):
            to(X_BIT, k, X_BIT).wait_recv()
            if k < chunks // 2:
                to(BOTH, k, Y_BIT, X_BIT).start()
            to(X_BIT | C_BIT, k, C_BIT, X_BIT).start()
            to(Y_BIT, k, Y_BIT).wait_recv()
            if k >= chunks // 2:
                to(BOTH, k, X_BIT, Y_BIT).start()
            to(Y_BIT | C_BIT, k, C_BIT, Y_BIT).start()

    def far():
        for k in range(chunks):
            to(BOTH, k, Y_BIT).wait_recv()
            to(BOTH | C_BIT, k, C_BIT, BOTH).start()

    def arrived(chip):
        for k in range(chunks):
            to(chip | C_BIT, k, C_BIT).wait_recv()

    def sent():
        for slot in range(1, 8):
            for k in range(chunks):
                to(slot, k, C_BIT).wait_send()

    return own, relay, far, arrived, sent


def gather_kernel(chunks, in_ref, out_ref, own_sem, send_sem, recv_sem):
    greet([other(C_BIT), other(X_BIT), other(Y_BIT)])
    copy = pltpu.make_async_copy(in_ref, out_ref.at[pl.ds(0, in_ref.shape[0])], own_sem)
    copy.start()
    own, relay, far, arrived, sent = gathering(chunks, in_ref, out_ref, send_sem, recv_sem)
    own()
    relay(0, chunks)
    far()
    copy.wait()
    for chip in (0, Y_BIT, X_BIT, BOTH):
        arrived(chip)
    sent()


def plane_gather(block, name, chunks=4):
    return pl.pallas_call(
        functools.partial(gather_kernel, chunks),
        out_shape=jax.ShapeDtypeStruct((8 * block.shape[0], block.shape[1]), block.dtype),
        in_specs=[pl.BlockSpec(memory_space=pl.ANY)],
        out_specs=pl.BlockSpec(memory_space=pl.ANY),
        scratch_shapes=[
            pltpu.SemaphoreType.DMA,
            pltpu.SemaphoreType.DMA((8, chunks)),
            pltpu.SemaphoreType.DMA((8, chunks)),
        ],
        compiler_params=pltpu.CompilerParams(collective_id=name, has_side_effects=True),
        cost_estimate=pl.CostEstimate(flops=0, bytes_accessed=160 * 2**20, transcendentals=0),
    )(block)


def row_loop(amount, do, size=32):
    @pl.loop(0, amount // size)
    def _(r):
        do(pl.ds(pl.multiple_of(r * size, size), size))


def scattering(
    out_ref, work_ref, near_ref, far_ref, near_send, near_recv, far_send, far_recv, produce
):
    greet([other(C_BIT), other(X_BIT), other(Y_BIT)])
    tokens = out_ref.shape[0]
    half = tokens // 2
    low, high = pl.ds(0, half), pl.ds(half, half)

    def near(n):
        return send(
            work_ref.at[n, pl.ds(tokens, tokens)], near_ref.at[n], near_send.at[n], near_recv.at[n], other(C_BIT)
        )

    def hop(i):
        n, part, bits = (
            (0, low, X_BIT), (0, high, Y_BIT), (1, low, X_BIT), (2, high, Y_BIT), (1, high, X_BIT), (2, low, Y_BIT)
        )[i]
        return send(work_ref.at[n, part], far_ref.at[i], far_send.at[i], far_recv.at[i], other(bits))

    def chip_sum(n):
        near(n).wait_recv()

        def keep(at):
            total = work_ref[n, at, :].astype(F32) + near_ref[n, at, :].astype(F32)
            work_ref[n, at, :] = total.astype(BF16)

        row_loop(tokens, keep)

    @pl.loop(0, 4)
    def _(n):
        produce(3 - n, work_ref.at[n])
        near(n).start()

        @pl.when(n > 0)
        def _():
            chip_sum(n - 1)
            pl.when(n == 1)(lambda: begin([hop(0), hop(1)]))
            pl.when(n == 2)(lambda: hop(2).start())
            pl.when(n == 3)(lambda: hop(3).start())

    near(3).wait_recv()

    def give(at):
        out_ref[at, :] = work_ref[3, at, :].astype(F32) + near_ref[3, at, :].astype(F32)

    row_loop(tokens, give)
    for came, n, first, on in ((0, 2, 0, 5), (1, 1, half, 4)):
        hop(came).wait_recv()

        def add(at, came=came, n=n, first=first):
            here = pl.ds(pl.multiple_of(first + at.start, 32), 32)
            total = work_ref[n, here, :].astype(F32) + far_ref[came, at, :].astype(F32)
            work_ref[n, here, :] = total.astype(BF16)

        row_loop(half, add)
        hop(on).start()

    def last(came, first):
        for i in came:
            hop(i).wait_recv()

        def add(at):
            here = pl.ds(pl.multiple_of(first + at.start, 32), 32)
            value = out_ref[here, :]
            for i in came:
                value = value + far_ref[i, at, :].astype(F32)
            out_ref[here, :] = value

        row_loop(half, add)

    last((2, 5), 0)
    last((3, 4), half)
    gone([*[near(n) for n in range(4)], *[hop(i) for i in range(6)]])


def scatter_scratch(tokens, wide):
    dma = pltpu.SemaphoreType.DMA
    return [
        pltpu.VMEM((4, 2 * tokens, wide), BF16),
        pltpu.VMEM((4, tokens, wide), BF16),
        pltpu.VMEM((6, tokens // 2, wide), BF16),
        dma((4,)), dma((4,)),
        dma((6,)), dma((6,)),
    ]


def vmem_call(kernel, out_shape, amount, scratch, name, flops, *arrays):
    vmem = pl.BlockSpec(memory_space=pltpu.VMEM)
    return pl.pallas_call(
        kernel,
        out_shape=out_shape,
        in_specs=[vmem] * amount,
        out_specs=[vmem] * len(out_shape),
        scratch_shapes=scratch,
        compiler_params=pltpu.CompilerParams(
            collective_id=name, has_side_effects=True, vmem_limit_bytes=VMEM_MOST
        ),
        cost_estimate=pl.CostEstimate(flops=flops, bytes_accessed=160 * 2**20, transcendentals=0),
    )(*arrays)


def turn(values, cosine, sine):
    half = values.shape[-1] // 2
    first, second = values[:, :half], values[:, half:]
    return jnp.concatenate([first * cosine - second * sine, second * cosine + first * sine], axis=1)


def masked_scores(queries, keys, begins):
    raw = contract(queries, keys, 1, 1) * HEAD_DIM**-0.5
    to = lax.broadcasted_iota(jnp.int32, raw.shape, 0)
    of = lax.broadcasted_iota(jnp.int32, raw.shape, 1)
    return jnp.where((of <= to) & (of >= begins), raw, NEGATIVE)


def halves(rank):
    half = rank // 2
    y = lax.axis_index("y")
    return (
        pl.ds(pl.multiple_of(y * half, half), half),
        pl.ds(pl.multiple_of(half - y * half, half), half),
    )


def attention_kernel(
    rank, rows_ref, own_ref, far_ref, out_w_ref, cos_ref, sin_ref, begin_ref,
    branch_ref, query_ref, lse_ref, att_ref, *rest,
):
    wide = out_w_ref.shape[1]
    tokens = branch_ref.shape[0]
    mine, theirs = halves(rank)

    def produce(chip, target):
        pair = pl.ds(pl.multiple_of(chip * 2 * tokens, 2 * tokens), 2 * tokens)
        queries = contract(rows_ref[pair, mine], own_ref[...], 1, 0)
        queries = queries + contract(rows_ref[pair, theirs], far_ref[...], 1, 0)
        for c in range(2):
            rows = pl.ds(pl.multiple_of((2 * chip + c) * tokens, tokens), tokens)
            keys = rows_ref[rows, rank : rank + HEAD_DIM]
            values = rows_ref[rows, rank + HEAD_DIM :]
            cosine, sine, begins = cos_ref[rows, :], sin_ref[rows, :], begin_ref[rows, :]
            for h in range(2):
                at = slice(h * HEAD_DIM, (h + 1) * HEAD_DIM)
                turned = turn(queries[c * tokens : (c + 1) * tokens, at], cosine, sine).astype(BF16)
                query_ref[rows, at] = turned
                scores = masked_scores(turned, keys, begins)
                peak = jnp.max(scores, axis=1, keepdims=True)
                lse = peak + jnp.log(jnp.sum(jnp.exp(scores - peak), axis=1, keepdims=True))
                lse_ref[rows, h : h + 1] = lse
                probs = jnp.exp(scores - lse).astype(BF16)
                att_ref[rows, at] = contract(probs, values, 1, 0).astype(BF16)

        @pl.loop(0, wide // 512)
        def _(i):
            at = pl.ds(pl.multiple_of(i * 512, 512), 512)
            target[:, at] = contract(att_ref[pair, :], out_w_ref[:, at], 1, 0).astype(BF16)

    scattering(branch_ref, *rest, produce)


def attention(rows, own, far, out_w, cosine, sine, begins, name):
    tokens, rank = rows.shape[0] // 8, 2 * own.shape[0]
    wide = out_w.shape[1]
    two = 2 * HEAD_DIM
    return vmem_call(
        functools.partial(attention_kernel, rank),
        [
            jax.ShapeDtypeStruct((tokens, wide), F32),
            jax.ShapeDtypeStruct((8 * tokens, two), BF16),
            jax.ShapeDtypeStruct((8 * tokens, 2), F32),
            jax.ShapeDtypeStruct((8 * tokens, two), BF16),
        ],
        7,
        scatter_scratch(tokens, wide),
        name,
        16 * tokens * two * (wide + rank + 2 * tokens),
        rows, own, far, out_w, cosine, sine, begins,
    )


def attention_back_kernel(
    rank, d_ref, rows_ref, own_ref, far_ref, out_w_ref, cos_ref, sin_ref, begin_ref, query_ref, lse_ref,
    back_ref, dq_ref, *rest,
):
    tokens = back_ref.shape[0]
    mine, theirs = halves(rank)
    scale = HEAD_DIM**-0.5

    def produce(chip, target):
        pair = pl.ds(pl.multiple_of(chip * 2 * tokens, 2 * tokens), 2 * tokens)
        d_pair = contract(d_ref[pair, :], out_w_ref[...], 1, 1).astype(BF16)
        for c in range(2):
            rows = pl.ds(pl.multiple_of((2 * chip + c) * tokens, tokens), tokens)
            here = slice(c * tokens, (c + 1) * tokens)
            keys = rows_ref[rows, rank : rank + HEAD_DIM]
            values = rows_ref[rows, rank + HEAD_DIM :]
            cosine, sine, begins = cos_ref[rows, :], sin_ref[rows, :], begin_ref[rows, :]
            d_keys = d_values = None
            for h in range(2):
                at = slice(h * HEAD_DIM, (h + 1) * HEAD_DIM)
                queries, d_att = query_ref[rows, at], d_pair[here, at]
                probs = jnp.exp(masked_scores(queries, keys, begins) - lse_ref[rows, h : h + 1])
                d_probs = contract(d_att, values, 1, 1)
                inner = jnp.sum(probs * d_probs, axis=1, keepdims=True)
                d_scores = (probs * (d_probs - inner)).astype(BF16)
                d_query = contract(d_scores, keys, 1, 0) * scale
                dq_ref[rows, at] = turn(d_query, cosine, -sine).astype(BF16)
                d_k = contract(d_scores, queries, 0, 0)
                d_v = contract(probs.astype(BF16), d_att, 0, 0)
                d_keys = d_k if h == 0 else d_keys + d_k
                d_values = d_v if h == 0 else d_values + d_v
            shared = turn(d_keys * scale, cosine, -sine) + d_values
            target[here, rank:] = shared.astype(BF16)
        target[:, mine] = contract(dq_ref[pair, :], own_ref[...], 1, 1).astype(BF16)
        target[:, theirs] = contract(dq_ref[pair, :], far_ref[...], 1, 1).astype(BF16)

    scattering(back_ref, *rest, produce)


def attention_back(d_rows, rows, own, far, out_w, cosine, sine, begins, queries, lse, name):
    tokens, rank = rows.shape[0] // 8, 2 * own.shape[0]
    wide = out_w.shape[1]
    two = 2 * HEAD_DIM
    full = rank + HEAD_DIM
    return vmem_call(
        functools.partial(attention_back_kernel, rank),
        [jax.ShapeDtypeStruct((tokens, full), F32), jax.ShapeDtypeStruct((8 * tokens, two), BF16)],
        10,
        scatter_scratch(tokens, full),
        name,
        16 * tokens * two * (wide + rank + 5 * tokens),
        d_rows, rows, own, far, out_w, cosine, sine, begins, queries, lse,
    )


def feed_kernel(
    chunks, in_ref, g_ref, both_ref, down_ref, two_ref, hidden_ref, d_both_ref,
    g_held, both_held, down_held, own_sem, load_sem, send_sem, recv_sem,
):
    step = 256
    tokens = in_ref.shape[0]
    padded = hidden_ref.shape[1]
    units = down_ref.shape[0]
    loads = [
        pltpu.make_async_copy(both_ref, both_held, load_sem.at[0]),
        pltpu.make_async_copy(g_ref, g_held, load_sem.at[1]),
        pltpu.make_async_copy(down_ref, down_held.at[pl.ds(0, units)], load_sem.at[2]),
        pltpu.make_async_copy(in_ref, two_ref.at[pl.ds(0, tokens)], own_sem),
    ]
    begin(loads)
    greet([other(C_BIT), other(X_BIT), other(Y_BIT)])
    own, relay, far, arrived, sent = gathering(chunks, in_ref, two_ref, send_sem, recv_sem)
    own()
    if units < padded:
        down_held[units:, :] = jnp.zeros((padded - units, down_held.shape[1]), BF16)
    for copy in loads:
        copy.wait()

    def units_of(chip):
        arrived(chip)
        pair = pl.ds(chip * tokens, 2 * tokens)

        @pl.loop(0, padded // step)
        def _(i):
            at = pl.ds(pl.multiple_of(i * step, step), step)
            up_at = pl.ds(pl.multiple_of(padded + i * step, step), step)
            gate = contract(two_ref[pair, :], both_held[:, at], 1, 0)
            upval = contract(two_ref[pair, :], both_held[:, up_at], 1, 0)
            d_hidden = contract(g_held[pair, :], down_held[at, :], 1, 1)
            sigma = 1.0 / (1.0 + jnp.exp(-gate))
            silu = gate * sigma
            hidden_ref[pair, at] = (silu * upval).astype(BF16)
            d_gate = d_hidden * upval * sigma * (1.0 + gate * (1.0 - sigma))
            d_both_ref[pair, at] = d_gate.astype(BF16)
            d_both_ref[pair, up_at] = (d_hidden * silu).astype(BF16)

    units_of(0)
    relay(0, chunks)
    units_of(X_BIT)
    units_of(Y_BIT)
    far()
    units_of(BOTH)
    sent()


def feed(rows, g, both, down, padded, name, chunks=4):
    tokens, width = rows.shape
    any_space, vmem = pl.BlockSpec(memory_space=pl.ANY), pl.BlockSpec(memory_space=pltpu.VMEM)
    dma = pltpu.SemaphoreType.DMA
    return pl.pallas_call(
        functools.partial(feed_kernel, chunks),
        out_shape=[
            jax.ShapeDtypeStruct((8 * tokens, width), BF16),
            jax.ShapeDtypeStruct((8 * tokens, padded), BF16),
            jax.ShapeDtypeStruct((8 * tokens, 2 * padded), BF16),
        ],
        in_specs=[any_space] * 4,
        out_specs=[vmem] * 3,
        scratch_shapes=[
            pltpu.VMEM(g.shape, BF16),
            pltpu.VMEM(both.shape, BF16),
            pltpu.VMEM((padded, width), BF16),
            dma,
            dma((3,)),
            dma((8, chunks)), dma((8, chunks)),
        ],
        compiler_params=pltpu.CompilerParams(
            collective_id=name, has_side_effects=True, vmem_limit_bytes=VMEM_MOST
        ),
        cost_estimate=pl.CostEstimate(
            flops=16 * tokens * 3 * width * padded, bytes_accessed=160 * 2**20, transcendentals=0
        ),
    )(rows, g, both, down)


def product_scatter_kernel(left_ref, right_ref, out_ref, *rest):
    tokens = out_ref.shape[0]
    step = 256

    def produce(chip, target):
        pair = pl.ds(pl.multiple_of(chip * 2 * tokens, 2 * tokens), 2 * tokens)

        @pl.loop(0, out_ref.shape[1] // step)
        def _(i):
            at = pl.ds(pl.multiple_of(i * step, step), step)
            target[:, at] = contract(left_ref[pair, :], right_ref[at, :], 1, 1).astype(BF16)

    scattering(out_ref, *rest, produce)


def product_scatter(left, right, name):
    tokens, wide = left.shape[0] // 8, right.shape[0]
    return vmem_call(
        product_scatter_kernel,
        [jax.ShapeDtypeStruct((tokens, wide), F32)],
        2,
        scatter_scratch(tokens, wide),
        name,
        16 * tokens * wide * left.shape[1],
        left, right,
    )[0]


def branch_gather_kernel(
    chunks, in_ref, hidden_ref, down_ref, out_ref, own_sum, chip_sums,
    down_held, work_ref, near_ref, own_sem, load_sem, send_sem, recv_sem, near_send, near_recv,
):
    tokens = in_ref.shape[0]
    wide = down_ref.shape[1]
    units, padded = down_ref.shape[0], down_held.shape[0]
    copies = [
        pltpu.make_async_copy(in_ref, out_ref.at[pl.ds(0, tokens)], own_sem),
        pltpu.make_async_copy(down_ref, down_held.at[pl.ds(0, units)], load_sem),
    ]
    begin(copies)
    greet([other(C_BIT), other(X_BIT), other(Y_BIT)])
    own, relay, far, arrived, sent = gathering(chunks, in_ref, out_ref, send_sem, recv_sem)
    own()
    if units < padded:
        down_held[units:, :] = jnp.zeros((padded - units, wide), BF16)
    for copy in copies:
        copy.wait()

    def near(n):
        return send(
            work_ref.at[n, pl.ds(tokens, tokens)], near_ref.at[n], near_send.at[n], near_recv.at[n], other(C_BIT)
        )

    def product(n):
        pair = slice((3 - n) * 2 * tokens, (4 - n) * 2 * tokens)

        @pl.loop(0, wide // 256)
        def _(i):
            at = pl.ds(pl.multiple_of(i * 256, 256), 256)
            work_ref[n, :, at] = contract(hidden_ref[pair, :], down_held[:, at], 1, 0).astype(BF16)

        near(n).start()

    product(0)
    product(1)
    relay(0, chunks // 2)
    product(2)
    relay(chunks // 2, chunks)
    product(3)
    for n in range(4):
        near(n).wait_recv()

        def add(at, n=n):
            total = work_ref[n, at, :].astype(F32) + near_ref[n, at, :].astype(F32)
            if n < 3:
                chip_sums[n, at, :] = total.astype(BF16)
            else:
                own_sum[at, :] = total

        row_loop(tokens, add)
    far()
    for chip in (0, Y_BIT, X_BIT, BOTH):
        arrived(chip)
    sent()
    gone([near(n) for n in range(4)])


def branch_gather(rows, hidden, down, name, chunks=4):
    tokens, width = rows.shape
    wide = down.shape[1]
    any_space, vmem = pl.BlockSpec(memory_space=pl.ANY), pl.BlockSpec(memory_space=pltpu.VMEM)
    dma = pltpu.SemaphoreType.DMA
    return pl.pallas_call(
        functools.partial(branch_gather_kernel, chunks),
        out_shape=[
            jax.ShapeDtypeStruct((8 * tokens, width), BF16),
            jax.ShapeDtypeStruct((tokens, wide), F32),
            jax.ShapeDtypeStruct((3, tokens, wide), BF16),
        ],
        in_specs=[any_space, vmem, any_space],
        out_specs=[any_space, vmem, vmem],
        scratch_shapes=[
            pltpu.VMEM((hidden.shape[1], wide), BF16),
            pltpu.VMEM((4, 2 * tokens, wide), BF16),
            pltpu.VMEM((4, tokens, wide), BF16),
            dma,
            dma,
            dma((8, chunks)), dma((8, chunks)),
            dma((4,)), dma((4,)),
        ],
        compiler_params=pltpu.CompilerParams(
            collective_id=name, has_side_effects=True, vmem_limit_bytes=VMEM_MOST
        ),
        cost_estimate=pl.CostEstimate(
            flops=16 * tokens * wide * hidden.shape[1], bytes_accessed=160 * 2**20, transcendentals=0
        ),
    )(rows, hidden, down)


def in_plane():
    return 4 * lax.axis_index("x") + 2 * lax.axis_index("c") + lax.axis_index("y")


class Parcel:
    def __init__(self, count, f_first, rank_rows, columns, kv_rows):
        self.count, self.f_first = count, f_first
        self.rank_rows, self.columns, self.kv_rows = rank_rows, columns, kv_rows
        self.windows = columns % 128 == 0

    def down_shape(self):
        if self.windows:
            return (2 * self.rank_rows, 4 * self.count * self.columns)
        return (8, self.count, self.rank_rows, self.columns)

    def down_from(self, array):
        if self.windows:
            return array
        array = array.reshape(2, 2, 2, self.count, self.rank_rows, self.columns)
        array = array.transpose((2, 4, 3, 0, 1, 5) if self.f_first else (2, 4, 0, 1, 3, 5))
        return array.reshape(2 * self.rank_rows, -1)

    def down_to(self, array):
        if self.windows:
            return array
        inner = (self.count, 2, 2) if self.f_first else (2, 2, self.count)
        array = array.reshape(2, self.rank_rows, *inner, self.columns)
        array = array.transpose((3, 4, 0, 2, 1, 5) if self.f_first else (2, 3, 0, 4, 1, 5))
        return array.reshape(self.down_shape())

    def blocks(self, refs, place, j):
        down, kv, small = refs
        pair, y = place // 2, place % 2
        at = j * 4 + pair if self.f_first else pair * self.count + j
        if self.windows:
            down = down.at[
                pl.ds(pl.multiple_of(y * self.rank_rows, self.rank_rows), self.rank_rows),
                pl.ds(pl.multiple_of(at * self.columns, self.columns), self.columns),
            ]
        else:
            down = down.at[place, j]
        start_row = pl.multiple_of((2 * at + y) * self.kv_rows, self.kv_rows)
        return down, kv.at[pl.ds(start_row, self.kv_rows)], small.at[place, j]

    def unit_pieces(self):
        for shard in range(8 * self.count):
            if self.f_first:
                yield shard % 8, shard // 8, shard
            else:
                yield shard // (2 * self.count) * 2 + shard % 2, shard // 2 % self.count, shard


def greet_all(count):
    f = lax.axis_index("f")
    lower, upper = f > 0, f < count - 1
    barrier = pltpu.get_barrier_semaphore()
    for bits in range(1, 8):
        pl.semaphore_signal(barrier, inc=1, device_id=other(bits))
    pl.when(lower)(lambda: pl.semaphore_signal(barrier, inc=1, device_id={"f": f - 1}))
    pl.when(upper)(lambda: pl.semaphore_signal(barrier, inc=1, device_id={"f": f + 1}))
    pl.semaphore_wait(barrier, 7 + lower.astype(jnp.int32) + upper.astype(jnp.int32))
    return lower, upper


FAR_FIRST = (7, 6, 5, 4, 3, 2, 1)


def as_place(bits):
    return (bits & 4) + 2 * (bits & 1) + (bits >> 1 & 1)


def start_kernel(
    parcel, chunks, units, padded, down_ref, kv_ref, small_ref, gate_ref, up_ref, rows_ref,
    down_all, kv_all, small_all, wide_all, rows_all,
    down_low, kv_low, wide_ref,
    local_sem, line_send, line_recv, plane_send, plane_recv, wide_send, wide_recv, rows_send, rows_recv,
):
    count = parcel.count
    f, me = lax.axis_index("f"), in_plane()
    lower, upper = greet_all(count)
    own = (down_low, kv_low, small_ref)
    alls = (down_all, kv_all, small_all)
    down_low[...] = down_ref[...].astype(BF16)
    kv_low[...] = kv_ref[...].astype(BF16)

    def hop(j, up, sources):
        return [
            send(
                source, target, line_send.at[i, 0 if up else 1, j], line_recv.at[i, j],
                {"f": f + 1 if up else f - 1},
            )
            for i, (source, target) in enumerate(zip(sources, parcel.blocks(alls, me, j)))
        ]

    def spread(slot, bits, j, sources):
        targets = parcel.blocks(alls, me ^ as_place(bits) ^ as_place(slot), j)
        return [
            send(source, target, plane_send.at[i, slot, j], plane_recv.at[i, slot, j], other(bits))
            for i, (source, target) in enumerate(zip(sources, targets))
        ]

    def to_plane(j, sources):
        for bits in (X_BIT, Y_BIT, C_BIT):
            begin(spread(bits, bits, j, sources))

    def line_step(step):
        @pl.when(f - step >= 0)
        def _():
            j = f - step
            blocks = parcel.blocks(alls, me, j)
            arrive(hop(j, True, blocks))
            pl.when(upper)(lambda: begin(hop(j, True, blocks)))
            to_plane(j, blocks)

        @pl.when(f + step <= count - 1)
        def _():
            j = f + step
            blocks = parcel.blocks(alls, me, j)
            arrive(hop(j, False, blocks))
            pl.when(lower)(lambda: begin(hop(j, False, blocks)))
            to_plane(j, blocks)

    def relay(j):
        by_x, by_y = parcel.blocks(alls, me ^ as_place(X_BIT), j), parcel.blocks(alls, me ^ as_place(Y_BIT), j)
        arrive(spread(X_BIT, X_BIT, j, by_x))
        pl.when(j % 2 == 0)(lambda: begin(spread(BOTH, Y_BIT, j, by_x)))
        begin(spread(X_BIT | C_BIT, C_BIT, j, by_x))
        arrive(spread(Y_BIT, Y_BIT, j, by_y))
        pl.when(j % 2 == 1)(lambda: begin(spread(BOTH, X_BIT, j, by_y)))
        begin(spread(Y_BIT | C_BIT, C_BIT, j, by_y))

    def relay_far(j):
        by_both = parcel.blocks(alls, me ^ as_place(BOTH), j)
        arrive(spread(BOTH, Y_BIT, j, by_both))
        begin(spread(BOTH | C_BIT, C_BIT, j, by_both))

    def in_order(do):
        do(f)
        for step in range(1, count):
            pl.when(f - step >= 0)(lambda: do(f - step))
            pl.when(f + step <= count - 1)(lambda: do(f + step))

    def wide(bits):
        return send(wide_ref.at[me ^ as_place(bits)], wide_all.at[me], wide_send.at[bits], wide_recv.at[bits], other(bits))

    pl.when(upper)(lambda: begin(hop(f, True, own)))
    pl.when(lower)(lambda: begin(hop(f, False, own)))
    to_plane(f, own)
    for place, j, shard in parcel.unit_pieces():
        for first, ref in ((0, gate_ref), (padded, up_ref)):
            piece = ref[:, shard * units : (shard + 1) * units].astype(BF16)
            wide_ref[place, :, first + j * units : first + (j + 1) * units] = piece
    for first in (count * units, padded + count * units):
        size = padded - count * units
        wide_ref[:, :, first : first + size] = jnp.zeros((8, wide_ref.shape[1], size), BF16)
    for bits in FAR_FIRST:
        wide(bits).start()
    locals_ = [
        pltpu.make_async_copy(source, target, local_sem.at[i])
        for i, (source, target) in enumerate(
            (
                *zip(own, parcel.blocks(alls, me, f)),
                (wide_ref.at[me], wide_all.at[me]),
                (rows_ref, rows_all.at[pl.ds(0, rows_ref.shape[0])]),
            )
        )
    ]
    begin(locals_)
    rows_own, rows_relay, rows_far, rows_arrived, rows_sent = gathering(chunks, rows_ref, rows_all, rows_send, rows_recv)
    for step in range(1, count):
        line_step(step)
    rows_own()
    in_order(relay)
    rows_relay(0, chunks // 2)
    in_order(relay_far)
    rows_relay(chunks // 2, chunks)
    rows_far()
    for copy in locals_:
        copy.wait()
    for j in range(count):
        pl.when(upper & (f >= j))(lambda: gone(hop(j, True, own)))
        pl.when(lower & (f <= j))(lambda: gone(hop(j, False, own)))
    for slot in range(1, 8):
        for j in range(count):
            for copy in spread(slot, slot, j, own):
                if slot & C_BIT:
                    copy.wait_recv()
                copy.wait_send()
    for bits in range(1, 8):
        wide(bits).wait_recv()
        wide(bits).wait_send()
    for chip in (0, Y_BIT, X_BIT, BOTH):
        rows_arrived(chip)
    rows_sent()


def start(parcel, down, kv, small, gate, up, rows, units, padded, name, chunks=4):
    count = parcel.count
    any_space, vmem = pl.BlockSpec(memory_space=pl.ANY), pl.BlockSpec(memory_space=pltpu.VMEM)
    dma = pltpu.SemaphoreType.DMA
    wide = (8, gate.shape[0], 2 * padded)
    return pl.pallas_call(
        functools.partial(start_kernel, parcel, chunks, units, padded),
        out_shape=[
            jax.ShapeDtypeStruct(parcel.down_shape(), BF16),
            jax.ShapeDtypeStruct((8 * count * kv.shape[0], kv.shape[1]), BF16),
            jax.ShapeDtypeStruct((8, count, *small.shape), BF16),
            jax.ShapeDtypeStruct(wide, BF16),
            jax.ShapeDtypeStruct((8 * rows.shape[0], rows.shape[1]), BF16),
        ],
        in_specs=[vmem] * 5 + [any_space],
        out_specs=[any_space] * 5,
        scratch_shapes=[
            pltpu.VMEM(down.shape, BF16),
            pltpu.VMEM(kv.shape, BF16),
            pltpu.VMEM(wide, BF16),
            dma((5,)),
            dma((3, 2, count)), dma((3, count)),
            dma((3, 8, count)), dma((3, 8, count)),
            dma((8,)), dma((8,)),
            dma((8, chunks)), dma((8, chunks)),
        ],
        compiler_params=pltpu.CompilerParams(
            collective_id=name, has_side_effects=True, vmem_limit_bytes=VMEM_MOST
        ),
        cost_estimate=pl.CostEstimate(flops=0, bytes_accessed=240 * 2**20, transcendentals=0),
    )(down, kv, small, gate, up, rows)


def end_kernel(
    parcel, units, padded, down_ref, kv_ref, small_ref, wide_ref,
    down_sum, kv_sum, small_sum, gate_sum, up_sum, *rest,
):
    count = parcel.count
    held = [rest[8 * i : 8 * i + 8] for i in range(3)]
    wide_all, near_send, near_recv, chip_send, chip_recv, line_send, line_recv, wide_send, wide_recv = rest[24:]
    f, me = lax.axis_index("f"), in_plane()
    lower, upper = greet_all(count)
    parts = (down_ref, kv_ref, small_ref)
    sums = (down_sum, kv_sum, small_sum)
    chips = (BOTH, X_BIT, Y_BIT, 0)

    def rows(amount, do):
        size = 16 if amount % 64 else 64

        @pl.loop(0, amount // size)
        def _(r):
            do(pl.ds(pl.multiple_of(r * size, size), size))

    def near(n, j):
        sources = parcel.blocks(parts, me ^ as_place(chips[n] | C_BIT), j)
        return [
            send(source, held[i][1].at[n, j], near_send.at[i, n, j], near_recv.at[i, n, j], other(C_BIT))
            for i, source in enumerate(sources)
        ]

    def far(n):
        return [
            send(held[i][2].at[n], held[i][3].at[n], chip_send.at[i, n], chip_recv.at[i, n], other(chips[n]))
            for i in range(3)
        ]

    def wide(bits):
        return send(wide_ref.at[me ^ as_place(bits)], wide_all.at[me], wide_send.at[bits], wide_recv.at[bits], other(bits))

    def hop(d, up):
        way = 0 if up else 1
        return [
            send(
                held[i][4 + 2 * way].at[d], held[i][5 + 2 * way].at[d],
                line_send.at[i, way, d], line_recv.at[i, way, d],
                {"f": f + 1 if up else f - 1},
            )
            for i in range(3)
        ]

    def pass_on(d, up):
        way = 0 if up else 1
        behind = lower if up else upper

        @pl.when((d > f) if up else (d < f))
        def _():
            @pl.when(behind)
            def _():
                for copy in hop(d, up):
                    copy.wait_recv()
                for total, outgoing, incoming in ((h[0], h[4 + 2 * way], h[5 + 2 * way]) for h in held):

                    def add(at, total=total, outgoing=outgoing, incoming=incoming):
                        outgoing[d, at, :] = (total[d, at, :] + incoming[d, at, :].astype(F32)).astype(BF16)

                    rows(total.shape[1], add)

            @pl.when(jnp.logical_not(behind))
            def _():
                for total, outgoing in ((h[0], h[4 + 2 * way]) for h in held):

                    def keep(at, total=total, outgoing=outgoing):
                        outgoing[d, at, :] = total[d, at, :].astype(BF16)

                    rows(total.shape[1], keep)

            for copy in hop(d, up):
                copy.start()

    for n in range(4):
        for j in range(count):
            for copy in near(n, j):
                copy.start()
    for n in range(4):
        for j in range(count):
            for copy in near(n, j):
                copy.wait_recv()
            for i, source in enumerate(parcel.blocks(parts, me ^ as_place(chips[n]), j)):
                total, near_ref, chip_ref = held[i][:3]

                def add(at, source=source, total=total, near_ref=near_ref, chip_ref=chip_ref):
                    both = source[at, :].astype(F32) + near_ref[n, j, at, :].astype(F32)
                    if n < 3:
                        chip_ref[n, j, at, :] = both.astype(BF16)
                    else:
                        total[j, at, :] = both

                rows(total.shape[1], add)
        if n < 3:
            for copy in far(n):
                copy.start()

    for bits in FAR_FIRST:
        wide(bits).start()
    wide_all[me] = wide_ref[me]
    for n in range(3):
        for copy in far(n):
            copy.wait_recv()
    for i in range(3):
        total, far_ref = held[i][0], held[i][3]
        for j in range(count):

            def add(at, total=total, far_ref=far_ref, j=j):
                value = total[j, at, :]
                for n in range(3):
                    value = value + far_ref[n, j, at, :].astype(F32)
                total[j, at, :] = value

            rows(total.shape[1], add)
    for step in range(1, count):
        pass_on(count - step, True)
        pass_on(step - 1, False)
    for i in range(3):

        def keep(at, i=i):
            sums[i][at, :] = held[i][0][f, at, :]

        rows(sums[i].shape[0], keep)
    for up, there in ((True, lower), (False, upper)):

        @pl.when(there)
        def _(up=up):
            for copy in hop(f, up):
                copy.wait_recv()
            for i in range(3):
                incoming = held[i][5 if up else 7]

                def add(at, i=i, incoming=incoming):
                    sums[i][at, :] = sums[i][at, :] + incoming[f, at, :].astype(F32)

                rows(sums[i].shape[0], add)

    for bits in range(1, 8):
        wide(bits).wait_recv()
    for place, j, shard in parcel.unit_pieces():
        for first, ref in ((0, gate_sum), (padded, up_sum)):
            piece = wide_all[place, :, first + j * units : first + (j + 1) * units]
            ref[:, shard * units : (shard + 1) * units] = piece.astype(F32)

    for d in range(count):
        pl.when(f < d)(lambda: gone(hop(d, True)))
        pl.when(f > d)(lambda: gone(hop(d, False)))
    for n in range(4):
        for j in range(count):
            for copy in near(n, j):
                copy.wait_send()
    for n in range(3):
        for copy in far(n):
            copy.wait_send()
    for bits in range(1, 8):
        wide(bits).wait_send()


def end(parcel, down, kv, small, wide, units, padded, name):
    vmem = pl.BlockSpec(memory_space=pltpu.VMEM)
    dma = pltpu.SemaphoreType.DMA
    count = parcel.count
    bodies = (
        (count, parcel.rank_rows, parcel.columns),
        (count, parcel.kv_rows, kv.shape[1]),
        (count, *small.shape[2:]),
    )
    scratch = []
    for body in bodies:
        low = pltpu.VMEM(body, BF16)
        three = pltpu.VMEM((3, *body), BF16)
        scratch += [pltpu.VMEM(body, F32), pltpu.VMEM((4, *body), BF16), three, three, low, low, low, low]
    every = 8 * count * units
    return pl.pallas_call(
        functools.partial(end_kernel, parcel, units, padded),
        out_shape=[
            *[jax.ShapeDtypeStruct(body[1:], F32) for body in bodies],
            *[jax.ShapeDtypeStruct((wide.shape[1], every), F32)] * 2,
        ],
        in_specs=[vmem] * 4,
        out_specs=[vmem] * 5,
        scratch_shapes=[
            *scratch,
            pltpu.VMEM(wide.shape, BF16),
            dma((3, 4, count)), dma((3, 4, count)),
            dma((3, 3)), dma((3, 3)),
            dma((3, 2, count)), dma((3, 2, count)),
            dma((8,)), dma((8,)),
        ],
        compiler_params=pltpu.CompilerParams(
            collective_id=name, has_side_effects=True, vmem_limit_bytes=VMEM_MOST
        ),
        cost_estimate=pl.CostEstimate(flops=0, bytes_accessed=240 * 2**20, transcendentals=0),
    )(down, kv, small, wide)


def by_owner(array, axis, count, f_first):
    lead, size, tail = array.shape[:axis], array.shape[axis], array.shape[axis + 1 :]
    part = size // (8 * count)
    n = len(lead)
    rest = [*range(n), n + 4, *range(n + 5, n + 5 + len(tail))]
    if f_first:
        array = array.reshape(*lead, count, 2, 2, 2, part, *tail)
        array = array.transpose(n, n + 1, n + 2, n + 3, *rest)
    else:
        array = array.reshape(*lead, 2, 2, count, 2, part, *tail)
        array = array.transpose(n + 2, n, n + 1, n + 3, *rest)
    return array.reshape(count, 8, *lead, part, *tail)


def from_owner(array, axis, f_first):
    count, _, *body = array.shape
    lead, part, tail = body[:axis], body[axis], body[axis + 1 :]
    n = axis
    array = array.reshape(count, 2, 2, 2, *body)
    inner = (0, 1, 2, 3) if f_first else (1, 2, 0, 3)
    array = array.transpose(
        *range(4, 4 + n), *inner, 4 + n, *range(5 + n, 5 + n + len(tail))
    )
    return array.reshape(*lead, 8 * count * part, *tail)


def per_device(
    count,
    f_first,
    block_input,
    seq_lens,
    attn_gain,
    latent_down,
    latent_gain,
    latent_up,
    shared_kv,
    out_proj,
    mlp_gain,
    gate_weight,
    up_weight,
    down_weight,
    out_cotangent,
):
    tokens, width = block_input.shape
    rank = 2 * latent_down.shape[0]
    half_rank = latent_down.shape[0]
    units = down_weight.shape[0]
    mine = units * count
    padded = -(-mine // 256) * 256
    y = lax.axis_index("y")
    place = lax.axis_index("f")
    x_c = 2 * lax.axis_index("x") + lax.axis_index("c")

    def rows_of(array):
        flat = array.reshape(-1)
        lines = -(-flat.shape[0] // 128)
        return jnp.pad(flat, (0, lines * 128 - flat.shape[0])).reshape(lines, 128)

    gain_high = latent_gain.astype(BF16)
    gain_low = (latent_gain - gain_high.astype(F32)).astype(BF16)
    gain_rows = attn_gain.shape[0]
    lat_lines = half_rank // 128
    small = jnp.concatenate(
        [
            rows_of(gain_high),
            rows_of(gain_low),
            rows_of(attn_gain.astype(BF16)),
            rows_of(mlp_gain.astype(BF16)),
            rows_of(seq_lens.astype(BF16)),
        ]
    )
    at_gain = 2 * lat_lines
    small = jnp.pad(small, ((0, -small.shape[0] % 16), (0, 0)))
    parcel = Parcel(count, f_first, half_rank, latent_down.shape[1], shared_kv.shape[0])
    down_full, kv_full, small, both, g_all = start(
        parcel, latent_down, shared_kv, small, gate_weight, up_weight, out_cotangent, units, padded, 0
    )
    down_full = parcel.down_from(down_full)

    half = count // 2
    per_head = count // 4
    up_line = lax.all_gather(latent_up.astype(BF16), "f", axis=0)
    out_line = lax.all_gather(out_proj.astype(BF16), "f", axis=0)

    def heads(line):
        own = lax.dynamic_slice_in_dim(line, half * y, half, 0)
        far = lax.dynamic_slice_in_dim(line, half - half * y, half, 0)
        return own, lax.ppermute(far, "y", SWAP)

    def join(own, other_part, axis):
        low = jnp.where(y == 0, own, other_part)
        high = jnp.where(y == 0, other_part, own)
        return jnp.stack([low, high], axis)

    up_own, up_far = (part.transpose(1, 0, 2).reshape(half_rank, -1) for part in heads(up_line))
    out_full = join(*heads(out_line), 1).reshape(2 * HEAD_DIM, width)

    both = lax.all_gather(both, "f", axis=0)
    both = from_owner(both, 0, f_first)
    ff_down = lax.all_gather(after(down_weight.astype(BF16), small), "f", axis=0)
    ff_down = ff_down.reshape(mine, width)

    gain_lat = small[:2, 0, :lat_lines].astype(F32) + small[:2, 0, lat_lines:at_gain].astype(F32)
    gain_lat = gain_lat.reshape(rank)
    by_line = small.transpose(1, 0, 2, 3)
    gain_one = from_owner(by_line[:, :, at_gain, :gain_rows], 0, f_first).astype(F32)
    gain_two = from_owner(by_line[:, :, at_gain + 1, :gain_rows], 0, f_first).astype(F32)
    lengths = lax.dynamic_index_in_dim(small[:, :, at_gain + 2, :3], place, 1, keepdims=False)
    lengths = jnp.stack(
        [lax.dynamic_index_in_dim(lengths, in_plane() ^ as_place(i), 0, keepdims=False) for i in range(8)]
    ).astype(jnp.int32)

    inputs = block_input.astype(F32)
    rms_one = lax.rsqrt(jnp.mean(inputs * inputs, axis=-1, keepdims=True) + EPS)
    normed = (inputs * rms_one * gain_one).astype(BF16)
    latent = contract(normed, down_full, 1, 1)
    rms_lat = lax.rsqrt(jnp.mean(latent * latent, axis=-1, keepdims=True) + EPS)
    latent_n = (latent * rms_lat * gain_lat).astype(BF16)
    shared = jnp.dot(normed, kv_full, preferred_element_type=F32)
    position, begins = layout(lengths, tokens)
    cosine, sine = rope_tables(position.reshape(-1), HEAD_DIM)
    k_own = rotate(shared, cosine[:tokens], sine[:tokens]).astype(BF16)

    rows_all = plane_gather(jnp.concatenate([latent_n, k_own, shared.astype(BF16)], axis=1), 1)
    begins = begins.reshape(-1, 1)
    branch, q_rot, lse, attended = attention(
        rows_all, up_own, up_far, out_full, cosine, sine, begins, 2
    )

    middle = inputs + branch
    rms_two = lax.rsqrt(jnp.mean(middle * middle, axis=-1, keepdims=True) + EPS)
    normed_two = (middle * rms_two * gain_two).astype(BF16)
    two_all, hidden, d_both = feed(normed_two, g_all, both, ff_down, padded, 3)
    down_grad = contract(hidden, g_all, 0, 0)[:mine].reshape(count, units, width).astype(BF16)
    both_grad = by_owner(contract(two_all, d_both, 0, 0).astype(BF16), 0, count, f_first)
    d_both, both_grad, down_grad = lax.optimization_barrier((d_both, both_grad, down_grad))
    both_grad = lax.psum_scatter(both_grad, "f", scatter_dimension=0)
    down_grad = lax.psum_scatter(down_grad, "f", scatter_dimension=0).astype(F32)
    d_two = product_scatter(d_both, both, 4)

    upstream = out_cotangent.astype(F32)
    gain_two_part = jnp.sum(d_two * middle * rms_two, axis=0)
    scaled_two = d_two * gain_two
    d_middle = (
        upstream
        + rms_two * scaled_two
        - middle * (rms_two**3) * jnp.mean(scaled_two * middle, axis=-1, keepdims=True)
    )

    d_branch, result, chip_sums = branch_gather(d_middle.astype(BF16), hidden, ff_down, 5)
    back, d_queries = attention_back(
        d_branch, rows_all, up_own, up_far, out_full, cosine, sine, begins, q_rot, lse, 6
    )
    d_lat_n, d_shared = back[:, :rank], back[:, rank:].astype(BF16)
    lat_all = rows_all[:, :rank]

    chip_sums = after(chip_sums, back)
    arrived = (
        lax.ppermute(chip_sums[0], ("x", "y"), DIAGONAL),
        lax.ppermute(chip_sums[1], "x", SWAP),
        lax.ppermute(chip_sums[2], "y", SWAP),
    )

    up_grad_heads = contract(lat_all, d_queries, 0, 0).reshape(2, half_rank, 2, HEAD_DIM)
    out_grad_heads = contract(attended, d_branch, 0, 0).reshape(2, per_head, 2, -1, width)

    def swap_halves(array, axis):
        own = lax.dynamic_index_in_dim(array, y, axis, keepdims=False)
        other = lax.dynamic_index_in_dim(array, 1 - y, axis, keepdims=False).astype(BF16)
        return own, lax.ppermute(other, "y", SWAP).astype(F32)

    up_line_grad = join(*swap_halves(up_grad_heads, 0), 1).reshape(half_rank, count, -1)
    up_line_grad = up_line_grad.transpose(1, 0, 2).astype(BF16)
    latent_up_grad = lax.psum_scatter(after(up_line_grad, both_grad, down_grad, back), "f", scatter_dimension=0).astype(F32)
    out_line_grad = join(*swap_halves(out_grad_heads, 2), 0)
    out_line_grad = out_line_grad.reshape(count, -1, width).astype(BF16)
    out_proj_grad = lax.psum_scatter(after(out_line_grad, both_grad, down_grad, back), "f", scatter_dimension=0).astype(F32)

    gain_lat_part = jnp.sum(d_lat_n * latent * rms_lat, axis=0)
    scaled_lat = d_lat_n * gain_lat
    inner_lat = jnp.sum(scaled_lat * latent, axis=-1, keepdims=True)
    d_latent = (rms_lat * scaled_lat - latent * (rms_lat**3) * inner_lat / rank).astype(BF16)
    d_normed = contract(d_shared, kv_full, 1, 1) + jnp.dot(
        d_latent, down_full, preferred_element_type=F32
    )
    gain_one_part = jnp.sum(d_normed * inputs * rms_one, axis=0)
    scaled_one = d_normed * gain_one
    input_grad = (
        d_middle
        + rms_one * scaled_one
        - inputs * (rms_one**3) * jnp.mean(scaled_one * inputs, axis=-1, keepdims=True)
    ).astype(BF16)

    down_part = parcel.down_to(contract(d_latent, normed, 0, 0).astype(BF16))
    kv_part = contract(normed, d_shared, 0, 0).astype(BF16)

    def gain_rows_of(part):
        part = by_owner(part.astype(BF16), 0, count, f_first).transpose(1, 0, 2)
        return jnp.pad(part, ((0, 0), (0, 0), (0, 128 - gain_rows)))[:, :, None]

    lat_rows = jnp.broadcast_to(
        gain_lat_part.astype(BF16).reshape(1, 2, 1, lat_lines, 128), (4, 2, count, lat_lines, 128)
    )
    small_part = jnp.concatenate(
        [
            lat_rows.reshape(8, count, lat_lines, 128),
            gain_rows_of(gain_one_part),
            gain_rows_of(gain_two_part),
        ],
        axis=2,
    )
    small_part = jnp.pad(small_part, ((0, 0), (0, 0), (0, -small_part.shape[2] % 16), (0, 0)))
    latent_down_grad, shared_kv_grad, small_sum, gate_grad, up_grad = end(
        parcel, down_part, kv_part, small_part, both_grad, units, padded, 7
    )
    latent_gain_grad = small_sum[:lat_lines].reshape(half_rank)
    attn_gain_grad = small_sum[lat_lines, :gain_rows]
    mlp_gain_grad = small_sum[lat_lines + 1, :gain_rows]
    arrived = after(arrived, small_sum)
    block_output = (middle + result + sum(part.astype(F32) for part in arrived)).astype(BF16)
    return (
        block_output,
        input_grad,
        attn_gain_grad,
        latent_down_grad,
        latent_gain_grad,
        latent_up_grad,
        shared_kv_grad,
        out_proj_grad,
        mlp_gain_grad,
        gate_grad,
        up_grad,
        down_grad,
    )


def solution(mesh):
    devices = mesh.devices
    split = devices.shape[0]
    count = split // 4
    f_first = split == HEADS
    if f_first:
        names, sizes = ("f", "x", "c", "y"), (count, 2, 2, 2)
    else:
        names, sizes = ("x", "c", "f", "y"), (2, 2, count, 2)
    fine = Mesh(devices.reshape(sizes), names)
    dp = names[:3]
    return jax.shard_map(
        functools.partial(per_device, count, f_first),
        mesh=fine,
        in_specs=(
            P(names, None),
            P(names, None),
            P(names),
            P("y", dp),
            P("y"),
            P("y", dp),
            P(names, None),
            P(names, None),
            P(names),
            P(names, None),
            P(names, None),
            P(names, None),
            P(names, None),
        ),
        out_specs=(
            P(names, None),
            P(names, None),
            P(names),
            P("y", dp),
            P("y"),
            P("y", dp),
            P(names, None),
            P(names, None),
            P(names),
            P(names, None),
            P(names, None),
            P(names, None),
        ),
        check_vma=False,
    )
```

```python
import functools
import math

import jax
import jax.numpy as jnp
from jax import lax
from jax.experimental import pallas as pl
from jax.experimental.pallas import tpu as pltpu
from jax.sharding import Mesh
from jax.sharding import PartitionSpec as P

HEADS = 16
HEAD_DIM = 256
EPS = 1e-06
NEGATIVE = -1e30
F32 = jnp.float32
BF16 = jnp.bfloat16


def contract(left, right, left_dim, right_dim):
    return lax.dot_general(
        left, right, (((left_dim,), (right_dim,)), ((), ())), preferred_element_type=F32
    )


def after(value, *first):
    return lax.optimization_barrier((value, *first))[0]


def layout(lengths, count):
    spots = jnp.arange(lengths.shape[-1], dtype=jnp.int32)
    ends = jnp.sum(jnp.where(spots[None, :] <= spots[:, None], lengths[..., None, :], 0), axis=-1)
    places = jnp.arange(count, dtype=jnp.int32)
    passed = places[:, None] >= ends[..., None, :]
    offset = jnp.sum(jnp.where(passed, lengths[..., None, :], 0), axis=-1)
    return (places - offset).astype(F32), offset


def rope_tables(position, width):
    half = width // 2
    steps = jnp.arange(half, dtype=F32)
    freqs = jnp.exp(steps * (-math.log(10000.0) / half))
    angles = position[..., None] * freqs
    return jnp.cos(angles), jnp.sin(angles)


def rotate(values, cosine, sine):
    half = values.shape[-1] // 2
    first, second = values[..., :half], values[..., half:]
    return jnp.concatenate(
        [first * cosine - second * sine, second * cosine + first * sine], axis=-1
    )


SWAP = [(0, 1), (1, 0)]
DIAGONAL = [(0, 3), (3, 0), (1, 2), (2, 1)]


X_BIT, Y_BIT, C_BIT = 4, 2, 1
BOTH = X_BIT | Y_BIT
VMEM_MOST = 60 * 2**20


def other(bits):
    flips = {"x": bits // 4, "y": bits // 2 % 2, "c": bits % 2}
    return {name: 1 - lax.axis_index(name) for name, flip in flips.items() if flip}


def greet(partners):
    barrier = pltpu.get_barrier_semaphore()
    for partner in partners:
        pl.semaphore_signal(barrier, inc=1, device_id=partner)
    pl.semaphore_wait(barrier, len(partners))


def send(source, target, send_sem, recv_sem, device):
    return pltpu.make_async_remote_copy(
        src_ref=source, dst_ref=target, send_sem=send_sem, recv_sem=recv_sem, device_id=device
    )


def begin(copies):
    for copy in copies:
        copy.start()


def arrive(copies):
    for copy in copies:
        copy.wait_recv()


def gone(copies):
    for copy in copies:
        copy.wait_send()


def gathering(chunks, in_ref, out_ref, send_sem, recv_sem):
    tokens = in_ref.shape[0]
    rows = tokens // chunks

    def to(slot, k, bits, source=None):
        target = out_ref.at[pl.ds(slot * tokens + k * rows, rows)]
        if source is None:
            source = in_ref.at[pl.ds(k * rows, rows)]
        else:
            source = out_ref.at[pl.ds(source * tokens + k * rows, rows)]
        return send(source, target, send_sem.at[slot, k], recv_sem.at[slot, k], other(bits))

    def own():
        for k in range(chunks):
            to(X_BIT, k, X_BIT).start()
            to(Y_BIT, k, Y_BIT).start()
        for k in range(chunks):
            to(C_BIT, k, C_BIT).start()

    def relay(first, last):
        for k in range(first, last):
            to(X_BIT, k, X_BIT).wait_recv()
            if k < chunks // 2:
                to(BOTH, k, Y_BIT, X_BIT).start()
            to(X_BIT | C_BIT, k, C_BIT, X_BIT).start()
            to(Y_BIT, k, Y_BIT).wait_recv()
            if k >= chunks // 2:
                to(BOTH, k, X_BIT, Y_BIT).start()
            to(Y_BIT | C_BIT, k, C_BIT, Y_BIT).start()

    def far():
        for k in range(chunks):
            to(BOTH, k, Y_BIT).wait_recv()
            to(BOTH | C_BIT, k, C_BIT, BOTH).start()

    def arrived(chip):
        for k in range(chunks):
            to(chip | C_BIT, k, C_BIT).wait_recv()

    def sent():
        for slot in range(1, 8):
            for k in range(chunks):
                to(slot, k, C_BIT).wait_send()

    return own, relay, far, arrived, sent


def gather_kernel(chunks, in_ref, out_ref, own_sem, send_sem, recv_sem):
    greet([other(C_BIT), other(X_BIT), other(Y_BIT)])
    copy = pltpu.make_async_copy(in_ref, out_ref.at[pl.ds(0, in_ref.shape[0])], own_sem)
    copy.start()
    own, relay, far, arrived, sent = gathering(chunks, in_ref, out_ref, send_sem, recv_sem)
    own()
    relay(0, chunks)
    far()
    copy.wait()
    for chip in (0, Y_BIT, X_BIT, BOTH):
        arrived(chip)
    sent()


def plane_gather(block, name, chunks=4):
    return pl.pallas_call(
        functools.partial(gather_kernel, chunks),
        out_shape=jax.ShapeDtypeStruct((8 * block.shape[0], block.shape[1]), block.dtype),
        in_specs=[pl.BlockSpec(memory_space=pl.ANY)],
        out_specs=pl.BlockSpec(memory_space=pl.ANY),
        scratch_shapes=[
            pltpu.SemaphoreType.DMA,
            pltpu.SemaphoreType.DMA((8, chunks)),
            pltpu.SemaphoreType.DMA((8, chunks)),
        ],
        compiler_params=pltpu.CompilerParams(collective_id=name, has_side_effects=True),
        cost_estimate=pl.CostEstimate(flops=0, bytes_accessed=160 * 2**20, transcendentals=0),
    )(block)


def row_loop(amount, do, size=32):
    @pl.loop(0, amount // size)
    def _(r):
        do(pl.ds(pl.multiple_of(r * size, size), size))


def scattering(
    out_ref, work_ref, near_ref, far_ref, near_send, near_recv, far_send, far_recv, produce,
    at_start=None, meanwhile=None, at_end=None,
):
    greet([other(C_BIT), other(X_BIT), other(Y_BIT)])
    tokens = out_ref.shape[0]
    half = tokens // 2
    low, high = pl.ds(0, half), pl.ds(half, half)

    def near(n):
        return send(
            work_ref.at[n, pl.ds(tokens, tokens)], near_ref.at[n], near_send.at[n], near_recv.at[n], other(C_BIT)
        )

    def hop(i):
        n, part, bits = (
            (0, low, X_BIT), (0, high, Y_BIT), (1, low, X_BIT), (2, high, Y_BIT), (1, high, X_BIT), (2, low, Y_BIT)
        )[i]
        return send(work_ref.at[n, part], far_ref.at[i], far_send.at[i], far_recv.at[i], other(bits))

    def chip_sum(n):
        near(n).wait_recv()

        def keep(at):
            total = work_ref[n, at, :].astype(F32) + near_ref[n, at, :].astype(F32)
            work_ref[n, at, :] = total.astype(BF16)

        row_loop(tokens, keep)

    if at_start is not None:
        at_start()

    @pl.loop(0, 4)
    def _(n):
        produce(3 - n, work_ref.at[n])
        near(n).start()

        @pl.when(n > 0)
        def _():
            chip_sum(n - 1)
            pl.when(n == 1)(lambda: begin([hop(0), hop(1)]))
            pl.when(n == 2)(lambda: hop(2).start())
            pl.when(n == 3)(lambda: hop(3).start())

    near(3).wait_recv()

    def give(at):
        out_ref[at, :] = work_ref[3, at, :].astype(F32) + near_ref[3, at, :].astype(F32)

    row_loop(tokens, give)
    for came, n, first, on in ((0, 2, 0, 5), (1, 1, half, 4)):
        hop(came).wait_recv()

        def add(at, came=came, n=n, first=first):
            here = pl.ds(pl.multiple_of(first + at.start, 32), 32)
            total = work_ref[n, here, :].astype(F32) + far_ref[came, at, :].astype(F32)
            work_ref[n, here, :] = total.astype(BF16)

        row_loop(half, add)
        hop(on).start()
    if meanwhile is not None:
        meanwhile()

    def last(came, first):
        for i in came:
            hop(i).wait_recv()

        def add(at):
            here = pl.ds(pl.multiple_of(first + at.start, 32), 32)
            value = out_ref[here, :]
            for i in came:
                value = value + far_ref[i, at, :].astype(F32)
            out_ref[here, :] = value

        row_loop(half, add)

    last((2, 5), 0)
    last((3, 4), half)
    gone([*[near(n) for n in range(4)], *[hop(i) for i in range(6)]])
    if at_end is not None:
        at_end()


def scatter_scratch(tokens, wide):
    dma = pltpu.SemaphoreType.DMA
    return [
        pltpu.VMEM((4, 2 * tokens, wide), BF16),
        pltpu.VMEM((4, tokens, wide), BF16),
        pltpu.VMEM((6, tokens // 2, wide), BF16),
        dma((4,)), dma((4,)),
        dma((6,)), dma((6,)),
    ]


def vmem_call(kernel, out_shape, stay, scratch, name, flops, *arrays):
    vmem, any_space = pl.BlockSpec(memory_space=pltpu.VMEM), pl.BlockSpec(memory_space=pl.ANY)
    return pl.pallas_call(
        kernel,
        out_shape=out_shape,
        in_specs=[vmem] * (len(arrays) - stay) + [any_space] * stay,
        out_specs=[vmem] * (len(out_shape) - stay) + [any_space] * stay,
        scratch_shapes=scratch,
        compiler_params=pltpu.CompilerParams(
            collective_id=name, has_side_effects=True, vmem_limit_bytes=VMEM_MOST
        ),
        cost_estimate=pl.CostEstimate(flops=flops, bytes_accessed=160 * 2**20, transcendentals=0),
    )(*arrays)


def turn(values, cosine, sine):
    half = values.shape[-1] // 2
    first, second = values[:, :half], values[:, half:]
    return jnp.concatenate([first * cosine - second * sine, second * cosine + first * sine], axis=1)


def masked_scores(queries, keys, begins):
    raw = contract(queries, keys, 1, 1) * HEAD_DIM**-0.5
    to = lax.broadcasted_iota(jnp.int32, raw.shape, 0)
    of = lax.broadcasted_iota(jnp.int32, raw.shape, 1)
    return jnp.where((of <= to) & (of >= begins), raw, NEGATIVE)


def halves(rank):
    half = rank // 2
    y = lax.axis_index("y")
    return (
        pl.ds(pl.multiple_of(y * half, half), half),
        pl.ds(pl.multiple_of(half - y * half, half), half),
    )


def attention_kernel(
    rank, rows_ref, head_ref, out_w_ref, cos_ref, sin_ref, begin_ref,
    branch_ref, query_ref, lse_ref, att_ref, *rest,
):
    wide = out_w_ref.shape[1]
    tokens = branch_ref.shape[0]
    mine, theirs = halves(rank)

    def produce(chip, target):
        pair = pl.ds(pl.multiple_of(chip * 2 * tokens, 2 * tokens), 2 * tokens)
        queries = [
            contract(rows_ref[pair, mine], head_ref[h], 1, 0) + contract(rows_ref[pair, theirs], head_ref[2 + h], 1, 0)
            for h in range(2)
        ]
        for c in range(2):
            rows = pl.ds(pl.multiple_of((2 * chip + c) * tokens, tokens), tokens)
            keys = rows_ref[rows, rank : rank + HEAD_DIM]
            values = rows_ref[rows, rank + HEAD_DIM :]
            cosine, sine, begins = cos_ref[rows, :], sin_ref[rows, :], begin_ref[rows, :]
            for h in range(2):
                at = slice(h * HEAD_DIM, (h + 1) * HEAD_DIM)
                turned = turn(queries[h][c * tokens : (c + 1) * tokens], cosine, sine).astype(BF16)
                query_ref[rows, at] = turned
                scores = masked_scores(turned, keys, begins)
                peak = jnp.max(scores, axis=1, keepdims=True)
                lse = peak + jnp.log(jnp.sum(jnp.exp(scores - peak), axis=1, keepdims=True))
                lse_ref[rows, h : h + 1] = lse
                probs = jnp.exp(scores - lse).astype(BF16)
                att_ref[rows, at] = contract(probs, values, 1, 0).astype(BF16)

        @pl.loop(0, wide // 512)
        def _(i):
            at = pl.ds(pl.multiple_of(i * 512, 512), 512)
            target[:, at] = contract(att_ref[pair, :], out_w_ref[: 2 * HEAD_DIM, at], 1, 0).astype(BF16)

    scattering(branch_ref, *rest, produce)


def attention(rows, heads, out_w, cosine, sine, begins, name):
    tokens, rank = rows.shape[0] // 8, 2 * heads.shape[1]
    wide = out_w.shape[1]
    two = 2 * HEAD_DIM
    return vmem_call(
        functools.partial(attention_kernel, rank),
        [
            jax.ShapeDtypeStruct((tokens, wide), F32),
            jax.ShapeDtypeStruct((8 * tokens, two), BF16),
            jax.ShapeDtypeStruct((8 * tokens, 2), F32),
            jax.ShapeDtypeStruct((8 * tokens, two), BF16),
        ],
        0,
        scatter_scratch(tokens, wide),
        name,
        16 * tokens * two * (wide + rank + 2 * tokens),
        rows, heads, out_w, cosine, sine, begins,
    )


def attention_back_kernel(
    rank, d_ref, rows_ref, head_ref, out_w_ref, cos_ref, sin_ref, begin_ref, query_ref, lse_ref, give_ref,
    back_ref, dq_ref, grad_ref, got_ref, *rest,
):
    tokens = back_ref.shape[0]
    mine, theirs = halves(rank)
    scale = HEAD_DIM**-0.5

    def produce(chip, target):
        pair = pl.ds(pl.multiple_of(chip * 2 * tokens, 2 * tokens), 2 * tokens)
        d_pair = contract(d_ref[pair, :], out_w_ref[: 2 * HEAD_DIM, :], 1, 1).astype(BF16)
        for c in range(2):
            rows = pl.ds(pl.multiple_of((2 * chip + c) * tokens, tokens), tokens)
            here = slice(c * tokens, (c + 1) * tokens)
            keys = rows_ref[rows, rank : rank + HEAD_DIM]
            values = rows_ref[rows, rank + HEAD_DIM :]
            cosine, sine, begins = cos_ref[rows, :], sin_ref[rows, :], begin_ref[rows, :]
            d_keys = d_values = None
            for h in range(2):
                at = slice(h * HEAD_DIM, (h + 1) * HEAD_DIM)
                queries, d_att = query_ref[rows, at], d_pair[here, at]
                probs = jnp.exp(masked_scores(queries, keys, begins) - lse_ref[rows, h : h + 1])
                d_probs = contract(d_att, values, 1, 1)
                inner = jnp.sum(probs * d_probs, axis=1, keepdims=True)
                d_scores = (probs * (d_probs - inner)).astype(BF16)
                d_query = contract(d_scores, keys, 1, 0) * scale
                dq_ref[rows, at] = turn(d_query, cosine, -sine).astype(BF16)
                d_k = contract(d_scores, queries, 0, 0)
                d_v = contract(probs.astype(BF16), d_att, 0, 0)
                d_keys = d_k if h == 0 else d_keys + d_k
                d_values = d_v if h == 0 else d_values + d_v
            shared = turn(d_keys * scale, cosine, -sine) + d_values
            target[here, rank:] = shared.astype(BF16)
        for first, part in ((0, mine), (2, theirs)):
            got = contract(dq_ref[pair, :HEAD_DIM], head_ref[first], 1, 1)
            got = got + contract(dq_ref[pair, HEAD_DIM:], head_ref[first + 1], 1, 1)
            target[:, part] = got.astype(BF16)

    *rest, send_sem, recv_sem = rest
    copy = send(give_ref, got_ref, send_sem, recv_sem, other(Y_BIT))

    def meanwhile():
        @pl.loop(0, rank // 256)
        def _(i):
            at = pl.ds(pl.multiple_of(i * 256, 256), 256)
            grad_ref[at, :] = contract(rows_ref[:, at], dq_ref[...], 0, 0).astype(BF16)

    scattering(back_ref, *rest, produce, at_start=copy.start, meanwhile=meanwhile, at_end=copy.wait)


def attention_back(d_rows, rows, heads, out_w, cosine, sine, begins, queries, lse, give, name):
    tokens, rank = rows.shape[0] // 8, 2 * heads.shape[1]
    wide = out_w.shape[1]
    two = 2 * HEAD_DIM
    full = rank + HEAD_DIM
    return vmem_call(
        functools.partial(attention_back_kernel, rank),
        [
            jax.ShapeDtypeStruct((tokens, full), F32),
            jax.ShapeDtypeStruct((8 * tokens, two), BF16),
            jax.ShapeDtypeStruct((rank, two), BF16),
            jax.ShapeDtypeStruct(give.shape, give.dtype),
        ],
        1,
        [*scatter_scratch(tokens, full), pltpu.SemaphoreType.DMA, pltpu.SemaphoreType.DMA],
        name,
        16 * tokens * two * (wide + rank + 5 * tokens),
        d_rows, rows, heads, out_w, cosine, sine, begins, queries, lse, give,
    )


def feed_kernel(
    chunks, in_ref, g_ref, both_ref, down_ref, two_ref, hidden_ref, d_both_ref, own_sum, chip_sums,
    g_held, both_held, down_held, work_ref, near_ref, own_sem, load_sem, send_sem, recv_sem, near_send, near_recv,
):
    step = 256
    tokens = in_ref.shape[0]
    padded = hidden_ref.shape[1]
    units = down_ref.shape[0]
    loads = [
        pltpu.make_async_copy(both_ref, both_held, load_sem.at[0]),
        pltpu.make_async_copy(g_ref, g_held, load_sem.at[1]),
        pltpu.make_async_copy(down_ref, down_held.at[pl.ds(0, units)], load_sem.at[2]),
        pltpu.make_async_copy(in_ref, two_ref.at[pl.ds(0, tokens)], own_sem),
    ]
    begin(loads)
    greet([other(C_BIT), other(X_BIT), other(Y_BIT)])
    own, relay, far, arrived, sent = gathering(chunks, in_ref, two_ref, send_sem, recv_sem)
    own()
    if units < padded:
        down_held[units:, :] = jnp.zeros((padded - units, down_held.shape[1]), BF16)
    for copy in loads:
        copy.wait()

    def near(n):
        return send(
            work_ref.at[n, pl.ds(tokens, tokens)], near_ref.at[n], near_send.at[n], near_recv.at[n], other(C_BIT)
        )

    def chip_sum(n):
        near(n).wait_recv()

        def add(at):
            total = work_ref[n, at, :].astype(F32) + near_ref[n, at, :].astype(F32)
            if n:
                chip_sums[n - 1, at, :] = total.astype(BF16)
            else:
                own_sum[at, :] = total

        row_loop(tokens, add)

    def outputs_of(chip):
        pair = pl.ds(chip * tokens, 2 * tokens)
        n = chip // 2

        @pl.loop(0, down_held.shape[1] // step)
        def _(i):
            at = pl.ds(pl.multiple_of(i * step, step), step)
            work_ref[n, :, at] = contract(hidden_ref[pair, :], down_held[:, at], 1, 0).astype(BF16)

        near(n).start()

    def units_of(chip):
        arrived(chip)
        pair = pl.ds(chip * tokens, 2 * tokens)

        @pl.loop(0, padded // step)
        def _(i):
            at = pl.ds(pl.multiple_of(i * step, step), step)
            up_at = pl.ds(pl.multiple_of(padded + i * step, step), step)
            gate = contract(two_ref[pair, :], both_held[:, at], 1, 0)
            upval = contract(two_ref[pair, :], both_held[:, up_at], 1, 0)
            d_hidden = contract(g_held[pair, :], down_held[at, :], 1, 1)
            sigma = 1.0 / (1.0 + jnp.exp(-gate))
            silu = gate * sigma
            hidden_ref[pair, at] = (silu * upval).astype(BF16)
            d_gate = d_hidden * upval * sigma * (1.0 + gate * (1.0 - sigma))
            d_both_ref[pair, at] = d_gate.astype(BF16)
            d_both_ref[pair, up_at] = (d_hidden * silu).astype(BF16)

    units_of(0)
    relay(0, chunks)
    units_of(X_BIT)
    units_of(Y_BIT)
    outputs_of(0)
    far()
    units_of(BOTH)
    outputs_of(X_BIT)
    outputs_of(Y_BIT)
    outputs_of(BOTH)
    for n in range(4):
        chip_sum(n)
    sent()
    gone([near(n) for n in range(4)])


def feed(rows, g, both, down, padded, name, chunks=4):
    tokens, width = rows.shape
    any_space, vmem = pl.BlockSpec(memory_space=pl.ANY), pl.BlockSpec(memory_space=pltpu.VMEM)
    dma = pltpu.SemaphoreType.DMA
    return pl.pallas_call(
        functools.partial(feed_kernel, chunks),
        out_shape=[
            jax.ShapeDtypeStruct((8 * tokens, width), BF16),
            jax.ShapeDtypeStruct((8 * tokens, padded), BF16),
            jax.ShapeDtypeStruct((8 * tokens, 2 * padded), BF16),
            jax.ShapeDtypeStruct((tokens, width), F32),
            jax.ShapeDtypeStruct((3, tokens, width), BF16),
        ],
        in_specs=[any_space] * 4,
        out_specs=[vmem] * 5,
        scratch_shapes=[
            pltpu.VMEM(g.shape, BF16),
            pltpu.VMEM(both.shape, BF16),
            pltpu.VMEM((padded, width), BF16),
            pltpu.VMEM((4, 2 * tokens, width), BF16),
            pltpu.VMEM((4, tokens, width), BF16),
            dma,
            dma((3,)),
            dma((8, chunks)), dma((8, chunks)),
            dma((4,)), dma((4,)),
        ],
        compiler_params=pltpu.CompilerParams(
            collective_id=name, has_side_effects=True, vmem_limit_bytes=VMEM_MOST
        ),
        cost_estimate=pl.CostEstimate(
            flops=16 * tokens * 3 * width * padded, bytes_accessed=160 * 2**20, transcendentals=0
        ),
    )(rows, g, both, down)


def product_scatter_kernel(left_ref, right_ref, side_ref, out_ref, grad_ref, *rest):
    tokens = out_ref.shape[0]
    step = 256

    def produce(chip, target):
        pair = pl.ds(pl.multiple_of(chip * 2 * tokens, 2 * tokens), 2 * tokens)

        @pl.loop(0, out_ref.shape[1] // step)
        def _(i):
            at = pl.ds(pl.multiple_of(i * step, step), step)
            target[:, at] = contract(left_ref[pair, :], right_ref[at, :], 1, 1).astype(BF16)

    def meanwhile():
        @pl.loop(0, grad_ref.shape[0] // step)
        def _(i):
            at = pl.ds(pl.multiple_of(i * step, step), step)
            grad_ref[at, :] = contract(side_ref[:, at], left_ref[...], 0, 0).astype(BF16)

    scattering(out_ref, *rest, produce, meanwhile=meanwhile)


def product_scatter(left, right, side, name):
    tokens, wide = left.shape[0] // 8, right.shape[0]
    return vmem_call(
        product_scatter_kernel,
        [
            jax.ShapeDtypeStruct((tokens, wide), F32),
            jax.ShapeDtypeStruct((side.shape[1], left.shape[1]), BF16),
        ],
        0,
        scatter_scratch(tokens, wide),
        name,
        32 * tokens * wide * left.shape[1],
        left, right, side,
    )


def in_plane():
    return 4 * lax.axis_index("x") + 2 * lax.axis_index("c") + lax.axis_index("y")


class Parcel:
    def __init__(self, count, f_first, rank_rows, columns, kv_rows):
        self.count, self.f_first = count, f_first
        self.rank_rows, self.columns, self.kv_rows = rank_rows, columns, kv_rows
        self.windows = columns == 128
        self.lines = rank_rows * columns // 128

    def down_shape(self):
        if self.windows:
            return (2 * self.rank_rows, 4 * self.count * self.columns)
        return (8, self.count, self.lines, 128)

    def down_from(self, array):
        if self.windows:
            return array
        array = array.reshape(2, 2, 2, self.count, self.rank_rows, self.columns)
        array = array.transpose((2, 4, 3, 0, 1, 5) if self.f_first else (2, 4, 0, 1, 3, 5))
        return array.reshape(2 * self.rank_rows, -1)

    def down_to(self, array):
        if self.windows:
            return array
        inner = (self.count, 2, 2) if self.f_first else (2, 2, self.count)
        array = array.reshape(2, self.rank_rows, *inner, self.columns)
        array = array.transpose((3, 4, 0, 2, 1, 5) if self.f_first else (2, 3, 0, 4, 1, 5))
        return array.reshape(self.down_shape())

    def blocks(self, refs, place, j):
        down, kv, small = refs
        pair, y = place // 2, place % 2
        at = j * 4 + pair if self.f_first else pair * self.count + j
        if self.windows:
            down = down.at[
                pl.ds(pl.multiple_of(y * self.rank_rows, self.rank_rows), self.rank_rows),
                pl.ds(pl.multiple_of(at * self.columns, self.columns), self.columns),
            ]
        else:
            down = down.at[place, j]
        start_row = pl.multiple_of((2 * at + y) * self.kv_rows, self.kv_rows)
        return down, kv.at[pl.ds(start_row, self.kv_rows)], small.at[place, j]

    def unit_pieces(self):
        for shard in range(8 * self.count):
            if self.f_first:
                yield shard % 8, shard // 8, shard
            else:
                yield shard // (2 * self.count) * 2 + shard % 2, shard // 2 % self.count, shard


def greet_all(count):
    f = lax.axis_index("f")
    lower, upper = f > 0, f < count - 1
    barrier = pltpu.get_barrier_semaphore()
    for bits in range(1, 8):
        pl.semaphore_signal(barrier, inc=1, device_id=other(bits))
    pl.when(lower)(lambda: pl.semaphore_signal(barrier, inc=1, device_id={"f": f - 1}))
    pl.when(upper)(lambda: pl.semaphore_signal(barrier, inc=1, device_id={"f": f + 1}))
    pl.semaphore_wait(barrier, 7 + lower.astype(jnp.int32) + upper.astype(jnp.int32))
    return lower, upper


FAR_FIRST = (7, 6, 5, 4, 3, 2, 1)


def as_place(bits):
    return (bits & 4) + 2 * (bits & 1) + (bits >> 1 & 1)


def start_kernel(
    parcel, chunks, units, padded, down_ref, kv_ref, small_ref, head_ref, out_ref, ff_ref, gate_ref, up_ref, rows_ref,
    down_all, kv_all, small_all, head_all, out_all, ff_all, wide_all, rows_all,
    down_low, kv_low, head_low, out_low, ff_low, wide_ref,
    local_sem, line_send, line_recv, plane_send, plane_recv, wide_send, wide_recv, rows_send, rows_recv,
    head_send, head_recv, far_send, far_recv,
):
    count = parcel.count
    f, me = lax.axis_index("f"), in_plane()
    lower, upper = greet_all(count)
    own = (down_low, kv_low, small_ref)
    alls = (down_all, kv_all, small_all)
    down_low[...] = down_ref[...].astype(BF16)
    kv_low[...] = kv_ref[...].astype(BF16)
    head_low[...] = head_ref[...].astype(BF16)
    out_low[...] = out_ref[...].astype(BF16)
    ff_low[...] = ff_ref[...].astype(BF16)

    half = count // 2
    y = lax.axis_index("y")

    def head_blocks(j):
        kept = (j // half == y).astype(jnp.int32)
        spare = (1 - kept) * (2 * half + j % half)
        return (
            head_all.at[kept * (j % half) + spare],
            out_all.at[kept * (2 * (j % half) + y) + spare],
            ff_all.at[j],
        )

    def head_hop(j, up, sources):
        return [
            send(
                source, target, head_send.at[i, 0 if up else 1, j], head_recv.at[i, j],
                {"f": f + 1 if up else f - 1},
            )
            for i, (source, target) in enumerate(zip(sources, head_blocks(j)))
        ]

    def across(slot, sources):
        targets = (head_all.at[half + slot], out_all.at[2 * slot + y])
        return [
            send(source, target, far_send.at[i, slot], far_recv.at[i, slot], other(Y_BIT))
            for i, (source, target) in enumerate(zip(sources, targets))
        ]

    def head_own():
        pl.when(upper)(lambda: begin(head_hop(f, True, own_heads)))
        pl.when(lower)(lambda: begin(head_hop(f, False, own_heads)))
        pl.when(f // half != y)(lambda: begin(across(f % half, own_heads)))

    def head_step(step):
        @pl.when(f - step >= 0)
        def _():
            j = f - step
            blocks = head_blocks(j)
            arrive(head_hop(j, True, blocks))
            pl.when(upper)(lambda: begin(head_hop(j, True, blocks)))
            pl.when(j // half != y)(lambda: begin(across(j % half, blocks)))

        @pl.when(f + step <= count - 1)
        def _():
            j = f + step
            blocks = head_blocks(j)
            arrive(head_hop(j, False, blocks))
            pl.when(lower)(lambda: begin(head_hop(j, False, blocks)))
            pl.when(j // half != y)(lambda: begin(across(j % half, blocks)))

    own_heads = (head_low, out_low, ff_low)

    def hop(j, up, sources):
        return [
            send(
                source, target, line_send.at[i, 0 if up else 1, j], line_recv.at[i, j],
                {"f": f + 1 if up else f - 1},
            )
            for i, (source, target) in enumerate(zip(sources, parcel.blocks(alls, me, j)))
        ]

    def spread(slot, bits, j, sources):
        targets = parcel.blocks(alls, me ^ as_place(bits) ^ as_place(slot), j)
        return [
            send(source, target, plane_send.at[i, slot, j], plane_recv.at[i, slot, j], other(bits))
            for i, (source, target) in enumerate(zip(sources, targets))
        ]

    def to_plane(j, sources):
        for bits in (X_BIT, Y_BIT, C_BIT):
            begin(spread(bits, bits, j, sources))

    def line_step(step):
        @pl.when(f - step >= 0)
        def _():
            j = f - step
            blocks = parcel.blocks(alls, me, j)
            arrive(hop(j, True, blocks))
            pl.when(upper)(lambda: begin(hop(j, True, blocks)))
            to_plane(j, blocks)

        @pl.when(f + step <= count - 1)
        def _():
            j = f + step
            blocks = parcel.blocks(alls, me, j)
            arrive(hop(j, False, blocks))
            pl.when(lower)(lambda: begin(hop(j, False, blocks)))
            to_plane(j, blocks)

    def relay(j):
        by_x, by_y = parcel.blocks(alls, me ^ as_place(X_BIT), j), parcel.blocks(alls, me ^ as_place(Y_BIT), j)
        arrive(spread(X_BIT, X_BIT, j, by_x))
        pl.when(j % 2 == 0)(lambda: begin(spread(BOTH, Y_BIT, j, by_x)))
        begin(spread(X_BIT | C_BIT, C_BIT, j, by_x))
        arrive(spread(Y_BIT, Y_BIT, j, by_y))
        pl.when(j % 2 == 1)(lambda: begin(spread(BOTH, X_BIT, j, by_y)))
        begin(spread(Y_BIT | C_BIT, C_BIT, j, by_y))

    def relay_far(j):
        by_both = parcel.blocks(alls, me ^ as_place(BOTH), j)
        arrive(spread(BOTH, Y_BIT, j, by_both))
        begin(spread(BOTH | C_BIT, C_BIT, j, by_both))

    def in_order(do):
        do(f)
        for step in range(1, count):
            pl.when(f - step >= 0)(lambda: do(f - step))
            pl.when(f + step <= count - 1)(lambda: do(f + step))

    def wide(bits):
        return send(wide_ref.at[me ^ as_place(bits)], wide_all.at[me], wide_send.at[bits], wide_recv.at[bits], other(bits))

    pl.when(upper)(lambda: begin(hop(f, True, own)))
    pl.when(lower)(lambda: begin(hop(f, False, own)))
    to_plane(f, own)
    for place, j, shard in parcel.unit_pieces():
        for first, ref in ((0, gate_ref), (padded, up_ref)):
            piece = ref[:, shard * units : (shard + 1) * units].astype(BF16)
            wide_ref[place, :, first + j * units : first + (j + 1) * units] = piece
    for first in (count * units, padded + count * units):
        size = padded - count * units
        wide_ref[:, :, first : first + size] = jnp.zeros((8, wide_ref.shape[1], size), BF16)
    for bits in FAR_FIRST:
        wide(bits).start()
    locals_ = [
        pltpu.make_async_copy(source, target, local_sem.at[i])
        for i, (source, target) in enumerate(
            (
                *zip(own, parcel.blocks(alls, me, f)),
                *zip(own_heads, head_blocks(f)),
                (wide_ref.at[me], wide_all.at[me]),
                (rows_ref, rows_all.at[pl.ds(0, rows_ref.shape[0])]),
            )
        )
    ]
    begin(locals_)
    rows_own, rows_relay, rows_far, rows_arrived, rows_sent = gathering(chunks, rows_ref, rows_all, rows_send, rows_recv)
    for step in range(1, count):
        line_step(step)
        if step == min(2, count - 1):
            head_own()
    rows_own()
    in_order(relay)
    head_step(1)
    rows_relay(0, chunks // 2)
    in_order(relay_far)
    rows_relay(chunks // 2, chunks)
    for step in range(2, count):
        head_step(step)
        if step == 2:
            rows_far()
    for copy in locals_:
        copy.wait()
    for j in range(count):
        pl.when(upper & (f >= j))(lambda: gone(hop(j, True, own)))
        pl.when(lower & (f <= j))(lambda: gone(hop(j, False, own)))
        pl.when(upper & (f >= j))(lambda: gone(head_hop(j, True, own_heads)))
        pl.when(lower & (f <= j))(lambda: gone(head_hop(j, False, own_heads)))
    for slot in range(half):
        arrive(across(slot, own_heads))
        gone(across(slot, own_heads))
    for slot in range(1, 8):
        for j in range(count):
            for copy in spread(slot, slot, j, own):
                if slot & C_BIT:
                    copy.wait_recv()
                copy.wait_send()
    for bits in range(1, 8):
        wide(bits).wait_recv()
        wide(bits).wait_send()
    for chip in (0, Y_BIT, X_BIT, BOTH):
        rows_arrived(chip)
    rows_sent()


def start(parcel, down, kv, small, head, out, ff, gate, up, rows, units, padded, name, chunks=4):
    count = parcel.count
    any_space, vmem = pl.BlockSpec(memory_space=pl.ANY), pl.BlockSpec(memory_space=pltpu.VMEM)
    dma = pltpu.SemaphoreType.DMA
    wide = (8, gate.shape[0], 2 * padded)
    return pl.pallas_call(
        functools.partial(start_kernel, parcel, chunks, units, padded),
        out_shape=[
            jax.ShapeDtypeStruct(parcel.down_shape(), BF16),
            jax.ShapeDtypeStruct((8 * count * kv.shape[0], kv.shape[1]), BF16),
            jax.ShapeDtypeStruct((8, count, *small.shape), BF16),
            jax.ShapeDtypeStruct((3 * count // 2, *head.shape), BF16),
            jax.ShapeDtypeStruct((3 * count // 2, *out.shape), BF16),
            jax.ShapeDtypeStruct((count, *ff.shape), BF16),
            jax.ShapeDtypeStruct(wide, BF16),
            jax.ShapeDtypeStruct((8 * rows.shape[0], rows.shape[1]), BF16),
        ],
        in_specs=[vmem] * 8 + [any_space],
        out_specs=[any_space] * 8,
        scratch_shapes=[
            pltpu.VMEM(down.shape, BF16),
            pltpu.VMEM(kv.shape, BF16),
            pltpu.VMEM(head.shape, BF16),
            pltpu.VMEM(out.shape, BF16),
            pltpu.VMEM(ff.shape, BF16),
            pltpu.VMEM(wide, BF16),
            dma((8,)),
            dma((3, 2, count)), dma((3, count)),
            dma((3, 8, count)), dma((3, 8, count)),
            dma((8,)), dma((8,)),
            dma((8, chunks)), dma((8, chunks)),
            dma((3, 2, count)), dma((3, count)),
            dma((2, count // 2)), dma((2, count // 2)),
        ],
        compiler_params=pltpu.CompilerParams(
            collective_id=name, has_side_effects=True, vmem_limit_bytes=VMEM_MOST
        ),
        cost_estimate=pl.CostEstimate(flops=0, bytes_accessed=240 * 2**20, transcendentals=0),
    )(down, kv, small, head, out, ff, gate, up, rows)


def own_back_kernel(
    back_ref, latent_ref, rms_lat_ref, gain_lat_ref, normed_ref, down_ref, kv_ref, in_ref, rms_ref, gain_ref, d_mid_ref,
    down_part, kv_part, d_in_ref, lat_sum, gain_sum, d_normed,
):
    rank = latent_ref.shape[1]
    width = in_ref.shape[1]
    step = 512
    d_lat_n, d_shared = back_ref[:, :rank], back_ref[:, rank:].astype(BF16)
    latent, rms_lat = latent_ref[...], rms_lat_ref[...]
    lat_sum[...] = jnp.sum(d_lat_n * latent * rms_lat, axis=0, keepdims=True)
    scaled = d_lat_n * gain_lat_ref[...]
    inner = jnp.sum(scaled * latent, axis=1, keepdims=True)
    d_latent = (rms_lat * scaled - latent * (rms_lat * rms_lat * rms_lat) * inner / rank).astype(BF16)

    @pl.loop(0, width // step)
    def _(i):
        at = pl.ds(pl.multiple_of(i * step, step), step)
        down_part[:, at] = contract(d_latent, normed_ref[:, at], 0, 0).astype(BF16)
        kv_part[at, :] = contract(normed_ref[:, at], d_shared, 0, 0).astype(BF16)
        d_normed[:, at] = contract(d_shared, kv_ref[at, :], 1, 1) + contract(d_latent, down_ref[:, at], 1, 0)

    inputs, rms = in_ref[...].astype(F32), rms_ref[...]
    gain_sum[...] = jnp.sum(d_normed[...] * inputs * rms, axis=0, keepdims=True)
    mean = jnp.sum(d_normed[...] * gain_ref[...] * inputs, axis=1, keepdims=True) / width
    k = d_normed[...] * gain_ref[...]
    d_in_ref[...] = (d_mid_ref[...] + rms * k - inputs * (rms * rms * rms) * mean).astype(BF16)


def own_back(back, latent, rms_lat, gain_lat, normed, down, kv, inputs, rms, gain, d_middle):
    vmem = pl.BlockSpec(memory_space=pltpu.VMEM)
    tokens, width = inputs.shape
    rank = latent.shape[1]
    return pl.pallas_call(
        own_back_kernel,
        out_shape=[
            jax.ShapeDtypeStruct((rank, width), BF16),
            jax.ShapeDtypeStruct(kv.shape, BF16),
            jax.ShapeDtypeStruct((tokens, width), BF16),
            jax.ShapeDtypeStruct((1, rank), F32),
            jax.ShapeDtypeStruct((1, width), F32),
        ],
        in_specs=[vmem] * 11,
        out_specs=[vmem] * 5,
        scratch_shapes=[pltpu.VMEM((tokens, width), F32)],
        compiler_params=pltpu.CompilerParams(vmem_limit_bytes=VMEM_MOST),
        cost_estimate=pl.CostEstimate(
            flops=4 * tokens * width * (rank + kv.shape[1]), bytes_accessed=16 * 2**20, transcendentals=0
        ),
    )(back, latent, rms_lat, gain_lat, normed, down, kv, inputs, rms, gain, d_middle)


def end_kernel(
    parcel, units, padded, down_ref, kv_ref, small_ref, wide_ref, head_ref,
    down_sum, kv_sum, small_sum, gate_sum, up_sum, head_sum, *rest,
):
    count = parcel.count
    held = [rest[8 * i : 8 * i + 8] for i in range(3)]
    head_held = (rest[24], None, None, None, *rest[25:29])
    head_got = rest[29]
    held.append(head_held)
    wide_all, near_send, near_recv, chip_send, chip_recv, line_send, line_recv, wide_send, wide_recv = rest[30:39]
    far_send, far_recv = rest[39:]
    f, me = lax.axis_index("f"), in_plane()
    lower, upper = greet_all(count)
    parts = (down_ref, kv_ref, small_ref)
    sums = (down_sum, kv_sum, small_sum, head_sum)
    chips = (BOTH, X_BIT, Y_BIT, 0)

    def rows(amount, do):
        size = 16 if amount % 64 else 64

        @pl.loop(0, amount // size)
        def _(r):
            do(pl.ds(pl.multiple_of(r * size, size), size))

    def near(n, j):
        sources = parcel.blocks(parts, me ^ as_place(chips[n] | C_BIT), j)
        return [
            send(source, held[i][1].at[n, j], near_send.at[i, n, j], near_recv.at[i, n, j], other(C_BIT))
            for i, source in enumerate(sources)
        ]

    def far(n, j):
        return [
            send(held[i][2].at[n, j], held[i][3].at[n, j], chip_send.at[i, n, j], chip_recv.at[i, n, j], other(chips[n]))
            for i in range(3)
        ]

    order = []
    for j in range(count // 2):
        order += [count - 1 - j, j]

    def wide(bits):
        return send(wide_ref.at[me ^ as_place(bits)], wide_all.at[me], wide_send.at[bits], wide_recv.at[bits], other(bits))

    def hop(d, up, group):
        way = 0 if up else 1
        return [
            send(
                held[i][4 + 2 * way].at[d], held[i][5 + 2 * way].at[d],
                line_send.at[i, way, d], line_recv.at[i, way, d],
                {"f": f + 1 if up else f - 1},
            )
            for i in group
        ]

    def pass_on(d, up, group):
        way = 0 if up else 1
        behind = lower if up else upper

        @pl.when((d > f) if up else (d < f))
        def _():
            @pl.when(behind)
            def _():
                arrive(hop(d, up, group))
                for total, outgoing, incoming in ((held[i][0], held[i][4 + 2 * way], held[i][5 + 2 * way]) for i in group):

                    def add(at, total=total, outgoing=outgoing, incoming=incoming):
                        outgoing[d, at, :] = (total[d, at, :] + incoming[d, at, :].astype(F32)).astype(BF16)

                    rows(total.shape[1], add)

            @pl.when(jnp.logical_not(behind))
            def _():
                for total, outgoing in ((held[i][0], held[i][4 + 2 * way]) for i in group):

                    def keep(at, total=total, outgoing=outgoing):
                        outgoing[d, at, :] = total[d, at, :].astype(BF16)

                    rows(total.shape[1], keep)

            begin(hop(d, up, group))

    def line_step(step, group):
        pass_on(count - step, True, group)
        pass_on(step - 1, False, group)

    half = count // 2
    y = lax.axis_index("y")
    rank_rows, columns = head_got.shape[0], head_got.shape[1] // half

    def half_rows(which):
        return pl.ds(pl.multiple_of(which * rank_rows, rank_rows), rank_rows)

    swap = send(head_ref.at[half_rows(1 - y)], head_got, far_send, far_recv, other(Y_BIT))
    swap.start()
    for j in order:
        for n in range(4):
            begin(near(n, j))
    for j in order:
        for n in range(4):
            arrive(near(n, j))
            for i, source in enumerate(parcel.blocks(parts, me ^ as_place(chips[n]), j)):
                total, near_ref, chip_ref = held[i][:3]

                def add(at, n=n, j=j, source=source, total=total, near_ref=near_ref, chip_ref=chip_ref):
                    both = source[at, :].astype(F32) + near_ref[n, j, at, :].astype(F32)
                    if n < 3:
                        chip_ref[n, j, at, :] = both.astype(BF16)
                    else:
                        total[j, at, :] = both

                rows(total.shape[1], add)
            if n < 3:
                begin(far(n, j))

    for bits in FAR_FIRST:
        wide(bits).start()
    wide_all[me] = wide_ref[me]
    swap.wait_recv()
    for slot in range(half):
        at_columns = slice(slot * columns, (slot + 1) * columns)
        head_held[0][y * half + slot] = head_ref[half_rows(y), at_columns].astype(F32)
        head_held[0][(1 - y) * half + slot] = head_got[:, at_columns].astype(F32)
    pair, head = (0, 1, 2), (3,)
    line_step(1, head)
    for at_order, j in enumerate(order):
        for n in range(3):
            arrive(far(n, j))
        for i in range(3):
            total, far_ref = held[i][0], held[i][3]

            def add(at, j=j, total=total, far_ref=far_ref):
                value = total[j, at, :]
                for n in range(3):
                    value = value + far_ref[n, j, at, :].astype(F32)
                total[j, at, :] = value

            rows(total.shape[1], add)
        pass_on(j, True, pair)
        pass_on(j, False, pair)
        if at_order == 1:
            for step in range(2, count):
                line_step(step, head)
    for i in range(4):

        def keep(at, i=i):
            sums[i][at, :] = held[i][0][f, at, :]

        rows(sums[i].shape[0], keep)
    for up, there in ((True, lower), (False, upper)):

        @pl.when(there)
        def _(up=up):
            arrive(hop(f, up, range(4)))
            for i in range(4):
                incoming = held[i][5 if up else 7]

                def add(at, i=i, incoming=incoming):
                    sums[i][at, :] = sums[i][at, :] + incoming[f, at, :].astype(F32)

                rows(sums[i].shape[0], add)

    for bits in range(1, 8):
        wide(bits).wait_recv()
    for place, j, shard in parcel.unit_pieces():
        for first, ref in ((0, gate_sum), (padded, up_sum)):
            piece = wide_all[place, :, first + j * units : first + (j + 1) * units]
            ref[:, shard * units : (shard + 1) * units] = piece

    for d in range(count):
        pl.when(f < d)(lambda: gone(hop(d, True, range(4))))
        pl.when(f > d)(lambda: gone(hop(d, False, range(4))))
    for n in range(4):
        for j in range(count):
            for copy in near(n, j):
                copy.wait_send()
    for n in range(3):
        for j in range(count):
            gone(far(n, j))
    for bits in range(1, 8):
        wide(bits).wait_send()
    swap.wait_send()


def end(parcel, down, kv, small, wide, head, units, padded, name):
    vmem = pl.BlockSpec(memory_space=pltpu.VMEM)
    dma = pltpu.SemaphoreType.DMA
    count = parcel.count
    bodies = (
        (count, parcel.lines, 128),
        (count, parcel.kv_rows, kv.shape[1]),
        (count, *small.shape[2:]),
    )
    scratch = []
    for body in bodies:
        low = pltpu.VMEM(body, BF16)
        three = pltpu.VMEM((3, *body), BF16)
        scratch += [pltpu.VMEM(body, F32), pltpu.VMEM((4, *body), BF16), three, three, low, low, low, low]
    lines = (count, parcel.rank_rows, 2 * head.shape[1] // count)
    every = 8 * count * units
    return pl.pallas_call(
        functools.partial(end_kernel, parcel, units, padded),
        out_shape=[
            *[jax.ShapeDtypeStruct(body[1:], F32) for body in bodies],
            *[jax.ShapeDtypeStruct((wide.shape[1], every), BF16)] * 2,
            jax.ShapeDtypeStruct(lines[1:], F32),
        ],
        in_specs=[vmem] * 5,
        out_specs=[vmem] * 6,
        scratch_shapes=[
            *scratch,
            pltpu.VMEM(lines, F32),
            *[pltpu.VMEM(lines, BF16)] * 4,
            pltpu.VMEM((parcel.rank_rows, head.shape[1]), BF16),
            pltpu.VMEM(wide.shape, BF16),
            dma((3, 4, count)), dma((3, 4, count)),
            dma((3, 3, count)), dma((3, 3, count)),
            dma((4, 2, count)), dma((4, 2, count)),
            dma((8,)), dma((8,)),
            dma, dma,
        ],
        compiler_params=pltpu.CompilerParams(
            collective_id=name, has_side_effects=True, vmem_limit_bytes=VMEM_MOST
        ),
        cost_estimate=pl.CostEstimate(flops=0, bytes_accessed=240 * 2**20, transcendentals=0),
    )(down, kv, small, wide, head)


def by_owner(array, axis, count, f_first):
    lead, size, tail = array.shape[:axis], array.shape[axis], array.shape[axis + 1 :]
    part = size // (8 * count)
    n = len(lead)
    rest = [*range(n), n + 4, *range(n + 5, n + 5 + len(tail))]
    if f_first:
        array = array.reshape(*lead, count, 2, 2, 2, part, *tail)
        array = array.transpose(n, n + 1, n + 2, n + 3, *rest)
    else:
        array = array.reshape(*lead, 2, 2, count, 2, part, *tail)
        array = array.transpose(n + 2, n, n + 1, n + 3, *rest)
    return array.reshape(count, 8, *lead, part, *tail)


def from_owner(array, axis, f_first):
    count, _, *body = array.shape
    lead, part, tail = body[:axis], body[axis], body[axis + 1 :]
    n = axis
    array = array.reshape(count, 2, 2, 2, *body)
    inner = (0, 1, 2, 3) if f_first else (1, 2, 0, 3)
    array = array.transpose(
        *range(4, 4 + n), *inner, 4 + n, *range(5 + n, 5 + n + len(tail))
    )
    return array.reshape(*lead, 8 * count * part, *tail)


def per_device(
    count,
    f_first,
    block_input,
    seq_lens,
    attn_gain,
    latent_down,
    latent_gain,
    latent_up,
    shared_kv,
    out_proj,
    mlp_gain,
    gate_weight,
    up_weight,
    down_weight,
    out_cotangent,
):
    tokens, width = block_input.shape
    rank = 2 * latent_down.shape[0]
    half_rank = latent_down.shape[0]
    units = down_weight.shape[0]
    mine = units * count
    padded = -(-mine // 256) * 256
    y = lax.axis_index("y")
    place = lax.axis_index("f")
    x_c = 2 * lax.axis_index("x") + lax.axis_index("c")

    def rows_of(array):
        flat = array.reshape(-1)
        lines = -(-flat.shape[0] // 128)
        return jnp.pad(flat, (0, lines * 128 - flat.shape[0])).reshape(lines, 128)

    gain_high = latent_gain.astype(BF16)
    gain_low = (latent_gain - gain_high.astype(F32)).astype(BF16)
    gain_rows = attn_gain.shape[0]
    lat_lines = half_rank // 128
    small = jnp.concatenate(
        [
            rows_of(gain_high),
            rows_of(gain_low),
            rows_of(attn_gain.astype(BF16)),
            rows_of(mlp_gain.astype(BF16)),
            rows_of(seq_lens.astype(BF16)),
        ]
    )
    at_gain = 2 * lat_lines
    small = jnp.pad(small, ((0, -small.shape[0] % 16), (0, 0)))
    parcel = Parcel(count, f_first, half_rank, latent_down.shape[1], shared_kv.shape[0])
    down_full, kv_full, small, heads, out_full, ff_down, both, g_all = start(
        parcel,
        latent_down.reshape(-1, 128),
        shared_kv,
        small,
        latent_up,
        out_proj,
        down_weight,
        gate_weight,
        up_weight,
        out_cotangent,
        units,
        padded,
        0,
    )
    down_full = parcel.down_from(down_full)

    half = count // 2
    per_head = count // 4
    if per_head > 1:
        heads = heads[: 2 * half].reshape(2, 2, per_head, half_rank, -1).transpose(0, 1, 3, 2, 4)
        heads = heads.reshape(4, half_rank, HEAD_DIM)
    out_full = out_full.reshape(-1, width)

    both = lax.all_gather(both, "f", axis=0)
    both = from_owner(both, 0, f_first)
    ff_down = ff_down.reshape(mine, width)

    gain_lat = small[:2, 0, :lat_lines].astype(F32) + small[:2, 0, lat_lines:at_gain].astype(F32)
    gain_lat = gain_lat.reshape(rank)
    by_line = small.transpose(1, 0, 2, 3)
    gain_one = from_owner(by_line[:, :, at_gain, :gain_rows], 0, f_first).astype(F32)
    gain_two = from_owner(by_line[:, :, at_gain + 1, :gain_rows], 0, f_first).astype(F32)
    lengths = lax.dynamic_index_in_dim(small[:, :, at_gain + 2, :3], place, 1, keepdims=False)
    lengths = jnp.stack(
        [lax.dynamic_index_in_dim(lengths, in_plane() ^ as_place(i), 0, keepdims=False) for i in range(8)]
    ).astype(jnp.int32)

    inputs = block_input.astype(F32)
    rms_one = lax.rsqrt(jnp.mean(inputs * inputs, axis=-1, keepdims=True) + EPS)
    normed = (inputs * rms_one * gain_one).astype(BF16)
    latent = contract(normed, down_full, 1, 1)
    rms_lat = lax.rsqrt(jnp.mean(latent * latent, axis=-1, keepdims=True) + EPS)
    latent_n = (latent * rms_lat * gain_lat).astype(BF16)
    shared = jnp.dot(normed, kv_full, preferred_element_type=F32)
    position, begins = layout(lengths, tokens)
    cosine, sine = rope_tables(position.reshape(-1), HEAD_DIM)
    k_own = rotate(shared, cosine[:tokens], sine[:tokens]).astype(BF16)

    rows_all = plane_gather(jnp.concatenate([latent_n, k_own, shared.astype(BF16)], axis=1), 1)
    begins = begins.reshape(-1, 1)
    branch, q_rot, lse, attended = attention(rows_all, heads, out_full, cosine, sine, begins, 2)

    middle = inputs + branch
    rms_two = lax.rsqrt(jnp.mean(middle * middle, axis=-1, keepdims=True) + EPS)
    normed_two = (middle * rms_two * gain_two).astype(BF16)
    two_all, hidden, d_both, result, chip_sums = feed(normed_two, g_all, both, ff_down, padded, 3)
    down_grad = contract(hidden, g_all, 0, 0)[:mine].reshape(count, units, width).astype(BF16)
    d_both, down_grad, chip_sums = lax.optimization_barrier((d_both, down_grad, chip_sums))
    down_grad = lax.psum_scatter(down_grad, "f", scatter_dimension=0).astype(F32)
    arrived = (
        lax.ppermute(chip_sums[2], ("x", "y"), DIAGONAL),
        lax.ppermute(chip_sums[1], "x", SWAP),
        lax.ppermute(chip_sums[0], "y", SWAP),
    )
    d_two, both_grad = product_scatter(d_both, both, two_all, 4)
    both_grad = by_owner(both_grad, 0, count, f_first)
    both_grad = lax.psum_scatter(both_grad, "f", scatter_dimension=0)

    upstream = out_cotangent.astype(F32)
    gain_two_part = jnp.sum(d_two * middle * rms_two, axis=0)
    scaled_two = d_two * gain_two
    d_middle = (
        upstream
        + rms_two * scaled_two
        - middle * (rms_two**3) * jnp.mean(scaled_two * middle, axis=-1, keepdims=True)
    )

    d_branch = plane_gather(d_middle.astype(BF16), 5)

    def join(own, other_part, axis):
        low = jnp.where(y == 0, own, other_part)
        high = jnp.where(y == 0, other_part, own)
        return jnp.stack([low, high], axis)

    def halves_of(array, axis):
        array = array.astype(BF16)
        own = lax.dynamic_index_in_dim(array, y, axis, keepdims=False)
        return own, lax.dynamic_index_in_dim(array, 1 - y, axis, keepdims=False)

    out_grad = contract(attended, d_branch, 0, 0).reshape(2, per_head, 2, -1, width)
    out_own, out_far = halves_of(out_grad, 2)
    back, d_queries, up_grad_part, out_far = attention_back(
        d_branch, rows_all, heads, out_full, cosine, sine, begins, q_rot, lse, out_far, 6
    )
    out_line_grad = join(out_own, out_far, 0).reshape(count, -1, width)
    out_proj_grad = lax.psum_scatter(after(out_line_grad, both_grad, down_grad), "f", scatter_dimension=0).astype(F32)

    down_part, kv_part, input_grad, gain_lat_part, gain_one_part = own_back(
        back, latent, rms_lat, gain_lat[None], normed, down_full, kv_full, block_input, rms_one, gain_one[None], d_middle
    )
    gain_one_part = gain_one_part.reshape(width)

    down_part = parcel.down_to(down_part)

    def gain_rows_of(part):
        part = by_owner(part.astype(BF16), 0, count, f_first).transpose(1, 0, 2)
        return jnp.pad(part, ((0, 0), (0, 0), (0, 128 - gain_rows)))[:, :, None]

    lat_rows = jnp.broadcast_to(
        gain_lat_part.astype(BF16).reshape(1, 2, 1, lat_lines, 128), (4, 2, count, lat_lines, 128)
    )
    small_part = jnp.concatenate(
        [
            lat_rows.reshape(8, count, lat_lines, 128),
            gain_rows_of(gain_one_part),
            gain_rows_of(gain_two_part),
        ],
        axis=2,
    )
    small_part = jnp.pad(small_part, ((0, 0), (0, 0), (0, -small_part.shape[2] % 16), (0, 0)))
    latent_down_grad, shared_kv_grad, small_sum, gate_grad, up_grad, latent_up_grad = end(
        parcel, down_part, kv_part, small_part, both_grad, up_grad_part, units, padded, 7
    )
    gate_grad, up_grad = gate_grad.astype(F32), up_grad.astype(F32)
    latent_down_grad = latent_down_grad.reshape(latent_down.shape)
    latent_gain_grad = small_sum[:lat_lines].reshape(half_rank)
    attn_gain_grad = small_sum[lat_lines, :gain_rows]
    mlp_gain_grad = small_sum[lat_lines + 1, :gain_rows]
    arrived = after(arrived, small_sum)
    block_output = (middle + result + sum(part.astype(F32) for part in arrived)).astype(BF16)
    return (
        block_output,
        input_grad,
        attn_gain_grad,
        latent_down_grad,
        latent_gain_grad,
        latent_up_grad,
        shared_kv_grad,
        out_proj_grad,
        mlp_gain_grad,
        gate_grad,
        up_grad,
        down_grad,
    )


def solution(mesh):
    devices = mesh.devices
    split = devices.shape[0]
    count = split // 4
    f_first = split == HEADS
    if f_first:
        names, sizes = ("f", "x", "c", "y"), (count, 2, 2, 2)
    else:
        names, sizes = ("x", "c", "f", "y"), (2, 2, count, 2)
    fine = Mesh(devices.reshape(sizes), names)
    dp = names[:3]
    return jax.shard_map(
        functools.partial(per_device, count, f_first),
        mesh=fine,
        in_specs=(
            P(names, None),
            P(names, None),
            P(names),
            P("y", dp),
            P("y"),
            P("y", dp),
            P(names, None),
            P(names, None),
            P(names),
            P(names, None),
            P(names, None),
            P(names, None),
            P(names, None),
        ),
        out_specs=(
            P(names, None),
            P(names, None),
            P(names),
            P("y", dp),
            P("y"),
            P("y", dp),
            P(names, None),
            P(names, None),
            P(names),
            P(names, None),
            P(names, None),
            P(names, None),
        ),
        check_vma=False,
    )
```

```python
import functools
import math

import jax
import jax.numpy as jnp
from jax import lax
from jax.experimental import pallas as pl
from jax.experimental.pallas import tpu as pltpu
from jax.sharding import Mesh
from jax.sharding import PartitionSpec as P

HEADS = 16
HEAD_DIM = 256
EPS = 1e-06
NEGATIVE = -1e30
F32 = jnp.float32
BF16 = jnp.bfloat16


def contract(left, right, left_dim, right_dim):
    return lax.dot_general(
        left, right, (((left_dim,), (right_dim,)), ((), ())), preferred_element_type=F32
    )


def after(value, *first):
    return lax.optimization_barrier((value, *first))[0]


def layout(lengths, count):
    spots = jnp.arange(lengths.shape[-1], dtype=jnp.int32)
    ends = jnp.sum(jnp.where(spots[None, :] <= spots[:, None], lengths[..., None, :], 0), axis=-1)
    places = jnp.arange(count, dtype=jnp.int32)
    passed = places[:, None] >= ends[..., None, :]
    offset = jnp.sum(jnp.where(passed, lengths[..., None, :], 0), axis=-1)
    return (places - offset).astype(F32), offset


def rope_tables(position, width):
    half = width // 2
    steps = jnp.arange(half, dtype=F32)
    freqs = jnp.exp(steps * (-math.log(10000.0) / half))
    angles = position[..., None] * freqs
    return jnp.cos(angles), jnp.sin(angles)


def rotate(values, cosine, sine):
    half = values.shape[-1] // 2
    first, second = values[..., :half], values[..., half:]
    return jnp.concatenate(
        [first * cosine - second * sine, second * cosine + first * sine], axis=-1
    )


DIAGONAL = [(0, 3), (3, 0), (1, 2), (2, 1)]


X_BIT, Y_BIT, C_BIT = 4, 2, 1
BOTH = X_BIT | Y_BIT
VMEM_MOST = 60 * 2**20


def other(bits):
    flips = {"x": bits // 4, "y": bits // 2 % 2, "c": bits % 2}
    return {name: 1 - lax.axis_index(name) for name, flip in flips.items() if flip}


def greet(partners):
    barrier = pltpu.get_barrier_semaphore()
    for partner in partners:
        pl.semaphore_signal(barrier, inc=1, device_id=partner)
    pl.semaphore_wait(barrier, len(partners))


def send(source, target, send_sem, recv_sem, device):
    return pltpu.make_async_remote_copy(
        src_ref=source, dst_ref=target, send_sem=send_sem, recv_sem=recv_sem, device_id=device
    )


def begin(copies):
    for copy in copies:
        copy.start()


def arrive(copies):
    for copy in copies:
        copy.wait_recv()


def gone(copies):
    for copy in copies:
        copy.wait_send()


def gathering(chunks, in_ref, out_ref, send_sem, recv_sem):
    tokens = in_ref.shape[0]
    rows = tokens // chunks

    def to(slot, k, bits, source=None):
        target = out_ref.at[pl.ds(slot * tokens + k * rows, rows)]
        if source is None:
            source = in_ref.at[pl.ds(k * rows, rows)]
        else:
            source = out_ref.at[pl.ds(source * tokens + k * rows, rows)]
        return send(source, target, send_sem.at[slot, k], recv_sem.at[slot, k], other(bits))

    def own():
        for k in range(chunks):
            to(X_BIT, k, X_BIT).start()
            to(Y_BIT, k, Y_BIT).start()
        for k in range(chunks):
            to(C_BIT, k, C_BIT).start()

    def relay(first, last):
        for k in range(first, last):
            to(X_BIT, k, X_BIT).wait_recv()
            if k < chunks // 2:
                to(BOTH, k, Y_BIT, X_BIT).start()
            to(X_BIT | C_BIT, k, C_BIT, X_BIT).start()
            to(Y_BIT, k, Y_BIT).wait_recv()
            if k >= chunks // 2:
                to(BOTH, k, X_BIT, Y_BIT).start()
            to(Y_BIT | C_BIT, k, C_BIT, Y_BIT).start()

    def far():
        for k in range(chunks):
            to(BOTH, k, Y_BIT).wait_recv()
            to(BOTH | C_BIT, k, C_BIT, BOTH).start()

    def arrived(chip):
        for k in range(chunks):
            to(chip | C_BIT, k, C_BIT).wait_recv()

    def sent():
        for slot in range(1, 8):
            for k in range(chunks):
                to(slot, k, C_BIT).wait_send()

    return own, relay, far, arrived, sent


def gather_kernel(chunks, in_ref, out_ref, own_sem, send_sem, recv_sem):
    greet([other(C_BIT), other(X_BIT), other(Y_BIT)])
    copy = pltpu.make_async_copy(in_ref, out_ref.at[pl.ds(0, in_ref.shape[0])], own_sem)
    copy.start()
    own, relay, far, arrived, sent = gathering(chunks, in_ref, out_ref, send_sem, recv_sem)
    own()
    relay(0, chunks)
    far()
    copy.wait()
    for chip in (0, Y_BIT, X_BIT, BOTH):
        arrived(chip)
    sent()


def plane_gather(block, name, chunks=4):
    return pl.pallas_call(
        functools.partial(gather_kernel, chunks),
        out_shape=jax.ShapeDtypeStruct((8 * block.shape[0], block.shape[1]), block.dtype),
        in_specs=[pl.BlockSpec(memory_space=pl.ANY)],
        out_specs=pl.BlockSpec(memory_space=pl.ANY),
        scratch_shapes=[
            pltpu.SemaphoreType.DMA,
            pltpu.SemaphoreType.DMA((8, chunks)),
            pltpu.SemaphoreType.DMA((8, chunks)),
        ],
        compiler_params=pltpu.CompilerParams(collective_id=name, has_side_effects=True),
        cost_estimate=pl.CostEstimate(flops=0, bytes_accessed=160 * 2**20, transcendentals=0),
    )(block)


def row_loop(amount, do, size=32):
    @pl.loop(0, amount // size)
    def _(r):
        do(pl.ds(pl.multiple_of(r * size, size), size))


def scattering(
    out_ref, work_ref, near_ref, far_ref, near_send, near_recv, far_send, far_recv, produce,
    at_start=None, meanwhile=None, at_end=None,
):
    greet([other(C_BIT), other(X_BIT), other(Y_BIT)])
    tokens = out_ref.shape[0]
    half = tokens // 2
    low, high = pl.ds(0, half), pl.ds(half, half)

    def near(n):
        return send(
            work_ref.at[n, pl.ds(tokens, tokens)], near_ref.at[n], near_send.at[n], near_recv.at[n], other(C_BIT)
        )

    def hop(i):
        n, part, bits = (
            (0, low, X_BIT), (0, high, Y_BIT), (1, low, X_BIT), (2, high, Y_BIT), (1, high, X_BIT), (2, low, Y_BIT)
        )[i]
        return send(work_ref.at[n, part], far_ref.at[i], far_send.at[i], far_recv.at[i], other(bits))

    def chip_sum(n):
        near(n).wait_recv()

        def keep(at):
            total = work_ref[n, at, :].astype(F32) + near_ref[n, at, :].astype(F32)
            work_ref[n, at, :] = total.astype(BF16)

        row_loop(tokens, keep)

    if at_start is not None:
        at_start()

    @pl.loop(0, 4)
    def _(n):
        produce(3 - n, work_ref.at[n])
        near(n).start()

        @pl.when(n > 0)
        def _():
            chip_sum(n - 1)
            pl.when(n == 1)(lambda: begin([hop(0), hop(1)]))
            pl.when(n == 2)(lambda: hop(2).start())
            pl.when(n == 3)(lambda: hop(3).start())

    near(3).wait_recv()

    def give(at):
        out_ref[at, :] = work_ref[3, at, :].astype(F32) + near_ref[3, at, :].astype(F32)

    row_loop(tokens, give)
    for came, n, first, on in ((0, 2, 0, 5), (1, 1, half, 4)):
        hop(came).wait_recv()

        def add(at, came=came, n=n, first=first):
            here = pl.ds(pl.multiple_of(first + at.start, 32), 32)
            total = work_ref[n, here, :].astype(F32) + far_ref[came, at, :].astype(F32)
            work_ref[n, here, :] = total.astype(BF16)

        row_loop(half, add)
        hop(on).start()
    if meanwhile is not None:
        meanwhile()

    def last(came, first):
        for i in came:
            hop(i).wait_recv()

        def add(at):
            here = pl.ds(pl.multiple_of(first + at.start, 32), 32)
            value = out_ref[here, :]
            for i in came:
                value = value + far_ref[i, at, :].astype(F32)
            out_ref[here, :] = value

        row_loop(half, add)

    last((2, 5), 0)
    last((3, 4), half)
    gone([*[near(n) for n in range(4)], *[hop(i) for i in range(6)]])
    if at_end is not None:
        at_end()


class PairLoads:
    def __init__(self, pairs, sem):
        self.pairs, self.sem = pairs, sem
        self.rows = pairs[0][0].shape[0] // 4

    def copies(self, chip):
        rows = pl.ds(pl.multiple_of(chip * self.rows, self.rows), self.rows)
        return [
            pltpu.make_async_copy(source.at[rows], target.at[rows], self.sem.at[i, chip])
            for i, (source, target) in enumerate(self.pairs)
        ]

    def start(self):
        for chip in (3, 2, 1, 0):
            begin(self.copies(chip))

    def wait(self, chip):
        for copy in self.copies(chip):
            copy.wait()


def scatter_scratch(tokens, wide):
    dma = pltpu.SemaphoreType.DMA
    return [
        pltpu.VMEM((4, 2 * tokens, wide), BF16),
        pltpu.VMEM((4, tokens, wide), BF16),
        pltpu.VMEM((6, tokens // 2, wide), BF16),
        dma((4,)), dma((4,)),
        dma((6,)), dma((6,)),
    ]


def vmem_call(kernel, out_shape, stay, scratch, name, flops, *arrays):
    stay_in, stay_out = stay
    vmem, any_space = pl.BlockSpec(memory_space=pltpu.VMEM), pl.BlockSpec(memory_space=pl.ANY)
    return pl.pallas_call(
        kernel,
        out_shape=out_shape,
        in_specs=[vmem] * (len(arrays) - stay_in) + [any_space] * stay_in,
        out_specs=[vmem] * (len(out_shape) - stay_out) + [any_space] * stay_out,
        scratch_shapes=scratch,
        compiler_params=pltpu.CompilerParams(
            collective_id=name, has_side_effects=True, vmem_limit_bytes=VMEM_MOST
        ),
        cost_estimate=pl.CostEstimate(flops=flops, bytes_accessed=160 * 2**20, transcendentals=0),
    )(*arrays)


def turn(values, cosine, sine):
    half = values.shape[-1] // 2
    first, second = values[:, :half], values[:, half:]
    return jnp.concatenate([first * cosine - second * sine, second * cosine + first * sine], axis=1)


def masked_scores(queries, keys, begins):
    raw = contract(queries, keys, 1, 1) * HEAD_DIM**-0.5
    to = lax.broadcasted_iota(jnp.int32, raw.shape, 0)
    of = lax.broadcasted_iota(jnp.int32, raw.shape, 1)
    return jnp.where((of <= to) & (of >= begins), raw, NEGATIVE)


def halves(rank):
    half = rank // 2
    y = lax.axis_index("y")
    return (
        pl.ds(pl.multiple_of(y * half, half), half),
        pl.ds(pl.multiple_of(half - y * half, half), half),
    )


def attention_kernel(
    rank, head_ref, out_w_ref, cos_ref, sin_ref, begin_ref, rows_in,
    branch_ref, query_ref, lse_ref, att_ref, *rest,
):
    wide = out_w_ref.shape[1]
    tokens = branch_ref.shape[0]
    mine, theirs = halves(rank)
    *rest, rows_ref, load_sem = rest
    loads = PairLoads([(rows_in, rows_ref)], load_sem)
    loads.start()

    def produce(chip, target):
        loads.wait(chip)
        pair = pl.ds(pl.multiple_of(chip * 2 * tokens, 2 * tokens), 2 * tokens)
        queries = [
            contract(rows_ref[pair, mine], head_ref[h], 1, 0) + contract(rows_ref[pair, theirs], head_ref[2 + h], 1, 0)
            for h in range(2)
        ]
        for c in range(2):
            rows = pl.ds(pl.multiple_of((2 * chip + c) * tokens, tokens), tokens)
            keys = rows_ref[rows, rank : rank + HEAD_DIM]
            values = rows_ref[rows, rank + HEAD_DIM :]
            cosine, sine, begins = cos_ref[rows, :], sin_ref[rows, :], begin_ref[rows, :]
            for h in range(2):
                at = slice(h * HEAD_DIM, (h + 1) * HEAD_DIM)
                turned = turn(queries[h][c * tokens : (c + 1) * tokens], cosine, sine).astype(BF16)
                query_ref[rows, at] = turned
                scores = masked_scores(turned, keys, begins)
                peak = jnp.max(scores, axis=1, keepdims=True)
                lse = peak + jnp.log(jnp.sum(jnp.exp(scores - peak), axis=1, keepdims=True))
                lse_ref[rows, h : h + 1] = lse
                probs = jnp.exp(scores - lse).astype(BF16)
                att_ref[rows, at] = contract(probs, values, 1, 0).astype(BF16)

        @pl.loop(0, wide // 512)
        def _(i):
            at = pl.ds(pl.multiple_of(i * 512, 512), 512)
            target[:, at] = contract(att_ref[pair, :], out_w_ref[: 2 * HEAD_DIM, at], 1, 0).astype(BF16)

    scattering(branch_ref, *rest, produce)


def attention(rows, heads, out_w, cosine, sine, begins, name):
    tokens, rank = rows.shape[0] // 8, 2 * heads.shape[1]
    wide = out_w.shape[1]
    two = 2 * HEAD_DIM
    return vmem_call(
        functools.partial(attention_kernel, rank),
        [
            jax.ShapeDtypeStruct((tokens, wide), F32),
            jax.ShapeDtypeStruct((8 * tokens, two), BF16),
            jax.ShapeDtypeStruct((8 * tokens, 2), F32),
            jax.ShapeDtypeStruct((8 * tokens, two), BF16),
        ],
        (1, 0),
        [*scatter_scratch(tokens, wide), pltpu.VMEM(rows.shape, BF16), pltpu.SemaphoreType.DMA((1, 4))],
        name,
        16 * tokens * two * (wide + rank + 2 * tokens),
        heads, out_w, cosine, sine, begins, rows,
    )


def attention_back_kernel(
    rank, head_ref, out_w_ref, cos_ref, sin_ref, begin_ref, lse_ref, d_in, rows_in, query_in, give_ref,
    back_ref, dq_ref, grad_ref, got_ref, *rest,
):
    tokens = back_ref.shape[0]
    mine, theirs = halves(rank)
    scale = HEAD_DIM**-0.5
    *rest, d_ref, rows_ref, query_ref, load_sem, send_sem, recv_sem = rest
    loads = PairLoads([(d_in, d_ref), (rows_in, rows_ref), (query_in, query_ref)], load_sem)
    loads.start()

    def produce(chip, target):
        loads.wait(chip)
        pair = pl.ds(pl.multiple_of(chip * 2 * tokens, 2 * tokens), 2 * tokens)
        d_pair = contract(d_ref[pair, :], out_w_ref[: 2 * HEAD_DIM, :], 1, 1).astype(BF16)
        for c in range(2):
            rows = pl.ds(pl.multiple_of((2 * chip + c) * tokens, tokens), tokens)
            here = slice(c * tokens, (c + 1) * tokens)
            keys = rows_ref[rows, rank : rank + HEAD_DIM]
            values = rows_ref[rows, rank + HEAD_DIM :]
            cosine, sine, begins = cos_ref[rows, :], sin_ref[rows, :], begin_ref[rows, :]
            d_keys = d_values = None
            for h in range(2):
                at = slice(h * HEAD_DIM, (h + 1) * HEAD_DIM)
                queries, d_att = query_ref[rows, at], d_pair[here, at]
                probs = jnp.exp(masked_scores(queries, keys, begins) - lse_ref[rows, h : h + 1])
                d_probs = contract(d_att, values, 1, 1)
                inner = jnp.sum(probs * d_probs, axis=1, keepdims=True)
                d_scores = (probs * (d_probs - inner)).astype(BF16)
                d_query = contract(d_scores, keys, 1, 0) * scale
                dq_ref[rows, at] = turn(d_query, cosine, -sine).astype(BF16)
                d_k = contract(d_scores, queries, 0, 0)
                d_v = contract(probs.astype(BF16), d_att, 0, 0)
                d_keys = d_k if h == 0 else d_keys + d_k
                d_values = d_v if h == 0 else d_values + d_v
            shared = turn(d_keys * scale, cosine, -sine) + d_values
            target[here, rank:] = shared.astype(BF16)
        for first, part in ((0, mine), (2, theirs)):
            got = contract(dq_ref[pair, :HEAD_DIM], head_ref[first], 1, 1)
            got = got + contract(dq_ref[pair, HEAD_DIM:], head_ref[first + 1], 1, 1)
            target[:, part] = got.astype(BF16)

    copy = send(give_ref, got_ref, send_sem, recv_sem, other(Y_BIT))

    def meanwhile():
        @pl.loop(0, rank // 256)
        def _(i):
            at = pl.ds(pl.multiple_of(i * 256, 256), 256)
            grad_ref[at, :] = contract(rows_ref[:, at], dq_ref[...], 0, 0).astype(BF16)

    scattering(back_ref, *rest, produce, at_start=copy.start, meanwhile=meanwhile, at_end=copy.wait)


def attention_back(d_rows, rows, heads, out_w, cosine, sine, begins, queries, lse, give, name):
    tokens, rank = rows.shape[0] // 8, 2 * heads.shape[1]
    wide = out_w.shape[1]
    two = 2 * HEAD_DIM
    full = rank + HEAD_DIM
    return vmem_call(
        functools.partial(attention_back_kernel, rank),
        [
            jax.ShapeDtypeStruct((tokens, full), F32),
            jax.ShapeDtypeStruct((8 * tokens, two), BF16),
            jax.ShapeDtypeStruct((rank, two), BF16),
            jax.ShapeDtypeStruct(give.shape, give.dtype),
        ],
        (4, 1),
        [
            *scatter_scratch(tokens, full),
            *[pltpu.VMEM(array.shape, BF16) for array in (d_rows, rows, queries)],
            pltpu.SemaphoreType.DMA((3, 4)),
            pltpu.SemaphoreType.DMA,
            pltpu.SemaphoreType.DMA,
        ],
        name,
        16 * tokens * two * (wide + rank + 5 * tokens),
        heads, out_w, cosine, sine, begins, lse, d_rows, rows, queries, give,
    )


def feed_kernel(
    chunks, in_ref, g_ref, both_ref, down_ref, two_out, hidden_out, d_both_out, own_sum, chip_sums,
    two_ref, hidden_ref, d_both_ref, g_held, both_held, down_held, work_ref, near_ref, own_sem, load_sem, send_sem, recv_sem, near_send, near_recv, out_sem,
):
    step = 256
    tokens = in_ref.shape[0]
    padded = hidden_out.shape[1]
    units = down_ref.shape[0]
    loads = [
        pltpu.make_async_copy(both_ref, both_held, load_sem.at[0]),
        pltpu.make_async_copy(g_ref, g_held, load_sem.at[1]),
        pltpu.make_async_copy(down_ref, down_held.at[pl.ds(0, units)], load_sem.at[2]),
        pltpu.make_async_copy(in_ref, two_ref.at[pl.ds(0, tokens)], own_sem),
    ]
    begin(loads)
    greet([other(C_BIT), other(X_BIT), other(Y_BIT)])
    own, relay, far, arrived, sent = gathering(chunks, in_ref, two_ref, send_sem, recv_sem)
    own()
    if units < padded:
        down_held[units:, :] = jnp.zeros((padded - units, down_held.shape[1]), BF16)
    for copy in loads:
        copy.wait()

    def near(n):
        return send(
            work_ref.at[n, pl.ds(tokens, tokens)], near_ref.at[n], near_send.at[n], near_recv.at[n], other(C_BIT)
        )

    def chip_sum(n):
        near(n).wait_recv()

        def add(at):
            total = work_ref[n, at, :].astype(F32) + near_ref[n, at, :].astype(F32)
            if n:
                chip_sums[n - 1, at, :] = total.astype(BF16)
            else:
                own_sum[at, :] = total

        row_loop(tokens, add)

    def leave(chip):
        pair = pl.ds(chip * tokens, 2 * tokens)
        results = ((two_ref, two_out), (hidden_ref, hidden_out), (d_both_ref, d_both_out))
        return [
            pltpu.make_async_copy(held.at[pair], result.at[pair], out_sem.at[i, chip // 2])
            for i, (held, result) in enumerate(results)
        ]

    def outputs_of(chip):
        pair = pl.ds(chip * tokens, 2 * tokens)
        n = chip // 2

        @pl.loop(0, down_held.shape[1] // step)
        def _(i):
            at = pl.ds(pl.multiple_of(i * step, step), step)
            work_ref[n, :, at] = contract(hidden_ref[pair, :], down_held[:, at], 1, 0).astype(BF16)

        near(n).start()

    def units_of(chip):
        arrived(chip)
        pair = pl.ds(chip * tokens, 2 * tokens)

        @pl.loop(0, padded // step)
        def _(i):
            at = pl.ds(pl.multiple_of(i * step, step), step)
            up_at = pl.ds(pl.multiple_of(padded + i * step, step), step)
            gate = contract(two_ref[pair, :], both_held[:, at], 1, 0)
            upval = contract(two_ref[pair, :], both_held[:, up_at], 1, 0)
            d_hidden = contract(g_held[pair, :], down_held[at, :], 1, 1)
            sigma = 1.0 / (1.0 + jnp.exp(-gate))
            silu = gate * sigma
            hidden_ref[pair, at] = (silu * upval).astype(BF16)
            d_gate = d_hidden * upval * sigma * (1.0 + gate * (1.0 - sigma))
            d_both_ref[pair, at] = d_gate.astype(BF16)
            d_both_ref[pair, up_at] = (d_hidden * silu).astype(BF16)

        begin(leave(chip))

    units_of(0)
    outputs_of(0)
    chip_sum(0)
    relay(0, chunks)
    units_of(X_BIT)
    outputs_of(X_BIT)
    units_of(Y_BIT)
    far()
    outputs_of(Y_BIT)
    units_of(BOTH)
    outputs_of(BOTH)
    for n in (2, 1, 3):
        chip_sum(n)
    for chip in (0, Y_BIT, X_BIT, BOTH):
        for copy in leave(chip):
            copy.wait()
    sent()
    gone([near(n) for n in range(4)])


def feed(rows, g, both, down, padded, name, chunks=4):
    tokens, width = rows.shape
    any_space, vmem = pl.BlockSpec(memory_space=pl.ANY), pl.BlockSpec(memory_space=pltpu.VMEM)
    dma = pltpu.SemaphoreType.DMA
    return pl.pallas_call(
        functools.partial(feed_kernel, chunks),
        out_shape=[
            jax.ShapeDtypeStruct((8 * tokens, width), BF16),
            jax.ShapeDtypeStruct((8 * tokens, padded), BF16),
            jax.ShapeDtypeStruct((8 * tokens, 2 * padded), BF16),
            jax.ShapeDtypeStruct((tokens, width), F32),
            jax.ShapeDtypeStruct((3, tokens, width), BF16),
        ],
        in_specs=[any_space] * 4,
        out_specs=[any_space] * 3 + [vmem] * 2,
        scratch_shapes=[
            pltpu.VMEM((8 * tokens, width), BF16),
            pltpu.VMEM((8 * tokens, padded), BF16),
            pltpu.VMEM((8 * tokens, 2 * padded), BF16),
            pltpu.VMEM(g.shape, BF16),
            pltpu.VMEM(both.shape, BF16),
            pltpu.VMEM((padded, width), BF16),
            pltpu.VMEM((4, 2 * tokens, width), BF16),
            pltpu.VMEM((4, tokens, width), BF16),
            dma,
            dma((3,)),
            dma((8, chunks)), dma((8, chunks)),
            dma((4,)), dma((4,)),
            dma((3, 4)),
        ],
        compiler_params=pltpu.CompilerParams(
            collective_id=name, has_side_effects=True, vmem_limit_bytes=VMEM_MOST
        ),
        cost_estimate=pl.CostEstimate(
            flops=16 * tokens * 3 * width * padded, bytes_accessed=160 * 2**20, transcendentals=0
        ),
    )(rows, g, both, down)


def product_scatter_kernel(left_in, right_in, side_in, give_ref, out_ref, grad_ref, got_ref, *rest):
    tokens = out_ref.shape[0]
    step = 256
    *rest, left_ref, right_ref, side_ref, grad_held, load_sem, pair_sem, grad_sem, give_send, give_recv = rest
    right_load = pltpu.make_async_copy(right_in, right_ref, load_sem.at[0])
    side_load = pltpu.make_async_copy(side_in, side_ref, load_sem.at[1])
    loads = PairLoads([(left_in, left_ref)], pair_sem)
    right_load.start()
    loads.start()
    side_load.start()

    def produce(chip, target):
        loads.wait(chip)
        pair = pl.ds(pl.multiple_of(chip * 2 * tokens, 2 * tokens), 2 * tokens)

        @pl.loop(0, out_ref.shape[1] // step)
        def _(i):
            at = pl.ds(pl.multiple_of(i * step, step), step)
            target[:, at] = contract(left_ref[pair, :], right_ref[at, :], 1, 1).astype(BF16)

    copies = [
        send(give_ref.at[i], got_ref.at[i], give_send.at[i], give_recv.at[i], other(bits))
        for i, bits in enumerate((Y_BIT, X_BIT))
    ]

    def grad_out(i):
        at = pl.ds(pl.multiple_of(i * step, step), step)
        return pltpu.make_async_copy(grad_held.at[at], grad_ref.at[at], grad_sem.at[i])

    steps = grad_ref.shape[0] // step

    def at_start():
        begin(copies)
        right_load.wait()

    def meanwhile():
        side_load.wait()

        @pl.loop(0, steps)
        def _(i):
            at = pl.ds(pl.multiple_of(i * step, step), step)
            grad_held[at, :] = contract(side_ref[:, at], left_ref[...], 0, 0).astype(BF16)
            grad_out(i).start()

    def at_end():
        for copy in copies:
            copy.wait()
        for i in range(steps):
            grad_out(i).wait()

    scattering(out_ref, *rest, produce, at_start, meanwhile, at_end)


def product_scatter(left, right, side, give, name):
    tokens, wide = left.shape[0] // 8, right.shape[0]
    grad = (side.shape[1], left.shape[1])
    dma = pltpu.SemaphoreType.DMA
    return vmem_call(
        product_scatter_kernel,
        [
            jax.ShapeDtypeStruct((tokens, wide), F32),
            jax.ShapeDtypeStruct(grad, BF16),
            jax.ShapeDtypeStruct((2, *give.shape[1:]), BF16),
        ],
        (4, 2),
        [
            *scatter_scratch(tokens, wide),
            *[pltpu.VMEM(array.shape, BF16) for array in (left, right, side)],
            pltpu.VMEM(grad, BF16),
            dma((2,)),
            dma((1, 4)),
            dma((grad[0] // 256,)),
            dma((2,)), dma((2,)),
        ],
        name,
        32 * tokens * wide * left.shape[1],
        left, right, side, give,
    )


def in_plane():
    return 4 * lax.axis_index("x") + 2 * lax.axis_index("c") + lax.axis_index("y")


class Parcel:
    def __init__(self, count, f_first, rank_rows, columns, kv_rows):
        self.count, self.f_first = count, f_first
        self.rank_rows, self.columns, self.kv_rows = rank_rows, columns, kv_rows
        self.windows = columns == 128
        self.lines = rank_rows * columns // 128

    def down_shape(self):
        if self.windows:
            return (2 * self.rank_rows, 4 * self.count * self.columns)
        return (8, self.count, self.lines, 128)

    def down_from(self, array):
        if self.windows:
            return array
        array = array.reshape(2, 2, 2, self.count, self.rank_rows, self.columns)
        array = array.transpose((2, 4, 3, 0, 1, 5) if self.f_first else (2, 4, 0, 1, 3, 5))
        return array.reshape(2 * self.rank_rows, -1)

    def down_to(self, array):
        if self.windows:
            return array
        inner = (self.count, 2, 2) if self.f_first else (2, 2, self.count)
        array = array.reshape(2, self.rank_rows, *inner, self.columns)
        array = array.transpose((3, 4, 0, 2, 1, 5) if self.f_first else (2, 3, 0, 4, 1, 5))
        return array.reshape(self.down_shape())

    def blocks(self, refs, place, j):
        down, kv, small = refs
        pair, y = place // 2, place % 2
        at = j * 4 + pair if self.f_first else pair * self.count + j
        if self.windows:
            down = down.at[
                pl.ds(pl.multiple_of(y * self.rank_rows, self.rank_rows), self.rank_rows),
                pl.ds(pl.multiple_of(at * self.columns, self.columns), self.columns),
            ]
        else:
            down = down.at[place, j]
        start_row = pl.multiple_of((2 * at + y) * self.kv_rows, self.kv_rows)
        return down, kv.at[pl.ds(start_row, self.kv_rows)], small.at[place, j]

    def unit_pieces(self):
        for shard in range(8 * self.count):
            if self.f_first:
                yield shard % 8, shard // 8, shard
            else:
                yield shard // (2 * self.count) * 2 + shard % 2, shard // 2 % self.count, shard


def greet_all(count):
    f = lax.axis_index("f")
    lower, upper = f > 0, f < count - 1
    barrier = pltpu.get_barrier_semaphore()
    for bits in range(1, 8):
        pl.semaphore_signal(barrier, inc=1, device_id=other(bits))
    pl.when(lower)(lambda: pl.semaphore_signal(barrier, inc=1, device_id={"f": f - 1}))
    pl.when(upper)(lambda: pl.semaphore_signal(barrier, inc=1, device_id={"f": f + 1}))
    pl.semaphore_wait(barrier, 7 + lower.astype(jnp.int32) + upper.astype(jnp.int32))
    return lower, upper


FAR_FIRST = (7, 6, 5, 4, 3, 2, 1)


def as_place(bits):
    return (bits & 4) + 2 * (bits & 1) + (bits >> 1 & 1)


def start_kernel(
    parcel, chunks, units, padded, down_ref, kv_ref, small_ref, head_ref, out_ref, ff_ref, gate_ref, up_ref, rows_ref,
    down_all, kv_all, small_all, head_all, out_all, ff_all, wide_all, rows_all,
    down_low, kv_low, head_low, out_low, ff_low, wide_ref,
    local_sem, line_send, line_recv, plane_send, plane_recv, wide_send, wide_recv, rows_send, rows_recv,
    head_send, head_recv, far_send, far_recv,
):
    count = parcel.count
    f, me = lax.axis_index("f"), in_plane()
    lower, upper = greet_all(count)
    own = (down_low, kv_low, small_ref)
    alls = (down_all, kv_all, small_all)
    down_low[...] = down_ref[...].astype(BF16)
    kv_low[...] = kv_ref[...].astype(BF16)
    head_low[...] = head_ref[...].astype(BF16)
    out_low[...] = out_ref[...].astype(BF16)
    ff_low[...] = ff_ref[...].astype(BF16)

    half = count // 2
    y = lax.axis_index("y")

    def head_blocks(j):
        kept = (j // half == y).astype(jnp.int32)
        spare = (1 - kept) * (2 * half + j % half)
        return (
            head_all.at[kept * (j % half) + spare],
            out_all.at[kept * (2 * (j % half) + y) + spare],
            ff_all.at[j],
        )

    def head_hop(j, up, sources, group):
        return [
            send(
                sources[i], head_blocks(j)[i], head_send.at[i, 0 if up else 1, j], head_recv.at[i, j],
                {"f": f + 1 if up else f - 1},
            )
            for i in group
        ]

    def across(slot, sources):
        targets = (head_all.at[half + slot], out_all.at[2 * slot + y])
        return [
            send(source, target, far_send.at[i, slot], far_recv.at[i, slot], other(Y_BIT))
            for i, (source, target) in enumerate(zip(sources, targets))
        ]

    heads, ff = (0, 1), (2,)

    def head_own(group):
        pl.when(upper)(lambda: begin(head_hop(f, True, own_heads, group)))
        pl.when(lower)(lambda: begin(head_hop(f, False, own_heads, group)))
        if group == heads:
            pl.when(f // half != y)(lambda: begin(across(f % half, own_heads)))

    def head_step(step, group):
        @pl.when(f - step >= 0)
        def _():
            j = f - step
            blocks = head_blocks(j)
            arrive(head_hop(j, True, blocks, group))
            pl.when(upper)(lambda: begin(head_hop(j, True, blocks, group)))
            if group == heads:
                pl.when(j // half != y)(lambda: begin(across(j % half, blocks)))

        @pl.when(f + step <= count - 1)
        def _():
            j = f + step
            blocks = head_blocks(j)
            arrive(head_hop(j, False, blocks, group))
            pl.when(lower)(lambda: begin(head_hop(j, False, blocks, group)))
            if group == heads:
                pl.when(j // half != y)(lambda: begin(across(j % half, blocks)))

    own_heads = (head_low, out_low, ff_low)

    def hop(j, up, sources):
        return [
            send(
                source, target, line_send.at[i, 0 if up else 1, j], line_recv.at[i, j],
                {"f": f + 1 if up else f - 1},
            )
            for i, (source, target) in enumerate(zip(sources, parcel.blocks(alls, me, j)))
        ]

    def spread(slot, bits, j, sources):
        targets = parcel.blocks(alls, me ^ as_place(bits) ^ as_place(slot), j)
        return [
            send(source, target, plane_send.at[i, slot, j], plane_recv.at[i, slot, j], other(bits))
            for i, (source, target) in enumerate(zip(sources, targets))
        ]

    def to_plane(j, sources):
        for bits in (X_BIT, Y_BIT, C_BIT):
            begin(spread(bits, bits, j, sources))

    def line_step(step):
        @pl.when(f - step >= 0)
        def _():
            j = f - step
            blocks = parcel.blocks(alls, me, j)
            arrive(hop(j, True, blocks))
            pl.when(upper)(lambda: begin(hop(j, True, blocks)))
            to_plane(j, blocks)

        @pl.when(f + step <= count - 1)
        def _():
            j = f + step
            blocks = parcel.blocks(alls, me, j)
            arrive(hop(j, False, blocks))
            pl.when(lower)(lambda: begin(hop(j, False, blocks)))
            to_plane(j, blocks)

    def relay(j):
        by_x, by_y = parcel.blocks(alls, me ^ as_place(X_BIT), j), parcel.blocks(alls, me ^ as_place(Y_BIT), j)
        arrive(spread(X_BIT, X_BIT, j, by_x))
        pl.when(j % 2 == 0)(lambda: begin(spread(BOTH, Y_BIT, j, by_x)))
        begin(spread(X_BIT | C_BIT, C_BIT, j, by_x))
        arrive(spread(Y_BIT, Y_BIT, j, by_y))
        pl.when(j % 2 == 1)(lambda: begin(spread(BOTH, X_BIT, j, by_y)))
        begin(spread(Y_BIT | C_BIT, C_BIT, j, by_y))

    def relay_far(j):
        by_both = parcel.blocks(alls, me ^ as_place(BOTH), j)
        arrive(spread(BOTH, Y_BIT, j, by_both))
        begin(spread(BOTH | C_BIT, C_BIT, j, by_both))

    def in_order(do):
        do(f)
        for step in range(1, count):
            pl.when(f - step >= 0)(lambda: do(f - step))
            pl.when(f + step <= count - 1)(lambda: do(f + step))

    def wide(bits):
        return send(wide_ref.at[me ^ as_place(bits)], wide_all.at[me], wide_send.at[bits], wide_recv.at[bits], other(bits))

    pl.when(upper)(lambda: begin(hop(f, True, own)))
    pl.when(lower)(lambda: begin(hop(f, False, own)))
    to_plane(f, own)
    head_own(heads)
    for place, j, shard in parcel.unit_pieces():
        for first, ref in ((0, gate_ref), (padded, up_ref)):
            piece = ref[:, shard * units : (shard + 1) * units].astype(BF16)
            wide_ref[place, :, first + j * units : first + (j + 1) * units] = piece
    for first in (count * units, padded + count * units):
        size = padded - count * units
        wide_ref[:, :, first : first + size] = jnp.zeros((8, wide_ref.shape[1], size), BF16)
    for bits in FAR_FIRST:
        wide(bits).start()
    locals_ = [
        pltpu.make_async_copy(source, target, local_sem.at[i])
        for i, (source, target) in enumerate(
            (
                *zip(own, parcel.blocks(alls, me, f)),
                *zip(own_heads, head_blocks(f)),
                (wide_ref.at[me], wide_all.at[me]),
                (rows_ref, rows_all.at[pl.ds(0, rows_ref.shape[0])]),
            )
        )
    ]
    begin(locals_)
    rows_own, rows_relay, rows_far, rows_arrived, rows_sent = gathering(chunks, rows_ref, rows_all, rows_send, rows_recv)
    for step in range(1, count):
        line_step(step)
        if step == 1:
            rows_own()
        if step < count - 1:
            head_step(step, heads)
    head_own(ff)
    in_order(relay)
    head_step(count - 1, heads)
    rows_relay(0, chunks // 2)
    in_order(relay_far)
    head_step(1, ff)
    rows_relay(chunks // 2, chunks)
    rows_far()
    for step in range(2, count):
        head_step(step, ff)
    for copy in locals_:
        copy.wait()
    for j in range(count):
        pl.when(upper & (f >= j))(lambda: gone(hop(j, True, own)))
        pl.when(lower & (f <= j))(lambda: gone(hop(j, False, own)))
        pl.when(upper & (f >= j))(lambda: gone(head_hop(j, True, own_heads, (0, 1, 2))))
        pl.when(lower & (f <= j))(lambda: gone(head_hop(j, False, own_heads, (0, 1, 2))))
    for slot in range(half):
        arrive(across(slot, own_heads))
        gone(across(slot, own_heads))
    for slot in range(1, 8):
        for j in range(count):
            for copy in spread(slot, slot, j, own):
                if slot & C_BIT:
                    copy.wait_recv()
                copy.wait_send()
    for bits in range(1, 8):
        wide(bits).wait_recv()
        wide(bits).wait_send()
    for chip in (0, Y_BIT, X_BIT, BOTH):
        rows_arrived(chip)
    rows_sent()


def start(parcel, down, kv, small, head, out, ff, gate, up, rows, units, padded, name, chunks=4):
    count = parcel.count
    any_space, vmem = pl.BlockSpec(memory_space=pl.ANY), pl.BlockSpec(memory_space=pltpu.VMEM)
    dma = pltpu.SemaphoreType.DMA
    wide = (8, gate.shape[0], 2 * padded)
    return pl.pallas_call(
        functools.partial(start_kernel, parcel, chunks, units, padded),
        out_shape=[
            jax.ShapeDtypeStruct(parcel.down_shape(), BF16),
            jax.ShapeDtypeStruct((8 * count * kv.shape[0], kv.shape[1]), BF16),
            jax.ShapeDtypeStruct((8, count, *small.shape), BF16),
            jax.ShapeDtypeStruct((3 * count // 2, *head.shape), BF16),
            jax.ShapeDtypeStruct((3 * count // 2, *out.shape), BF16),
            jax.ShapeDtypeStruct((count, *ff.shape), BF16),
            jax.ShapeDtypeStruct(wide, BF16),
            jax.ShapeDtypeStruct((8 * rows.shape[0], rows.shape[1]), BF16),
        ],
        in_specs=[vmem] * 8 + [any_space],
        out_specs=[any_space] * 8,
        scratch_shapes=[
            pltpu.VMEM(down.shape, BF16),
            pltpu.VMEM(kv.shape, BF16),
            pltpu.VMEM(head.shape, BF16),
            pltpu.VMEM(out.shape, BF16),
            pltpu.VMEM(ff.shape, BF16),
            pltpu.VMEM(wide, BF16),
            dma((8,)),
            dma((3, 2, count)), dma((3, count)),
            dma((3, 8, count)), dma((3, 8, count)),
            dma((8,)), dma((8,)),
            dma((8, chunks)), dma((8, chunks)),
            dma((3, 2, count)), dma((3, count)),
            dma((2, count // 2)), dma((2, count // 2)),
        ],
        compiler_params=pltpu.CompilerParams(
            collective_id=name, has_side_effects=True, vmem_limit_bytes=VMEM_MOST
        ),
        cost_estimate=pl.CostEstimate(flops=0, bytes_accessed=240 * 2**20, transcendentals=0),
    )(down, kv, small, head, out, ff, gate, up, rows)


def own_back_kernel(
    back_ref, latent_ref, rms_lat_ref, gain_lat_ref, normed_ref, down_ref, kv_ref, in_ref, rms_ref, gain_ref, d_mid_ref,
    down_part, kv_part, d_in_ref, lat_sum, gain_sum, d_normed,
):
    rank = latent_ref.shape[1]
    width = in_ref.shape[1]
    step = 512
    d_lat_n, d_shared = back_ref[:, :rank], back_ref[:, rank:].astype(BF16)
    latent, rms_lat = latent_ref[...], rms_lat_ref[...]
    lat_sum[...] = jnp.sum(d_lat_n * latent * rms_lat, axis=0, keepdims=True)
    scaled = d_lat_n * gain_lat_ref[...]
    inner = jnp.sum(scaled * latent, axis=1, keepdims=True)
    d_latent = (rms_lat * scaled - latent * (rms_lat * rms_lat * rms_lat) * inner / rank).astype(BF16)

    @pl.loop(0, width // step)
    def _(i):
        at = pl.ds(pl.multiple_of(i * step, step), step)
        down_part[:, at] = contract(d_latent, normed_ref[:, at], 0, 0).astype(BF16)
        kv_part[at, :] = contract(normed_ref[:, at], d_shared, 0, 0).astype(BF16)
        d_normed[:, at] = contract(d_shared, kv_ref[at, :], 1, 1) + contract(d_latent, down_ref[:, at], 1, 0)

    inputs, rms = in_ref[...].astype(F32), rms_ref[...]
    gain_sum[...] = jnp.sum(d_normed[...] * inputs * rms, axis=0, keepdims=True)
    mean = jnp.sum(d_normed[...] * gain_ref[...] * inputs, axis=1, keepdims=True) / width
    k = d_normed[...] * gain_ref[...]
    d_in_ref[...] = (d_mid_ref[...] + rms * k - inputs * (rms * rms * rms) * mean).astype(BF16)


def own_back(back, latent, rms_lat, gain_lat, normed, down, kv, inputs, rms, gain, d_middle):
    vmem = pl.BlockSpec(memory_space=pltpu.VMEM)
    tokens, width = inputs.shape
    rank = latent.shape[1]
    return pl.pallas_call(
        own_back_kernel,
        out_shape=[
            jax.ShapeDtypeStruct((rank, width), BF16),
            jax.ShapeDtypeStruct(kv.shape, BF16),
            jax.ShapeDtypeStruct((tokens, width), BF16),
            jax.ShapeDtypeStruct((1, rank), F32),
            jax.ShapeDtypeStruct((1, width), F32),
        ],
        in_specs=[vmem] * 11,
        out_specs=[vmem] * 5,
        scratch_shapes=[pltpu.VMEM((tokens, width), F32)],
        compiler_params=pltpu.CompilerParams(vmem_limit_bytes=VMEM_MOST),
        cost_estimate=pl.CostEstimate(
            flops=4 * tokens * width * (rank + kv.shape[1]), bytes_accessed=16 * 2**20, transcendentals=0
        ),
    )(back, latent, rms_lat, gain_lat, normed, down, kv, inputs, rms, gain, d_middle)


def end_kernel(
    parcel, units, padded, down_ref, kv_ref, small_ref, wide_ref, head_ref,
    down_sum, kv_sum, small_sum, gate_sum, up_sum, head_sum, *rest,
):
    count = parcel.count
    held = [rest[8 * i : 8 * i + 8] for i in range(3)]
    head_held = (rest[24], None, None, None, *rest[25:29])
    head_got = rest[29]
    held.append(head_held)
    wide_all, near_send, near_recv, chip_send, chip_recv, line_send, line_recv, wide_send, wide_recv = rest[30:39]
    far_send, far_recv = rest[39:]
    f, me = lax.axis_index("f"), in_plane()
    lower, upper = greet_all(count)
    parts = (down_ref, kv_ref, small_ref)
    sums = (down_sum, kv_sum, small_sum, head_sum)
    chips = (BOTH, X_BIT, Y_BIT, 0)

    def rows(amount, do):
        size = 16 if amount % 64 else 64

        @pl.loop(0, amount // size)
        def _(r):
            do(pl.ds(pl.multiple_of(r * size, size), size))

    def near(n, j):
        sources = parcel.blocks(parts, me ^ as_place(chips[n] | C_BIT), j)
        return [
            send(source, held[i][1].at[n, j], near_send.at[i, n, j], near_recv.at[i, n, j], other(C_BIT))
            for i, source in enumerate(sources)
        ]

    def far(n, j):
        return [
            send(held[i][2].at[n, j], held[i][3].at[n, j], chip_send.at[i, n, j], chip_recv.at[i, n, j], other(chips[n]))
            for i in range(3)
        ]

    order = []
    for j in range(count // 2):
        order += [count - 1 - j, j]

    def wide(bits):
        return send(wide_ref.at[me ^ as_place(bits)], wide_all.at[me], wide_send.at[bits], wide_recv.at[bits], other(bits))

    def hop(d, up, group):
        way = 0 if up else 1
        return [
            send(
                held[i][4 + 2 * way].at[d], held[i][5 + 2 * way].at[d],
                line_send.at[i, way, d], line_recv.at[i, way, d],
                {"f": f + 1 if up else f - 1},
            )
            for i in group
        ]

    def pass_on(d, up, group):
        way = 0 if up else 1
        behind = lower if up else upper

        @pl.when((d > f) if up else (d < f))
        def _():
            @pl.when(behind)
            def _():
                arrive(hop(d, up, group))
                for total, outgoing, incoming in ((held[i][0], held[i][4 + 2 * way], held[i][5 + 2 * way]) for i in group):

                    def add(at, total=total, outgoing=outgoing, incoming=incoming):
                        outgoing[d, at, :] = (total[d, at, :] + incoming[d, at, :].astype(F32)).astype(BF16)

                    rows(total.shape[1], add)

            @pl.when(jnp.logical_not(behind))
            def _():
                for total, outgoing in ((held[i][0], held[i][4 + 2 * way]) for i in group):

                    def keep(at, total=total, outgoing=outgoing):
                        outgoing[d, at, :] = total[d, at, :].astype(BF16)

                    rows(total.shape[1], keep)

            begin(hop(d, up, group))

    def line_step(step, group):
        pass_on(count - step, True, group)
        pass_on(step - 1, False, group)

    half = count // 2
    y = lax.axis_index("y")
    rank_rows, columns = head_got.shape[0], head_got.shape[1] // half

    def half_rows(which):
        return pl.ds(pl.multiple_of(which * rank_rows, rank_rows), rank_rows)

    swap = send(head_ref.at[half_rows(1 - y)], head_got, far_send, far_recv, other(Y_BIT))
    swap.start()
    for j in order:
        for n in range(4):
            begin(near(n, j))
    for j in order:
        for n in range(4):
            arrive(near(n, j))
            for i, source in enumerate(parcel.blocks(parts, me ^ as_place(chips[n]), j)):
                total, near_ref, chip_ref = held[i][:3]

                def add(at, n=n, j=j, source=source, total=total, near_ref=near_ref, chip_ref=chip_ref):
                    both = source[at, :].astype(F32) + near_ref[n, j, at, :].astype(F32)
                    if n < 3:
                        chip_ref[n, j, at, :] = both.astype(BF16)
                    else:
                        total[j, at, :] = both

                rows(total.shape[1], add)
            if n < 3:
                begin(far(n, j))

    for bits in FAR_FIRST:
        wide(bits).start()
    wide_all[me] = wide_ref[me]
    swap.wait_recv()
    for slot in range(half):
        at_columns = slice(slot * columns, (slot + 1) * columns)
        head_held[0][y * half + slot] = head_ref[half_rows(y), at_columns].astype(F32)
        head_held[0][(1 - y) * half + slot] = head_got[:, at_columns].astype(F32)
    pair, head = (0, 1, 2), (3,)
    line_step(1, head)
    for at_order, j in enumerate(order):
        for n in range(3):
            arrive(far(n, j))
        for i in range(3):
            total, far_ref = held[i][0], held[i][3]

            def add(at, j=j, total=total, far_ref=far_ref):
                value = total[j, at, :]
                for n in range(3):
                    value = value + far_ref[n, j, at, :].astype(F32)
                total[j, at, :] = value

            rows(total.shape[1], add)
        pass_on(j, True, pair)
        pass_on(j, False, pair)
        if at_order == 1:
            for step in range(2, count):
                line_step(step, head)
    for i in range(4):

        def keep(at, i=i):
            sums[i][at, :] = held[i][0][f, at, :]

        rows(sums[i].shape[0], keep)
    for up, there in ((True, lower), (False, upper)):

        @pl.when(there)
        def _(up=up):
            arrive(hop(f, up, range(4)))
            for i in range(4):
                incoming = held[i][5 if up else 7]

                def add(at, i=i, incoming=incoming):
                    sums[i][at, :] = sums[i][at, :] + incoming[f, at, :].astype(F32)

                rows(sums[i].shape[0], add)

    for bits in range(1, 8):
        wide(bits).wait_recv()
    for place, j, shard in parcel.unit_pieces():
        for first, ref in ((0, gate_sum), (padded, up_sum)):
            piece = wide_all[place, :, first + j * units : first + (j + 1) * units]
            ref[:, shard * units : (shard + 1) * units] = piece

    for d in range(count):
        pl.when(f < d)(lambda: gone(hop(d, True, range(4))))
        pl.when(f > d)(lambda: gone(hop(d, False, range(4))))
    for n in range(4):
        for j in range(count):
            for copy in near(n, j):
                copy.wait_send()
    for n in range(3):
        for j in range(count):
            gone(far(n, j))
    for bits in range(1, 8):
        wide(bits).wait_send()
    swap.wait_send()


def end(parcel, down, kv, small, wide, head, units, padded, name):
    vmem = pl.BlockSpec(memory_space=pltpu.VMEM)
    dma = pltpu.SemaphoreType.DMA
    count = parcel.count
    bodies = (
        (count, parcel.lines, 128),
        (count, parcel.kv_rows, kv.shape[1]),
        (count, *small.shape[2:]),
    )
    scratch = []
    for body in bodies:
        low = pltpu.VMEM(body, BF16)
        three = pltpu.VMEM((3, *body), BF16)
        scratch += [pltpu.VMEM(body, F32), pltpu.VMEM((4, *body), BF16), three, three, low, low, low, low]
    lines = (count, parcel.rank_rows, 2 * head.shape[1] // count)
    every = 8 * count * units
    return pl.pallas_call(
        functools.partial(end_kernel, parcel, units, padded),
        out_shape=[
            *[jax.ShapeDtypeStruct(body[1:], F32) for body in bodies],
            *[jax.ShapeDtypeStruct((wide.shape[1], every), BF16)] * 2,
            jax.ShapeDtypeStruct(lines[1:], F32),
        ],
        in_specs=[vmem] * 5,
        out_specs=[vmem] * 6,
        scratch_shapes=[
            *scratch,
            pltpu.VMEM(lines, F32),
            *[pltpu.VMEM(lines, BF16)] * 4,
            pltpu.VMEM((parcel.rank_rows, head.shape[1]), BF16),
            pltpu.VMEM(wide.shape, BF16),
            dma((3, 4, count)), dma((3, 4, count)),
            dma((3, 3, count)), dma((3, 3, count)),
            dma((4, 2, count)), dma((4, 2, count)),
            dma((8,)), dma((8,)),
            dma, dma,
        ],
        compiler_params=pltpu.CompilerParams(
            collective_id=name, has_side_effects=True, vmem_limit_bytes=VMEM_MOST
        ),
        cost_estimate=pl.CostEstimate(flops=0, bytes_accessed=240 * 2**20, transcendentals=0),
    )(down, kv, small, wide, head)


def by_owner(array, axis, count, f_first):
    lead, size, tail = array.shape[:axis], array.shape[axis], array.shape[axis + 1 :]
    part = size // (8 * count)
    n = len(lead)
    rest = [*range(n), n + 4, *range(n + 5, n + 5 + len(tail))]
    if f_first:
        array = array.reshape(*lead, count, 2, 2, 2, part, *tail)
        array = array.transpose(n, n + 1, n + 2, n + 3, *rest)
    else:
        array = array.reshape(*lead, 2, 2, count, 2, part, *tail)
        array = array.transpose(n + 2, n, n + 1, n + 3, *rest)
    return array.reshape(count, 8, *lead, part, *tail)


def from_owner(array, axis, f_first):
    count, _, *body = array.shape
    lead, part, tail = body[:axis], body[axis], body[axis + 1 :]
    n = axis
    array = array.reshape(count, 2, 2, 2, *body)
    inner = (0, 1, 2, 3) if f_first else (1, 2, 0, 3)
    array = array.transpose(
        *range(4, 4 + n), *inner, 4 + n, *range(5 + n, 5 + n + len(tail))
    )
    return array.reshape(*lead, 8 * count * part, *tail)


def per_device(
    count,
    f_first,
    block_input,
    seq_lens,
    attn_gain,
    latent_down,
    latent_gain,
    latent_up,
    shared_kv,
    out_proj,
    mlp_gain,
    gate_weight,
    up_weight,
    down_weight,
    out_cotangent,
):
    tokens, width = block_input.shape
    rank = 2 * latent_down.shape[0]
    half_rank = latent_down.shape[0]
    units = down_weight.shape[0]
    mine = units * count
    padded = -(-mine // 256) * 256
    y = lax.axis_index("y")
    place = lax.axis_index("f")
    x_c = 2 * lax.axis_index("x") + lax.axis_index("c")

    def rows_of(array):
        flat = array.reshape(-1)
        lines = -(-flat.shape[0] // 128)
        return jnp.pad(flat, (0, lines * 128 - flat.shape[0])).reshape(lines, 128)

    gain_high = latent_gain.astype(BF16)
    gain_low = (latent_gain - gain_high.astype(F32)).astype(BF16)
    gain_rows = attn_gain.shape[0]
    lat_lines = half_rank // 128
    small = jnp.concatenate(
        [
            rows_of(gain_high),
            rows_of(gain_low),
            rows_of(attn_gain.astype(BF16)),
            rows_of(mlp_gain.astype(BF16)),
            rows_of(seq_lens.astype(BF16)),
        ]
    )
    at_gain = 2 * lat_lines
    small = jnp.pad(small, ((0, -small.shape[0] % 16), (0, 0)))
    parcel = Parcel(count, f_first, half_rank, latent_down.shape[1], shared_kv.shape[0])
    down_full, kv_full, small, heads, out_full, ff_down, both, g_all = start(
        parcel,
        latent_down.reshape(-1, 128),
        shared_kv,
        small,
        latent_up,
        out_proj,
        down_weight,
        gate_weight,
        up_weight,
        out_cotangent,
        units,
        padded,
        0,
    )
    down_full = parcel.down_from(down_full)

    half = count // 2
    per_head = count // 4
    if per_head > 1:
        heads = heads[: 2 * half].reshape(2, 2, per_head, half_rank, -1).transpose(0, 1, 3, 2, 4)
        heads = heads.reshape(4, half_rank, HEAD_DIM)
    out_full = out_full.reshape(-1, width)

    both = lax.all_gather(both, "f", axis=0)
    both = from_owner(both, 0, f_first)
    ff_down = ff_down.reshape(mine, width)

    gain_lat = small[:2, 0, :lat_lines].astype(F32) + small[:2, 0, lat_lines:at_gain].astype(F32)
    gain_lat = gain_lat.reshape(rank)
    by_line = small.transpose(1, 0, 2, 3)
    gain_one = from_owner(by_line[:, :, at_gain, :gain_rows], 0, f_first).astype(F32)
    gain_two = from_owner(by_line[:, :, at_gain + 1, :gain_rows], 0, f_first).astype(F32)
    lengths = lax.dynamic_index_in_dim(small[:, :, at_gain + 2, :3], place, 1, keepdims=False)
    lengths = jnp.stack(
        [lax.dynamic_index_in_dim(lengths, in_plane() ^ as_place(i), 0, keepdims=False) for i in range(8)]
    ).astype(jnp.int32)

    inputs = block_input.astype(F32)
    rms_one = lax.rsqrt(jnp.mean(inputs * inputs, axis=-1, keepdims=True) + EPS)
    normed = (inputs * rms_one * gain_one).astype(BF16)
    latent = contract(normed, down_full, 1, 1)
    rms_lat = lax.rsqrt(jnp.mean(latent * latent, axis=-1, keepdims=True) + EPS)
    latent_n = (latent * rms_lat * gain_lat).astype(BF16)
    shared = jnp.dot(normed, kv_full, preferred_element_type=F32)
    position, begins = layout(lengths, tokens)
    cosine, sine = rope_tables(position.reshape(-1), HEAD_DIM)
    k_own = rotate(shared, cosine[:tokens], sine[:tokens]).astype(BF16)

    rows_all = plane_gather(jnp.concatenate([latent_n, k_own, shared.astype(BF16)], axis=1), 1)
    begins = begins.reshape(-1, 1)
    branch, q_rot, lse, attended = attention(rows_all, heads, out_full, cosine, sine, begins, 2)

    middle = inputs + branch
    rms_two = lax.rsqrt(jnp.mean(middle * middle, axis=-1, keepdims=True) + EPS)
    normed_two = (middle * rms_two * gain_two).astype(BF16)
    two_all, hidden, d_both, result, chip_sums = feed(normed_two, g_all, both, ff_down, padded, 3)
    down_grad = contract(hidden, g_all, 0, 0)[:mine].reshape(count, units, width).astype(BF16)
    d_both, down_grad, chip_sums = lax.optimization_barrier((d_both, down_grad, chip_sums))
    down_grad = lax.psum_scatter(down_grad, "f", scatter_dimension=0).astype(F32)
    d_two, both_grad, arrived = product_scatter(d_both, both, two_all, chip_sums, 4)
    farthest = lax.ppermute(chip_sums[2], ("x", "y"), DIAGONAL)
    both_grad = by_owner(both_grad, 0, count, f_first)
    both_grad = lax.psum_scatter(both_grad, "f", scatter_dimension=0)

    upstream = out_cotangent.astype(F32)
    gain_two_part = jnp.sum(d_two * middle * rms_two, axis=0)
    scaled_two = d_two * gain_two
    d_middle = (
        upstream
        + rms_two * scaled_two
        - middle * (rms_two**3) * jnp.mean(scaled_two * middle, axis=-1, keepdims=True)
    )

    d_branch = plane_gather(d_middle.astype(BF16), 5)

    def join(own, other_part, axis):
        low = jnp.where(y == 0, own, other_part)
        high = jnp.where(y == 0, other_part, own)
        return jnp.stack([low, high], axis)

    def halves_of(array, axis):
        array = array.astype(BF16)
        own = lax.dynamic_index_in_dim(array, y, axis, keepdims=False)
        return own, lax.dynamic_index_in_dim(array, 1 - y, axis, keepdims=False)

    out_grad = contract(attended, d_branch, 0, 0).reshape(2, per_head, 2, -1, width)
    out_own, out_far = halves_of(out_grad, 2)
    back, d_queries, up_grad_part, out_far = attention_back(
        d_branch, rows_all, heads, out_full, cosine, sine, begins, q_rot, lse, out_far, 6
    )
    out_line_grad = join(out_own, out_far, 0).reshape(count, -1, width)
    out_proj_grad = lax.psum_scatter(after(out_line_grad, both_grad, down_grad), "f", scatter_dimension=0).astype(F32)

    down_part, kv_part, input_grad, gain_lat_part, gain_one_part = own_back(
        back, latent, rms_lat, gain_lat[None], normed, down_full, kv_full, block_input, rms_one, gain_one[None], d_middle
    )
    gain_one_part = gain_one_part.reshape(width)

    down_part = parcel.down_to(down_part)

    def gain_rows_of(part):
        part = by_owner(part.astype(BF16), 0, count, f_first).transpose(1, 0, 2)
        return jnp.pad(part, ((0, 0), (0, 0), (0, 128 - gain_rows)))[:, :, None]

    lat_rows = jnp.broadcast_to(
        gain_lat_part.astype(BF16).reshape(1, 2, 1, lat_lines, 128), (4, 2, count, lat_lines, 128)
    )
    small_part = jnp.concatenate(
        [
            lat_rows.reshape(8, count, lat_lines, 128),
            gain_rows_of(gain_one_part),
            gain_rows_of(gain_two_part),
        ],
        axis=2,
    )
    small_part = jnp.pad(small_part, ((0, 0), (0, 0), (0, -small_part.shape[2] % 16), (0, 0)))
    latent_down_grad, shared_kv_grad, small_sum, gate_grad, up_grad, latent_up_grad = end(
        parcel, down_part, kv_part, small_part, both_grad, up_grad_part, units, padded, 7
    )
    gate_grad, up_grad = gate_grad.astype(F32), up_grad.astype(F32)
    latent_down_grad = latent_down_grad.reshape(latent_down.shape)
    latent_gain_grad = small_sum[:lat_lines].reshape(half_rank)
    attn_gain_grad = small_sum[lat_lines, :gain_rows]
    mlp_gain_grad = small_sum[lat_lines + 1, :gain_rows]
    farthest = after(farthest, small_sum).astype(F32)
    block_output = (middle + result + arrived[0].astype(F32) + arrived[1].astype(F32) + farthest).astype(BF16)
    return (
        block_output,
        input_grad,
        attn_gain_grad,
        latent_down_grad,
        latent_gain_grad,
        latent_up_grad,
        shared_kv_grad,
        out_proj_grad,
        mlp_gain_grad,
        gate_grad,
        up_grad,
        down_grad,
    )


def solution(mesh):
    devices = mesh.devices
    split = devices.shape[0]
    count = split // 4
    f_first = split == HEADS
    if f_first:
        names, sizes = ("f", "x", "c", "y"), (count, 2, 2, 2)
    else:
        names, sizes = ("x", "c", "f", "y"), (2, 2, count, 2)
    fine = Mesh(devices.reshape(sizes), names)
    dp = names[:3]
    return jax.shard_map(
        functools.partial(per_device, count, f_first),
        mesh=fine,
        in_specs=(
            P(names, None),
            P(names, None),
            P(names),
            P("y", dp),
            P("y"),
            P("y", dp),
            P(names, None),
            P(names, None),
            P(names),
            P(names, None),
            P(names, None),
            P(names, None),
            P(names, None),
        ),
        out_specs=(
            P(names, None),
            P(names, None),
            P(names),
            P("y", dp),
            P("y"),
            P("y", dp),
            P(names, None),
            P(names, None),
            P(names),
            P(names, None),
            P(names, None),
            P(names, None),
        ),
        check_vma=False,
    )
```

```python
import functools
import math

import jax
import jax.numpy as jnp
from jax import lax
from jax.experimental import pallas as pl
from jax.experimental.pallas import tpu as pltpu
from jax.sharding import Mesh
from jax.sharding import PartitionSpec as P

HEADS = 16
HEAD_DIM = 256
EPS = 1e-06
NEGATIVE = -1e30
F32 = jnp.float32
BF16 = jnp.bfloat16


def contract(left, right, left_dim, right_dim):
    return lax.dot_general(
        left, right, (((left_dim,), (right_dim,)), ((), ())), preferred_element_type=F32
    )


def after(value, *first):
    return lax.optimization_barrier((value, *first))[0]


def layout(lengths, count):
    spots = jnp.arange(lengths.shape[-1], dtype=jnp.int32)
    ends = jnp.sum(jnp.where(spots[None, :] <= spots[:, None], lengths[..., None, :], 0), axis=-1)
    places = jnp.arange(count, dtype=jnp.int32)
    passed = places[:, None] >= ends[..., None, :]
    offset = jnp.sum(jnp.where(passed, lengths[..., None, :], 0), axis=-1)
    return (places - offset).astype(F32), offset


def rope_tables(position, width):
    half = width // 2
    steps = jnp.arange(half, dtype=F32)
    freqs = jnp.exp(steps * (-math.log(10000.0) / half))
    angles = position[..., None] * freqs
    return jnp.cos(angles), jnp.sin(angles)


def rotate(values, cosine, sine):
    half = values.shape[-1] // 2
    first, second = values[..., :half], values[..., half:]
    return jnp.concatenate(
        [first * cosine - second * sine, second * cosine + first * sine], axis=-1
    )


DIAGONAL = [(0, 3), (3, 0), (1, 2), (2, 1)]


X_BIT, Y_BIT, C_BIT = 4, 2, 1
BOTH = X_BIT | Y_BIT
VMEM_MOST = 60 * 2**20


def other(bits):
    flips = {"x": bits // 4, "y": bits // 2 % 2, "c": bits % 2}
    return {name: 1 - lax.axis_index(name) for name, flip in flips.items() if flip}


def greet(partners):
    barrier = pltpu.get_barrier_semaphore()
    for partner in partners:
        pl.semaphore_signal(barrier, inc=1, device_id=partner)
    pl.semaphore_wait(barrier, len(partners))


def send(source, target, send_sem, recv_sem, device):
    return pltpu.make_async_remote_copy(
        src_ref=source, dst_ref=target, send_sem=send_sem, recv_sem=recv_sem, device_id=device
    )


def begin(copies):
    for copy in copies:
        copy.start()


def arrive(copies):
    for copy in copies:
        copy.wait_recv()


def gone(copies):
    for copy in copies:
        copy.wait_send()


def gathering(chunks, in_ref, out_ref, send_sem, recv_sem):
    tokens = in_ref.shape[0]
    rows = tokens // chunks

    def to(slot, k, bits, source=None):
        target = out_ref.at[pl.ds(slot * tokens + k * rows, rows)]
        if source is None:
            source = in_ref.at[pl.ds(k * rows, rows)]
        else:
            source = out_ref.at[pl.ds(source * tokens + k * rows, rows)]
        return send(source, target, send_sem.at[slot, k], recv_sem.at[slot, k], other(bits))

    def own():
        for k in range(chunks):
            to(X_BIT, k, X_BIT).start()
            to(Y_BIT, k, Y_BIT).start()
        for k in range(chunks):
            to(C_BIT, k, C_BIT).start()

    def relay(first, last):
        for k in range(first, last):
            to(X_BIT, k, X_BIT).wait_recv()
            if k < chunks // 2:
                to(BOTH, k, Y_BIT, X_BIT).start()
            to(X_BIT | C_BIT, k, C_BIT, X_BIT).start()
            to(Y_BIT, k, Y_BIT).wait_recv()
            if k >= chunks // 2:
                to(BOTH, k, X_BIT, Y_BIT).start()
            to(Y_BIT | C_BIT, k, C_BIT, Y_BIT).start()

    def far():
        for k in range(chunks):
            to(BOTH, k, Y_BIT).wait_recv()
            to(BOTH | C_BIT, k, C_BIT, BOTH).start()

    def arrived(chip):
        for k in range(chunks):
            to(chip | C_BIT, k, C_BIT).wait_recv()

    def sent():
        for slot in range(1, 8):
            for k in range(chunks):
                to(slot, k, C_BIT).wait_send()

    return own, relay, far, arrived, sent


def gather_kernel(chunks, in_ref, out_ref, own_sem, send_sem, recv_sem):
    greet([other(C_BIT), other(X_BIT), other(Y_BIT)])
    copy = pltpu.make_async_copy(in_ref, out_ref.at[pl.ds(0, in_ref.shape[0])], own_sem)
    copy.start()
    own, relay, far, arrived, sent = gathering(chunks, in_ref, out_ref, send_sem, recv_sem)
    own()
    relay(0, chunks)
    far()
    copy.wait()
    for chip in (0, Y_BIT, X_BIT, BOTH):
        arrived(chip)
    sent()


def plane_gather(block, name, chunks=4):
    return pl.pallas_call(
        functools.partial(gather_kernel, chunks),
        out_shape=jax.ShapeDtypeStruct((8 * block.shape[0], block.shape[1]), block.dtype),
        in_specs=[pl.BlockSpec(memory_space=pl.ANY)],
        out_specs=pl.BlockSpec(memory_space=pl.ANY),
        scratch_shapes=[
            pltpu.SemaphoreType.DMA,
            pltpu.SemaphoreType.DMA((8, chunks)),
            pltpu.SemaphoreType.DMA((8, chunks)),
        ],
        compiler_params=pltpu.CompilerParams(collective_id=name, has_side_effects=True),
        cost_estimate=pl.CostEstimate(flops=0, bytes_accessed=160 * 2**20, transcendentals=0),
    )(block)


def row_loop(amount, do, size=32):
    @pl.loop(0, amount // size)
    def _(r):
        do(pl.ds(pl.multiple_of(r * size, size), size))


def scattering(
    out_ref, work_ref, near_ref, far_ref, near_send, near_recv, far_send, far_recv, produce,
    at_start=None, meanwhile=None, at_end=None,
):
    greet([other(C_BIT), other(X_BIT), other(Y_BIT)])
    tokens = out_ref.shape[0]
    half = tokens // 2
    low, high = pl.ds(0, half), pl.ds(half, half)

    def near(n):
        return send(
            work_ref.at[n, pl.ds(tokens, tokens)], near_ref.at[n], near_send.at[n], near_recv.at[n], other(C_BIT)
        )

    def hop(i):
        n, part, bits = (
            (0, low, X_BIT), (0, high, Y_BIT), (1, low, X_BIT), (2, high, Y_BIT), (1, high, X_BIT), (2, low, Y_BIT)
        )[i]
        return send(work_ref.at[n, part], far_ref.at[i], far_send.at[i], far_recv.at[i], other(bits))

    def chip_sum(n):
        near(n).wait_recv()

        def keep(at):
            total = work_ref[n, at, :].astype(F32) + near_ref[n, at, :].astype(F32)
            work_ref[n, at, :] = total.astype(BF16)

        row_loop(tokens, keep)

    if at_start is not None:
        at_start()

    @pl.loop(0, 4)
    def _(n):
        produce(3 - n, work_ref.at[n])
        near(n).start()

        @pl.when(n > 0)
        def _():
            chip_sum(n - 1)
            pl.when(n == 1)(lambda: begin([hop(0), hop(1)]))
            pl.when(n == 2)(lambda: hop(2).start())
            pl.when(n == 3)(lambda: hop(3).start())

    near(3).wait_recv()

    def give(at):
        out_ref[at, :] = work_ref[3, at, :].astype(F32) + near_ref[3, at, :].astype(F32)

    row_loop(tokens, give)
    for came, n, first, on in ((0, 2, 0, 5), (1, 1, half, 4)):
        hop(came).wait_recv()

        def add(at, came=came, n=n, first=first):
            here = pl.ds(pl.multiple_of(first + at.start, 32), 32)
            total = work_ref[n, here, :].astype(F32) + far_ref[came, at, :].astype(F32)
            work_ref[n, here, :] = total.astype(BF16)

        row_loop(half, add)
        hop(on).start()
    if meanwhile is not None:
        meanwhile()

    def last(came, first):
        for i in came:
            hop(i).wait_recv()

        def add(at):
            here = pl.ds(pl.multiple_of(first + at.start, 32), 32)
            value = out_ref[here, :]
            for i in came:
                value = value + far_ref[i, at, :].astype(F32)
            out_ref[here, :] = value

        row_loop(half, add)

    last((2, 5), 0)
    last((3, 4), half)
    gone([*[near(n) for n in range(4)], *[hop(i) for i in range(6)]])
    if at_end is not None:
        at_end()


class PairLoads:
    def __init__(self, pairs, sem):
        self.pairs, self.sem = pairs, sem
        self.rows = pairs[0][0].shape[0] // 4

    def copies(self, chip):
        rows = pl.ds(pl.multiple_of(chip * self.rows, self.rows), self.rows)
        return [
            pltpu.make_async_copy(source.at[rows], target.at[rows], self.sem.at[i, chip])
            for i, (source, target) in enumerate(self.pairs)
        ]

    def start(self):
        for chip in (3, 2, 1, 0):
            begin(self.copies(chip))

    def wait(self, chip):
        for copy in self.copies(chip):
            copy.wait()


def scatter_scratch(tokens, wide):
    dma = pltpu.SemaphoreType.DMA
    return [
        pltpu.VMEM((4, 2 * tokens, wide), BF16),
        pltpu.VMEM((4, tokens, wide), BF16),
        pltpu.VMEM((6, tokens // 2, wide), BF16),
        dma((4,)), dma((4,)),
        dma((6,)), dma((6,)),
    ]


def vmem_call(kernel, out_shape, stay, scratch, name, flops, *arrays):
    stay_in, stay_out = stay
    vmem, any_space = pl.BlockSpec(memory_space=pltpu.VMEM), pl.BlockSpec(memory_space=pl.ANY)
    return pl.pallas_call(
        kernel,
        out_shape=out_shape,
        in_specs=[vmem] * (len(arrays) - stay_in) + [any_space] * stay_in,
        out_specs=[vmem] * (len(out_shape) - stay_out) + [any_space] * stay_out,
        scratch_shapes=scratch,
        compiler_params=pltpu.CompilerParams(
            collective_id=name, has_side_effects=True, vmem_limit_bytes=VMEM_MOST
        ),
        cost_estimate=pl.CostEstimate(flops=flops, bytes_accessed=160 * 2**20, transcendentals=0),
    )(*arrays)


def turn(values, cosine, sine):
    half = values.shape[-1] // 2
    first, second = values[:, :half], values[:, half:]
    return jnp.concatenate([first * cosine - second * sine, second * cosine + first * sine], axis=1)


def masked_scores(queries, keys, begins):
    raw = contract(queries, keys, 1, 1) * HEAD_DIM**-0.5
    to = lax.broadcasted_iota(jnp.int32, raw.shape, 0)
    of = lax.broadcasted_iota(jnp.int32, raw.shape, 1)
    return jnp.where((of <= to) & (of >= begins), raw, NEGATIVE)


def halves(rank):
    half = rank // 2
    y = lax.axis_index("y")
    return (
        pl.ds(pl.multiple_of(y * half, half), half),
        pl.ds(pl.multiple_of(half - y * half, half), half),
    )


def attention_kernel(
    rank, head_ref, out_w_ref, cos_ref, sin_ref, begin_ref, rows_in,
    branch_ref, query_ref, lse_ref, att_ref, *rest,
):
    wide = out_w_ref.shape[1]
    tokens = branch_ref.shape[0]
    mine, theirs = halves(rank)
    *rest, rows_ref, load_sem = rest
    loads = PairLoads([(rows_in, rows_ref)], load_sem)
    loads.start()

    def produce(chip, target):
        loads.wait(chip)
        pair = pl.ds(pl.multiple_of(chip * 2 * tokens, 2 * tokens), 2 * tokens)
        queries = [
            contract(rows_ref[pair, mine], head_ref[h], 1, 0) + contract(rows_ref[pair, theirs], head_ref[2 + h], 1, 0)
            for h in range(2)
        ]
        for c in range(2):
            rows = pl.ds(pl.multiple_of((2 * chip + c) * tokens, tokens), tokens)
            keys = rows_ref[rows, rank : rank + HEAD_DIM]
            values = rows_ref[rows, rank + HEAD_DIM :]
            cosine, sine, begins = cos_ref[rows, :], sin_ref[rows, :], begin_ref[rows, :]
            for h in range(2):
                at = slice(h * HEAD_DIM, (h + 1) * HEAD_DIM)
                turned = turn(queries[h][c * tokens : (c + 1) * tokens], cosine, sine).astype(BF16)
                query_ref[rows, at] = turned
                scores = masked_scores(turned, keys, begins)
                peak = jnp.max(scores, axis=1, keepdims=True)
                lse = peak + jnp.log(jnp.sum(jnp.exp(scores - peak), axis=1, keepdims=True))
                lse_ref[rows, h : h + 1] = lse
                probs = jnp.exp(scores - lse).astype(BF16)
                att_ref[rows, at] = contract(probs, values, 1, 0).astype(BF16)

        @pl.loop(0, wide // 512)
        def _(i):
            at = pl.ds(pl.multiple_of(i * 512, 512), 512)
            target[:, at] = contract(att_ref[pair, :], out_w_ref[: 2 * HEAD_DIM, at], 1, 0).astype(BF16)

    scattering(branch_ref, *rest, produce)


def attention(rows, heads, out_w, cosine, sine, begins, name):
    tokens, rank = rows.shape[0] // 8, 2 * heads.shape[1]
    wide = out_w.shape[1]
    two = 2 * HEAD_DIM
    return vmem_call(
        functools.partial(attention_kernel, rank),
        [
            jax.ShapeDtypeStruct((tokens, wide), F32),
            jax.ShapeDtypeStruct((8 * tokens, two), BF16),
            jax.ShapeDtypeStruct((8 * tokens, 2), F32),
            jax.ShapeDtypeStruct((8 * tokens, two), BF16),
        ],
        (1, 0),
        [*scatter_scratch(tokens, wide), pltpu.VMEM(rows.shape, BF16), pltpu.SemaphoreType.DMA((1, 4))],
        name,
        16 * tokens * two * (wide + rank + 2 * tokens),
        heads, out_w, cosine, sine, begins, rows,
    )


def attention_back_kernel(
    rank, head_ref, out_w_ref, cos_ref, sin_ref, begin_ref, lse_ref, d_in, rows_in, query_in, give_ref,
    back_ref, dq_ref, grad_ref, got_ref, *rest,
):
    tokens = back_ref.shape[0]
    mine, theirs = halves(rank)
    scale = HEAD_DIM**-0.5
    *rest, d_ref, rows_ref, query_ref, load_sem, keep_sem, send_sem, recv_sem = rest
    loads = PairLoads([(d_in, d_ref), (rows_in, rows_ref), (query_in, query_ref)], load_sem)
    loads.start()

    def produce(chip, target):
        loads.wait(chip)
        pair = pl.ds(pl.multiple_of(chip * 2 * tokens, 2 * tokens), 2 * tokens)
        d_pair = contract(d_ref[pair, :], out_w_ref[: 2 * HEAD_DIM, :], 1, 1).astype(BF16)
        for c in range(2):
            rows = pl.ds(pl.multiple_of((2 * chip + c) * tokens, tokens), tokens)
            here = slice(c * tokens, (c + 1) * tokens)
            keys = rows_ref[rows, rank : rank + HEAD_DIM]
            values = rows_ref[rows, rank + HEAD_DIM :]
            cosine, sine, begins = cos_ref[rows, :], sin_ref[rows, :], begin_ref[rows, :]
            d_keys = d_values = None
            for h in range(2):
                at = slice(h * HEAD_DIM, (h + 1) * HEAD_DIM)
                queries, d_att = query_ref[rows, at], d_pair[here, at]
                probs = jnp.exp(masked_scores(queries, keys, begins) - lse_ref[rows, h : h + 1])
                d_probs = contract(d_att, values, 1, 1)
                inner = jnp.sum(probs * d_probs, axis=1, keepdims=True)
                d_scores = (probs * (d_probs - inner)).astype(BF16)
                d_query = contract(d_scores, keys, 1, 0) * scale
                dq_ref[rows, at] = turn(d_query, cosine, -sine).astype(BF16)
                d_k = contract(d_scores, queries, 0, 0)
                d_v = contract(probs.astype(BF16), d_att, 0, 0)
                d_keys = d_k if h == 0 else d_keys + d_k
                d_values = d_v if h == 0 else d_values + d_v
            shared = turn(d_keys * scale, cosine, -sine) + d_values
            target[here, rank:] = shared.astype(BF16)
        for first, part in ((0, mine), (2, theirs)):
            got = contract(dq_ref[pair, :HEAD_DIM], head_ref[first], 1, 1)
            got = got + contract(dq_ref[pair, HEAD_DIM:], head_ref[first + 1], 1, 1)
            target[:, part] = got.astype(BF16)

    y = lax.axis_index("y")
    half = got_ref.shape[0] // 2
    size = got_ref.shape[1]

    def grad_copies(s):
        rows = [pl.ds(pl.multiple_of((2 * s + which) * size, size), size) for which in (y, 1 - y)]
        target = got_ref.at[y * half + s]
        return (
            pltpu.make_async_copy(give_ref.at[rows[0]], target, keep_sem.at[s]),
            send(give_ref.at[rows[1]], target, send_sem.at[s], recv_sem.at[s], other(Y_BIT)),
        )

    def at_start():
        for s in range(half):
            begin(grad_copies(s))

    def at_end():
        for s in range(half):
            for copy in grad_copies(s):
                copy.wait()

    def meanwhile():
        @pl.loop(0, rank // 256)
        def _(i):
            at = pl.ds(pl.multiple_of(i * 256, 256), 256)
            grad_ref[at, :] = contract(rows_ref[:, at], dq_ref[...], 0, 0).astype(BF16)

    scattering(back_ref, *rest, produce, at_start, meanwhile, at_end)


def attention_back(d_rows, rows, heads, out_w, cosine, sine, begins, queries, lse, give, lines, name):
    tokens, rank = rows.shape[0] // 8, 2 * heads.shape[1]
    wide = out_w.shape[1]
    two = 2 * HEAD_DIM
    full = rank + HEAD_DIM
    return vmem_call(
        functools.partial(attention_back_kernel, rank),
        [
            jax.ShapeDtypeStruct((tokens, full), F32),
            jax.ShapeDtypeStruct((8 * tokens, two), BF16),
            jax.ShapeDtypeStruct((rank, two), BF16),
            jax.ShapeDtypeStruct((lines, give.shape[0] // lines, give.shape[1]), give.dtype),
        ],
        (4, 1),
        [
            *scatter_scratch(tokens, full),
            *[pltpu.VMEM(array.shape, BF16) for array in (d_rows, rows, queries)],
            pltpu.SemaphoreType.DMA((3, 4)),
            *[pltpu.SemaphoreType.DMA((lines // 2,))] * 3,
        ],
        name,
        16 * tokens * two * (wide + rank + 5 * tokens),
        heads, out_w, cosine, sine, begins, lse, d_rows, rows, queries, give,
    )


def feed_kernel(
    chunks, in_ref, g_ref, both_ref, down_ref, two_out, hidden_out, d_both_out, own_sum, chip_sums,
    two_ref, hidden_ref, d_both_ref, g_held, both_held, down_held, work_ref, near_ref, own_sem, load_sem, send_sem, recv_sem, near_send, near_recv, out_sem,
):
    step = 256
    tokens = in_ref.shape[0]
    padded = hidden_out.shape[1]
    units = down_ref.shape[0]
    loads = [
        pltpu.make_async_copy(both_ref, both_held, load_sem.at[0]),
        pltpu.make_async_copy(g_ref, g_held, load_sem.at[1]),
        pltpu.make_async_copy(down_ref, down_held.at[pl.ds(0, units)], load_sem.at[2]),
        pltpu.make_async_copy(in_ref, two_ref.at[pl.ds(0, tokens)], own_sem),
    ]
    begin(loads)
    greet([other(C_BIT), other(X_BIT), other(Y_BIT)])
    own, relay, far, arrived, sent = gathering(chunks, in_ref, two_ref, send_sem, recv_sem)
    own()
    if units < padded:
        down_held[units:, :] = jnp.zeros((padded - units, down_held.shape[1]), BF16)
    for copy in loads:
        copy.wait()

    def near(n):
        return send(
            work_ref.at[n, pl.ds(tokens, tokens)], near_ref.at[n], near_send.at[n], near_recv.at[n], other(C_BIT)
        )

    def chip_sum(n):
        near(n).wait_recv()

        def add(at):
            total = work_ref[n, at, :].astype(F32) + near_ref[n, at, :].astype(F32)
            if n:
                chip_sums[n - 1, at, :] = total.astype(BF16)
            else:
                own_sum[at, :] = total

        row_loop(tokens, add)

    def leave(chip):
        pair = pl.ds(chip * tokens, 2 * tokens)
        results = ((two_ref, two_out), (hidden_ref, hidden_out), (d_both_ref, d_both_out))
        return [
            pltpu.make_async_copy(held.at[pair], result.at[pair], out_sem.at[i, chip // 2])
            for i, (held, result) in enumerate(results)
        ]

    def outputs_of(chip):
        pair = pl.ds(chip * tokens, 2 * tokens)
        n = chip // 2

        @pl.loop(0, down_held.shape[1] // step)
        def _(i):
            at = pl.ds(pl.multiple_of(i * step, step), step)
            work_ref[n, :, at] = contract(hidden_ref[pair, :], down_held[:, at], 1, 0).astype(BF16)

        near(n).start()

    def units_of(chip):
        arrived(chip)
        pair = pl.ds(chip * tokens, 2 * tokens)

        @pl.loop(0, padded // step)
        def _(i):
            at = pl.ds(pl.multiple_of(i * step, step), step)
            up_at = pl.ds(pl.multiple_of(padded + i * step, step), step)
            gate = contract(two_ref[pair, :], both_held[:, at], 1, 0)
            upval = contract(two_ref[pair, :], both_held[:, up_at], 1, 0)
            d_hidden = contract(g_held[pair, :], down_held[at, :], 1, 1)
            sigma = 1.0 / (1.0 + jnp.exp(-gate))
            silu = gate * sigma
            hidden_ref[pair, at] = (silu * upval).astype(BF16)
            d_gate = d_hidden * upval * sigma * (1.0 + gate * (1.0 - sigma))
            d_both_ref[pair, at] = d_gate.astype(BF16)
            d_both_ref[pair, up_at] = (d_hidden * silu).astype(BF16)

        begin(leave(chip))

    units_of(0)
    outputs_of(0)
    chip_sum(0)
    relay(0, chunks)
    units_of(X_BIT)
    outputs_of(X_BIT)
    units_of(Y_BIT)
    far()
    outputs_of(Y_BIT)
    units_of(BOTH)
    outputs_of(BOTH)
    for n in (2, 1, 3):
        chip_sum(n)
    for chip in (0, Y_BIT, X_BIT, BOTH):
        for copy in leave(chip):
            copy.wait()
    sent()
    gone([near(n) for n in range(4)])


def feed(rows, g, both, down, padded, name, chunks=4):
    tokens, width = rows.shape
    any_space, vmem = pl.BlockSpec(memory_space=pl.ANY), pl.BlockSpec(memory_space=pltpu.VMEM)
    dma = pltpu.SemaphoreType.DMA
    return pl.pallas_call(
        functools.partial(feed_kernel, chunks),
        out_shape=[
            jax.ShapeDtypeStruct((8 * tokens, width), BF16),
            jax.ShapeDtypeStruct((8 * tokens, padded), BF16),
            jax.ShapeDtypeStruct((8 * tokens, 2 * padded), BF16),
            jax.ShapeDtypeStruct((tokens, width), F32),
            jax.ShapeDtypeStruct((3, tokens, width), BF16),
        ],
        in_specs=[any_space] * 4,
        out_specs=[any_space] * 3 + [vmem] * 2,
        scratch_shapes=[
            pltpu.VMEM((8 * tokens, width), BF16),
            pltpu.VMEM((8 * tokens, padded), BF16),
            pltpu.VMEM((8 * tokens, 2 * padded), BF16),
            pltpu.VMEM(g.shape, BF16),
            pltpu.VMEM(both.shape, BF16),
            pltpu.VMEM((padded, width), BF16),
            pltpu.VMEM((4, 2 * tokens, width), BF16),
            pltpu.VMEM((4, tokens, width), BF16),
            dma,
            dma((3,)),
            dma((8, chunks)), dma((8, chunks)),
            dma((4,)), dma((4,)),
            dma((3, 4)),
        ],
        compiler_params=pltpu.CompilerParams(
            collective_id=name, has_side_effects=True, vmem_limit_bytes=VMEM_MOST
        ),
        cost_estimate=pl.CostEstimate(
            flops=16 * tokens * 3 * width * padded, bytes_accessed=160 * 2**20, transcendentals=0
        ),
    )(rows, g, both, down)


def product_scatter_kernel(left_in, right_in, side_in, give_ref, out_ref, grad_ref, got_ref, *rest):
    tokens = out_ref.shape[0]
    step = 256
    *rest, left_ref, right_ref, side_ref, grad_held, load_sem, pair_sem, grad_sem, give_send, give_recv = rest
    right_load = pltpu.make_async_copy(right_in, right_ref, load_sem.at[0])
    side_load = pltpu.make_async_copy(side_in, side_ref, load_sem.at[1])
    loads = PairLoads([(left_in, left_ref)], pair_sem)
    right_load.start()
    loads.start()
    side_load.start()

    def produce(chip, target):
        loads.wait(chip)
        pair = pl.ds(pl.multiple_of(chip * 2 * tokens, 2 * tokens), 2 * tokens)

        @pl.loop(0, out_ref.shape[1] // step)
        def _(i):
            at = pl.ds(pl.multiple_of(i * step, step), step)
            target[:, at] = contract(left_ref[pair, :], right_ref[at, :], 1, 1).astype(BF16)

    copies = [
        send(give_ref.at[i], got_ref.at[i], give_send.at[i], give_recv.at[i], other(bits))
        for i, bits in enumerate((Y_BIT, X_BIT))
    ]

    def grad_out(i):
        at = pl.ds(pl.multiple_of(i * step, step), step)
        return pltpu.make_async_copy(grad_held.at[at], grad_ref.at[at], grad_sem.at[i])

    steps = grad_ref.shape[0] // step

    def at_start():
        begin(copies)
        right_load.wait()

    def meanwhile():
        side_load.wait()

        @pl.loop(0, steps)
        def _(i):
            at = pl.ds(pl.multiple_of(i * step, step), step)
            grad_held[at, :] = contract(side_ref[:, at], left_ref[...], 0, 0).astype(BF16)
            grad_out(i).start()

    def at_end():
        for copy in copies:
            copy.wait()
        for i in range(steps):
            grad_out(i).wait()

    scattering(out_ref, *rest, produce, at_start, meanwhile, at_end)


def product_scatter(left, right, side, give, name):
    tokens, wide = left.shape[0] // 8, right.shape[0]
    grad = (side.shape[1], left.shape[1])
    dma = pltpu.SemaphoreType.DMA
    return vmem_call(
        product_scatter_kernel,
        [
            jax.ShapeDtypeStruct((tokens, wide), F32),
            jax.ShapeDtypeStruct(grad, BF16),
            jax.ShapeDtypeStruct((2, *give.shape[1:]), BF16),
        ],
        (4, 2),
        [
            *scatter_scratch(tokens, wide),
            *[pltpu.VMEM(array.shape, BF16) for array in (left, right, side)],
            pltpu.VMEM(grad, BF16),
            dma((2,)),
            dma((1, 4)),
            dma((grad[0] // 256,)),
            dma((2,)), dma((2,)),
        ],
        name,
        32 * tokens * wide * left.shape[1],
        left, right, side, give,
    )


def branch_gather_kernel(
    chunks, in_ref, att_ref, out_ref, grad_ref, held_ref, total_ref, own_sem, out_sem, send_sem, recv_sem
):
    tokens = in_ref.shape[0]
    step = 512
    copy = pltpu.make_async_copy(in_ref, held_ref.at[pl.ds(0, tokens)], own_sem)
    copy.start()
    greet([other(C_BIT), other(X_BIT), other(Y_BIT)])
    own, relay, far, arrived, sent = gathering(chunks, in_ref, held_ref, send_sem, recv_sem)

    def leave(chip):
        pair = pl.ds(chip * tokens, 2 * tokens)
        return pltpu.make_async_copy(held_ref.at[pair], out_ref.at[pair], out_sem.at[chip // 2])

    def grad_of(chip):
        arrived(chip)
        leave(chip).start()
        pair = pl.ds(chip * tokens, 2 * tokens)

        @pl.loop(0, grad_ref.shape[1] // step)
        def _(i):
            at = pl.ds(pl.multiple_of(i * step, step), step)
            got = contract(att_ref[pair, :], held_ref[pair, at], 0, 0)
            if chip == 0:
                total_ref[:, at] = got
            elif chip == BOTH:
                grad_ref[:, at] = (total_ref[:, at] + got).astype(BF16)
            else:
                total_ref[:, at] = total_ref[:, at] + got

    own()
    copy.wait()
    grad_of(0)
    relay(0, chunks)
    grad_of(X_BIT)
    grad_of(Y_BIT)
    far()
    grad_of(BOTH)
    sent()
    for chip in (0, Y_BIT, X_BIT, BOTH):
        leave(chip).wait()


def branch_gather(rows, att, name, chunks=4):
    tokens, width = rows.shape
    any_space, vmem = pl.BlockSpec(memory_space=pl.ANY), pl.BlockSpec(memory_space=pltpu.VMEM)
    dma = pltpu.SemaphoreType.DMA
    return pl.pallas_call(
        functools.partial(branch_gather_kernel, chunks),
        out_shape=[
            jax.ShapeDtypeStruct((8 * tokens, width), BF16),
            jax.ShapeDtypeStruct((att.shape[1], width), BF16),
        ],
        in_specs=[any_space, vmem],
        out_specs=[any_space, vmem],
        scratch_shapes=[
            pltpu.VMEM((8 * tokens, width), BF16),
            pltpu.VMEM((att.shape[1], width), F32),
            dma,
            dma((4,)),
            dma((8, chunks)), dma((8, chunks)),
        ],
        compiler_params=pltpu.CompilerParams(
            collective_id=name, has_side_effects=True, vmem_limit_bytes=VMEM_MOST
        ),
        cost_estimate=pl.CostEstimate(
            flops=16 * tokens * width * att.shape[1], bytes_accessed=160 * 2**20, transcendentals=0
        ),
    )(rows, att)


def in_plane():
    return 4 * lax.axis_index("x") + 2 * lax.axis_index("c") + lax.axis_index("y")


class Parcel:
    def __init__(self, count, f_first, rank_rows, columns, kv_rows):
        self.count, self.f_first = count, f_first
        self.rank_rows, self.columns, self.kv_rows = rank_rows, columns, kv_rows
        self.windows = columns == 128
        self.lines = rank_rows * columns // 128

    def down_shape(self):
        if self.windows:
            return (2 * self.rank_rows, 4 * self.count * self.columns)
        return (8, self.count, self.lines, 128)

    def down_from(self, array):
        if self.windows:
            return array
        array = array.reshape(2, 2, 2, self.count, self.rank_rows, self.columns)
        array = array.transpose((2, 4, 3, 0, 1, 5) if self.f_first else (2, 4, 0, 1, 3, 5))
        return array.reshape(2 * self.rank_rows, -1)

    def down_to(self, array):
        if self.windows:
            return array
        inner = (self.count, 2, 2) if self.f_first else (2, 2, self.count)
        array = array.reshape(2, self.rank_rows, *inner, self.columns)
        array = array.transpose((3, 4, 0, 2, 1, 5) if self.f_first else (2, 3, 0, 4, 1, 5))
        return array.reshape(self.down_shape())

    def blocks(self, refs, place, j):
        down, kv, small = refs
        pair, y = place // 2, place % 2
        at = j * 4 + pair if self.f_first else pair * self.count + j
        if self.windows:
            down = down.at[
                pl.ds(pl.multiple_of(y * self.rank_rows, self.rank_rows), self.rank_rows),
                pl.ds(pl.multiple_of(at * self.columns, self.columns), self.columns),
            ]
        else:
            down = down.at[place, j]
        start_row = pl.multiple_of((2 * at + y) * self.kv_rows, self.kv_rows)
        return down, kv.at[pl.ds(start_row, self.kv_rows)], small.at[place, j]

    def unit_pieces(self):
        for shard in range(8 * self.count):
            if self.f_first:
                yield shard % 8, shard // 8, shard
            else:
                yield shard // (2 * self.count) * 2 + shard % 2, shard // 2 % self.count, shard


def greet_all(count):
    f = lax.axis_index("f")
    lower, upper = f > 0, f < count - 1
    barrier = pltpu.get_barrier_semaphore()
    for bits in range(1, 8):
        pl.semaphore_signal(barrier, inc=1, device_id=other(bits))
    pl.when(lower)(lambda: pl.semaphore_signal(barrier, inc=1, device_id={"f": f - 1}))
    pl.when(upper)(lambda: pl.semaphore_signal(barrier, inc=1, device_id={"f": f + 1}))
    pl.semaphore_wait(barrier, 7 + lower.astype(jnp.int32) + upper.astype(jnp.int32))
    return lower, upper


FAR_FIRST = (7, 6, 5, 4, 3, 2, 1)


def as_place(bits):
    return (bits & 4) + 2 * (bits & 1) + (bits >> 1 & 1)


def start_kernel(
    parcel, chunks, units, padded, down_ref, kv_ref, small_ref, head_ref, out_ref, ff_ref, gate_ref, up_ref, rows_ref,
    down_all, kv_all, small_all, head_all, out_all, ff_all, wide_all, rows_all,
    down_low, kv_low, head_low, out_low, ff_low, wide_ref,
    local_sem, line_send, line_recv, plane_send, plane_recv, wide_send, wide_recv, rows_send, rows_recv,
    head_send, head_recv, far_send, far_recv,
):
    count = parcel.count
    f, me = lax.axis_index("f"), in_plane()
    lower, upper = greet_all(count)
    own = (down_low, kv_low, small_ref)
    alls = (down_all, kv_all, small_all)
    down_low[...] = down_ref[...].astype(BF16)
    kv_low[...] = kv_ref[...].astype(BF16)
    head_low[...] = head_ref[...].astype(BF16)
    out_low[...] = out_ref[...].astype(BF16)
    ff_low[...] = ff_ref[...].astype(BF16)

    half = count // 2
    y = lax.axis_index("y")

    def head_blocks(j):
        kept = (j // half == y).astype(jnp.int32)
        spare = (1 - kept) * (2 * half + j % half)
        return (
            head_all.at[kept * (j % half) + spare],
            out_all.at[kept * (2 * (j % half) + y) + spare],
            ff_all.at[j],
        )

    def head_hop(j, up, sources, group):
        return [
            send(
                sources[i], head_blocks(j)[i], head_send.at[i, 0 if up else 1, j], head_recv.at[i, j],
                {"f": f + 1 if up else f - 1},
            )
            for i in group
        ]

    def across(slot, sources):
        targets = (head_all.at[half + slot], out_all.at[2 * slot + y])
        return [
            send(source, target, far_send.at[i, slot], far_recv.at[i, slot], other(Y_BIT))
            for i, (source, target) in enumerate(zip(sources, targets))
        ]

    heads, ff = (0, 1), (2,)

    def head_own(group):
        pl.when(upper)(lambda: begin(head_hop(f, True, own_heads, group)))
        pl.when(lower)(lambda: begin(head_hop(f, False, own_heads, group)))
        if group == heads:
            pl.when(f // half != y)(lambda: begin(across(f % half, own_heads)))

    def head_step(step, group):
        @pl.when(f - step >= 0)
        def _():
            j = f - step
            blocks = head_blocks(j)
            arrive(head_hop(j, True, blocks, group))
            pl.when(upper)(lambda: begin(head_hop(j, True, blocks, group)))
            if group == heads:
                pl.when(j // half != y)(lambda: begin(across(j % half, blocks)))

        @pl.when(f + step <= count - 1)
        def _():
            j = f + step
            blocks = head_blocks(j)
            arrive(head_hop(j, False, blocks, group))
            pl.when(lower)(lambda: begin(head_hop(j, False, blocks, group)))
            if group == heads:
                pl.when(j // half != y)(lambda: begin(across(j % half, blocks)))

    own_heads = (head_low, out_low, ff_low)

    def hop(j, up, sources):
        return [
            send(
                source, target, line_send.at[i, 0 if up else 1, j], line_recv.at[i, j],
                {"f": f + 1 if up else f - 1},
            )
            for i, (source, target) in enumerate(zip(sources, parcel.blocks(alls, me, j)))
        ]

    def spread(slot, bits, j, sources):
        targets = parcel.blocks(alls, me ^ as_place(bits) ^ as_place(slot), j)
        return [
            send(source, target, plane_send.at[i, slot, j], plane_recv.at[i, slot, j], other(bits))
            for i, (source, target) in enumerate(zip(sources, targets))
        ]

    def to_plane(j, sources):
        for bits in (X_BIT, Y_BIT, C_BIT):
            begin(spread(bits, bits, j, sources))

    def line_step(step):
        @pl.when(f - step >= 0)
        def _():
            j = f - step
            blocks = parcel.blocks(alls, me, j)
            arrive(hop(j, True, blocks))
            pl.when(upper)(lambda: begin(hop(j, True, blocks)))
            to_plane(j, blocks)

        @pl.when(f + step <= count - 1)
        def _():
            j = f + step
            blocks = parcel.blocks(alls, me, j)
            arrive(hop(j, False, blocks))
            pl.when(lower)(lambda: begin(hop(j, False, blocks)))
            to_plane(j, blocks)

    def relay(j):
        by_x, by_y = parcel.blocks(alls, me ^ as_place(X_BIT), j), parcel.blocks(alls, me ^ as_place(Y_BIT), j)
        arrive(spread(X_BIT, X_BIT, j, by_x))
        pl.when(j % 2 == 0)(lambda: begin(spread(BOTH, Y_BIT, j, by_x)))
        begin(spread(X_BIT | C_BIT, C_BIT, j, by_x))
        arrive(spread(Y_BIT, Y_BIT, j, by_y))
        pl.when(j % 2 == 1)(lambda: begin(spread(BOTH, X_BIT, j, by_y)))
        begin(spread(Y_BIT | C_BIT, C_BIT, j, by_y))

    def relay_far(j):
        by_both = parcel.blocks(alls, me ^ as_place(BOTH), j)
        arrive(spread(BOTH, Y_BIT, j, by_both))
        begin(spread(BOTH | C_BIT, C_BIT, j, by_both))

    def in_order(do):
        do(f)
        for step in range(1, count):
            pl.when(f - step >= 0)(lambda: do(f - step))
            pl.when(f + step <= count - 1)(lambda: do(f + step))

    def wide(bits):
        return send(wide_ref.at[me ^ as_place(bits)], wide_all.at[me], wide_send.at[bits], wide_recv.at[bits], other(bits))

    pl.when(upper)(lambda: begin(hop(f, True, own)))
    pl.when(lower)(lambda: begin(hop(f, False, own)))
    to_plane(f, own)
    rows_own, rows_relay, rows_far, rows_arrived, rows_sent = gathering(chunks, rows_ref, rows_all, rows_send, rows_recv)
    rows_own()
    head_own(heads)
    for place, j, shard in parcel.unit_pieces():
        for first, ref in ((0, gate_ref), (padded, up_ref)):
            piece = ref[:, shard * units : (shard + 1) * units].astype(BF16)
            wide_ref[place, :, first + j * units : first + (j + 1) * units] = piece
    for first in (count * units, padded + count * units):
        size = padded - count * units
        wide_ref[:, :, first : first + size] = jnp.zeros((8, wide_ref.shape[1], size), BF16)
    for bits in FAR_FIRST:
        wide(bits).start()
    locals_ = [
        pltpu.make_async_copy(source, target, local_sem.at[i])
        for i, (source, target) in enumerate(
            (
                *zip(own, parcel.blocks(alls, me, f)),
                *zip(own_heads, head_blocks(f)),
                (wide_ref.at[me], wide_all.at[me]),
                (rows_ref, rows_all.at[pl.ds(0, rows_ref.shape[0])]),
            )
        )
    ]
    begin(locals_)
    for step in range(1, count):
        line_step(step)
        if step < count - 1:
            head_step(step, heads)
    head_own(ff)
    rows_relay(0, chunks)
    in_order(relay)
    head_step(count - 1, heads)
    head_step(1, ff)
    in_order(relay_far)
    rows_far()
    for step in range(2, count):
        head_step(step, ff)
    for copy in locals_:
        copy.wait()
    for j in range(count):
        pl.when(upper & (f >= j))(lambda: gone(hop(j, True, own)))
        pl.when(lower & (f <= j))(lambda: gone(hop(j, False, own)))
        pl.when(upper & (f >= j))(lambda: gone(head_hop(j, True, own_heads, (0, 1, 2))))
        pl.when(lower & (f <= j))(lambda: gone(head_hop(j, False, own_heads, (0, 1, 2))))
    for slot in range(half):
        arrive(across(slot, own_heads))
        gone(across(slot, own_heads))
    for slot in range(1, 8):
        for j in range(count):
            for copy in spread(slot, slot, j, own):
                if slot & C_BIT:
                    copy.wait_recv()
                copy.wait_send()
    for bits in range(1, 8):
        wide(bits).wait_recv()
        wide(bits).wait_send()
    for chip in (0, Y_BIT, X_BIT, BOTH):
        rows_arrived(chip)
    rows_sent()


def start(parcel, down, kv, small, head, out, ff, gate, up, rows, units, padded, name, chunks=4):
    count = parcel.count
    any_space, vmem = pl.BlockSpec(memory_space=pl.ANY), pl.BlockSpec(memory_space=pltpu.VMEM)
    dma = pltpu.SemaphoreType.DMA
    wide = (8, gate.shape[0], 2 * padded)
    return pl.pallas_call(
        functools.partial(start_kernel, parcel, chunks, units, padded),
        out_shape=[
            jax.ShapeDtypeStruct(parcel.down_shape(), BF16),
            jax.ShapeDtypeStruct((8 * count * kv.shape[0], kv.shape[1]), BF16),
            jax.ShapeDtypeStruct((8, count, *small.shape), BF16),
            jax.ShapeDtypeStruct((3 * count // 2, *head.shape), BF16),
            jax.ShapeDtypeStruct((3 * count // 2, *out.shape), BF16),
            jax.ShapeDtypeStruct((count, *ff.shape), BF16),
            jax.ShapeDtypeStruct(wide, BF16),
            jax.ShapeDtypeStruct((8 * rows.shape[0], rows.shape[1]), BF16),
        ],
        in_specs=[vmem] * 8 + [any_space],
        out_specs=[any_space] * 8,
        scratch_shapes=[
            pltpu.VMEM(down.shape, BF16),
            pltpu.VMEM(kv.shape, BF16),
            pltpu.VMEM(head.shape, BF16),
            pltpu.VMEM(out.shape, BF16),
            pltpu.VMEM(ff.shape, BF16),
            pltpu.VMEM(wide, BF16),
            dma((8,)),
            dma((3, 2, count)), dma((3, count)),
            dma((3, 8, count)), dma((3, 8, count)),
            dma((8,)), dma((8,)),
            dma((8, chunks)), dma((8, chunks)),
            dma((3, 2, count)), dma((3, count)),
            dma((2, count // 2)), dma((2, count // 2)),
        ],
        compiler_params=pltpu.CompilerParams(
            collective_id=name, has_side_effects=True, vmem_limit_bytes=VMEM_MOST
        ),
        cost_estimate=pl.CostEstimate(flops=0, bytes_accessed=240 * 2**20, transcendentals=0),
    )(down, kv, small, head, out, ff, gate, up, rows)


def own_back_kernel(
    back_ref, latent_ref, rms_lat_ref, gain_lat_ref, normed_ref, down_ref, kv_ref, in_ref, rms_ref, gain_ref, d_mid_ref,
    down_part, kv_part, d_in_ref, lat_sum, gain_sum, d_normed,
):
    rank = latent_ref.shape[1]
    width = in_ref.shape[1]
    step = 512
    d_lat_n, d_shared = back_ref[:, :rank], back_ref[:, rank:].astype(BF16)
    latent, rms_lat = latent_ref[...], rms_lat_ref[...]
    lat_sum[...] = jnp.sum(d_lat_n * latent * rms_lat, axis=0, keepdims=True)
    scaled = d_lat_n * gain_lat_ref[...]
    inner = jnp.sum(scaled * latent, axis=1, keepdims=True)
    d_latent = (rms_lat * scaled - latent * (rms_lat * rms_lat * rms_lat) * inner / rank).astype(BF16)

    @pl.loop(0, width // step)
    def _(i):
        at = pl.ds(pl.multiple_of(i * step, step), step)
        down_part[:, at] = contract(d_latent, normed_ref[:, at], 0, 0).astype(BF16)
        kv_part[at, :] = contract(normed_ref[:, at], d_shared, 0, 0).astype(BF16)
        d_normed[:, at] = contract(d_shared, kv_ref[at, :], 1, 1) + contract(d_latent, down_ref[:, at], 1, 0)

    inputs, rms = in_ref[...].astype(F32), rms_ref[...]
    gain_sum[...] = jnp.sum(d_normed[...] * inputs * rms, axis=0, keepdims=True)
    mean = jnp.sum(d_normed[...] * gain_ref[...] * inputs, axis=1, keepdims=True) / width
    k = d_normed[...] * gain_ref[...]
    d_in_ref[...] = (d_mid_ref[...] + rms * k - inputs * (rms * rms * rms) * mean).astype(BF16)


def own_back(back, latent, rms_lat, gain_lat, normed, down, kv, inputs, rms, gain, d_middle):
    vmem = pl.BlockSpec(memory_space=pltpu.VMEM)
    tokens, width = inputs.shape
    rank = latent.shape[1]
    return pl.pallas_call(
        own_back_kernel,
        out_shape=[
            jax.ShapeDtypeStruct((rank, width), BF16),
            jax.ShapeDtypeStruct(kv.shape, BF16),
            jax.ShapeDtypeStruct((tokens, width), BF16),
            jax.ShapeDtypeStruct((1, rank), F32),
            jax.ShapeDtypeStruct((1, width), F32),
        ],
        in_specs=[vmem] * 11,
        out_specs=[vmem] * 5,
        scratch_shapes=[pltpu.VMEM((tokens, width), F32)],
        compiler_params=pltpu.CompilerParams(vmem_limit_bytes=VMEM_MOST),
        cost_estimate=pl.CostEstimate(
            flops=4 * tokens * width * (rank + kv.shape[1]), bytes_accessed=16 * 2**20, transcendentals=0
        ),
    )(back, latent, rms_lat, gain_lat, normed, down, kv, inputs, rms, gain, d_middle)


def end_kernel(
    parcel, units, padded, down_ref, kv_ref, small_ref, wide_ref, head_ref,
    down_sum, kv_sum, small_sum, gate_sum, up_sum, head_sum, *rest,
):
    count = parcel.count
    held = [rest[8 * i : 8 * i + 8] for i in range(3)]
    head_held = (rest[24], None, None, None, *rest[25:29])
    head_got = rest[29]
    held.append(head_held)
    wide_all, near_send, near_recv, chip_send, chip_recv, line_send, line_recv, wide_send, wide_recv = rest[30:39]
    far_send, far_recv = rest[39:]
    f, me = lax.axis_index("f"), in_plane()
    lower, upper = greet_all(count)
    parts = (down_ref, kv_ref, small_ref)
    sums = (down_sum, kv_sum, small_sum, head_sum)
    chips = (BOTH, X_BIT, Y_BIT, 0)

    def rows(amount, do):
        size = 16 if amount % 64 else 64

        @pl.loop(0, amount // size)
        def _(r):
            do(pl.ds(pl.multiple_of(r * size, size), size))

    def near(n, j):
        sources = parcel.blocks(parts, me ^ as_place(chips[n] | C_BIT), j)
        return [
            send(source, held[i][1].at[n, j], near_send.at[i, n, j], near_recv.at[i, n, j], other(C_BIT))
            for i, source in enumerate(sources)
        ]

    def far(n, j):
        return [
            send(held[i][2].at[n, j], held[i][3].at[n, j], chip_send.at[i, n, j], chip_recv.at[i, n, j], other(chips[n]))
            for i in range(3)
        ]

    order = []
    for j in range(count // 2):
        order += [count - 1 - j, j]

    def wide(bits):
        return send(wide_ref.at[me ^ as_place(bits)], wide_all.at[me], wide_send.at[bits], wide_recv.at[bits], other(bits))

    def hop(d, up, group):
        way = 0 if up else 1
        return [
            send(
                held[i][4 + 2 * way].at[d], held[i][5 + 2 * way].at[d],
                line_send.at[i, way, d], line_recv.at[i, way, d],
                {"f": f + 1 if up else f - 1},
            )
            for i in group
        ]

    def pass_on(d, up, group):
        way = 0 if up else 1
        behind = lower if up else upper

        @pl.when((d > f) if up else (d < f))
        def _():
            @pl.when(behind)
            def _():
                arrive(hop(d, up, group))
                for total, outgoing, incoming in ((held[i][0], held[i][4 + 2 * way], held[i][5 + 2 * way]) for i in group):

                    def add(at, total=total, outgoing=outgoing, incoming=incoming):
                        outgoing[d, at, :] = (total[d, at, :] + incoming[d, at, :].astype(F32)).astype(BF16)

                    rows(total.shape[1], add)

            @pl.when(jnp.logical_not(behind))
            def _():
                for total, outgoing in ((held[i][0], held[i][4 + 2 * way]) for i in group):

                    def keep(at, total=total, outgoing=outgoing):
                        outgoing[d, at, :] = total[d, at, :].astype(BF16)

                    rows(total.shape[1], keep)

            begin(hop(d, up, group))

    def line_step(step, group):
        pass_on(count - step, True, group)
        pass_on(step - 1, False, group)

    half = count // 2
    y = lax.axis_index("y")
    rank_rows, columns = head_got.shape[0], head_got.shape[1] // half

    def half_rows(which):
        return pl.ds(pl.multiple_of(which * rank_rows, rank_rows), rank_rows)

    swap = send(head_ref.at[half_rows(1 - y)], head_got, far_send, far_recv, other(Y_BIT))
    swap.start()
    for j in order:
        for n in range(4):
            begin(near(n, j))
    for j in order:
        for n in range(4):
            arrive(near(n, j))
            for i, source in enumerate(parcel.blocks(parts, me ^ as_place(chips[n]), j)):
                total, near_ref, chip_ref = held[i][:3]

                def add(at, n=n, j=j, source=source, total=total, near_ref=near_ref, chip_ref=chip_ref):
                    both = source[at, :].astype(F32) + near_ref[n, j, at, :].astype(F32)
                    if n < 3:
                        chip_ref[n, j, at, :] = both.astype(BF16)
                    else:
                        total[j, at, :] = both

                rows(total.shape[1], add)
            if n < 3:
                begin(far(n, j))

    for bits in FAR_FIRST:
        wide(bits).start()
    wide_all[me] = wide_ref[me]
    swap.wait_recv()
    for slot in range(half):
        at_columns = slice(slot * columns, (slot + 1) * columns)
        head_held[0][y * half + slot] = head_ref[half_rows(y), at_columns].astype(F32)
        head_held[0][(1 - y) * half + slot] = head_got[:, at_columns].astype(F32)
    pair, head = (0, 1, 2), (3,)
    line_step(1, head)
    for at_order, j in enumerate(order):
        for n in range(3):
            arrive(far(n, j))
        for i in range(3):
            total, far_ref = held[i][0], held[i][3]

            def add(at, j=j, total=total, far_ref=far_ref):
                value = total[j, at, :]
                for n in range(3):
                    value = value + far_ref[n, j, at, :].astype(F32)
                total[j, at, :] = value

            rows(total.shape[1], add)
        pass_on(j, True, pair)
        pass_on(j, False, pair)
        if at_order == 1:
            for step in range(2, count):
                line_step(step, head)
    for i in range(4):

        def keep(at, i=i):
            sums[i][at, :] = held[i][0][f, at, :]

        rows(sums[i].shape[0], keep)
    for up, there in ((True, lower), (False, upper)):

        @pl.when(there)
        def _(up=up):
            arrive(hop(f, up, range(4)))
            for i in range(4):
                incoming = held[i][5 if up else 7]

                def add(at, i=i, incoming=incoming):
                    sums[i][at, :] = sums[i][at, :] + incoming[f, at, :].astype(F32)

                rows(sums[i].shape[0], add)

    for bits in range(1, 8):
        wide(bits).wait_recv()
    for place, j, shard in parcel.unit_pieces():
        for first, ref in ((0, gate_sum), (padded, up_sum)):
            piece = wide_all[place, :, first + j * units : first + (j + 1) * units]
            ref[:, shard * units : (shard + 1) * units] = piece.astype(F32)

    for d in range(count):
        pl.when(f < d)(lambda: gone(hop(d, True, range(4))))
        pl.when(f > d)(lambda: gone(hop(d, False, range(4))))
    for n in range(4):
        for j in range(count):
            for copy in near(n, j):
                copy.wait_send()
    for n in range(3):
        for j in range(count):
            gone(far(n, j))
    for bits in range(1, 8):
        wide(bits).wait_send()
    swap.wait_send()


def end(parcel, down, kv, small, wide, head, units, padded, name):
    vmem = pl.BlockSpec(memory_space=pltpu.VMEM)
    dma = pltpu.SemaphoreType.DMA
    count = parcel.count
    bodies = (
        (count, parcel.lines, 128),
        (count, parcel.kv_rows, kv.shape[1]),
        (count, *small.shape[2:]),
    )
    scratch = []
    for body in bodies:
        low = pltpu.VMEM(body, BF16)
        three = pltpu.VMEM((3, *body), BF16)
        scratch += [pltpu.VMEM(body, F32), pltpu.VMEM((4, *body), BF16), three, three, low, low, low, low]
    lines = (count, parcel.rank_rows, 2 * head.shape[1] // count)
    every = 8 * count * units
    return pl.pallas_call(
        functools.partial(end_kernel, parcel, units, padded),
        out_shape=[
            *[jax.ShapeDtypeStruct(body[1:], F32) for body in bodies],
            *[jax.ShapeDtypeStruct((wide.shape[1], every), F32)] * 2,
            jax.ShapeDtypeStruct(lines[1:], F32),
        ],
        in_specs=[vmem] * 5,
        out_specs=[vmem] * 6,
        scratch_shapes=[
            *scratch,
            pltpu.VMEM(lines, F32),
            *[pltpu.VMEM(lines, BF16)] * 4,
            pltpu.VMEM((parcel.rank_rows, head.shape[1]), BF16),
            pltpu.VMEM(wide.shape, BF16),
            dma((3, 4, count)), dma((3, 4, count)),
            dma((3, 3, count)), dma((3, 3, count)),
            dma((4, 2, count)), dma((4, 2, count)),
            dma((8,)), dma((8,)),
            dma, dma,
        ],
        compiler_params=pltpu.CompilerParams(
            collective_id=name, has_side_effects=True, vmem_limit_bytes=VMEM_MOST
        ),
        cost_estimate=pl.CostEstimate(flops=0, bytes_accessed=240 * 2**20, transcendentals=0),
    )(down, kv, small, wide, head)


def by_owner(array, axis, count, f_first):
    lead, size, tail = array.shape[:axis], array.shape[axis], array.shape[axis + 1 :]
    part = size // (8 * count)
    n = len(lead)
    rest = [*range(n), n + 4, *range(n + 5, n + 5 + len(tail))]
    if f_first:
        array = array.reshape(*lead, count, 2, 2, 2, part, *tail)
        array = array.transpose(n, n + 1, n + 2, n + 3, *rest)
    else:
        array = array.reshape(*lead, 2, 2, count, 2, part, *tail)
        array = array.transpose(n + 2, n, n + 1, n + 3, *rest)
    return array.reshape(count, 8, *lead, part, *tail)


def from_owner(array, axis, f_first):
    count, _, *body = array.shape
    lead, part, tail = body[:axis], body[axis], body[axis + 1 :]
    n = axis
    array = array.reshape(count, 2, 2, 2, *body)
    inner = (0, 1, 2, 3) if f_first else (1, 2, 0, 3)
    array = array.transpose(
        *range(4, 4 + n), *inner, 4 + n, *range(5 + n, 5 + n + len(tail))
    )
    return array.reshape(*lead, 8 * count * part, *tail)


def per_device(
    count,
    f_first,
    block_input,
    seq_lens,
    attn_gain,
    latent_down,
    latent_gain,
    latent_up,
    shared_kv,
    out_proj,
    mlp_gain,
    gate_weight,
    up_weight,
    down_weight,
    out_cotangent,
):
    tokens, width = block_input.shape
    rank = 2 * latent_down.shape[0]
    half_rank = latent_down.shape[0]
    units = down_weight.shape[0]
    mine = units * count
    padded = -(-mine // 256) * 256
    place = lax.axis_index("f")

    def rows_of(array):
        flat = array.reshape(-1)
        lines = -(-flat.shape[0] // 128)
        return jnp.pad(flat, (0, lines * 128 - flat.shape[0])).reshape(lines, 128)

    gain_high = latent_gain.astype(BF16)
    gain_low = (latent_gain - gain_high.astype(F32)).astype(BF16)
    gain_rows = attn_gain.shape[0]
    lat_lines = half_rank // 128
    small = jnp.concatenate(
        [
            rows_of(gain_high),
            rows_of(gain_low),
            rows_of(attn_gain.astype(BF16)),
            rows_of(mlp_gain.astype(BF16)),
            rows_of(seq_lens.astype(BF16)),
        ]
    )
    at_gain = 2 * lat_lines
    small = jnp.pad(small, ((0, -small.shape[0] % 16), (0, 0)))
    parcel = Parcel(count, f_first, half_rank, latent_down.shape[1], shared_kv.shape[0])
    down_full, kv_full, small, heads, out_full, ff_down, both, g_all = start(
        parcel,
        latent_down.reshape(-1, 128),
        shared_kv,
        small,
        latent_up,
        out_proj,
        down_weight,
        gate_weight,
        up_weight,
        out_cotangent,
        units,
        padded,
        0,
    )
    down_full = parcel.down_from(down_full)

    half = count // 2
    per_head = count // 4
    if per_head > 1:
        heads = heads[: 2 * half].reshape(2, 2, per_head, half_rank, -1).transpose(0, 1, 3, 2, 4)
        heads = heads.reshape(4, half_rank, HEAD_DIM)
    out_full = out_full.reshape(-1, width)

    both = lax.all_gather(both, "f", axis=0)
    both = from_owner(both, 0, f_first)
    ff_down = ff_down.reshape(mine, width)

    gain_lat = small[:2, 0, :lat_lines].astype(F32) + small[:2, 0, lat_lines:at_gain].astype(F32)
    gain_lat = gain_lat.reshape(rank)
    by_line = small.transpose(1, 0, 2, 3)
    gain_one = from_owner(by_line[:, :, at_gain, :gain_rows], 0, f_first).astype(F32)
    gain_two = from_owner(by_line[:, :, at_gain + 1, :gain_rows], 0, f_first).astype(F32)
    lengths = lax.dynamic_index_in_dim(small[:, :, at_gain + 2, :3], place, 1, keepdims=False)
    lengths = jnp.stack(
        [lax.dynamic_index_in_dim(lengths, in_plane() ^ as_place(i), 0, keepdims=False) for i in range(8)]
    ).astype(jnp.int32)

    inputs = block_input.astype(F32)
    rms_one = lax.rsqrt(jnp.mean(inputs * inputs, axis=-1, keepdims=True) + EPS)
    normed = (inputs * rms_one * gain_one).astype(BF16)
    latent = contract(normed, down_full, 1, 1)
    rms_lat = lax.rsqrt(jnp.mean(latent * latent, axis=-1, keepdims=True) + EPS)
    latent_n = (latent * rms_lat * gain_lat).astype(BF16)
    shared = jnp.dot(normed, kv_full, preferred_element_type=F32)
    position, begins = layout(lengths, tokens)
    cosine, sine = rope_tables(position.reshape(-1), HEAD_DIM)
    k_own = rotate(shared, cosine[:tokens], sine[:tokens]).astype(BF16)

    rows_all = plane_gather(jnp.concatenate([latent_n, k_own, shared.astype(BF16)], axis=1), 1)
    begins = begins.reshape(-1, 1)
    branch, q_rot, lse, attended = attention(rows_all, heads, out_full, cosine, sine, begins, 2)

    middle = inputs + branch
    rms_two = lax.rsqrt(jnp.mean(middle * middle, axis=-1, keepdims=True) + EPS)
    normed_two = (middle * rms_two * gain_two).astype(BF16)
    two_all, hidden, d_both, result, chip_sums = feed(normed_two, g_all, both, ff_down, padded, 3)
    down_grad = contract(hidden, g_all, 0, 0)[:mine].reshape(count, units, width).astype(BF16)
    d_both, down_grad, chip_sums = lax.optimization_barrier((d_both, down_grad, chip_sums))
    down_grad = lax.psum_scatter(down_grad, "f", scatter_dimension=0).astype(F32)
    d_two, both_grad, arrived = product_scatter(d_both, both, two_all, chip_sums, 4)
    farthest = lax.ppermute(chip_sums[2], ("x", "y"), DIAGONAL)
    both_grad = by_owner(both_grad, 0, count, f_first)
    both_grad = lax.psum_scatter(both_grad, "f", scatter_dimension=0)

    upstream = out_cotangent.astype(F32)
    gain_two_part = jnp.sum(d_two * middle * rms_two, axis=0)
    scaled_two = d_two * gain_two
    d_middle = (
        upstream
        + rms_two * scaled_two
        - middle * (rms_two**3) * jnp.mean(scaled_two * middle, axis=-1, keepdims=True)
    )

    d_branch, out_grad = branch_gather(d_middle.astype(BF16), attended, 5)
    back, d_queries, up_grad_part, out_grad = attention_back(
        d_branch, rows_all, heads, out_full, cosine, sine, begins, q_rot, lse, out_grad, count, 6
    )
    down_part, kv_part, input_grad, gain_lat_part, gain_one_part = own_back(
        back, latent, rms_lat, gain_lat[None], normed, down_full, kv_full, block_input, rms_one, gain_one[None], d_middle
    )
    gain_one_part = gain_one_part.reshape(width)
    out_grad = after(out_grad, both_grad, down_grad, gain_one_part)
    out_proj_grad = lax.psum_scatter(out_grad, "f", scatter_dimension=0).astype(F32)

    down_part = parcel.down_to(down_part)

    def gain_rows_of(part):
        part = by_owner(part.astype(BF16), 0, count, f_first).transpose(1, 0, 2)
        return jnp.pad(part, ((0, 0), (0, 0), (0, 128 - gain_rows)))[:, :, None]

    lat_rows = jnp.broadcast_to(
        gain_lat_part.astype(BF16).reshape(1, 2, 1, lat_lines, 128), (4, 2, count, lat_lines, 128)
    )
    small_part = jnp.concatenate(
        [
            lat_rows.reshape(8, count, lat_lines, 128),
            gain_rows_of(gain_one_part),
            gain_rows_of(gain_two_part),
        ],
        axis=2,
    )
    small_part = jnp.pad(small_part, ((0, 0), (0, 0), (0, -small_part.shape[2] % 16), (0, 0)))
    latent_down_grad, shared_kv_grad, small_sum, gate_grad, up_grad, latent_up_grad = end(
        parcel, down_part, kv_part, small_part, both_grad, up_grad_part, units, padded, 7
    )
    latent_down_grad = latent_down_grad.reshape(latent_down.shape)
    latent_gain_grad = small_sum[:lat_lines].reshape(half_rank)
    attn_gain_grad = small_sum[lat_lines, :gain_rows]
    mlp_gain_grad = small_sum[lat_lines + 1, :gain_rows]
    farthest = after(farthest, small_sum).astype(F32)
    block_output = (middle + result + arrived[0].astype(F32) + arrived[1].astype(F32) + farthest).astype(BF16)
    return (
        block_output,
        input_grad,
        attn_gain_grad,
        latent_down_grad,
        latent_gain_grad,
        latent_up_grad,
        shared_kv_grad,
        out_proj_grad,
        mlp_gain_grad,
        gate_grad,
        up_grad,
        down_grad,
    )


def solution(mesh):
    devices = mesh.devices
    split = devices.shape[0]
    count = split // 4
    f_first = split == HEADS
    if f_first:
        names, sizes = ("f", "x", "c", "y"), (count, 2, 2, 2)
    else:
        names, sizes = ("x", "c", "f", "y"), (2, 2, count, 2)
    fine = Mesh(devices.reshape(sizes), names)
    dp = names[:3]
    return jax.shard_map(
        functools.partial(per_device, count, f_first),
        mesh=fine,
        in_specs=(
            P(names, None),
            P(names, None),
            P(names),
            P("y", dp),
            P("y"),
            P("y", dp),
            P(names, None),
            P(names, None),
            P(names),
            P(names, None),
            P(names, None),
            P(names, None),
            P(names, None),
        ),
        out_specs=(
            P(names, None),
            P(names, None),
            P(names),
            P("y", dp),
            P("y"),
            P("y", dp),
            P(names, None),
            P(names, None),
            P(names),
            P(names, None),
            P(names, None),
            P(names, None),
        ),
        check_vma=False,
    )
```

```python
import functools
import math

import jax
import jax.numpy as jnp
from jax import lax
from jax.experimental import pallas as pl
from jax.experimental.pallas import tpu as pltpu
from jax.sharding import Mesh
from jax.sharding import PartitionSpec as P

HEADS = 16
HEAD_DIM = 256
EPS = 1e-06
NEGATIVE = -1e30
F32 = jnp.float32
BF16 = jnp.bfloat16


def contract(left, right, left_dim, right_dim):
    return lax.dot_general(
        left, right, (((left_dim,), (right_dim,)), ((), ())), preferred_element_type=F32
    )


def after(value, *first):
    return lax.optimization_barrier((value, *first))[0]


def layout(lengths, count):
    spots = jnp.arange(lengths.shape[-1], dtype=jnp.int32)
    ends = jnp.sum(jnp.where(spots[None, :] <= spots[:, None], lengths[..., None, :], 0), axis=-1)
    places = jnp.arange(count, dtype=jnp.int32)
    passed = places[:, None] >= ends[..., None, :]
    offset = jnp.sum(jnp.where(passed, lengths[..., None, :], 0), axis=-1)
    return (places - offset).astype(F32), offset


def rope_tables(position, width):
    half = width // 2
    steps = jnp.arange(half, dtype=F32)
    freqs = jnp.exp(steps * (-math.log(10000.0) / half))
    angles = position[..., None] * freqs
    return jnp.cos(angles), jnp.sin(angles)


def rotate(values, cosine, sine):
    half = values.shape[-1] // 2
    first, second = values[..., :half], values[..., half:]
    return jnp.concatenate(
        [first * cosine - second * sine, second * cosine + first * sine], axis=-1
    )


DIAGONAL = [(0, 3), (3, 0), (1, 2), (2, 1)]


X_BIT, Y_BIT, C_BIT = 4, 2, 1
BOTH = X_BIT | Y_BIT
VMEM_MOST = 60 * 2**20


def other(bits):
    flips = {"x": bits // 4, "y": bits // 2 % 2, "c": bits % 2}
    return {name: 1 - lax.axis_index(name) for name, flip in flips.items() if flip}


def greet(partners):
    barrier = pltpu.get_barrier_semaphore()
    for partner in partners:
        pl.semaphore_signal(barrier, inc=1, device_id=partner)
    pl.semaphore_wait(barrier, len(partners))


def send(source, target, send_sem, recv_sem, device):
    return pltpu.make_async_remote_copy(
        src_ref=source, dst_ref=target, send_sem=send_sem, recv_sem=recv_sem, device_id=device
    )


def begin(copies):
    for copy in copies:
        copy.start()


def arrive(copies):
    for copy in copies:
        copy.wait_recv()


def gone(copies):
    for copy in copies:
        copy.wait_send()


def gathering(chunks, in_ref, out_ref, send_sem, recv_sem):
    tokens = in_ref.shape[0]
    rows = tokens // chunks

    def to(slot, k, bits, source=None):
        target = out_ref.at[pl.ds(slot * tokens + k * rows, rows)]
        if source is None:
            source = in_ref.at[pl.ds(k * rows, rows)]
        else:
            source = out_ref.at[pl.ds(source * tokens + k * rows, rows)]
        return send(source, target, send_sem.at[slot, k], recv_sem.at[slot, k], other(bits))

    def own():
        for k in range(chunks):
            to(X_BIT, k, X_BIT).start()
            to(Y_BIT, k, Y_BIT).start()
        for k in range(chunks):
            to(C_BIT, k, C_BIT).start()

    def relay(first, last):
        for k in range(first, last):
            to(X_BIT, k, X_BIT).wait_recv()
            if k < chunks // 2:
                to(BOTH, k, Y_BIT, X_BIT).start()
            to(X_BIT | C_BIT, k, C_BIT, X_BIT).start()
            to(Y_BIT, k, Y_BIT).wait_recv()
            if k >= chunks // 2:
                to(BOTH, k, X_BIT, Y_BIT).start()
            to(Y_BIT | C_BIT, k, C_BIT, Y_BIT).start()

    def far():
        for k in range(chunks):
            to(BOTH, k, Y_BIT).wait_recv()
            to(BOTH | C_BIT, k, C_BIT, BOTH).start()

    def arrived(chip):
        for k in range(chunks):
            to(chip | C_BIT, k, C_BIT).wait_recv()

    def sent():
        for slot in range(1, 8):
            for k in range(chunks):
                to(slot, k, C_BIT).wait_send()

    return own, relay, far, arrived, sent


def gather_kernel(chunks, in_ref, out_ref, own_sem, send_sem, recv_sem):
    greet([other(C_BIT), other(X_BIT), other(Y_BIT)])
    copy = pltpu.make_async_copy(in_ref, out_ref.at[pl.ds(0, in_ref.shape[0])], own_sem)
    copy.start()
    own, relay, far, arrived, sent = gathering(chunks, in_ref, out_ref, send_sem, recv_sem)
    own()
    relay(0, chunks)
    far()
    copy.wait()
    for chip in (0, Y_BIT, X_BIT, BOTH):
        arrived(chip)
    sent()


def plane_gather(block, name, chunks=4):
    return pl.pallas_call(
        functools.partial(gather_kernel, chunks),
        out_shape=jax.ShapeDtypeStruct((8 * block.shape[0], block.shape[1]), block.dtype),
        in_specs=[pl.BlockSpec(memory_space=pl.ANY)],
        out_specs=pl.BlockSpec(memory_space=pl.ANY),
        scratch_shapes=[
            pltpu.SemaphoreType.DMA,
            pltpu.SemaphoreType.DMA((8, chunks)),
            pltpu.SemaphoreType.DMA((8, chunks)),
        ],
        compiler_params=pltpu.CompilerParams(collective_id=name, has_side_effects=True),
        cost_estimate=pl.CostEstimate(flops=0, bytes_accessed=160 * 2**20, transcendentals=0),
    )(block)


def row_loop(amount, do, size=32):
    @pl.loop(0, amount // size)
    def _(r):
        do(pl.ds(pl.multiple_of(r * size, size), size))


def scattering(
    out_ref, work_ref, near_ref, far_ref, near_send, near_recv, far_send, far_recv, produce,
    at_start=None, meanwhile=None, at_end=None,
):
    greet([other(C_BIT), other(X_BIT), other(Y_BIT)])
    tokens = out_ref.shape[0]
    half = tokens // 2
    low, high = pl.ds(0, half), pl.ds(half, half)

    def near(n):
        return send(
            work_ref.at[n, pl.ds(tokens, tokens)], near_ref.at[n], near_send.at[n], near_recv.at[n], other(C_BIT)
        )

    def hop(i):
        n, part, bits = (
            (0, low, X_BIT), (0, high, Y_BIT), (1, low, X_BIT), (2, high, Y_BIT), (1, high, X_BIT), (2, low, Y_BIT)
        )[i]
        return send(work_ref.at[n, part], far_ref.at[i], far_send.at[i], far_recv.at[i], other(bits))

    def chip_sum(n):
        near(n).wait_recv()

        def keep(at):
            total = work_ref[n, at, :].astype(F32) + near_ref[n, at, :].astype(F32)
            work_ref[n, at, :] = total.astype(BF16)

        row_loop(tokens, keep)

    if at_start is not None:
        at_start()

    @pl.loop(0, 4)
    def _(n):
        produce(3 - n, work_ref.at[n])
        near(n).start()

        @pl.when(n > 0)
        def _():
            chip_sum(n - 1)
            pl.when(n == 1)(lambda: begin([hop(0), hop(1)]))
            pl.when(n == 2)(lambda: hop(2).start())
            pl.when(n == 3)(lambda: hop(3).start())

    near(3).wait_recv()

    def give(at):
        out_ref[at, :] = work_ref[3, at, :].astype(F32) + near_ref[3, at, :].astype(F32)

    row_loop(tokens, give)
    for came, n, first, on in ((0, 2, 0, 5), (1, 1, half, 4)):
        hop(came).wait_recv()

        def add(at, came=came, n=n, first=first):
            here = pl.ds(pl.multiple_of(first + at.start, 32), 32)
            total = work_ref[n, here, :].astype(F32) + far_ref[came, at, :].astype(F32)
            work_ref[n, here, :] = total.astype(BF16)

        row_loop(half, add)
        hop(on).start()
    if meanwhile is not None:
        meanwhile()

    def last(came, first):
        for i in came:
            hop(i).wait_recv()

        def add(at):
            here = pl.ds(pl.multiple_of(first + at.start, 32), 32)
            value = out_ref[here, :]
            for i in came:
                value = value + far_ref[i, at, :].astype(F32)
            out_ref[here, :] = value

        row_loop(half, add)

    last((2, 5), 0)
    last((3, 4), half)
    gone([*[near(n) for n in range(4)], *[hop(i) for i in range(6)]])
    if at_end is not None:
        at_end()


class PairLoads:
    def __init__(self, pairs, sem):
        self.pairs, self.sem = pairs, sem
        self.rows = pairs[0][0].shape[0] // 4

    def copies(self, chip):
        rows = pl.ds(pl.multiple_of(chip * self.rows, self.rows), self.rows)
        return [
            pltpu.make_async_copy(source.at[rows], target.at[rows], self.sem.at[i, chip])
            for i, (source, target) in enumerate(self.pairs)
        ]

    def start(self):
        for chip in (3, 2, 1, 0):
            begin(self.copies(chip))

    def wait(self, chip):
        for copy in self.copies(chip):
            copy.wait()


def scatter_scratch(tokens, wide):
    dma = pltpu.SemaphoreType.DMA
    return [
        pltpu.VMEM((4, 2 * tokens, wide), BF16),
        pltpu.VMEM((4, tokens, wide), BF16),
        pltpu.VMEM((6, tokens // 2, wide), BF16),
        dma((4,)), dma((4,)),
        dma((6,)), dma((6,)),
    ]


def vmem_call(kernel, out_shape, stay, scratch, name, flops, *arrays):
    stay_in, stay_out = stay
    vmem, any_space = pl.BlockSpec(memory_space=pltpu.VMEM), pl.BlockSpec(memory_space=pl.ANY)
    return pl.pallas_call(
        kernel,
        out_shape=out_shape,
        in_specs=[vmem] * (len(arrays) - stay_in) + [any_space] * stay_in,
        out_specs=[vmem] * (len(out_shape) - stay_out) + [any_space] * stay_out,
        scratch_shapes=scratch,
        compiler_params=pltpu.CompilerParams(
            collective_id=name, has_side_effects=True, vmem_limit_bytes=VMEM_MOST
        ),
        cost_estimate=pl.CostEstimate(flops=flops, bytes_accessed=160 * 2**20, transcendentals=0),
    )(*arrays)


def turn(values, cosine, sine):
    half = values.shape[-1] // 2
    first, second = values[:, :half], values[:, half:]
    return jnp.concatenate([first * cosine - second * sine, second * cosine + first * sine], axis=1)


def masked_scores(queries, keys, begins):
    raw = contract(queries, keys, 1, 1) * HEAD_DIM**-0.5
    to = lax.broadcasted_iota(jnp.int32, raw.shape, 0)
    of = lax.broadcasted_iota(jnp.int32, raw.shape, 1)
    return jnp.where((of <= to) & (of >= begins), raw, NEGATIVE)


def halves(rank):
    half = rank // 2
    y = lax.axis_index("y")
    return (
        pl.ds(pl.multiple_of(y * half, half), half),
        pl.ds(pl.multiple_of(half - y * half, half), half),
    )


def attention_kernel(
    rank, head_ref, out_w_ref, cos_ref, sin_ref, begin_ref, rows_in,
    branch_ref, query_ref, lse_ref, att_ref, *rest,
):
    wide = out_w_ref.shape[1]
    tokens = branch_ref.shape[0]
    mine, theirs = halves(rank)
    *rest, rows_ref, load_sem = rest
    loads = PairLoads([(rows_in, rows_ref)], load_sem)
    loads.start()

    def produce(chip, target):
        loads.wait(chip)
        pair = pl.ds(pl.multiple_of(chip * 2 * tokens, 2 * tokens), 2 * tokens)
        queries = [
            contract(rows_ref[pair, mine], head_ref[h], 1, 0) + contract(rows_ref[pair, theirs], head_ref[2 + h], 1, 0)
            for h in range(2)
        ]
        for c in range(2):
            rows = pl.ds(pl.multiple_of((2 * chip + c) * tokens, tokens), tokens)
            keys = rows_ref[rows, rank : rank + HEAD_DIM]
            values = rows_ref[rows, rank + HEAD_DIM :]
            cosine, sine, begins = cos_ref[rows, :], sin_ref[rows, :], begin_ref[rows, :]
            for h in range(2):
                at = slice(h * HEAD_DIM, (h + 1) * HEAD_DIM)
                turned = turn(queries[h][c * tokens : (c + 1) * tokens], cosine, sine).astype(BF16)
                query_ref[rows, at] = turned
                scores = masked_scores(turned, keys, begins)
                peak = jnp.max(scores, axis=1, keepdims=True)
                lse = peak + jnp.log(jnp.sum(jnp.exp(scores - peak), axis=1, keepdims=True))
                lse_ref[rows, h : h + 1] = lse
                probs = jnp.exp(scores - lse).astype(BF16)
                att_ref[rows, at] = contract(probs, values, 1, 0).astype(BF16)

        @pl.loop(0, wide // 512)
        def _(i):
            at = pl.ds(pl.multiple_of(i * 512, 512), 512)
            target[:, at] = contract(att_ref[pair, :], out_w_ref[: 2 * HEAD_DIM, at], 1, 0).astype(BF16)

    scattering(branch_ref, *rest, produce)


def attention(rows, heads, out_w, cosine, sine, begins, name):
    tokens, rank = rows.shape[0] // 8, 2 * heads.shape[1]
    wide = out_w.shape[1]
    two = 2 * HEAD_DIM
    return vmem_call(
        functools.partial(attention_kernel, rank),
        [
            jax.ShapeDtypeStruct((tokens, wide), F32),
            jax.ShapeDtypeStruct((8 * tokens, two), BF16),
            jax.ShapeDtypeStruct((8 * tokens, 2), F32),
            jax.ShapeDtypeStruct((8 * tokens, two), BF16),
        ],
        (1, 0),
        [*scatter_scratch(tokens, wide), pltpu.VMEM(rows.shape, BF16), pltpu.SemaphoreType.DMA((1, 4))],
        name,
        16 * tokens * two * (wide + rank + 2 * tokens),
        heads, out_w, cosine, sine, begins, rows,
    )


def attention_back_kernel(
    rank, head_ref, out_w_ref, cos_ref, sin_ref, begin_ref, lse_ref, d_in, rows_in, query_in, give_ref,
    back_ref, dq_ref, grad_ref, got_ref, *rest,
):
    tokens = back_ref.shape[0]
    mine, theirs = halves(rank)
    scale = HEAD_DIM**-0.5
    *rest, d_ref, rows_ref, query_ref, load_sem, keep_sem, send_sem, recv_sem = rest
    loads = PairLoads([(d_in, d_ref), (rows_in, rows_ref), (query_in, query_ref)], load_sem)
    loads.start()

    def produce(chip, target):
        loads.wait(chip)
        pair = pl.ds(pl.multiple_of(chip * 2 * tokens, 2 * tokens), 2 * tokens)
        d_pair = contract(d_ref[pair, :], out_w_ref[: 2 * HEAD_DIM, :], 1, 1).astype(BF16)
        for c in range(2):
            rows = pl.ds(pl.multiple_of((2 * chip + c) * tokens, tokens), tokens)
            here = slice(c * tokens, (c + 1) * tokens)
            keys = rows_ref[rows, rank : rank + HEAD_DIM]
            values = rows_ref[rows, rank + HEAD_DIM :]
            cosine, sine, begins = cos_ref[rows, :], sin_ref[rows, :], begin_ref[rows, :]
            d_keys = d_values = None
            for h in range(2):
                at = slice(h * HEAD_DIM, (h + 1) * HEAD_DIM)
                queries, d_att = query_ref[rows, at], d_pair[here, at]
                probs = jnp.exp(masked_scores(queries, keys, begins) - lse_ref[rows, h : h + 1])
                d_probs = contract(d_att, values, 1, 1)
                inner = jnp.sum(probs * d_probs, axis=1, keepdims=True)
                d_scores = (probs * (d_probs - inner)).astype(BF16)
                d_query = contract(d_scores, keys, 1, 0) * scale
                dq_ref[rows, at] = turn(d_query, cosine, -sine).astype(BF16)
                d_k = contract(d_scores, queries, 0, 0)
                d_v = contract(probs.astype(BF16), d_att, 0, 0)
                d_keys = d_k if h == 0 else d_keys + d_k
                d_values = d_v if h == 0 else d_values + d_v
            shared = turn(d_keys * scale, cosine, -sine) + d_values
            target[here, rank:] = shared.astype(BF16)
        for first, part in ((0, mine), (2, theirs)):
            got = contract(dq_ref[pair, :HEAD_DIM], head_ref[first], 1, 1)
            got = got + contract(dq_ref[pair, HEAD_DIM:], head_ref[first + 1], 1, 1)
            target[:, part] = got.astype(BF16)

    y = lax.axis_index("y")
    half = got_ref.shape[0] // 2
    size = got_ref.shape[1]

    def grad_copies(s):
        rows = [pl.ds(pl.multiple_of((2 * s + which) * size, size), size) for which in (y, 1 - y)]
        target = got_ref.at[y * half + s]
        return (
            pltpu.make_async_copy(give_ref.at[rows[0]], target, keep_sem.at[s]),
            send(give_ref.at[rows[1]], target, send_sem.at[s], recv_sem.at[s], other(Y_BIT)),
        )

    def at_start():
        for s in range(half):
            begin(grad_copies(s))

    def at_end():
        for s in range(half):
            for copy in grad_copies(s):
                copy.wait()

    def meanwhile():
        @pl.loop(0, rank // 256)
        def _(i):
            at = pl.ds(pl.multiple_of(i * 256, 256), 256)
            grad_ref[at, :] = contract(rows_ref[:, at], dq_ref[...], 0, 0).astype(BF16)

    scattering(back_ref, *rest, produce, at_start, meanwhile, at_end)


def attention_back(d_rows, rows, heads, out_w, cosine, sine, begins, queries, lse, give, lines, name):
    tokens, rank = rows.shape[0] // 8, 2 * heads.shape[1]
    wide = out_w.shape[1]
    two = 2 * HEAD_DIM
    full = rank + HEAD_DIM
    return vmem_call(
        functools.partial(attention_back_kernel, rank),
        [
            jax.ShapeDtypeStruct((tokens, full), F32),
            jax.ShapeDtypeStruct((8 * tokens, two), BF16),
            jax.ShapeDtypeStruct((rank, two), BF16),
            jax.ShapeDtypeStruct((lines, give.shape[0] // lines, give.shape[1]), give.dtype),
        ],
        (4, 1),
        [
            *scatter_scratch(tokens, full),
            *[pltpu.VMEM(array.shape, BF16) for array in (d_rows, rows, queries)],
            pltpu.SemaphoreType.DMA((3, 4)),
            *[pltpu.SemaphoreType.DMA((lines // 2,))] * 3,
        ],
        name,
        16 * tokens * two * (wide + rank + 5 * tokens),
        heads, out_w, cosine, sine, begins, lse, d_rows, rows, queries, give,
    )


def feed_kernel(
    chunks, in_ref, g_ref, both_ref, down_ref, two_out, hidden_out, d_both_out, own_sum, chip_sums,
    two_ref, hidden_ref, d_both_ref, g_held, both_held, down_held, work_ref, near_ref, own_sem, load_sem, send_sem, recv_sem, near_send, near_recv, out_sem,
):
    step = 256
    tokens = in_ref.shape[0]
    padded = hidden_out.shape[1]
    units = down_ref.shape[0]
    loads = [
        pltpu.make_async_copy(both_ref, both_held, load_sem.at[0]),
        pltpu.make_async_copy(g_ref, g_held, load_sem.at[1]),
        pltpu.make_async_copy(down_ref, down_held.at[pl.ds(0, units)], load_sem.at[2]),
        pltpu.make_async_copy(in_ref, two_ref.at[pl.ds(0, tokens)], own_sem),
    ]
    begin(loads)
    greet([other(C_BIT), other(X_BIT), other(Y_BIT)])
    own, relay, far, arrived, sent = gathering(chunks, in_ref, two_ref, send_sem, recv_sem)
    own()
    if units < padded:
        down_held[units:, :] = jnp.zeros((padded - units, down_held.shape[1]), BF16)
    for copy in loads:
        copy.wait()

    def near(n):
        return send(
            work_ref.at[n, pl.ds(tokens, tokens)], near_ref.at[n], near_send.at[n], near_recv.at[n], other(C_BIT)
        )

    def chip_sum(n):
        near(n).wait_recv()

        def add(at):
            total = work_ref[n, at, :].astype(F32) + near_ref[n, at, :].astype(F32)
            if n:
                chip_sums[n - 1, at, :] = total.astype(BF16)
            else:
                own_sum[at, :] = total

        row_loop(tokens, add)

    def leave(chip):
        pair = pl.ds(chip * tokens, 2 * tokens)
        results = ((two_ref, two_out), (hidden_ref, hidden_out), (d_both_ref, d_both_out))
        return [
            pltpu.make_async_copy(held.at[pair], result.at[pair], out_sem.at[i, chip // 2])
            for i, (held, result) in enumerate(results)
        ]

    def outputs_of(chip):
        pair = pl.ds(chip * tokens, 2 * tokens)
        n = chip // 2

        @pl.loop(0, down_held.shape[1] // step)
        def _(i):
            at = pl.ds(pl.multiple_of(i * step, step), step)
            work_ref[n, :, at] = contract(hidden_ref[pair, :], down_held[:, at], 1, 0).astype(BF16)

        near(n).start()

    def units_of(chip):
        arrived(chip)
        pair = pl.ds(chip * tokens, 2 * tokens)

        @pl.loop(0, padded // step)
        def _(i):
            at = pl.ds(pl.multiple_of(i * step, step), step)
            up_at = pl.ds(pl.multiple_of(padded + i * step, step), step)
            gate = contract(two_ref[pair, :], both_held[:, at], 1, 0)
            upval = contract(two_ref[pair, :], both_held[:, up_at], 1, 0)
            d_hidden = contract(g_held[pair, :], down_held[at, :], 1, 1)
            sigma = 1.0 / (1.0 + jnp.exp(-gate))
            silu = gate * sigma
            hidden_ref[pair, at] = (silu * upval).astype(BF16)
            d_gate = d_hidden * upval * sigma * (1.0 + gate * (1.0 - sigma))
            d_both_ref[pair, at] = d_gate.astype(BF16)
            d_both_ref[pair, up_at] = (d_hidden * silu).astype(BF16)

        begin(leave(chip))

    units_of(0)
    outputs_of(0)
    chip_sum(0)
    relay(0, chunks)
    units_of(X_BIT)
    outputs_of(X_BIT)
    units_of(Y_BIT)
    far()
    outputs_of(Y_BIT)
    units_of(BOTH)
    outputs_of(BOTH)
    for n in (2, 1, 3):
        chip_sum(n)
    for chip in (0, Y_BIT, X_BIT, BOTH):
        for copy in leave(chip):
            copy.wait()
    sent()
    gone([near(n) for n in range(4)])


def feed(rows, g, both, down, padded, name, chunks=4):
    tokens, width = rows.shape
    any_space, vmem = pl.BlockSpec(memory_space=pl.ANY), pl.BlockSpec(memory_space=pltpu.VMEM)
    dma = pltpu.SemaphoreType.DMA
    return pl.pallas_call(
        functools.partial(feed_kernel, chunks),
        out_shape=[
            jax.ShapeDtypeStruct((8 * tokens, width), BF16),
            jax.ShapeDtypeStruct((8 * tokens, padded), BF16),
            jax.ShapeDtypeStruct((8 * tokens, 2 * padded), BF16),
            jax.ShapeDtypeStruct((tokens, width), F32),
            jax.ShapeDtypeStruct((3, tokens, width), BF16),
        ],
        in_specs=[any_space] * 4,
        out_specs=[any_space] * 3 + [vmem] * 2,
        scratch_shapes=[
            pltpu.VMEM((8 * tokens, width), BF16),
            pltpu.VMEM((8 * tokens, padded), BF16),
            pltpu.VMEM((8 * tokens, 2 * padded), BF16),
            pltpu.VMEM(g.shape, BF16),
            pltpu.VMEM(both.shape, BF16),
            pltpu.VMEM((padded, width), BF16),
            pltpu.VMEM((4, 2 * tokens, width), BF16),
            pltpu.VMEM((4, tokens, width), BF16),
            dma,
            dma((3,)),
            dma((8, chunks)), dma((8, chunks)),
            dma((4,)), dma((4,)),
            dma((3, 4)),
        ],
        compiler_params=pltpu.CompilerParams(
            collective_id=name, has_side_effects=True, vmem_limit_bytes=VMEM_MOST
        ),
        cost_estimate=pl.CostEstimate(
            flops=16 * tokens * 3 * width * padded, bytes_accessed=160 * 2**20, transcendentals=0
        ),
    )(rows, g, both, down)


def product_scatter_kernel(left_in, right_in, side_in, give_ref, out_ref, grad_ref, got_ref, *rest):
    tokens = out_ref.shape[0]
    step = 256
    *rest, left_ref, right_ref, side_ref, grad_held, load_sem, pair_sem, grad_sem, give_send, give_recv = rest
    right_load = pltpu.make_async_copy(right_in, right_ref, load_sem.at[0])
    side_load = pltpu.make_async_copy(side_in, side_ref, load_sem.at[1])
    loads = PairLoads([(left_in, left_ref)], pair_sem)
    right_load.start()
    loads.start()
    side_load.start()

    def produce(chip, target):
        loads.wait(chip)
        pair = pl.ds(pl.multiple_of(chip * 2 * tokens, 2 * tokens), 2 * tokens)

        @pl.loop(0, out_ref.shape[1] // step)
        def _(i):
            at = pl.ds(pl.multiple_of(i * step, step), step)
            target[:, at] = contract(left_ref[pair, :], right_ref[at, :], 1, 1).astype(BF16)

    copies = [
        send(give_ref.at[i], got_ref.at[i], give_send.at[i], give_recv.at[i], other(bits))
        for i, bits in enumerate((Y_BIT, X_BIT))
    ]

    def grad_out(i):
        at = pl.ds(pl.multiple_of(i * step, step), step)
        return pltpu.make_async_copy(grad_held.at[at], grad_ref.at[at], grad_sem.at[i])

    steps = grad_ref.shape[0] // step

    def at_start():
        begin(copies)
        right_load.wait()

    def meanwhile():
        side_load.wait()

        @pl.loop(0, steps)
        def _(i):
            at = pl.ds(pl.multiple_of(i * step, step), step)
            grad_held[at, :] = contract(side_ref[:, at], left_ref[...], 0, 0).astype(BF16)
            grad_out(i).start()

    def at_end():
        for copy in copies:
            copy.wait()
        for i in range(steps):
            grad_out(i).wait()

    scattering(out_ref, *rest, produce, at_start, meanwhile, at_end)


def product_scatter(left, right, side, give, name):
    tokens, wide = left.shape[0] // 8, right.shape[0]
    grad = (side.shape[1], left.shape[1])
    dma = pltpu.SemaphoreType.DMA
    return vmem_call(
        product_scatter_kernel,
        [
            jax.ShapeDtypeStruct((tokens, wide), F32),
            jax.ShapeDtypeStruct(grad, BF16),
            jax.ShapeDtypeStruct((2, *give.shape[1:]), BF16),
        ],
        (4, 2),
        [
            *scatter_scratch(tokens, wide),
            *[pltpu.VMEM(array.shape, BF16) for array in (left, right, side)],
            pltpu.VMEM(grad, BF16),
            dma((2,)),
            dma((1, 4)),
            dma((grad[0] // 256,)),
            dma((2,)), dma((2,)),
        ],
        name,
        32 * tokens * wide * left.shape[1],
        left, right, side, give,
    )


def branch_gather_kernel(
    chunks, in_ref, att_ref, out_ref, grad_ref, held_ref, total_ref, own_sem, out_sem, send_sem, recv_sem
):
    tokens = in_ref.shape[0]
    step = 512
    copy = pltpu.make_async_copy(in_ref, held_ref.at[pl.ds(0, tokens)], own_sem)
    copy.start()
    greet([other(C_BIT), other(X_BIT), other(Y_BIT)])
    own, relay, far, arrived, sent = gathering(chunks, in_ref, held_ref, send_sem, recv_sem)

    def leave(chip):
        pair = pl.ds(chip * tokens, 2 * tokens)
        return pltpu.make_async_copy(held_ref.at[pair], out_ref.at[pair], out_sem.at[chip // 2])

    def grad_of(chip):
        arrived(chip)
        leave(chip).start()
        pair = pl.ds(chip * tokens, 2 * tokens)

        @pl.loop(0, grad_ref.shape[1] // step)
        def _(i):
            at = pl.ds(pl.multiple_of(i * step, step), step)
            got = contract(att_ref[pair, :], held_ref[pair, at], 0, 0)
            if chip == 0:
                total_ref[:, at] = got
            elif chip == BOTH:
                grad_ref[:, at] = (total_ref[:, at] + got).astype(BF16)
            else:
                total_ref[:, at] = total_ref[:, at] + got

    own()
    copy.wait()
    grad_of(0)
    relay(0, chunks)
    grad_of(X_BIT)
    grad_of(Y_BIT)
    far()
    grad_of(BOTH)
    sent()
    for chip in (0, Y_BIT, X_BIT, BOTH):
        leave(chip).wait()


def branch_gather(rows, att, name, chunks=4):
    tokens, width = rows.shape
    any_space, vmem = pl.BlockSpec(memory_space=pl.ANY), pl.BlockSpec(memory_space=pltpu.VMEM)
    dma = pltpu.SemaphoreType.DMA
    return pl.pallas_call(
        functools.partial(branch_gather_kernel, chunks),
        out_shape=[
            jax.ShapeDtypeStruct((8 * tokens, width), BF16),
            jax.ShapeDtypeStruct((att.shape[1], width), BF16),
        ],
        in_specs=[any_space, vmem],
        out_specs=[any_space, vmem],
        scratch_shapes=[
            pltpu.VMEM((8 * tokens, width), BF16),
            pltpu.VMEM((att.shape[1], width), F32),
            dma,
            dma((4,)),
            dma((8, chunks)), dma((8, chunks)),
        ],
        compiler_params=pltpu.CompilerParams(
            collective_id=name, has_side_effects=True, vmem_limit_bytes=VMEM_MOST
        ),
        cost_estimate=pl.CostEstimate(
            flops=16 * tokens * width * att.shape[1], bytes_accessed=160 * 2**20, transcendentals=0
        ),
    )(rows, att)


def in_plane():
    return 4 * lax.axis_index("x") + 2 * lax.axis_index("c") + lax.axis_index("y")


class Parcel:
    def __init__(self, count, f_first, rank_rows, columns, kv_rows):
        self.count, self.f_first = count, f_first
        self.rank_rows, self.columns, self.kv_rows = rank_rows, columns, kv_rows
        self.windows = columns == 128
        self.lines = rank_rows * columns // 128

    def down_shape(self):
        if self.windows:
            return (2 * self.rank_rows, 4 * self.count * self.columns)
        return (8, self.count, self.lines, 128)

    def down_from(self, array):
        if self.windows:
            return array
        array = array.reshape(2, 2, 2, self.count, self.rank_rows, self.columns)
        array = array.transpose((2, 4, 3, 0, 1, 5) if self.f_first else (2, 4, 0, 1, 3, 5))
        return array.reshape(2 * self.rank_rows, -1)

    def down_to(self, array):
        if self.windows:
            return array
        inner = (self.count, 2, 2) if self.f_first else (2, 2, self.count)
        array = array.reshape(2, self.rank_rows, *inner, self.columns)
        array = array.transpose((3, 4, 0, 2, 1, 5) if self.f_first else (2, 3, 0, 4, 1, 5))
        return array.reshape(self.down_shape())

    def blocks(self, refs, place, j):
        down, kv, small = refs
        pair, y = place // 2, place % 2
        at = j * 4 + pair if self.f_first else pair * self.count + j
        if self.windows:
            down = down.at[
                pl.ds(pl.multiple_of(y * self.rank_rows, self.rank_rows), self.rank_rows),
                pl.ds(pl.multiple_of(at * self.columns, self.columns), self.columns),
            ]
        else:
            down = down.at[place, j]
        start_row = pl.multiple_of((2 * at + y) * self.kv_rows, self.kv_rows)
        return down, kv.at[pl.ds(start_row, self.kv_rows)], small.at[place, j]

    def unit_pieces(self):
        for shard in range(8 * self.count):
            if self.f_first:
                yield shard % 8, shard // 8, shard
            else:
                yield shard // (2 * self.count) * 2 + shard % 2, shard // 2 % self.count, shard


def greet_all(count):
    f = lax.axis_index("f")
    lower, upper = f > 0, f < count - 1
    barrier = pltpu.get_barrier_semaphore()
    for bits in range(1, 8):
        pl.semaphore_signal(barrier, inc=1, device_id=other(bits))
    pl.when(lower)(lambda: pl.semaphore_signal(barrier, inc=1, device_id={"f": f - 1}))
    pl.when(upper)(lambda: pl.semaphore_signal(barrier, inc=1, device_id={"f": f + 1}))
    pl.semaphore_wait(barrier, 7 + lower.astype(jnp.int32) + upper.astype(jnp.int32))
    return lower, upper


FAR_FIRST = (7, 6, 5, 4, 3, 2, 1)


def as_place(bits):
    return (bits & 4) + 2 * (bits & 1) + (bits >> 1 & 1)


def start_kernel(
    parcel, chunks, units, padded, down_ref, kv_ref, small_ref, head_ref, out_ref, ff_ref, gate_ref, up_ref, rows_ref,
    down_all, kv_all, small_all, head_all, out_all, ff_all, wide_all, rows_all,
    down_low, kv_low, head_low, out_low, ff_low, wide_ref,
    local_sem, line_send, line_recv, plane_send, plane_recv, wide_send, wide_recv, rows_send, rows_recv,
    head_send, head_recv, far_send, far_recv,
):
    count = parcel.count
    f, me = lax.axis_index("f"), in_plane()
    lower, upper = greet_all(count)
    own = (down_low, kv_low, small_ref)
    alls = (down_all, kv_all, small_all)
    down_low[...] = down_ref[...].astype(BF16)
    kv_low[...] = kv_ref[...].astype(BF16)
    head_low[...] = head_ref[...].astype(BF16)
    out_low[...] = out_ref[...].astype(BF16)
    ff_low[...] = ff_ref[...].astype(BF16)

    half = count // 2
    y = lax.axis_index("y")

    def head_blocks(j):
        kept = (j // half == y).astype(jnp.int32)
        spare = (1 - kept) * (2 * half + j % half)
        return (
            head_all.at[kept * (j % half) + spare],
            out_all.at[kept * (2 * (j % half) + y) + spare],
            ff_all.at[j],
        )

    def head_hop(j, up, sources, group):
        return [
            send(
                sources[i], head_blocks(j)[i], head_send.at[i, 0 if up else 1, j], head_recv.at[i, j],
                {"f": f + 1 if up else f - 1},
            )
            for i in group
        ]

    def across(slot, sources):
        targets = (head_all.at[half + slot], out_all.at[2 * slot + y])
        return [
            send(source, target, far_send.at[i, slot], far_recv.at[i, slot], other(Y_BIT))
            for i, (source, target) in enumerate(zip(sources, targets))
        ]

    heads, ff = (0, 1), (2,)

    def head_own(group):
        pl.when(upper)(lambda: begin(head_hop(f, True, own_heads, group)))
        pl.when(lower)(lambda: begin(head_hop(f, False, own_heads, group)))
        if group == heads:
            pl.when(f // half != y)(lambda: begin(across(f % half, own_heads)))

    def head_step(step, group):
        @pl.when(f - step >= 0)
        def _():
            j = f - step
            blocks = head_blocks(j)
            arrive(head_hop(j, True, blocks, group))
            pl.when(upper)(lambda: begin(head_hop(j, True, blocks, group)))
            if group == heads:
                pl.when(j // half != y)(lambda: begin(across(j % half, blocks)))

        @pl.when(f + step <= count - 1)
        def _():
            j = f + step
            blocks = head_blocks(j)
            arrive(head_hop(j, False, blocks, group))
            pl.when(lower)(lambda: begin(head_hop(j, False, blocks, group)))
            if group == heads:
                pl.when(j // half != y)(lambda: begin(across(j % half, blocks)))

    own_heads = (head_low, out_low, ff_low)

    def hop(j, up, sources):
        return [
            send(
                source, target, line_send.at[i, 0 if up else 1, j], line_recv.at[i, j],
                {"f": f + 1 if up else f - 1},
            )
            for i, (source, target) in enumerate(zip(sources, parcel.blocks(alls, me, j)))
        ]

    def spread(slot, bits, j, sources):
        targets = parcel.blocks(alls, me ^ as_place(bits) ^ as_place(slot), j)
        return [
            send(source, target, plane_send.at[i, slot, j], plane_recv.at[i, slot, j], other(bits))
            for i, (source, target) in enumerate(zip(sources, targets))
        ]

    def to_plane(j, sources):
        for bits in (X_BIT, Y_BIT, C_BIT):
            begin(spread(bits, bits, j, sources))

    def line_step(step):
        @pl.when(f - step >= 0)
        def _():
            j = f - step
            blocks = parcel.blocks(alls, me, j)
            arrive(hop(j, True, blocks))
            pl.when(upper)(lambda: begin(hop(j, True, blocks)))
            to_plane(j, blocks)

        @pl.when(f + step <= count - 1)
        def _():
            j = f + step
            blocks = parcel.blocks(alls, me, j)
            arrive(hop(j, False, blocks))
            pl.when(lower)(lambda: begin(hop(j, False, blocks)))
            to_plane(j, blocks)

    def relay(j):
        by_x, by_y = parcel.blocks(alls, me ^ as_place(X_BIT), j), parcel.blocks(alls, me ^ as_place(Y_BIT), j)
        arrive(spread(X_BIT, X_BIT, j, by_x))
        pl.when(j % 2 == 0)(lambda: begin(spread(BOTH, Y_BIT, j, by_x)))
        begin(spread(X_BIT | C_BIT, C_BIT, j, by_x))
        arrive(spread(Y_BIT, Y_BIT, j, by_y))
        pl.when(j % 2 == 1)(lambda: begin(spread(BOTH, X_BIT, j, by_y)))
        begin(spread(Y_BIT | C_BIT, C_BIT, j, by_y))

    def relay_far(j):
        by_both = parcel.blocks(alls, me ^ as_place(BOTH), j)
        arrive(spread(BOTH, Y_BIT, j, by_both))
        begin(spread(BOTH | C_BIT, C_BIT, j, by_both))

    def in_order(do):
        do(f)
        for step in range(1, count):
            pl.when(f - step >= 0)(lambda: do(f - step))
            pl.when(f + step <= count - 1)(lambda: do(f + step))

    def wide(bits):
        return send(wide_ref.at[me ^ as_place(bits)], wide_all.at[me], wide_send.at[bits], wide_recv.at[bits], other(bits))

    pl.when(upper)(lambda: begin(hop(f, True, own)))
    pl.when(lower)(lambda: begin(hop(f, False, own)))
    to_plane(f, own)
    rows_own, rows_relay, rows_far, rows_arrived, rows_sent = gathering(chunks, rows_ref, rows_all, rows_send, rows_recv)
    rows_own()
    head_own(heads)
    for place, j, shard in parcel.unit_pieces():
        for first, ref in ((0, gate_ref), (padded, up_ref)):
            piece = ref[:, shard * units : (shard + 1) * units].astype(BF16)
            wide_ref[place, :, first + j * units : first + (j + 1) * units] = piece
    for first in (count * units, padded + count * units):
        size = padded - count * units
        wide_ref[:, :, first : first + size] = jnp.zeros((8, wide_ref.shape[1], size), BF16)
    for bits in FAR_FIRST:
        wide(bits).start()
    locals_ = [
        pltpu.make_async_copy(source, target, local_sem.at[i])
        for i, (source, target) in enumerate(
            (
                *zip(own, parcel.blocks(alls, me, f)),
                *zip(own_heads, head_blocks(f)),
                (wide_ref.at[me], wide_all.at[me]),
                (rows_ref, rows_all.at[pl.ds(0, rows_ref.shape[0])]),
            )
        )
    ]
    begin(locals_)
    for step in range(1, count):
        line_step(step)
        if step < count - 1:
            head_step(step, heads)
    head_own(ff)
    rows_relay(0, chunks)
    in_order(relay)
    head_step(count - 1, heads)
    head_step(1, ff)
    in_order(relay_far)
    rows_far()
    for step in range(2, count):
        head_step(step, ff)
    for copy in locals_:
        copy.wait()
    for j in range(count):
        pl.when(upper & (f >= j))(lambda: gone(hop(j, True, own)))
        pl.when(lower & (f <= j))(lambda: gone(hop(j, False, own)))
        pl.when(upper & (f >= j))(lambda: gone(head_hop(j, True, own_heads, (0, 1, 2))))
        pl.when(lower & (f <= j))(lambda: gone(head_hop(j, False, own_heads, (0, 1, 2))))
    for slot in range(half):
        arrive(across(slot, own_heads))
        gone(across(slot, own_heads))
    for slot in range(1, 8):
        for j in range(count):
            for copy in spread(slot, slot, j, own):
                if slot & C_BIT:
                    copy.wait_recv()
                copy.wait_send()
    for bits in range(1, 8):
        wide(bits).wait_recv()
        wide(bits).wait_send()
    for chip in (0, Y_BIT, X_BIT, BOTH):
        rows_arrived(chip)
    rows_sent()


def start(parcel, down, kv, small, head, out, ff, gate, up, rows, units, padded, name, chunks=4):
    count = parcel.count
    any_space, vmem = pl.BlockSpec(memory_space=pl.ANY), pl.BlockSpec(memory_space=pltpu.VMEM)
    dma = pltpu.SemaphoreType.DMA
    wide = (8, gate.shape[0], 2 * padded)
    return pl.pallas_call(
        functools.partial(start_kernel, parcel, chunks, units, padded),
        out_shape=[
            jax.ShapeDtypeStruct(parcel.down_shape(), BF16),
            jax.ShapeDtypeStruct((8 * count * kv.shape[0], kv.shape[1]), BF16),
            jax.ShapeDtypeStruct((8, count, *small.shape), BF16),
            jax.ShapeDtypeStruct((3 * count // 2, *head.shape), BF16),
            jax.ShapeDtypeStruct((3 * count // 2, *out.shape), BF16),
            jax.ShapeDtypeStruct((count, *ff.shape), BF16),
            jax.ShapeDtypeStruct(wide, BF16),
            jax.ShapeDtypeStruct((8 * rows.shape[0], rows.shape[1]), BF16),
        ],
        in_specs=[vmem] * 8 + [any_space],
        out_specs=[any_space] * 8,
        scratch_shapes=[
            pltpu.VMEM(down.shape, BF16),
            pltpu.VMEM(kv.shape, BF16),
            pltpu.VMEM(head.shape, BF16),
            pltpu.VMEM(out.shape, BF16),
            pltpu.VMEM(ff.shape, BF16),
            pltpu.VMEM(wide, BF16),
            dma((8,)),
            dma((3, 2, count)), dma((3, count)),
            dma((3, 8, count)), dma((3, 8, count)),
            dma((8,)), dma((8,)),
            dma((8, chunks)), dma((8, chunks)),
            dma((3, 2, count)), dma((3, count)),
            dma((2, count // 2)), dma((2, count // 2)),
        ],
        compiler_params=pltpu.CompilerParams(
            collective_id=name, has_side_effects=True, vmem_limit_bytes=VMEM_MOST
        ),
        cost_estimate=pl.CostEstimate(flops=0, bytes_accessed=240 * 2**20, transcendentals=0),
    )(down, kv, small, head, out, ff, gate, up, rows)


def own_back_kernel(
    back_ref, latent_ref, rms_lat_ref, gain_lat_ref, normed_ref, down_ref, kv_ref, in_ref, rms_ref, gain_ref, d_mid_ref,
    down_part, kv_part, d_in_ref, lat_sum, gain_sum, d_normed,
):
    rank = latent_ref.shape[1]
    width = in_ref.shape[1]
    step = 512
    d_lat_n, d_shared = back_ref[:, :rank], back_ref[:, rank:].astype(BF16)
    latent, rms_lat = latent_ref[...], rms_lat_ref[...]
    lat_sum[...] = jnp.sum(d_lat_n * latent * rms_lat, axis=0, keepdims=True)
    scaled = d_lat_n * gain_lat_ref[...]
    inner = jnp.sum(scaled * latent, axis=1, keepdims=True)
    d_latent = (rms_lat * scaled - latent * (rms_lat * rms_lat * rms_lat) * inner / rank).astype(BF16)

    @pl.loop(0, width // step)
    def _(i):
        at = pl.ds(pl.multiple_of(i * step, step), step)
        down_part[:, at] = contract(d_latent, normed_ref[:, at], 0, 0).astype(BF16)
        kv_part[at, :] = contract(normed_ref[:, at], d_shared, 0, 0).astype(BF16)
        d_normed[:, at] = contract(d_shared, kv_ref[at, :], 1, 1) + contract(d_latent, down_ref[:, at], 1, 0)

    inputs, rms = in_ref[...].astype(F32), rms_ref[...]
    gain_sum[...] = jnp.sum(d_normed[...] * inputs * rms, axis=0, keepdims=True)
    mean = jnp.sum(d_normed[...] * gain_ref[...] * inputs, axis=1, keepdims=True) / width
    k = d_normed[...] * gain_ref[...]
    d_in_ref[...] = (d_mid_ref[...] + rms * k - inputs * (rms * rms * rms) * mean).astype(BF16)


def own_back(back, latent, rms_lat, gain_lat, normed, down, kv, inputs, rms, gain, d_middle):
    vmem = pl.BlockSpec(memory_space=pltpu.VMEM)
    tokens, width = inputs.shape
    rank = latent.shape[1]
    return pl.pallas_call(
        own_back_kernel,
        out_shape=[
            jax.ShapeDtypeStruct((rank, width), BF16),
            jax.ShapeDtypeStruct(kv.shape, BF16),
            jax.ShapeDtypeStruct((tokens, width), BF16),
            jax.ShapeDtypeStruct((1, rank), F32),
            jax.ShapeDtypeStruct((1, width), F32),
        ],
        in_specs=[vmem] * 11,
        out_specs=[vmem] * 5,
        scratch_shapes=[pltpu.VMEM((tokens, width), F32)],
        compiler_params=pltpu.CompilerParams(vmem_limit_bytes=VMEM_MOST),
        cost_estimate=pl.CostEstimate(
            flops=4 * tokens * width * (rank + kv.shape[1]), bytes_accessed=16 * 2**20, transcendentals=0
        ),
    )(back, latent, rms_lat, gain_lat, normed, down, kv, inputs, rms, gain, d_middle)


def end_kernel(
    parcel, units, padded, down_ref, kv_ref, small_ref, wide_ref, head_ref,
    down_sum, kv_sum, small_sum, gate_sum, up_sum, head_sum, *rest,
):
    count = parcel.count
    held = [rest[8 * i : 8 * i + 8] for i in range(3)]
    head_held = (rest[24], None, None, None, *rest[25:29])
    head_got = rest[29]
    held.append(head_held)
    wide_all, near_send, near_recv, chip_send, chip_recv, line_send, line_recv, wide_send, wide_recv = rest[30:39]
    far_send, far_recv = rest[39:]
    f, me = lax.axis_index("f"), in_plane()
    lower, upper = greet_all(count)
    parts = (down_ref, kv_ref, small_ref)
    sums = (down_sum, kv_sum, small_sum, head_sum)
    chips = (BOTH, X_BIT, Y_BIT, 0)

    def rows(amount, do):
        size = amount if amount % 256 else 256

        @pl.loop(0, amount // size)
        def _(r):
            do(pl.ds(pl.multiple_of(r * size, size), size))

    def near(n, j):
        sources = parcel.blocks(parts, me ^ as_place(chips[n] | C_BIT), j)
        return [
            send(source, held[i][1].at[n, j], near_send.at[i, n, j], near_recv.at[i, n, j], other(C_BIT))
            for i, source in enumerate(sources)
        ]

    def far(step, j):
        by_x = (step != 2) == (j % 2 == 0)
        n = 0 if step == 0 else (1 if by_x else 2)
        slot = (2, 0, 1)[step]
        return [
            send(
                held[i][2].at[n, j], held[i][3].at[slot, j], chip_send.at[i, step, j], chip_recv.at[i, step, j],
                other(X_BIT if by_x else Y_BIT),
            )
            for i in range(3)
        ]

    order = []
    for j in range(count // 2):
        order += [count - 1 - j, j]

    def wide(bits):
        return send(wide_ref.at[me ^ as_place(bits)], wide_all.at[me], wide_send.at[bits], wide_recv.at[bits], other(bits))

    def hop(d, up, group):
        way = 0 if up else 1
        return [
            send(
                held[i][4 + 2 * way].at[d], held[i][5 + 2 * way].at[d],
                line_send.at[i, way, d], line_recv.at[i, way, d],
                {"f": f + 1 if up else f - 1},
            )
            for i in group
        ]

    def pass_on(d, up, group):
        way = 0 if up else 1
        behind = lower if up else upper

        @pl.when((d > f) if up else (d < f))
        def _():
            @pl.when(behind)
            def _():
                arrive(hop(d, up, group))
                for total, outgoing, incoming in ((held[i][0], held[i][4 + 2 * way], held[i][5 + 2 * way]) for i in group):

                    def add(at, total=total, outgoing=outgoing, incoming=incoming):
                        outgoing[d, at, :] = (total[d, at, :] + incoming[d, at, :].astype(F32)).astype(BF16)

                    rows(total.shape[1], add)

            @pl.when(jnp.logical_not(behind))
            def _():
                for total, outgoing in ((held[i][0], held[i][4 + 2 * way]) for i in group):

                    def keep(at, total=total, outgoing=outgoing):
                        outgoing[d, at, :] = total[d, at, :].astype(BF16)

                    rows(total.shape[1], keep)

            begin(hop(d, up, group))

    def line_step(step, group):
        pass_on(count - step, True, group)
        pass_on(step - 1, False, group)

    half = count // 2
    y = lax.axis_index("y")
    rank_rows, columns = head_got.shape[0], head_got.shape[1] // half

    def half_rows(which):
        return pl.ds(pl.multiple_of(which * rank_rows, rank_rows), rank_rows)

    swap = send(head_ref.at[half_rows(1 - y)], head_got, far_send, far_recv, other(Y_BIT))
    swap.start()
    for j in order:
        for n in range(4):
            begin(near(n, j))
    for j in order:
        for n in range(4):
            arrive(near(n, j))
            for i, source in enumerate(parcel.blocks(parts, me ^ as_place(chips[n]), j)):
                total, near_ref, chip_ref = held[i][:3]

                def add(at, n=n, j=j, source=source, total=total, near_ref=near_ref, chip_ref=chip_ref):
                    both = source[at, :].astype(F32) + near_ref[n, j, at, :].astype(F32)
                    if n < 3:
                        chip_ref[n, j, at, :] = both.astype(BF16)
                    else:
                        total[j, at, :] = both

                rows(total.shape[1], add)
            if n == 0:
                begin(far(0, j))
            if n == 2:
                begin(far(1, j))

    for j in order:
        arrive(far(0, j))
        n = 2 if j % 2 == 0 else 1
        for i in range(3):
            chip_ref, far_ref = held[i][2:4]

            def add(at, n=n, j=j, chip_ref=chip_ref, far_ref=far_ref):
                both = chip_ref[n, j, at, :].astype(F32) + far_ref[2, j, at, :].astype(F32)
                chip_ref[n, j, at, :] = both.astype(BF16)

            rows(chip_ref.shape[2], add)
        begin(far(2, j))

    for bits in FAR_FIRST:
        wide(bits).start()
    wide_all[me] = wide_ref[me]
    swap.wait_recv()
    for slot in range(half):
        at_columns = slice(slot * columns, (slot + 1) * columns)
        head_held[0][y * half + slot] = head_ref[half_rows(y), at_columns].astype(F32)
        head_held[0][(1 - y) * half + slot] = head_got[:, at_columns].astype(F32)
    pair, head = (0, 1, 2), (3,)
    line_step(1, head)
    for at_order, j in enumerate(order):
        arrive(far(1, j))
        arrive(far(2, j))
        for i in range(3):
            total, far_ref = held[i][0], held[i][3]

            def add(at, j=j, total=total, far_ref=far_ref):
                value = total[j, at, :]
                for n in range(2):
                    value = value + far_ref[n, j, at, :].astype(F32)
                total[j, at, :] = value

            rows(total.shape[1], add)
        pass_on(j, True, pair)
        pass_on(j, False, pair)
        if at_order == 1:
            for step in range(2, count):
                line_step(step, head)
    for i in range(4):

        def keep(at, i=i):
            sums[i][at, :] = held[i][0][f, at, :]

        rows(sums[i].shape[0], keep)
    for up, there in ((True, lower), (False, upper)):

        @pl.when(there)
        def _(up=up):
            arrive(hop(f, up, range(4)))
            for i in range(4):
                incoming = held[i][5 if up else 7]

                def add(at, i=i, incoming=incoming):
                    sums[i][at, :] = sums[i][at, :] + incoming[f, at, :].astype(F32)

                rows(sums[i].shape[0], add)

    for bits in range(1, 8):
        wide(bits).wait_recv()
    for place, j, shard in parcel.unit_pieces():
        for first, ref in ((0, gate_sum), (padded, up_sum)):
            piece = wide_all[place, :, first + j * units : first + (j + 1) * units]
            ref[:, shard * units : (shard + 1) * units] = piece.astype(F32)

    for d in range(count):
        pl.when(f < d)(lambda: gone(hop(d, True, range(4))))
        pl.when(f > d)(lambda: gone(hop(d, False, range(4))))
    for n in range(4):
        for j in range(count):
            for copy in near(n, j):
                copy.wait_send()
    for n in range(3):
        for j in range(count):
            gone(far(n, j))
    for bits in range(1, 8):
        wide(bits).wait_send()
    swap.wait_send()


def end(parcel, down, kv, small, wide, head, units, padded, name):
    vmem = pl.BlockSpec(memory_space=pltpu.VMEM)
    dma = pltpu.SemaphoreType.DMA
    count = parcel.count
    bodies = (
        (count, parcel.lines, 128),
        (count, parcel.kv_rows, kv.shape[1]),
        (count, *small.shape[2:]),
    )
    scratch = []
    for body in bodies:
        low = pltpu.VMEM(body, BF16)
        three = pltpu.VMEM((3, *body), BF16)
        scratch += [pltpu.VMEM(body, F32), pltpu.VMEM((4, *body), BF16), three, three, low, low, low, low]
    lines = (count, parcel.rank_rows, 2 * head.shape[1] // count)
    every = 8 * count * units
    return pl.pallas_call(
        functools.partial(end_kernel, parcel, units, padded),
        out_shape=[
            *[jax.ShapeDtypeStruct(body[1:], F32) for body in bodies],
            *[jax.ShapeDtypeStruct((wide.shape[1], every), F32)] * 2,
            jax.ShapeDtypeStruct(lines[1:], F32),
        ],
        in_specs=[vmem] * 5,
        out_specs=[vmem] * 6,
        scratch_shapes=[
            *scratch,
            pltpu.VMEM(lines, F32),
            *[pltpu.VMEM(lines, BF16)] * 4,
            pltpu.VMEM((parcel.rank_rows, head.shape[1]), BF16),
            pltpu.VMEM(wide.shape, BF16),
            dma((3, 4, count)), dma((3, 4, count)),
            dma((3, 3, count)), dma((3, 3, count)),
            dma((4, 2, count)), dma((4, 2, count)),
            dma((8,)), dma((8,)),
            dma, dma,
        ],
        compiler_params=pltpu.CompilerParams(
            collective_id=name, has_side_effects=True, vmem_limit_bytes=VMEM_MOST
        ),
        cost_estimate=pl.CostEstimate(flops=0, bytes_accessed=240 * 2**20, transcendentals=0),
    )(down, kv, small, wide, head)


def by_owner(array, axis, count, f_first):
    lead, size, tail = array.shape[:axis], array.shape[axis], array.shape[axis + 1 :]
    part = size // (8 * count)
    n = len(lead)
    rest = [*range(n), n + 4, *range(n + 5, n + 5 + len(tail))]
    if f_first:
        array = array.reshape(*lead, count, 2, 2, 2, part, *tail)
        array = array.transpose(n, n + 1, n + 2, n + 3, *rest)
    else:
        array = array.reshape(*lead, 2, 2, count, 2, part, *tail)
        array = array.transpose(n + 2, n, n + 1, n + 3, *rest)
    return array.reshape(count, 8, *lead, part, *tail)


def from_owner(array, axis, f_first):
    count, _, *body = array.shape
    lead, part, tail = body[:axis], body[axis], body[axis + 1 :]
    n = axis
    array = array.reshape(count, 2, 2, 2, *body)
    inner = (0, 1, 2, 3) if f_first else (1, 2, 0, 3)
    array = array.transpose(
        *range(4, 4 + n), *inner, 4 + n, *range(5 + n, 5 + n + len(tail))
    )
    return array.reshape(*lead, 8 * count * part, *tail)


def per_device(
    count,
    f_first,
    block_input,
    seq_lens,
    attn_gain,
    latent_down,
    latent_gain,
    latent_up,
    shared_kv,
    out_proj,
    mlp_gain,
    gate_weight,
    up_weight,
    down_weight,
    out_cotangent,
):
    tokens, width = block_input.shape
    rank = 2 * latent_down.shape[0]
    half_rank = latent_down.shape[0]
    units = down_weight.shape[0]
    mine = units * count
    padded = -(-mine // 256) * 256
    place = lax.axis_index("f")

    def rows_of(array):
        flat = array.reshape(-1)
        lines = -(-flat.shape[0] // 128)
        return jnp.pad(flat, (0, lines * 128 - flat.shape[0])).reshape(lines, 128)

    gain_high = latent_gain.astype(BF16)
    gain_low = (latent_gain - gain_high.astype(F32)).astype(BF16)
    gain_rows = attn_gain.shape[0]
    lat_lines = half_rank // 128
    small = jnp.concatenate(
        [
            rows_of(gain_high),
            rows_of(gain_low),
            rows_of(attn_gain.astype(BF16)),
            rows_of(mlp_gain.astype(BF16)),
            rows_of(seq_lens.astype(BF16)),
        ]
    )
    at_gain = 2 * lat_lines
    small = jnp.pad(small, ((0, -small.shape[0] % 16), (0, 0)))
    parcel = Parcel(count, f_first, half_rank, latent_down.shape[1], shared_kv.shape[0])
    down_full, kv_full, small, heads, out_full, ff_down, both, g_all = start(
        parcel,
        latent_down.reshape(-1, 128),
        shared_kv,
        small,
        latent_up,
        out_proj,
        down_weight,
        gate_weight,
        up_weight,
        out_cotangent,
        units,
        padded,
        0,
    )
    down_full = parcel.down_from(down_full)

    half = count // 2
    per_head = count // 4
    if per_head > 1:
        heads = heads[: 2 * half].reshape(2, 2, per_head, half_rank, -1).transpose(0, 1, 3, 2, 4)
        heads = heads.reshape(4, half_rank, HEAD_DIM)
    out_full = out_full.reshape(-1, width)

    both = lax.all_gather(both, "f", axis=0)
    both = from_owner(both, 0, f_first)
    ff_down = ff_down.reshape(mine, width)

    gain_lat = small[:2, 0, :lat_lines].astype(F32) + small[:2, 0, lat_lines:at_gain].astype(F32)
    gain_lat = gain_lat.reshape(rank)
    by_line = small.transpose(1, 0, 2, 3)
    gain_one = from_owner(by_line[:, :, at_gain, :gain_rows], 0, f_first).astype(F32)
    gain_two = from_owner(by_line[:, :, at_gain + 1, :gain_rows], 0, f_first).astype(F32)
    lengths = lax.dynamic_index_in_dim(small[:, :, at_gain + 2, :3], place, 1, keepdims=False)
    lengths = jnp.stack(
        [lax.dynamic_index_in_dim(lengths, in_plane() ^ as_place(i), 0, keepdims=False) for i in range(8)]
    ).astype(jnp.int32)

    inputs = block_input.astype(F32)
    rms_one = lax.rsqrt(jnp.mean(inputs * inputs, axis=-1, keepdims=True) + EPS)
    normed = (inputs * rms_one * gain_one).astype(BF16)
    latent = contract(normed, down_full, 1, 1)
    rms_lat = lax.rsqrt(jnp.mean(latent * latent, axis=-1, keepdims=True) + EPS)
    latent_n = (latent * rms_lat * gain_lat).astype(BF16)
    shared = jnp.dot(normed, kv_full, preferred_element_type=F32)
    position, begins = layout(lengths, tokens)
    cosine, sine = rope_tables(position.reshape(-1), HEAD_DIM)
    k_own = rotate(shared, cosine[:tokens], sine[:tokens]).astype(BF16)

    rows_all = plane_gather(jnp.concatenate([latent_n, k_own, shared.astype(BF16)], axis=1), 1)
    begins = begins.reshape(-1, 1)
    branch, q_rot, lse, attended = attention(rows_all, heads, out_full, cosine, sine, begins, 2)

    middle = inputs + branch
    rms_two = lax.rsqrt(jnp.mean(middle * middle, axis=-1, keepdims=True) + EPS)
    normed_two = (middle * rms_two * gain_two).astype(BF16)
    two_all, hidden, d_both, result, chip_sums = feed(normed_two, g_all, both, ff_down, padded, 3)
    down_grad = contract(hidden, g_all, 0, 0)[:mine].reshape(count, units, width).astype(BF16)
    d_both, down_grad, chip_sums = lax.optimization_barrier((d_both, down_grad, chip_sums))
    down_grad = lax.psum_scatter(down_grad, "f", scatter_dimension=0).astype(F32)
    d_two, both_grad, arrived = product_scatter(d_both, both, two_all, chip_sums, 4)
    farthest = lax.ppermute(chip_sums[2], ("x", "y"), DIAGONAL)
    both_grad = by_owner(both_grad, 0, count, f_first)
    both_grad = lax.psum_scatter(both_grad, "f", scatter_dimension=0)

    upstream = out_cotangent.astype(F32)
    gain_two_part = jnp.sum(d_two * middle * rms_two, axis=0)
    scaled_two = d_two * gain_two
    d_middle = (
        upstream
        + rms_two * scaled_two
        - middle * (rms_two**3) * jnp.mean(scaled_two * middle, axis=-1, keepdims=True)
    )

    d_branch, out_grad = branch_gather(d_middle.astype(BF16), attended, 5)
    back, d_queries, up_grad_part, out_grad = attention_back(
        d_branch, rows_all, heads, out_full, cosine, sine, begins, q_rot, lse, out_grad, count, 6
    )
    down_part, kv_part, input_grad, gain_lat_part, gain_one_part = own_back(
        back, latent, rms_lat, gain_lat[None], normed, down_full, kv_full, block_input, rms_one, gain_one[None], d_middle
    )
    gain_one_part = gain_one_part.reshape(width)
    out_grad = after(out_grad, both_grad, down_grad, gain_one_part)
    out_proj_grad = lax.psum_scatter(out_grad, "f", scatter_dimension=0).astype(F32)

    down_part = parcel.down_to(down_part)

    def gain_rows_of(part):
        part = by_owner(part.astype(BF16), 0, count, f_first).transpose(1, 0, 2)
        return jnp.pad(part, ((0, 0), (0, 0), (0, 128 - gain_rows)))[:, :, None]

    lat_rows = jnp.broadcast_to(
        gain_lat_part.astype(BF16).reshape(1, 2, 1, lat_lines, 128), (4, 2, count, lat_lines, 128)
    )
    small_part = jnp.concatenate(
        [
            lat_rows.reshape(8, count, lat_lines, 128),
            gain_rows_of(gain_one_part),
            gain_rows_of(gain_two_part),
        ],
        axis=2,
    )
    small_part = jnp.pad(small_part, ((0, 0), (0, 0), (0, -small_part.shape[2] % 16), (0, 0)))
    latent_down_grad, shared_kv_grad, small_sum, gate_grad, up_grad, latent_up_grad = end(
        parcel, down_part, kv_part, small_part, both_grad, up_grad_part, units, padded, 7
    )
    latent_down_grad = latent_down_grad.reshape(latent_down.shape)
    latent_gain_grad = small_sum[:lat_lines].reshape(half_rank)
    attn_gain_grad = small_sum[lat_lines, :gain_rows]
    mlp_gain_grad = small_sum[lat_lines + 1, :gain_rows]
    farthest = after(farthest, small_sum).astype(F32)
    block_output = (middle + result + arrived[0].astype(F32) + arrived[1].astype(F32) + farthest).astype(BF16)
    return (
        block_output,
        input_grad,
        attn_gain_grad,
        latent_down_grad,
        latent_gain_grad,
        latent_up_grad,
        shared_kv_grad,
        out_proj_grad,
        mlp_gain_grad,
        gate_grad,
        up_grad,
        down_grad,
    )


def solution(mesh):
    devices = mesh.devices
    split = devices.shape[0]
    count = split // 4
    f_first = split == HEADS
    if f_first:
        names, sizes = ("f", "x", "c", "y"), (count, 2, 2, 2)
    else:
        names, sizes = ("x", "c", "f", "y"), (2, 2, count, 2)
    fine = Mesh(devices.reshape(sizes), names)
    dp = names[:3]
    return jax.shard_map(
        functools.partial(per_device, count, f_first),
        mesh=fine,
        in_specs=(
            P(names, None),
            P(names, None),
            P(names),
            P("y", dp),
            P("y"),
            P("y", dp),
            P(names, None),
            P(names, None),
            P(names),
            P(names, None),
            P(names, None),
            P(names, None),
            P(names, None),
        ),
        out_specs=(
            P(names, None),
            P(names, None),
            P(names),
            P("y", dp),
            P("y"),
            P("y", dp),
            P(names, None),
            P(names, None),
            P(names),
            P(names, None),
            P(names, None),
            P(names, None),
        ),
        check_vma=False,
    )
```

```python
import functools
import math

import jax
import jax.numpy as jnp
from jax import lax
from jax.experimental import pallas as pl
from jax.experimental.pallas import tpu as pltpu
from jax.sharding import Mesh
from jax.sharding import PartitionSpec as P

HEADS = 16
HEAD_DIM = 256
EPS = 1e-06
NEGATIVE = -1e30
F32 = jnp.float32
BF16 = jnp.bfloat16


def contract(left, right, left_dim, right_dim):
    return lax.dot_general(
        left, right, (((left_dim,), (right_dim,)), ((), ())), preferred_element_type=F32
    )


def after(value, *first):
    return lax.optimization_barrier((value, *first))[0]


def layout(lengths, count):
    spots = jnp.arange(lengths.shape[-1], dtype=jnp.int32)
    ends = jnp.sum(jnp.where(spots[None, :] <= spots[:, None], lengths[..., None, :], 0), axis=-1)
    places = jnp.arange(count, dtype=jnp.int32)
    passed = places[:, None] >= ends[..., None, :]
    offset = jnp.sum(jnp.where(passed, lengths[..., None, :], 0), axis=-1)
    return (places - offset).astype(F32), offset


def rope_tables(position, width):
    half = width // 2
    steps = jnp.arange(half, dtype=F32)
    freqs = jnp.exp(steps * (-math.log(10000.0) / half))
    angles = position[..., None] * freqs
    return jnp.cos(angles), jnp.sin(angles)


def rotate(values, cosine, sine):
    half = values.shape[-1] // 2
    first, second = values[..., :half], values[..., half:]
    return jnp.concatenate(
        [first * cosine - second * sine, second * cosine + first * sine], axis=-1
    )


DIAGONAL = [(0, 3), (3, 0), (1, 2), (2, 1)]


X_BIT, Y_BIT, C_BIT = 4, 2, 1
BOTH = X_BIT | Y_BIT
VMEM_MOST = 60 * 2**20


def other(bits):
    flips = {"x": bits // 4, "y": bits // 2 % 2, "c": bits % 2}
    return {name: 1 - lax.axis_index(name) for name, flip in flips.items() if flip}


def greet(partners):
    barrier = pltpu.get_barrier_semaphore()
    for partner in partners:
        pl.semaphore_signal(barrier, inc=1, device_id=partner)
    pl.semaphore_wait(barrier, len(partners))


def send(source, target, send_sem, recv_sem, device):
    return pltpu.make_async_remote_copy(
        src_ref=source, dst_ref=target, send_sem=send_sem, recv_sem=recv_sem, device_id=device
    )


def begin(copies):
    for copy in copies:
        copy.start()


def arrive(copies):
    for copy in copies:
        copy.wait_recv()


def gone(copies):
    for copy in copies:
        copy.wait_send()


def gathering(chunks, in_ref, out_ref, send_sem, recv_sem):
    tokens = in_ref.shape[0]
    rows = tokens // chunks

    def to(slot, k, bits, source=None):
        target = out_ref.at[pl.ds(slot * tokens + k * rows, rows)]
        if source is None:
            source = in_ref.at[pl.ds(k * rows, rows)]
        else:
            source = out_ref.at[pl.ds(source * tokens + k * rows, rows)]
        return send(source, target, send_sem.at[slot, k], recv_sem.at[slot, k], other(bits))

    def own():
        for k in range(chunks):
            to(X_BIT, k, X_BIT).start()
            to(Y_BIT, k, Y_BIT).start()
        for k in range(chunks):
            to(C_BIT, k, C_BIT).start()

    def relay(first, last):
        for k in range(first, last):
            to(X_BIT, k, X_BIT).wait_recv()
            if k < chunks // 2:
                to(BOTH, k, Y_BIT, X_BIT).start()
            to(X_BIT | C_BIT, k, C_BIT, X_BIT).start()
            to(Y_BIT, k, Y_BIT).wait_recv()
            if k >= chunks // 2:
                to(BOTH, k, X_BIT, Y_BIT).start()
            to(Y_BIT | C_BIT, k, C_BIT, Y_BIT).start()

    def far():
        for k in range(chunks):
            to(BOTH, k, Y_BIT).wait_recv()
            to(BOTH | C_BIT, k, C_BIT, BOTH).start()

    def arrived(chip):
        for k in range(chunks):
            to(chip | C_BIT, k, C_BIT).wait_recv()

    def sent():
        for slot in range(1, 8):
            for k in range(chunks):
                to(slot, k, C_BIT).wait_send()

    return own, relay, far, arrived, sent


def gather_kernel(chunks, in_ref, out_ref, own_sem, send_sem, recv_sem):
    greet([other(C_BIT), other(X_BIT), other(Y_BIT)])
    copy = pltpu.make_async_copy(in_ref, out_ref.at[pl.ds(0, in_ref.shape[0])], own_sem)
    copy.start()
    own, relay, far, arrived, sent = gathering(chunks, in_ref, out_ref, send_sem, recv_sem)
    own()
    relay(0, chunks)
    far()
    copy.wait()
    for chip in (0, Y_BIT, X_BIT, BOTH):
        arrived(chip)
    sent()


def plane_gather(block, name, chunks=4):
    return pl.pallas_call(
        functools.partial(gather_kernel, chunks),
        out_shape=jax.ShapeDtypeStruct((8 * block.shape[0], block.shape[1]), block.dtype),
        in_specs=[pl.BlockSpec(memory_space=pl.ANY)],
        out_specs=pl.BlockSpec(memory_space=pl.ANY),
        scratch_shapes=[
            pltpu.SemaphoreType.DMA,
            pltpu.SemaphoreType.DMA((8, chunks)),
            pltpu.SemaphoreType.DMA((8, chunks)),
        ],
        compiler_params=pltpu.CompilerParams(collective_id=name, has_side_effects=True),
        cost_estimate=pl.CostEstimate(flops=0, bytes_accessed=160 * 2**20, transcendentals=0),
    )(block)


def row_loop(amount, do, size=32):
    @pl.loop(0, amount // size)
    def _(r):
        do(pl.ds(pl.multiple_of(r * size, size), size))


def scattering(
    out_ref, work_ref, near_ref, far_ref, near_send, near_recv, far_send, far_recv, produce,
    at_start=None, meanwhile=None, at_end=None,
):
    greet([other(C_BIT), other(X_BIT), other(Y_BIT)])
    tokens = out_ref.shape[0]
    half = tokens // 2
    low, high = pl.ds(0, half), pl.ds(half, half)

    def near(n):
        return send(
            work_ref.at[n, pl.ds(tokens, tokens)], near_ref.at[n], near_send.at[n], near_recv.at[n], other(C_BIT)
        )

    def hop(i):
        n, part, bits = (
            (0, low, X_BIT), (0, high, Y_BIT), (1, low, X_BIT), (2, high, Y_BIT), (1, high, X_BIT), (2, low, Y_BIT)
        )[i]
        return send(work_ref.at[n, part], far_ref.at[i], far_send.at[i], far_recv.at[i], other(bits))

    def chip_sum(n):
        near(n).wait_recv()

        def keep(at):
            total = work_ref[n, at, :].astype(F32) + near_ref[n, at, :].astype(F32)
            work_ref[n, at, :] = total.astype(BF16)

        row_loop(tokens, keep)

    if at_start is not None:
        at_start()

    @pl.loop(0, 4)
    def _(n):
        produce(3 - n, work_ref.at[n])
        near(n).start()

        @pl.when(n > 0)
        def _():
            chip_sum(n - 1)
            pl.when(n == 1)(lambda: begin([hop(0), hop(1)]))
            pl.when(n == 2)(lambda: hop(2).start())
            pl.when(n == 3)(lambda: hop(3).start())

    near(3).wait_recv()

    def give(at):
        out_ref[at, :] = work_ref[3, at, :].astype(F32) + near_ref[3, at, :].astype(F32)

    row_loop(tokens, give)
    for came, n, first, on in ((0, 2, 0, 5), (1, 1, half, 4)):
        hop(came).wait_recv()

        def add(at, came=came, n=n, first=first):
            here = pl.ds(pl.multiple_of(first + at.start, 32), 32)
            total = work_ref[n, here, :].astype(F32) + far_ref[came, at, :].astype(F32)
            work_ref[n, here, :] = total.astype(BF16)

        row_loop(half, add)
        hop(on).start()
    if meanwhile is not None:
        meanwhile()

    def last(came, first):
        for i in came:
            hop(i).wait_recv()

        def add(at):
            here = pl.ds(pl.multiple_of(first + at.start, 32), 32)
            value = out_ref[here, :]
            for i in came:
                value = value + far_ref[i, at, :].astype(F32)
            out_ref[here, :] = value

        row_loop(half, add)

    last((2, 5), 0)
    last((3, 4), half)
    gone([*[near(n) for n in range(4)], *[hop(i) for i in range(6)]])
    if at_end is not None:
        at_end()


class PairLoads:
    def __init__(self, pairs, sem):
        self.pairs, self.sem = pairs, sem
        self.rows = pairs[0][0].shape[0] // 4

    def copies(self, chip):
        rows = pl.ds(pl.multiple_of(chip * self.rows, self.rows), self.rows)
        return [
            pltpu.make_async_copy(source.at[rows], target.at[rows], self.sem.at[i, chip])
            for i, (source, target) in enumerate(self.pairs)
        ]

    def start(self):
        for chip in (3, 2, 1, 0):
            begin(self.copies(chip))

    def wait(self, chip):
        for copy in self.copies(chip):
            copy.wait()


def scatter_scratch(tokens, wide):
    dma = pltpu.SemaphoreType.DMA
    return [
        pltpu.VMEM((4, 2 * tokens, wide), BF16),
        pltpu.VMEM((4, tokens, wide), BF16),
        pltpu.VMEM((6, tokens // 2, wide), BF16),
        dma((4,)), dma((4,)),
        dma((6,)), dma((6,)),
    ]


def vmem_call(kernel, out_shape, stay, scratch, name, flops, *arrays):
    stay_in, stay_out = stay
    vmem, any_space = pl.BlockSpec(memory_space=pltpu.VMEM), pl.BlockSpec(memory_space=pl.ANY)
    return pl.pallas_call(
        kernel,
        out_shape=out_shape,
        in_specs=[vmem] * (len(arrays) - stay_in) + [any_space] * stay_in,
        out_specs=[vmem] * (len(out_shape) - stay_out) + [any_space] * stay_out,
        scratch_shapes=scratch,
        compiler_params=pltpu.CompilerParams(
            collective_id=name, has_side_effects=True, vmem_limit_bytes=VMEM_MOST
        ),
        cost_estimate=pl.CostEstimate(flops=flops, bytes_accessed=160 * 2**20, transcendentals=0),
    )(*arrays)


def turn(values, cosine, sine):
    half = values.shape[-1] // 2
    first, second = values[:, :half], values[:, half:]
    return jnp.concatenate([first * cosine - second * sine, second * cosine + first * sine], axis=1)


def masked_scores(queries, keys, begins):
    raw = contract(queries, keys, 1, 1) * HEAD_DIM**-0.5
    to = lax.broadcasted_iota(jnp.int32, raw.shape, 0)
    of = lax.broadcasted_iota(jnp.int32, raw.shape, 1)
    return jnp.where((of <= to) & (of >= begins), raw, NEGATIVE)


def halves(rank):
    half = rank // 2
    y = lax.axis_index("y")
    return (
        pl.ds(pl.multiple_of(y * half, half), half),
        pl.ds(pl.multiple_of(half - y * half, half), half),
    )


def attention_kernel(
    rank, head_ref, out_w_ref, cos_ref, sin_ref, begin_ref, rows_in,
    branch_ref, query_ref, lse_ref, att_ref, *rest,
):
    wide = out_w_ref.shape[1]
    tokens = branch_ref.shape[0]
    mine, theirs = halves(rank)
    *rest, rows_ref, load_sem = rest
    loads = PairLoads([(rows_in, rows_ref)], load_sem)
    loads.start()

    def produce(chip, target):
        loads.wait(chip)
        pair = pl.ds(pl.multiple_of(chip * 2 * tokens, 2 * tokens), 2 * tokens)
        queries = [
            contract(rows_ref[pair, mine], head_ref[h], 1, 0) + contract(rows_ref[pair, theirs], head_ref[2 + h], 1, 0)
            for h in range(2)
        ]
        for c in range(2):
            rows = pl.ds(pl.multiple_of((2 * chip + c) * tokens, tokens), tokens)
            keys = rows_ref[rows, rank : rank + HEAD_DIM]
            values = rows_ref[rows, rank + HEAD_DIM :]
            cosine, sine, begins = cos_ref[rows, :], sin_ref[rows, :], begin_ref[rows, :]
            for h in range(2):
                at = slice(h * HEAD_DIM, (h + 1) * HEAD_DIM)
                turned = turn(queries[h][c * tokens : (c + 1) * tokens], cosine, sine).astype(BF16)
                query_ref[rows, at] = turned
                scores = masked_scores(turned, keys, begins)
                peak = jnp.max(scores, axis=1, keepdims=True)
                lse = peak + jnp.log(jnp.sum(jnp.exp(scores - peak), axis=1, keepdims=True))
                lse_ref[rows, h : h + 1] = lse
                probs = jnp.exp(scores - lse).astype(BF16)
                att_ref[rows, at] = contract(probs, values, 1, 0).astype(BF16)

        @pl.loop(0, wide // 512)
        def _(i):
            at = pl.ds(pl.multiple_of(i * 512, 512), 512)
            target[:, at] = contract(att_ref[pair, :], out_w_ref[: 2 * HEAD_DIM, at], 1, 0).astype(BF16)

    scattering(branch_ref, *rest, produce)


def attention(rows, heads, out_w, cosine, sine, begins, name):
    tokens, rank = rows.shape[0] // 8, 2 * heads.shape[1]
    wide = out_w.shape[1]
    two = 2 * HEAD_DIM
    return vmem_call(
        functools.partial(attention_kernel, rank),
        [
            jax.ShapeDtypeStruct((tokens, wide), F32),
            jax.ShapeDtypeStruct((8 * tokens, two), BF16),
            jax.ShapeDtypeStruct((8 * tokens, 2), F32),
            jax.ShapeDtypeStruct((8 * tokens, two), BF16),
        ],
        (1, 0),
        [*scatter_scratch(tokens, wide), pltpu.VMEM(rows.shape, BF16), pltpu.SemaphoreType.DMA((1, 4))],
        name,
        16 * tokens * two * (wide + rank + 2 * tokens),
        heads, out_w, cosine, sine, begins, rows,
    )


def attention_back_kernel(
    rank, head_ref, out_w_ref, cos_ref, sin_ref, begin_ref, lse_ref, d_in, rows_in, query_in, give_ref,
    back_ref, dq_ref, grad_ref, got_ref, *rest,
):
    tokens = back_ref.shape[0]
    mine, theirs = halves(rank)
    scale = HEAD_DIM**-0.5
    *rest, d_ref, rows_ref, query_ref, load_sem, keep_sem, send_sem, recv_sem = rest
    loads = PairLoads([(d_in, d_ref), (rows_in, rows_ref), (query_in, query_ref)], load_sem)
    loads.start()

    def produce(chip, target):
        loads.wait(chip)
        pair = pl.ds(pl.multiple_of(chip * 2 * tokens, 2 * tokens), 2 * tokens)
        d_pair = contract(d_ref[pair, :], out_w_ref[: 2 * HEAD_DIM, :], 1, 1).astype(BF16)
        for c in range(2):
            rows = pl.ds(pl.multiple_of((2 * chip + c) * tokens, tokens), tokens)
            here = slice(c * tokens, (c + 1) * tokens)
            keys = rows_ref[rows, rank : rank + HEAD_DIM]
            values = rows_ref[rows, rank + HEAD_DIM :]
            cosine, sine, begins = cos_ref[rows, :], sin_ref[rows, :], begin_ref[rows, :]
            d_keys = d_values = None
            for h in range(2):
                at = slice(h * HEAD_DIM, (h + 1) * HEAD_DIM)
                queries, d_att = query_ref[rows, at], d_pair[here, at]
                probs = jnp.exp(masked_scores(queries, keys, begins) - lse_ref[rows, h : h + 1])
                d_probs = contract(d_att, values, 1, 1)
                inner = jnp.sum(probs * d_probs, axis=1, keepdims=True)
                d_scores = (probs * (d_probs - inner)).astype(BF16)
                d_query = contract(d_scores, keys, 1, 0) * scale
                dq_ref[rows, at] = turn(d_query, cosine, -sine).astype(BF16)
                d_k = contract(d_scores, queries, 0, 0)
                d_v = contract(probs.astype(BF16), d_att, 0, 0)
                d_keys = d_k if h == 0 else d_keys + d_k
                d_values = d_v if h == 0 else d_values + d_v
            shared = turn(d_keys * scale, cosine, -sine) + d_values
            target[here, rank:] = shared.astype(BF16)
        for first, part in ((0, mine), (2, theirs)):
            got = contract(dq_ref[pair, :HEAD_DIM], head_ref[first], 1, 1)
            got = got + contract(dq_ref[pair, HEAD_DIM:], head_ref[first + 1], 1, 1)
            target[:, part] = got.astype(BF16)

    y = lax.axis_index("y")
    half = got_ref.shape[0] // 2
    size = got_ref.shape[1]

    def grad_copies(s):
        rows = [pl.ds(pl.multiple_of((2 * s + which) * size, size), size) for which in (y, 1 - y)]
        target = got_ref.at[y * half + s]
        return (
            pltpu.make_async_copy(give_ref.at[rows[0]], target, keep_sem.at[s]),
            send(give_ref.at[rows[1]], target, send_sem.at[s], recv_sem.at[s], other(Y_BIT)),
        )

    def at_start():
        for s in range(half):
            begin(grad_copies(s))

    def at_end():
        for s in range(half):
            for copy in grad_copies(s):
                copy.wait()

    def meanwhile():
        @pl.loop(0, rank // 256)
        def _(i):
            at = pl.ds(pl.multiple_of(i * 256, 256), 256)
            grad_ref[at, :] = contract(rows_ref[:, at], dq_ref[...], 0, 0).astype(BF16)

    scattering(back_ref, *rest, produce, at_start, meanwhile, at_end)


def attention_back(d_rows, rows, heads, out_w, cosine, sine, begins, queries, lse, give, lines, name):
    tokens, rank = rows.shape[0] // 8, 2 * heads.shape[1]
    wide = out_w.shape[1]
    two = 2 * HEAD_DIM
    full = rank + HEAD_DIM
    return vmem_call(
        functools.partial(attention_back_kernel, rank),
        [
            jax.ShapeDtypeStruct((tokens, full), F32),
            jax.ShapeDtypeStruct((8 * tokens, two), BF16),
            jax.ShapeDtypeStruct((rank, two), BF16),
            jax.ShapeDtypeStruct((lines, give.shape[0] // lines, give.shape[1]), give.dtype),
        ],
        (4, 1),
        [
            *scatter_scratch(tokens, full),
            *[pltpu.VMEM(array.shape, BF16) for array in (d_rows, rows, queries)],
            pltpu.SemaphoreType.DMA((3, 4)),
            *[pltpu.SemaphoreType.DMA((lines // 2,))] * 3,
        ],
        name,
        16 * tokens * two * (wide + rank + 5 * tokens),
        heads, out_w, cosine, sine, begins, lse, d_rows, rows, queries, give,
    )


def feed_kernel(
    chunks, in_ref, g_ref, both_ref, down_ref, two_out, hidden_out, d_both_out, own_sum, chip_sums,
    two_ref, hidden_ref, d_both_ref, g_held, both_held, down_held, work_ref, near_ref, own_sem, load_sem, send_sem, recv_sem, near_send, near_recv, out_sem,
):
    step = 256
    tokens = in_ref.shape[0]
    padded = hidden_out.shape[1]
    units = down_ref.shape[0]
    loads = [
        pltpu.make_async_copy(both_ref, both_held, load_sem.at[0]),
        pltpu.make_async_copy(g_ref, g_held, load_sem.at[1]),
        pltpu.make_async_copy(down_ref, down_held.at[pl.ds(0, units)], load_sem.at[2]),
        pltpu.make_async_copy(in_ref, two_ref.at[pl.ds(0, tokens)], own_sem),
    ]
    begin(loads)
    greet([other(C_BIT), other(X_BIT), other(Y_BIT)])
    own, relay, far, arrived, sent = gathering(chunks, in_ref, two_ref, send_sem, recv_sem)
    own()
    if units < padded:
        down_held[units:, :] = jnp.zeros((padded - units, down_held.shape[1]), BF16)
    for copy in loads:
        copy.wait()

    def near(n):
        return send(
            work_ref.at[n, pl.ds(tokens, tokens)], near_ref.at[n], near_send.at[n], near_recv.at[n], other(C_BIT)
        )

    def chip_sum(n):
        near(n).wait_recv()

        def add(at):
            total = work_ref[n, at, :].astype(F32) + near_ref[n, at, :].astype(F32)
            if n:
                chip_sums[n - 1, at, :] = total.astype(BF16)
            else:
                own_sum[at, :] = total

        row_loop(tokens, add)

    def leave(chip):
        pair = pl.ds(chip * tokens, 2 * tokens)
        results = ((two_ref, two_out), (hidden_ref, hidden_out), (d_both_ref, d_both_out))
        return [
            pltpu.make_async_copy(held.at[pair], result.at[pair], out_sem.at[i, chip // 2])
            for i, (held, result) in enumerate(results)
        ]

    def outputs_of(chip):
        pair = pl.ds(chip * tokens, 2 * tokens)
        n = chip // 2

        @pl.loop(0, down_held.shape[1] // step)
        def _(i):
            at = pl.ds(pl.multiple_of(i * step, step), step)
            work_ref[n, :, at] = contract(hidden_ref[pair, :], down_held[:, at], 1, 0).astype(BF16)

        near(n).start()

    def units_of(chip):
        arrived(chip)
        pair = pl.ds(chip * tokens, 2 * tokens)

        @pl.loop(0, padded // step)
        def _(i):
            at = pl.ds(pl.multiple_of(i * step, step), step)
            up_at = pl.ds(pl.multiple_of(padded + i * step, step), step)
            gate = contract(two_ref[pair, :], both_held[:, at], 1, 0)
            upval = contract(two_ref[pair, :], both_held[:, up_at], 1, 0)
            d_hidden = contract(g_held[pair, :], down_held[at, :], 1, 1)
            sigma = 1.0 / (1.0 + jnp.exp(-gate))
            silu = gate * sigma
            hidden_ref[pair, at] = (silu * upval).astype(BF16)
            d_gate = d_hidden * upval * sigma * (1.0 + gate * (1.0 - sigma))
            d_both_ref[pair, at] = d_gate.astype(BF16)
            d_both_ref[pair, up_at] = (d_hidden * silu).astype(BF16)

        begin(leave(chip))

    units_of(0)
    outputs_of(0)
    chip_sum(0)
    relay(0, chunks)
    units_of(X_BIT)
    outputs_of(X_BIT)
    units_of(Y_BIT)
    far()
    outputs_of(Y_BIT)
    units_of(BOTH)
    outputs_of(BOTH)
    for n in (2, 1, 3):
        chip_sum(n)
    for chip in (0, Y_BIT, X_BIT, BOTH):
        for copy in leave(chip):
            copy.wait()
    sent()
    gone([near(n) for n in range(4)])


def feed(rows, g, both, down, padded, name, chunks=4):
    tokens, width = rows.shape
    any_space, vmem = pl.BlockSpec(memory_space=pl.ANY), pl.BlockSpec(memory_space=pltpu.VMEM)
    dma = pltpu.SemaphoreType.DMA
    return pl.pallas_call(
        functools.partial(feed_kernel, chunks),
        out_shape=[
            jax.ShapeDtypeStruct((8 * tokens, width), BF16),
            jax.ShapeDtypeStruct((8 * tokens, padded), BF16),
            jax.ShapeDtypeStruct((8 * tokens, 2 * padded), BF16),
            jax.ShapeDtypeStruct((tokens, width), F32),
            jax.ShapeDtypeStruct((3, tokens, width), BF16),
        ],
        in_specs=[any_space] * 4,
        out_specs=[any_space] * 3 + [vmem] * 2,
        scratch_shapes=[
            pltpu.VMEM((8 * tokens, width), BF16),
            pltpu.VMEM((8 * tokens, padded), BF16),
            pltpu.VMEM((8 * tokens, 2 * padded), BF16),
            pltpu.VMEM(g.shape, BF16),
            pltpu.VMEM(both.shape, BF16),
            pltpu.VMEM((padded, width), BF16),
            pltpu.VMEM((4, 2 * tokens, width), BF16),
            pltpu.VMEM((4, tokens, width), BF16),
            dma,
            dma((3,)),
            dma((8, chunks)), dma((8, chunks)),
            dma((4,)), dma((4,)),
            dma((3, 4)),
        ],
        compiler_params=pltpu.CompilerParams(
            collective_id=name, has_side_effects=True, vmem_limit_bytes=VMEM_MOST
        ),
        cost_estimate=pl.CostEstimate(
            flops=16 * tokens * 3 * width * padded, bytes_accessed=160 * 2**20, transcendentals=0
        ),
    )(rows, g, both, down)


def product_scatter_kernel(left_in, right_in, side_in, give_ref, out_ref, grad_ref, got_ref, *rest):
    tokens = out_ref.shape[0]
    step = 256
    *rest, left_ref, right_ref, side_ref, grad_held, load_sem, pair_sem, grad_sem, give_send, give_recv = rest
    right_load = pltpu.make_async_copy(right_in, right_ref, load_sem.at[0])
    side_load = pltpu.make_async_copy(side_in, side_ref, load_sem.at[1])
    loads = PairLoads([(left_in, left_ref)], pair_sem)
    right_load.start()
    loads.start()
    side_load.start()

    def produce(chip, target):
        loads.wait(chip)
        pair = pl.ds(pl.multiple_of(chip * 2 * tokens, 2 * tokens), 2 * tokens)

        @pl.loop(0, out_ref.shape[1] // step)
        def _(i):
            at = pl.ds(pl.multiple_of(i * step, step), step)
            target[:, at] = contract(left_ref[pair, :], right_ref[at, :], 1, 1).astype(BF16)

    copies = [
        send(give_ref.at[i], got_ref.at[i], give_send.at[i], give_recv.at[i], other(bits))
        for i, bits in enumerate((Y_BIT, X_BIT))
    ]

    def grad_out(i):
        at = pl.ds(pl.multiple_of(i * step, step), step)
        return pltpu.make_async_copy(grad_held.at[at], grad_ref.at[at], grad_sem.at[i])

    steps = grad_ref.shape[0] // step

    def at_start():
        begin(copies)
        right_load.wait()

    def meanwhile():
        side_load.wait()

        @pl.loop(0, steps)
        def _(i):
            at = pl.ds(pl.multiple_of(i * step, step), step)
            grad_held[at, :] = contract(side_ref[:, at], left_ref[...], 0, 0).astype(BF16)
            grad_out(i).start()

    def at_end():
        for copy in copies:
            copy.wait()
        for i in range(steps):
            grad_out(i).wait()

    scattering(out_ref, *rest, produce, at_start, meanwhile, at_end)


def product_scatter(left, right, side, give, name):
    tokens, wide = left.shape[0] // 8, right.shape[0]
    grad = (side.shape[1], left.shape[1])
    dma = pltpu.SemaphoreType.DMA
    return vmem_call(
        product_scatter_kernel,
        [
            jax.ShapeDtypeStruct((tokens, wide), F32),
            jax.ShapeDtypeStruct(grad, BF16),
            jax.ShapeDtypeStruct((2, *give.shape[1:]), BF16),
        ],
        (4, 2),
        [
            *scatter_scratch(tokens, wide),
            *[pltpu.VMEM(array.shape, BF16) for array in (left, right, side)],
            pltpu.VMEM(grad, BF16),
            dma((2,)),
            dma((1, 4)),
            dma((grad[0] // 256,)),
            dma((2,)), dma((2,)),
        ],
        name,
        32 * tokens * wide * left.shape[1],
        left, right, side, give,
    )


def branch_gather_kernel(
    chunks, in_ref, att_ref, out_ref, grad_ref, held_ref, total_ref, own_sem, out_sem, send_sem, recv_sem
):
    tokens = in_ref.shape[0]
    step = 512
    copy = pltpu.make_async_copy(in_ref, held_ref.at[pl.ds(0, tokens)], own_sem)
    copy.start()
    greet([other(C_BIT), other(X_BIT), other(Y_BIT)])
    own, relay, far, arrived, sent = gathering(chunks, in_ref, held_ref, send_sem, recv_sem)

    def leave(chip):
        pair = pl.ds(chip * tokens, 2 * tokens)
        return pltpu.make_async_copy(held_ref.at[pair], out_ref.at[pair], out_sem.at[chip // 2])

    def grad_of(chip):
        arrived(chip)
        leave(chip).start()
        pair = pl.ds(chip * tokens, 2 * tokens)

        @pl.loop(0, grad_ref.shape[1] // step)
        def _(i):
            at = pl.ds(pl.multiple_of(i * step, step), step)
            got = contract(att_ref[pair, :], held_ref[pair, at], 0, 0)
            if chip == 0:
                total_ref[:, at] = got
            elif chip == BOTH:
                grad_ref[:, at] = (total_ref[:, at] + got).astype(BF16)
            else:
                total_ref[:, at] = total_ref[:, at] + got

    own()
    copy.wait()
    grad_of(0)
    relay(0, chunks)
    grad_of(X_BIT)
    grad_of(Y_BIT)
    far()
    grad_of(BOTH)
    sent()
    for chip in (0, Y_BIT, X_BIT, BOTH):
        leave(chip).wait()


def branch_gather(rows, att, name, chunks=4):
    tokens, width = rows.shape
    any_space, vmem = pl.BlockSpec(memory_space=pl.ANY), pl.BlockSpec(memory_space=pltpu.VMEM)
    dma = pltpu.SemaphoreType.DMA
    return pl.pallas_call(
        functools.partial(branch_gather_kernel, chunks),
        out_shape=[
            jax.ShapeDtypeStruct((8 * tokens, width), BF16),
            jax.ShapeDtypeStruct((att.shape[1], width), BF16),
        ],
        in_specs=[any_space, vmem],
        out_specs=[any_space, vmem],
        scratch_shapes=[
            pltpu.VMEM((8 * tokens, width), BF16),
            pltpu.VMEM((att.shape[1], width), F32),
            dma,
            dma((4,)),
            dma((8, chunks)), dma((8, chunks)),
        ],
        compiler_params=pltpu.CompilerParams(
            collective_id=name, has_side_effects=True, vmem_limit_bytes=VMEM_MOST
        ),
        cost_estimate=pl.CostEstimate(
            flops=16 * tokens * width * att.shape[1], bytes_accessed=160 * 2**20, transcendentals=0
        ),
    )(rows, att)


def in_plane():
    return 4 * lax.axis_index("x") + 2 * lax.axis_index("c") + lax.axis_index("y")


class Parcel:
    def __init__(self, count, f_first, rank_rows, columns, kv_rows):
        self.count, self.f_first = count, f_first
        self.rank_rows, self.columns, self.kv_rows = rank_rows, columns, kv_rows
        self.windows = columns == 128
        self.lines = rank_rows * columns // 128

    def down_shape(self):
        if self.windows:
            return (2 * self.rank_rows, 4 * self.count * self.columns)
        return (8, self.count, self.lines, 128)

    def down_from(self, array):
        if self.windows:
            return array
        array = array.reshape(2, 2, 2, self.count, self.rank_rows, self.columns)
        array = array.transpose((2, 4, 3, 0, 1, 5) if self.f_first else (2, 4, 0, 1, 3, 5))
        return array.reshape(2 * self.rank_rows, -1)

    def down_to(self, array):
        if self.windows:
            return array
        inner = (self.count, 2, 2) if self.f_first else (2, 2, self.count)
        array = array.reshape(2, self.rank_rows, *inner, self.columns)
        array = array.transpose((3, 4, 0, 2, 1, 5) if self.f_first else (2, 3, 0, 4, 1, 5))
        return array.reshape(self.down_shape())

    def blocks(self, refs, place, j):
        down, kv, small = refs
        pair, y = place // 2, place % 2
        at = j * 4 + pair if self.f_first else pair * self.count + j
        if self.windows:
            down = down.at[
                pl.ds(pl.multiple_of(y * self.rank_rows, self.rank_rows), self.rank_rows),
                pl.ds(pl.multiple_of(at * self.columns, self.columns), self.columns),
            ]
        else:
            down = down.at[place, j]
        start_row = pl.multiple_of((2 * at + y) * self.kv_rows, self.kv_rows)
        return down, kv.at[pl.ds(start_row, self.kv_rows)], small.at[place, j]

    def unit_pieces(self):
        for shard in range(8 * self.count):
            if self.f_first:
                yield shard % 8, shard // 8, shard
            else:
                yield shard // (2 * self.count) * 2 + shard % 2, shard // 2 % self.count, shard


def greet_all(count):
    f = lax.axis_index("f")
    lower, upper = f > 0, f < count - 1
    barrier = pltpu.get_barrier_semaphore()
    for bits in range(1, 8):
        pl.semaphore_signal(barrier, inc=1, device_id=other(bits))
    pl.when(lower)(lambda: pl.semaphore_signal(barrier, inc=1, device_id={"f": f - 1}))
    pl.when(upper)(lambda: pl.semaphore_signal(barrier, inc=1, device_id={"f": f + 1}))
    pl.semaphore_wait(barrier, 7 + lower.astype(jnp.int32) + upper.astype(jnp.int32))
    return lower, upper


FAR_FIRST = (7, 6, 5, 4, 3, 2, 1)


def as_place(bits):
    return (bits & 4) + 2 * (bits & 1) + (bits >> 1 & 1)


def start_kernel(
    parcel, chunks, units, padded, down_ref, kv_ref, small_ref, head_ref, out_ref, ff_ref, gate_ref, up_ref, rows_ref,
    down_all, kv_all, small_all, head_all, out_all, ff_all, wide_all, rows_all,
    down_low, kv_low, head_low, out_low, ff_low, wide_ref,
    local_sem, line_send, line_recv, plane_send, plane_recv, wide_send, wide_recv, rows_send, rows_recv,
    head_send, head_recv, far_send, far_recv,
):
    count = parcel.count
    f, me = lax.axis_index("f"), in_plane()
    lower, upper = greet_all(count)
    own = (down_low, kv_low, small_ref)
    alls = (down_all, kv_all, small_all)
    down_low[...] = down_ref[...].astype(BF16)
    kv_low[...] = kv_ref[...].astype(BF16)
    head_low[...] = head_ref[...].astype(BF16)
    out_low[...] = out_ref[...].astype(BF16)
    ff_low[...] = ff_ref[...].astype(BF16)

    half = count // 2
    y = lax.axis_index("y")

    def head_blocks(j):
        kept = (j // half == y).astype(jnp.int32)
        spare = (1 - kept) * (2 * half + j % half)
        return (
            head_all.at[kept * (j % half) + spare],
            out_all.at[kept * (2 * (j % half) + y) + spare],
            ff_all.at[j],
        )

    def head_hop(j, up, sources, group):
        return [
            send(
                sources[i], head_blocks(j)[i], head_send.at[i, 0 if up else 1, j], head_recv.at[i, j],
                {"f": f + 1 if up else f - 1},
            )
            for i in group
        ]

    def across(slot, sources):
        targets = (head_all.at[half + slot], out_all.at[2 * slot + y])
        return [
            send(source, target, far_send.at[i, slot], far_recv.at[i, slot], other(Y_BIT))
            for i, (source, target) in enumerate(zip(sources, targets))
        ]

    heads, ff = (0, 1), (2,)

    def head_own(group):
        pl.when(upper)(lambda: begin(head_hop(f, True, own_heads, group)))
        pl.when(lower)(lambda: begin(head_hop(f, False, own_heads, group)))
        if group == heads:
            pl.when(f // half != y)(lambda: begin(across(f % half, own_heads)))

    def head_step(step, group):
        @pl.when(f - step >= 0)
        def _():
            j = f - step
            blocks = head_blocks(j)
            arrive(head_hop(j, True, blocks, group))
            pl.when(upper)(lambda: begin(head_hop(j, True, blocks, group)))
            if group == heads:
                pl.when(j // half != y)(lambda: begin(across(j % half, blocks)))

        @pl.when(f + step <= count - 1)
        def _():
            j = f + step
            blocks = head_blocks(j)
            arrive(head_hop(j, False, blocks, group))
            pl.when(lower)(lambda: begin(head_hop(j, False, blocks, group)))
            if group == heads:
                pl.when(j // half != y)(lambda: begin(across(j % half, blocks)))

    own_heads = (head_low, out_low, ff_low)

    def hop(j, up, sources):
        return [
            send(
                source, target, line_send.at[i, 0 if up else 1, j], line_recv.at[i, j],
                {"f": f + 1 if up else f - 1},
            )
            for i, (source, target) in enumerate(zip(sources, parcel.blocks(alls, me, j)))
        ]

    def spread(slot, bits, j, sources):
        targets = parcel.blocks(alls, me ^ as_place(bits) ^ as_place(slot), j)
        return [
            send(source, target, plane_send.at[i, slot, j], plane_recv.at[i, slot, j], other(bits))
            for i, (source, target) in enumerate(zip(sources, targets))
        ]

    def to_plane(j, sources):
        for bits in (X_BIT, Y_BIT, C_BIT):
            begin(spread(bits, bits, j, sources))

    def line_step(step):
        @pl.when(f - step >= 0)
        def _():
            j = f - step
            blocks = parcel.blocks(alls, me, j)
            arrive(hop(j, True, blocks))
            pl.when(upper)(lambda: begin(hop(j, True, blocks)))
            to_plane(j, blocks)

        @pl.when(f + step <= count - 1)
        def _():
            j = f + step
            blocks = parcel.blocks(alls, me, j)
            arrive(hop(j, False, blocks))
            pl.when(lower)(lambda: begin(hop(j, False, blocks)))
            to_plane(j, blocks)

    def relay(j):
        by_x, by_y = parcel.blocks(alls, me ^ as_place(X_BIT), j), parcel.blocks(alls, me ^ as_place(Y_BIT), j)
        arrive(spread(X_BIT, X_BIT, j, by_x))
        pl.when(j % 2 == 0)(lambda: begin(spread(BOTH, Y_BIT, j, by_x)))
        begin(spread(X_BIT | C_BIT, C_BIT, j, by_x))
        arrive(spread(Y_BIT, Y_BIT, j, by_y))
        pl.when(j % 2 == 1)(lambda: begin(spread(BOTH, X_BIT, j, by_y)))
        begin(spread(Y_BIT | C_BIT, C_BIT, j, by_y))

    def relay_far(j):
        by_both = parcel.blocks(alls, me ^ as_place(BOTH), j)
        arrive(spread(BOTH, Y_BIT, j, by_both))
        begin(spread(BOTH | C_BIT, C_BIT, j, by_both))

    def in_order(do):
        do(f)
        for step in range(1, count):
            pl.when(f - step >= 0)(lambda: do(f - step))
            pl.when(f + step <= count - 1)(lambda: do(f + step))

    def wide(bits):
        return send(wide_ref.at[me ^ as_place(bits)], wide_all.at[me], wide_send.at[bits], wide_recv.at[bits], other(bits))

    pl.when(upper)(lambda: begin(hop(f, True, own)))
    pl.when(lower)(lambda: begin(hop(f, False, own)))
    to_plane(f, own)
    rows_own, rows_relay, rows_far, rows_arrived, rows_sent = gathering(chunks, rows_ref, rows_all, rows_send, rows_recv)
    rows_own()
    head_own(heads)
    for place, j, shard in parcel.unit_pieces():
        for first, ref in ((0, gate_ref), (padded, up_ref)):
            piece = ref[:, shard * units : (shard + 1) * units].astype(BF16)
            wide_ref[place, :, first + j * units : first + (j + 1) * units] = piece
    for first in (count * units, padded + count * units):
        size = padded - count * units
        wide_ref[:, :, first : first + size] = jnp.zeros((8, wide_ref.shape[1], size), BF16)
    for bits in FAR_FIRST:
        wide(bits).start()
    locals_ = [
        pltpu.make_async_copy(source, target, local_sem.at[i])
        for i, (source, target) in enumerate(
            (
                *zip(own, parcel.blocks(alls, me, f)),
                *zip(own_heads, head_blocks(f)),
                (wide_ref.at[me], wide_all.at[me]),
                (rows_ref, rows_all.at[pl.ds(0, rows_ref.shape[0])]),
            )
        )
    ]
    begin(locals_)
    for step in range(1, count):
        line_step(step)
        if step < count - 1:
            head_step(step, heads)
    head_own(ff)
    rows_relay(0, chunks)
    in_order(relay)
    head_step(count - 1, heads)
    head_step(1, ff)
    in_order(relay_far)
    rows_far()
    for step in range(2, count):
        head_step(step, ff)
    for copy in locals_:
        copy.wait()
    for j in range(count):
        pl.when(upper & (f >= j))(lambda: gone(hop(j, True, own)))
        pl.when(lower & (f <= j))(lambda: gone(hop(j, False, own)))
        pl.when(upper & (f >= j))(lambda: gone(head_hop(j, True, own_heads, (0, 1, 2))))
        pl.when(lower & (f <= j))(lambda: gone(head_hop(j, False, own_heads, (0, 1, 2))))
    for slot in range(half):
        arrive(across(slot, own_heads))
        gone(across(slot, own_heads))
    for slot in range(1, 8):
        for j in range(count):
            for copy in spread(slot, slot, j, own):
                if slot & C_BIT:
                    copy.wait_recv()
                copy.wait_send()
    for bits in range(1, 8):
        wide(bits).wait_recv()
        wide(bits).wait_send()
    for chip in (0, Y_BIT, X_BIT, BOTH):
        rows_arrived(chip)
    rows_sent()


def start(parcel, down, kv, small, head, out, ff, gate, up, rows, units, padded, name, chunks=4):
    count = parcel.count
    any_space, vmem = pl.BlockSpec(memory_space=pl.ANY), pl.BlockSpec(memory_space=pltpu.VMEM)
    dma = pltpu.SemaphoreType.DMA
    wide = (8, gate.shape[0], 2 * padded)
    return pl.pallas_call(
        functools.partial(start_kernel, parcel, chunks, units, padded),
        out_shape=[
            jax.ShapeDtypeStruct(parcel.down_shape(), BF16),
            jax.ShapeDtypeStruct((8 * count * kv.shape[0], kv.shape[1]), BF16),
            jax.ShapeDtypeStruct((8, count, *small.shape), BF16),
            jax.ShapeDtypeStruct((3 * count // 2, *head.shape), BF16),
            jax.ShapeDtypeStruct((3 * count // 2, *out.shape), BF16),
            jax.ShapeDtypeStruct((count, *ff.shape), BF16),
            jax.ShapeDtypeStruct(wide, BF16),
            jax.ShapeDtypeStruct((8 * rows.shape[0], rows.shape[1]), BF16),
        ],
        in_specs=[vmem] * 8 + [any_space],
        out_specs=[any_space] * 8,
        scratch_shapes=[
            pltpu.VMEM(down.shape, BF16),
            pltpu.VMEM(kv.shape, BF16),
            pltpu.VMEM(head.shape, BF16),
            pltpu.VMEM(out.shape, BF16),
            pltpu.VMEM(ff.shape, BF16),
            pltpu.VMEM(wide, BF16),
            dma((8,)),
            dma((3, 2, count)), dma((3, count)),
            dma((3, 8, count)), dma((3, 8, count)),
            dma((8,)), dma((8,)),
            dma((8, chunks)), dma((8, chunks)),
            dma((3, 2, count)), dma((3, count)),
            dma((2, count // 2)), dma((2, count // 2)),
        ],
        compiler_params=pltpu.CompilerParams(
            collective_id=name, has_side_effects=True, vmem_limit_bytes=VMEM_MOST
        ),
        cost_estimate=pl.CostEstimate(flops=0, bytes_accessed=240 * 2**20, transcendentals=0),
    )(down, kv, small, head, out, ff, gate, up, rows)


def own_back_kernel(
    back_ref, latent_ref, rms_lat_ref, gain_lat_ref, normed_ref, down_ref, kv_ref, in_ref, rms_ref, gain_ref, d_mid_ref,
    down_part, kv_part, d_in_ref, lat_sum, gain_sum, d_normed,
):
    rank = latent_ref.shape[1]
    width = in_ref.shape[1]
    step = 512
    d_lat_n, d_shared = back_ref[:, :rank], back_ref[:, rank:].astype(BF16)
    latent, rms_lat = latent_ref[...], rms_lat_ref[...]
    lat_sum[...] = jnp.sum(d_lat_n * latent * rms_lat, axis=0, keepdims=True)
    scaled = d_lat_n * gain_lat_ref[...]
    inner = jnp.sum(scaled * latent, axis=1, keepdims=True)
    d_latent = (rms_lat * scaled - latent * (rms_lat * rms_lat * rms_lat) * inner / rank).astype(BF16)

    @pl.loop(0, width // step)
    def _(i):
        at = pl.ds(pl.multiple_of(i * step, step), step)
        down_part[:, at] = contract(d_latent, normed_ref[:, at], 0, 0).astype(BF16)
        kv_part[at, :] = contract(normed_ref[:, at], d_shared, 0, 0).astype(BF16)
        d_normed[:, at] = contract(d_shared, kv_ref[at, :], 1, 1) + contract(d_latent, down_ref[:, at], 1, 0)

    inputs, rms = in_ref[...].astype(F32), rms_ref[...]
    gain_sum[...] = jnp.sum(d_normed[...] * inputs * rms, axis=0, keepdims=True)
    mean = jnp.sum(d_normed[...] * gain_ref[...] * inputs, axis=1, keepdims=True) / width
    k = d_normed[...] * gain_ref[...]
    d_in_ref[...] = (d_mid_ref[...] + rms * k - inputs * (rms * rms * rms) * mean).astype(BF16)


def own_back(back, latent, rms_lat, gain_lat, normed, down, kv, inputs, rms, gain, d_middle):
    vmem = pl.BlockSpec(memory_space=pltpu.VMEM)
    tokens, width = inputs.shape
    rank = latent.shape[1]
    return pl.pallas_call(
        own_back_kernel,
        out_shape=[
            jax.ShapeDtypeStruct((rank, width), BF16),
            jax.ShapeDtypeStruct(kv.shape, BF16),
            jax.ShapeDtypeStruct((tokens, width), BF16),
            jax.ShapeDtypeStruct((1, rank), F32),
            jax.ShapeDtypeStruct((1, width), F32),
        ],
        in_specs=[vmem] * 11,
        out_specs=[vmem] * 5,
        scratch_shapes=[pltpu.VMEM((tokens, width), F32)],
        compiler_params=pltpu.CompilerParams(vmem_limit_bytes=VMEM_MOST),
        cost_estimate=pl.CostEstimate(
            flops=4 * tokens * width * (rank + kv.shape[1]), bytes_accessed=16 * 2**20, transcendentals=0
        ),
    )(back, latent, rms_lat, gain_lat, normed, down, kv, inputs, rms, gain, d_middle)


def end_kernel(
    parcel, units, padded, down_ref, kv_ref, small_ref, wide_ref, head_ref,
    down_sum, kv_sum, small_sum, gate_sum, up_sum, head_sum, *rest,
):
    count = parcel.count
    held = [rest[8 * i : 8 * i + 8] for i in range(3)]
    head_held = (rest[24], None, None, None, *rest[25:29])
    head_got = rest[29]
    held.append(head_held)
    wide_all, near_send, near_recv, chip_send, chip_recv, line_send, line_recv, wide_send, wide_recv = rest[30:39]
    far_send, far_recv = rest[39:]
    f, me = lax.axis_index("f"), in_plane()
    lower, upper = greet_all(count)
    parts = (down_ref, kv_ref, small_ref)
    sums = (down_sum, kv_sum, small_sum, head_sum)
    chips = (BOTH, X_BIT, Y_BIT, 0)

    def rows(amount, do):
        size = amount if amount % 256 else 256

        @pl.loop(0, amount // size)
        def _(r):
            do(pl.ds(pl.multiple_of(r * size, size), size))

    def near(n, j):
        sources = parcel.blocks(parts, me ^ as_place(chips[n] | C_BIT), j)
        return [
            send(source, held[i][1].at[n, j], near_send.at[i, n, j], near_recv.at[i, n, j], other(C_BIT))
            for i, source in enumerate(sources)
        ]

    def far(step, j):
        by_x = (step != 2) == (j % 2 == 0)
        n = 0 if step == 0 else (1 if by_x else 2)
        slot = (2, 0, 1)[step]
        return [
            send(
                held[i][2].at[n, j], held[i][3].at[slot, j], chip_send.at[i, step, j], chip_recv.at[i, step, j],
                other(X_BIT if by_x else Y_BIT),
            )
            for i in range(3)
        ]

    order = []
    for j in range(count // 2):
        order += [count - 1 - j, j]

    def wide(bits):
        return send(wide_ref.at[me ^ as_place(bits)], wide_all.at[me], wide_send.at[bits], wide_recv.at[bits], other(bits))

    def hop(d, up, group):
        way = 0 if up else 1
        return [
            send(
                held[i][4 + 2 * way].at[d], held[i][5 + 2 * way].at[d],
                line_send.at[i, way, d], line_recv.at[i, way, d],
                {"f": f + 1 if up else f - 1},
            )
            for i in group
        ]

    def pass_on(d, up, group):
        way = 0 if up else 1
        behind = lower if up else upper

        @pl.when((d > f) if up else (d < f))
        def _():
            @pl.when(behind)
            def _():
                arrive(hop(d, up, group))
                for total, outgoing, incoming in ((held[i][0], held[i][4 + 2 * way], held[i][5 + 2 * way]) for i in group):

                    def add(at, total=total, outgoing=outgoing, incoming=incoming):
                        outgoing[d, at, :] = (total[d, at, :] + incoming[d, at, :].astype(F32)).astype(BF16)

                    rows(total.shape[1], add)

            @pl.when(jnp.logical_not(behind))
            def _():
                for total, outgoing in ((held[i][0], held[i][4 + 2 * way]) for i in group):

                    def keep(at, total=total, outgoing=outgoing):
                        outgoing[d, at, :] = total[d, at, :].astype(BF16)

                    rows(total.shape[1], keep)

            begin(hop(d, up, group))

    def line_step(step, group):
        pass_on(count - step, True, group)
        pass_on(step - 1, False, group)

    half = count // 2
    y = lax.axis_index("y")
    rank_rows, columns = head_got.shape[0], head_got.shape[1] // half

    def half_rows(which):
        return pl.ds(pl.multiple_of(which * rank_rows, rank_rows), rank_rows)

    swap = send(head_ref.at[half_rows(1 - y)], head_got, far_send, far_recv, other(Y_BIT))
    swap.start()
    for j in order:
        for n in range(4):
            begin(near(n, j))
    for j in order:
        for n in range(4):
            arrive(near(n, j))
            for i, source in enumerate(parcel.blocks(parts, me ^ as_place(chips[n]), j)):
                total, near_ref, chip_ref = held[i][:3]

                def add(at, n=n, j=j, source=source, total=total, near_ref=near_ref, chip_ref=chip_ref):
                    both = source[at, :].astype(F32) + near_ref[n, j, at, :].astype(F32)
                    if n < 3:
                        chip_ref[n, j, at, :] = both.astype(BF16)
                    else:
                        total[j, at, :] = both

                rows(total.shape[1], add)
            if n == 0:
                begin(far(0, j))
            if n == 2:
                begin(far(1, j))

    for j in order:
        arrive(far(0, j))
        n = 2 if j % 2 == 0 else 1
        for i in range(3):
            chip_ref, far_ref = held[i][2:4]

            def add(at, n=n, j=j, chip_ref=chip_ref, far_ref=far_ref):
                both = chip_ref[n, j, at, :].astype(F32) + far_ref[2, j, at, :].astype(F32)
                chip_ref[n, j, at, :] = both.astype(BF16)

            rows(chip_ref.shape[2], add)
        begin(far(2, j))

    for bits in FAR_FIRST:
        wide(bits).start()
    wide_all[me] = wide_ref[me]
    swap.wait_recv()
    for slot in range(half):
        at_columns = slice(slot * columns, (slot + 1) * columns)
        head_held[0][y * half + slot] = head_ref[half_rows(y), at_columns].astype(F32)
        head_held[0][(1 - y) * half + slot] = head_got[:, at_columns].astype(F32)
    pair, head = (0, 1, 2), (3,)
    line_step(1, head)
    for at_order, j in enumerate(order):
        arrive(far(1, j))
        arrive(far(2, j))
        for i in range(3):
            total, far_ref = held[i][0], held[i][3]

            def add(at, j=j, total=total, far_ref=far_ref):
                value = total[j, at, :]
                for n in range(2):
                    value = value + far_ref[n, j, at, :].astype(F32)
                total[j, at, :] = value

            rows(total.shape[1], add)
        pass_on(j, True, pair)
        pass_on(j, False, pair)
        if at_order == 1:
            for step in range(2, count):
                line_step(step, head)
    for i in range(4):

        def keep(at, i=i):
            sums[i][at, :] = held[i][0][f, at, :]

        rows(sums[i].shape[0], keep)
    for up, there in ((True, lower), (False, upper)):

        @pl.when(there)
        def _(up=up):
            arrive(hop(f, up, range(4)))
            for i in range(4):
                incoming = held[i][5 if up else 7]

                def add(at, i=i, incoming=incoming):
                    sums[i][at, :] = sums[i][at, :] + incoming[f, at, :].astype(F32)

                rows(sums[i].shape[0], add)

    for bits in range(1, 8):
        wide(bits).wait_recv()
    for place, j, shard in parcel.unit_pieces():
        for first, ref in ((0, gate_sum), (padded, up_sum)):
            piece = wide_all[place, :, first + j * units : first + (j + 1) * units]
            ref[:, shard * units : (shard + 1) * units] = piece.astype(F32)

    for d in range(count):
        pl.when(f < d)(lambda: gone(hop(d, True, range(4))))
        pl.when(f > d)(lambda: gone(hop(d, False, range(4))))
    for n in range(4):
        for j in range(count):
            for copy in near(n, j):
                copy.wait_send()
    for n in range(3):
        for j in range(count):
            gone(far(n, j))
    for bits in range(1, 8):
        wide(bits).wait_send()
    swap.wait_send()


def end(parcel, down, kv, small, wide, head, units, padded, name):
    vmem = pl.BlockSpec(memory_space=pltpu.VMEM)
    dma = pltpu.SemaphoreType.DMA
    count = parcel.count
    bodies = (
        (count, parcel.lines, 128),
        (count, parcel.kv_rows, kv.shape[1]),
        (count, *small.shape[2:]),
    )
    scratch = []
    for body in bodies:
        low = pltpu.VMEM(body, BF16)
        three = pltpu.VMEM((3, *body), BF16)
        scratch += [pltpu.VMEM(body, F32), pltpu.VMEM((4, *body), BF16), three, three, low, low, low, low]
    lines = (count, parcel.rank_rows, 2 * head.shape[1] // count)
    every = 8 * count * units
    return pl.pallas_call(
        functools.partial(end_kernel, parcel, units, padded),
        out_shape=[
            *[jax.ShapeDtypeStruct(body[1:], F32) for body in bodies],
            *[jax.ShapeDtypeStruct((wide.shape[1], every), F32)] * 2,
            jax.ShapeDtypeStruct(lines[1:], F32),
        ],
        in_specs=[vmem] * 5,
        out_specs=[vmem] * 6,
        scratch_shapes=[
            *scratch,
            pltpu.VMEM(lines, F32),
            *[pltpu.VMEM(lines, BF16)] * 4,
            pltpu.VMEM((parcel.rank_rows, head.shape[1]), BF16),
            pltpu.VMEM(wide.shape, BF16),
            dma((3, 4, count)), dma((3, 4, count)),
            dma((3, 3, count)), dma((3, 3, count)),
            dma((4, 2, count)), dma((4, 2, count)),
            dma((8,)), dma((8,)),
            dma, dma,
        ],
        compiler_params=pltpu.CompilerParams(
            collective_id=name, has_side_effects=True, vmem_limit_bytes=VMEM_MOST
        ),
        cost_estimate=pl.CostEstimate(flops=0, bytes_accessed=240 * 2**20, transcendentals=0),
    )(down, kv, small, wide, head)


def by_owner(array, axis, count, f_first):
    lead, size, tail = array.shape[:axis], array.shape[axis], array.shape[axis + 1 :]
    part = size // (8 * count)
    n = len(lead)
    rest = [*range(n), n + 4, *range(n + 5, n + 5 + len(tail))]
    if f_first:
        array = array.reshape(*lead, count, 2, 2, 2, part, *tail)
        array = array.transpose(n, n + 1, n + 2, n + 3, *rest)
    else:
        array = array.reshape(*lead, 2, 2, count, 2, part, *tail)
        array = array.transpose(n + 2, n, n + 1, n + 3, *rest)
    return array.reshape(count, 8, *lead, part, *tail)


def from_owner(array, axis, f_first):
    count, _, *body = array.shape
    lead, part, tail = body[:axis], body[axis], body[axis + 1 :]
    n = axis
    array = array.reshape(count, 2, 2, 2, *body)
    inner = (0, 1, 2, 3) if f_first else (1, 2, 0, 3)
    array = array.transpose(
        *range(4, 4 + n), *inner, 4 + n, *range(5 + n, 5 + n + len(tail))
    )
    return array.reshape(*lead, 8 * count * part, *tail)


def per_device(
    count,
    f_first,
    block_input,
    seq_lens,
    attn_gain,
    latent_down,
    latent_gain,
    latent_up,
    shared_kv,
    out_proj,
    mlp_gain,
    gate_weight,
    up_weight,
    down_weight,
    out_cotangent,
):
    tokens, width = block_input.shape
    rank = 2 * latent_down.shape[0]
    half_rank = latent_down.shape[0]
    units = down_weight.shape[0]
    mine = units * count
    padded = -(-mine // 256) * 256
    place = lax.axis_index("f")

    def rows_of(array):
        flat = array.reshape(-1)
        lines = -(-flat.shape[0] // 128)
        return jnp.pad(flat, (0, lines * 128 - flat.shape[0])).reshape(lines, 128)

    gain_high = latent_gain.astype(BF16)
    gain_low = (latent_gain - gain_high.astype(F32)).astype(BF16)
    gain_rows = attn_gain.shape[0]
    lat_lines = half_rank // 128
    small = jnp.concatenate(
        [
            rows_of(gain_high),
            rows_of(gain_low),
            rows_of(attn_gain.astype(BF16)),
            rows_of(mlp_gain.astype(BF16)),
            rows_of(seq_lens.astype(BF16)),
        ]
    )
    at_gain = 2 * lat_lines
    small = jnp.pad(small, ((0, -small.shape[0] % 16), (0, 0)))
    parcel = Parcel(count, f_first, half_rank, latent_down.shape[1], shared_kv.shape[0])
    down_full, kv_full, small, heads, out_full, ff_down, both, g_all = start(
        parcel,
        latent_down.reshape(-1, 128),
        shared_kv,
        small,
        latent_up,
        out_proj,
        down_weight,
        gate_weight,
        up_weight,
        out_cotangent,
        units,
        padded,
        0,
    )
    down_full = parcel.down_from(down_full)

    half = count // 2
    per_head = count // 4
    if per_head > 1:
        heads = heads[: 2 * half].reshape(2, 2, per_head, half_rank, -1).transpose(0, 1, 3, 2, 4)
        heads = heads.reshape(4, half_rank, HEAD_DIM)
    out_full = out_full.reshape(-1, width)

    both = lax.all_gather(both, "f", axis=0)
    both = from_owner(both, 0, f_first)
    ff_down = ff_down.reshape(mine, width)

    gain_lat = small[:2, 0, :lat_lines].astype(F32) + small[:2, 0, lat_lines:at_gain].astype(F32)
    gain_lat = gain_lat.reshape(rank)
    by_line = small.transpose(1, 0, 2, 3)
    gain_one = from_owner(by_line[:, :, at_gain, :gain_rows], 0, f_first).astype(F32)
    gain_two = from_owner(by_line[:, :, at_gain + 1, :gain_rows], 0, f_first).astype(F32)
    lengths = lax.dynamic_index_in_dim(small[:, :, at_gain + 2, :3], place, 1, keepdims=False)
    lengths = jnp.stack(
        [lax.dynamic_index_in_dim(lengths, in_plane() ^ as_place(i), 0, keepdims=False) for i in range(8)]
    ).astype(jnp.int32)

    inputs = block_input.astype(F32)
    rms_one = lax.rsqrt(jnp.mean(inputs * inputs, axis=-1, keepdims=True) + EPS)
    normed = (inputs * rms_one * gain_one).astype(BF16)
    latent = contract(normed, down_full, 1, 1)
    rms_lat = lax.rsqrt(jnp.mean(latent * latent, axis=-1, keepdims=True) + EPS)
    latent_n = (latent * rms_lat * gain_lat).astype(BF16)
    shared = jnp.dot(normed, kv_full, preferred_element_type=F32)
    position, begins = layout(lengths, tokens)
    cosine, sine = rope_tables(position.reshape(-1), HEAD_DIM)
    k_own = rotate(shared, cosine[:tokens], sine[:tokens]).astype(BF16)

    rows_all = plane_gather(jnp.concatenate([latent_n, k_own, shared.astype(BF16)], axis=1), 1)
    begins = begins.reshape(-1, 1)
    branch, q_rot, lse, attended = attention(rows_all, heads, out_full, cosine, sine, begins, 2)

    middle = inputs + branch
    rms_two = lax.rsqrt(jnp.mean(middle * middle, axis=-1, keepdims=True) + EPS)
    normed_two = (middle * rms_two * gain_two).astype(BF16)
    two_all, hidden, d_both, result, chip_sums = feed(normed_two, g_all, both, ff_down, padded, 3)
    down_grad = contract(hidden, g_all, 0, 0)[:mine].reshape(count, units, width).astype(BF16)
    d_both, down_grad, chip_sums = lax.optimization_barrier((d_both, down_grad, chip_sums))
    down_grad = lax.psum_scatter(down_grad, "f", scatter_dimension=0).astype(F32)
    d_two, both_grad, arrived = product_scatter(d_both, both, two_all, chip_sums, 4)
    farthest = lax.ppermute(chip_sums[2], ("x", "y"), DIAGONAL)
    both_grad = by_owner(both_grad, 0, count, f_first)
    both_grad = lax.psum_scatter(both_grad, "f", scatter_dimension=0)

    upstream = out_cotangent.astype(F32)
    gain_two_part = jnp.sum(d_two * middle * rms_two, axis=0)
    scaled_two = d_two * gain_two
    d_middle = (
        upstream
        + rms_two * scaled_two
        - middle * (rms_two**3) * jnp.mean(scaled_two * middle, axis=-1, keepdims=True)
    )

    d_branch, out_grad = branch_gather(d_middle.astype(BF16), attended, 5)
    back, d_queries, up_grad_part, out_grad = attention_back(
        d_branch, rows_all, heads, out_full, cosine, sine, begins, q_rot, lse, out_grad, count, 6
    )
    down_part, kv_part, input_grad, gain_lat_part, gain_one_part = own_back(
        back, latent, rms_lat, gain_lat[None], normed, down_full, kv_full, block_input, rms_one, gain_one[None], d_middle
    )
    gain_one_part = gain_one_part.reshape(width)
    out_grad = after(out_grad, both_grad, down_grad, gain_one_part)
    out_proj_grad = lax.psum_scatter(out_grad, "f", scatter_dimension=0).astype(F32)

    nearer = middle + result + arrived[0].astype(F32) + arrived[1].astype(F32)
    down_part, nearer = lax.optimization_barrier((down_part, nearer))
    down_part = parcel.down_to(down_part)

    def gain_rows_of(part):
        part = by_owner(part.astype(BF16), 0, count, f_first).transpose(1, 0, 2)
        return jnp.pad(part, ((0, 0), (0, 0), (0, 128 - gain_rows)))[:, :, None]

    lat_rows = jnp.broadcast_to(
        gain_lat_part.astype(BF16).reshape(1, 2, 1, lat_lines, 128), (4, 2, count, lat_lines, 128)
    )
    small_part = jnp.concatenate(
        [
            lat_rows.reshape(8, count, lat_lines, 128),
            gain_rows_of(gain_one_part),
            gain_rows_of(gain_two_part),
        ],
        axis=2,
    )
    small_part = jnp.pad(small_part, ((0, 0), (0, 0), (0, -small_part.shape[2] % 16), (0, 0)))
    latent_down_grad, shared_kv_grad, small_sum, gate_grad, up_grad, latent_up_grad = end(
        parcel, down_part, kv_part, small_part, both_grad, up_grad_part, units, padded, 7
    )
    latent_down_grad = latent_down_grad.reshape(latent_down.shape)
    latent_gain_grad = small_sum[:lat_lines].reshape(half_rank)
    attn_gain_grad = small_sum[lat_lines, :gain_rows]
    mlp_gain_grad = small_sum[lat_lines + 1, :gain_rows]
    farthest = after(farthest, small_sum).astype(F32)
    block_output = (nearer + farthest).astype(BF16)
    return (
        block_output,
        input_grad,
        attn_gain_grad,
        latent_down_grad,
        latent_gain_grad,
        latent_up_grad,
        shared_kv_grad,
        out_proj_grad,
        mlp_gain_grad,
        gate_grad,
        up_grad,
        down_grad,
    )


def solution(mesh):
    devices = mesh.devices
    split = devices.shape[0]
    count = split // 4
    f_first = split == HEADS
    if f_first:
        names, sizes = ("f", "x", "c", "y"), (count, 2, 2, 2)
    else:
        names, sizes = ("x", "c", "f", "y"), (2, 2, count, 2)
    fine = Mesh(devices.reshape(sizes), names)
    dp = names[:3]
    return jax.shard_map(
        functools.partial(per_device, count, f_first),
        mesh=fine,
        in_specs=(
            P(names, None),
            P(names, None),
            P(names),
            P("y", dp),
            P("y"),
            P("y", dp),
            P(names, None),
            P(names, None),
            P(names),
            P(names, None),
            P(names, None),
            P(names, None),
            P(names, None),
        ),
        out_specs=(
            P(names, None),
            P(names, None),
            P(names),
            P("y", dp),
            P("y"),
            P("y", dp),
            P(names, None),
            P(names, None),
            P(names),
            P(names, None),
            P(names, None),
            P(names, None),
        ),
        check_vma=False,
    )
```
